32 devices in a mesh: areal: 16 (over z, y, x), layer: 2 (over core).
Axes of the slice: x: 2, y: 2, z: 4, core: 2. Of those that a mesh axis runs over, the one named last changes fastest.
Arguments:
- rhs: bfloat16 [16, 4, 112, 384], P('areal', 'layer'), may hold values from -6 to 6
- areal_blocks: bfloat16 [16, 4, 6, 384, 384], P('areal', 'layer'), may hold values from -0.078125 to 0.078125
- vertical_blocks: bfloat16 [16, 4, 2, 384, 384], P('areal', 'layer'), may hold values from -0.078125 to 0.078125
- conn_src: int32 [16, 2, 6], P('areal', 'layer'), may hold values from 0 to 31, as said below
- conn_count: int32 [16, 2], P('areal', 'layer'), may hold values from 1 to 6, as said below
- tile_map: int32 [32], replicated, may hold values from 0 to 31, as said below
- well_cells: int32 [16, 4, 4], P('areal', 'layer'), may hold values from 0 to 127
- well_gain: float32 [16, 4, 4], P('areal', 'layer'), may hold values from -24 to 24
- sens: float32 [16, 4, 3, 128], P('areal', 'layer'), may hold values from -6 to 6
- basis: bfloat16 [16, 4, 128, 256], P('areal', 'layer'), may hold values from -0.0625 to 0.0625
Outputs:
- adjoint: bfloat16 [16, 4, 112, 384], P('areal', 'layer')
- coefficients: bfloat16 [112, 256], P('layer', 'areal')
The draws below stay inside these ranges and needn't reach their ends.
Inputs may be any that keep to these rules, and one draw needn't show every extreme that they name: Tile t of a layer group's plane is held by device column tile_map[t] // 2 in tile layer 2 g + tile_map[t] % 2; each value is held by one tile. `conn_src`: the 6 sources of device column c lie, in some order, on the 6 device columns (c + k) mod 16 with k one of 1 to 2, their negatives, 8 and 9, one on each. `conn_count`: the live connections of a device are its first ones. `well_cells`: cells of a tile, repeats allowed.
All inputs are finite; a program needn't handle non-finite values.
Results may differ from the reference program's by a relative error of at most 0.02.
Values may be sent and summed in bfloat16 or wider, within the bound.
No kernel may reach another device: no remote copies, remote signals or barrier semaphores. Data moves between devices by JAX's collectives and lax.ppermute only.
A program may use at most 64 MiB of HBM per device.

```python
import jax
import jax.numpy as jnp
from jax import lax

CELLS = 128
PHASES = 3
UNKNOWNS = 384
MODES = 256
RHS = 112
NS = 6
WELLS = 4
ITERS = 3
COLUMNS = 16
GROUPS = 2
LAYERS = 4


def common_map(key):
    return jax.random.permutation(jax.random.fold_in(key, 7), 2 * COLUMNS).astype(jnp.int32)


def draw_tile_map(key, part):
    return common_map(key)


def draw_conn_src(key, part):
    placed = common_map(key)
    holder = jnp.argsort(placed, stable=True).astype(jnp.int32)
    half = NS // 2 - 1
    reach = jnp.arange(1, half + 1, dtype=jnp.int32)
    far_reach = jnp.array([COLUMNS // 2, COLUMNS // 2 + 1], dtype=jnp.int32)
    deltas = jnp.concatenate([reach, -reach, far_reach]).astype(jnp.int32)
    keys = jax.random.split(jax.random.fold_in(key, 13), COLUMNS * GROUPS)
    order = jax.vmap(lambda one: jax.random.permutation(one, NS))(keys)
    offsets = deltas[order.reshape(COLUMNS, GROUPS, NS).astype(jnp.int32)]
    column = jnp.arange(COLUMNS, dtype=jnp.int32)[:, None, None]
    peer = (column + offsets + COLUMNS) % COLUMNS
    slot = jax.random.randint(jax.random.fold_in(key, 17), (COLUMNS, GROUPS, NS), 0, 2).astype(jnp.int32)
    return holder[peer * 2 + slot].astype(jnp.int32)


def draw_conn_count(key, part):
    total = COLUMNS * GROUPS
    counts = jax.random.randint(jax.random.fold_in(key, 19), (total,), 1, NS + 1).astype(jnp.int32)
    first = jax.random.randint(jax.random.fold_in(key, 23), (), 0, total).astype(jnp.int32)
    second = (first + 1 + jax.random.randint(jax.random.fold_in(key, 29), (), 0, total - 1).astype(jnp.int32)) % total
    spots = jnp.arange(total, dtype=jnp.int32)
    counts = jnp.where(spots == first, NS, jnp.where(spots == second, 1, counts))
    return counts.reshape(COLUMNS, GROUPS).astype(jnp.int32)


def touch_ends(values, key, least, largest):
    spot = [jax.random.randint(jax.random.fold_in(key, axis), (), 0, length) for axis, length in enumerate(values.shape)]
    widest = values.shape.index(max(values.shape))
    next_to = spot[:widest] + [(spot[widest] + 1) % values.shape[widest]] + spot[widest + 1:]
    return values.at[tuple(spot)].set(least).at[tuple(next_to)].set(largest)


def steps_of(own_key, dims, cuts, low, high):
    def one(axis_at, blocks):
        steps = jax.random.uniform(jax.random.fold_in(jax.random.fold_in(own_key, 6), axis_at), (blocks,), jnp.float32, low / len(cuts), high / len(cuts))
        return jnp.repeat(jnp.exp(steps), dims[axis_at] // blocks).reshape((-1,) + (1,) * (len(dims) - axis_at - 1))

    loudness = one(*cuts[0])
    for cut in cuts[1:]:
        loudness = loudness * one(*cut)
    return loudness


def gaussian(own_key, shape, deviation, bound, cuts=(), held_as=jnp.bfloat16):
    values = deviation * jax.random.normal(own_key, shape, jnp.float32)
    if cuts:
        values = values * steps_of(own_key, shape, cuts, -0.22, 0.18)
    return jnp.clip(values, -bound, bound).astype(held_as)


def setup_inputs(seed: int = 0) -> dict:
    splits = jax.random.split(jax.random.key(seed), 11)
    rhs = gaussian(splits[0], (COLUMNS, LAYERS, RHS, UNKNOWNS), 1.0, 6.0, ((0, 16), (1, 2)))
    areal_blocks = gaussian(splits[1], (COLUMNS, LAYERS, NS, UNKNOWNS, UNKNOWNS), (2 * UNKNOWNS * (NS + 2)) ** -0.5, 0.078125, ((0, 16), (1, 2)))
    vertical_blocks = gaussian(splits[2], (COLUMNS, LAYERS, 2, UNKNOWNS, UNKNOWNS), (2 * UNKNOWNS * (NS + 2)) ** -0.5, 0.078125, ((0, 16), (1, 2)))
    conn_src = draw_conn_src(jax.random.fold_in(splits[10], 71), 0)
    conn_count = draw_conn_count(jax.random.fold_in(splits[10], 71), 0)
    tile_map = draw_tile_map(jax.random.fold_in(splits[10], 71), 0)
    well_cells = touch_ends(jax.random.randint(splits[6], (COLUMNS, LAYERS, WELLS), 0, CELLS), jax.random.fold_in(splits[6], 1), 0, CELLS - 1).astype(jnp.int32)
    well_gain = gaussian(splits[7], (COLUMNS, LAYERS, WELLS), 4.0, 24.0, ((0, 16), (1, 2)), jnp.float32)
    sens = gaussian(splits[8], (COLUMNS, LAYERS, PHASES, CELLS), 1.0, 6.0, ((0, 16), (1, 2)), jnp.float32)
    basis = gaussian(splits[9], (COLUMNS, LAYERS, CELLS, MODES), (CELLS * LAYERS * COLUMNS) ** -0.5, 0.0625, ((0, 16), (1, 2)))
    return dict(rhs=rhs, areal_blocks=areal_blocks, vertical_blocks=vertical_blocks, conn_src=conn_src, conn_count=conn_count, tile_map=tile_map, well_cells=well_cells, well_gain=well_gain, sens=sens, basis=basis)


def apply_once(lam, rhs, areal_blocks, vertical_blocks, peer, slot, live):
    zero = jnp.zeros_like(lam[:, :1])
    below = jnp.concatenate([zero, lam[:, :-1]], axis=1)
    above = jnp.concatenate([lam[:, 1:], zero], axis=1)
    layer_pos = 2 * jnp.arange(GROUPS, dtype=jnp.int32)

    def per_column(column):
        peer_col = peer[column]
        slot_col = slot[column]
        chosen = lam[peer_col, layer_pos[:, None] + slot_col]
        chosen = jnp.where(live[column][:, :, None, None], chosen, jnp.zeros_like(chosen))
        blocks = areal_blocks[column].reshape(GROUPS, 2, NS, UNKNOWNS, UNKNOWNS)
        areal = jnp.einsum("gsru,gdsuv->gdrv", chosen.astype(jnp.float32), blocks.astype(jnp.float32))
        areal = areal.reshape(LAYERS, RHS, UNKNOWNS)
        vblocks = vertical_blocks[column].astype(jnp.float32)
        vert = jnp.einsum("jru,juv->jrv", below[column].astype(jnp.float32), vblocks[:, 0])
        vert = vert + jnp.einsum("jru,juv->jrv", above[column].astype(jnp.float32), vblocks[:, 1])
        return areal + vert

    off = lax.map(per_column, jnp.arange(COLUMNS, dtype=jnp.int32))
    return (rhs.astype(jnp.float32) - off).astype(jnp.bfloat16)


def reference(rhs, areal_blocks, vertical_blocks, conn_src, conn_count, tile_map, well_cells, well_gain, sens, basis):
    place = tile_map[conn_src]
    peer = place // 2
    slot = place % 2
    live = jnp.arange(NS, dtype=jnp.int32)[None, None, :] < conn_count[:, :, None]
    lam = rhs
    for step in range(ITERS):
        lam = apply_once(lam, rhs, areal_blocks, vertical_blocks, peer, slot, live)
    lamf = lam.astype(jnp.float32).reshape(COLUMNS, LAYERS, RHS, PHASES, CELLS)
    grad = jnp.sum(lamf * sens[:, :, None, :, :], axis=3)
    hits = well_cells[:, :, :, None] == jnp.arange(CELLS, dtype=jnp.int32)[None, None, None, :]
    well_sum = jnp.sum(jnp.where(hits, well_gain[:, :, :, None], 0.0), axis=2)
    grad = (grad + well_sum[:, :, None, :] * lamf[:, :, :, 0, :]).astype(jnp.bfloat16)
    coefficients = jnp.einsum("ajrc,ajcm->rm", grad.astype(jnp.float32), basis.astype(jnp.float32))
    return lam, coefficients.astype(jnp.bfloat16)
```

```python
import jax
import jax.numpy as jnp
from jax import lax
from jax.sharding import PartitionSpec as P

ITERS = 3


def column_steps(count, columns):
    near = list(range(1, count // 2))
    return near + [-k for k in near] + [columns // 2, columns // 2 + 1]


def exchange_layers(lam):
    groups = lax.axis_size("layer")
    if groups == 2:
        mine = lax.axis_index("layer")
        sent = jnp.where(mine == 0, lam[1], lam[0])
        other = lax.ppermute(sent, "layer", [(0, 1), (1, 0)])
        zero = jnp.zeros_like(other)
        return jnp.where(mine == 0, zero, other), jnp.where(mine == 0, other, zero)
    up = [(i, i + 1) for i in range(groups - 1)]
    down = [(i + 1, i) for i in range(groups - 1)]
    return lax.ppermute(lam[1], "layer", up), lax.ppermute(lam[0], "layer", down)


def on_device(
    rhs,
    areal_blocks,
    vertical_blocks,
    conn_src,
    conn_count,
    tile_map,
    well_cells,
    well_gain,
    sens,
    basis,
):
    columns = lax.axis_size("areal")
    groups = lax.axis_size("layer")
    me = lax.axis_index("areal")
    cells = sens.shape[-1]
    phases = sens.shape[-2]
    rows = rhs.shape[2]
    modes = basis.shape[-1]
    count = conn_src.shape[-1]
    steps = column_steps(count, columns)

    place = jnp.take(tile_map, conn_src[0, 0])
    peer = place // 2
    slot = place % 2
    live = jnp.arange(count, dtype=jnp.int32) < conn_count[0, 0]
    source_of_step = (me + jnp.array(steps, dtype=jnp.int32)) % columns
    step_of_conn = jnp.argmax(peer[:, None] == source_of_step[None, :], axis=1)
    asked = jnp.sum(
        jnp.where(peer[:, None] == jnp.arange(columns, dtype=jnp.int32)[None, :], slot[:, None], 0),
        axis=0,
    )
    wanted = lax.all_to_all(asked, "areal", 0, 0, tiled=True)

    blocks = areal_blocks[0]
    vert_blocks = vertical_blocks[0]
    rhs_float = rhs[0].astype(jnp.float32)
    lam = rhs[0]
    for step in range(ITERS):
        below, above = exchange_layers(lam)
        arrived = []
        for k in steps[::-1]:
            slot_sent = lax.dynamic_index_in_dim(wanted, (me - k) % columns, keepdims=False)
            tile = lax.dynamic_index_in_dim(lam, slot_sent, keepdims=False)
            pairs = [(i, (i - k) % columns) for i in range(columns)]
            arrived.append(lax.ppermute(tile, "areal", pairs))
        near = jnp.stack([jnp.stack([below, lam[1]]), jnp.stack([lam[0], above])])
        off = jnp.einsum(
            "dkru,dkuv->drv", near, vert_blocks, preferred_element_type=jnp.float32
        )
        chosen = jnp.take(jnp.stack(arrived[::-1]), step_of_conn, axis=0)
        chosen = jnp.where(live[:, None, None], chosen, jnp.zeros_like(chosen))
        off = off + jnp.einsum(
            "sru,dsuv->drv", chosen, blocks, preferred_element_type=jnp.float32
        )
        lam = (rhs_float - off).astype(jnp.bfloat16)

    lamf = lam.astype(jnp.float32).reshape(2, rows, phases, cells)
    grad = jnp.sum(lamf * sens[0][:, None, :, :], axis=2)
    hits = well_cells[0][:, :, None] == jnp.arange(cells, dtype=jnp.int32)[None, None, :]
    well_sum = jnp.sum(jnp.where(hits, well_gain[0][:, :, None], 0.0), axis=1)
    grad = (grad + well_sum[:, None, :] * lamf[:, :, 0, :]).astype(jnp.bfloat16)
    partial = jnp.einsum("jrc,jcm->mr", grad, basis[0], preferred_element_type=jnp.float32)
    partial = partial.reshape(columns, modes // columns, groups, rows // groups)
    partial = partial.transpose(0, 2, 1, 3).reshape(
        columns * groups, modes // columns, rows // groups
    )
    pieces = lax.all_to_all(partial, ("areal", "layer"), 0, 0, tiled=True)
    coefficients = jnp.sum(pieces, axis=0).T
    return (lam[None], coefficients.astype(jnp.bfloat16))


def solution(mesh):
    in_specs = (
        P("areal", "layer", None, None),
        P("areal", "layer", None, None, None),
        P("areal", "layer", None, None, None),
        P("areal", "layer", None),
        P("areal", "layer"),
        P(),
        P("areal", "layer", None),
        P("areal", "layer", None),
        P("areal", "layer", None, None),
        P("areal", "layer", None, None),
    )
    out_specs = (P("areal", "layer", None, None), P("layer", "areal"))
    return jax.shard_map(
        on_device, mesh=mesh, in_specs=in_specs, out_specs=out_specs, check_vma=False
    )
```

```python
import functools

import jax
import jax.numpy as jnp
from jax import lax
from jax.experimental import pallas as pl
from jax.experimental.pallas import tpu as pltpu
from jax.sharding import PartitionSpec as P

ITERS = 3
F32 = jnp.float32
BF16 = jnp.bfloat16
SMEM = pl.BlockSpec(memory_space=pltpu.SMEM)
VMEM = pl.BlockSpec(memory_space=pltpu.VMEM)
LIMIT = 32 * 1024 * 1024


def near_steps(count):
    near = list(range(1, count // 2))
    return near + [-k for k in near]


def far_steps(columns):
    return [columns // 2, columns // 2 + 1]


def held(x):
    return pltpu.with_memory_space_constraint(x, pltpu.VMEM)


def dot(a, b):
    return jnp.dot(a, b, preferred_element_type=F32)


def plan_kernel(columns, steps, src, count, tile_map, me, meta, *asks):
    number = len(steps)
    conn = [0] * number
    slots = [0] * number
    for s in range(number):
        place = tile_map[src[s]]
        peer = lax.shift_right_logical(place, 1)
        slot = lax.bitwise_and(place, 1)
        away = peer - me[0]
        away = jnp.where(away < 0, away + columns, away)
        for i, k in enumerate(steps):
            hit = away == k % columns
            conn[i] = jnp.where(hit, s, conn[i])
            slots[i] = jnp.where(hit, slot, slots[i])
    for i in range(number):
        meta[i] = conn[i]
        meta[number + i] = slots[i]
        meta[2 * number + i] = jnp.where(conn[i] < count[0], 1, 0)
        asks[i][...] = jnp.full(asks[i].shape, slots[i], jnp.int32).astype(F32)


def pick_kernel(number, rhs, *refs):
    wanted, sends = refs[:number], refs[number:]
    low, high = rhs[0].astype(F32), rhs[1].astype(F32)
    for mask, send in zip(wanted, sends):
        send[...] = jnp.where(mask[0:1, :] > 0.5, high, low).astype(BF16)


def own_kernel(lam, rhs, vert, part):
    part[0] = rhs[0].astype(F32) - dot(lam[1], vert[0, 1])
    part[1] = rhs[1].astype(F32) - dot(lam[0], vert[1, 0])


def gather_rows(number, pairs, meta, arrived, joined):
    width = arrived[0].shape[-1]
    for i in range(number):
        tile = arrived[i][meta[number + i]] if pairs[i] else arrived[i][...]
        tile = jnp.where(meta[2 * number + i] > 0, tile, jnp.zeros_like(tile))
        at = pl.multiple_of(meta[i] * width, 128)
        joined[:, pl.ds(at, width)] = tile


def updated(number, pairs, two, paired, meta, group, part, blocks, vert, arrived, beside, joined, total):
    gather_rows(number, pairs, meta, arrived, joined)
    rows = joined[...]
    depth, width = rows.shape[1], blocks.shape[-1]
    for d in range(2):
        total[d] = part[d] - dot(rows, blocks[d].reshape(depth, width))
    if two:
        mine = group[0]
        d = 1 - mine
        other = beside[0][mine] if paired else beside[0][...]
        total[d] = total[d] - dot(other, vert[d, d])
    else:
        for d in range(2):
            other = beside[d][1 - d] if paired else beside[d][...]
            total[d] = total[d] - dot(other, vert[d, d])


def apply_kernel(number, pairs, two, paired, meta, group, part, blocks, vert, *refs):
    sides = 1 if two else 2
    arrived, refs = refs[:number], refs[number:]
    beside, refs = refs[:sides], refs[sides:]
    wanted, refs = refs[:number], refs[number:]
    lam, sends, refs = refs[0], refs[1 : 1 + number], refs[1 + number :]
    outer, (joined, total) = refs[:sides], refs[sides:]
    updated(number, pairs, two, paired, meta, group, part, blocks, vert, arrived, beside, joined, total)
    low, high = total[0], total[1]
    lam[0] = low.astype(BF16)
    lam[1] = high.astype(BF16)
    for mask, send in zip(wanted, sends):
        send[...] = jnp.where(mask[0:1, :] > 0.5, high, low).astype(BF16)
    if two:
        outer[0][...] = jnp.where(group[0] == 0, high, low).astype(BF16)
    else:
        outer[0][...] = high.astype(BF16)
        outer[1][...] = low.astype(BF16)


def last_kernel(number, pairs, two, paired, columns, groups, meta, group, wells, gains, part, blocks, vert, sens, basis, *refs):
    sides = 1 if two else 2
    arrived, refs = refs[:number], refs[number:]
    beside, refs = refs[:sides], refs[sides:]
    lam, pieces, joined, total = refs
    updated(number, pairs, two, paired, meta, group, part, blocks, vert, arrived, beside, joined, total)
    cells = sens.shape[-1]
    phases = sens.shape[-2]
    spot = lax.broadcasted_iota(jnp.int32, (1, cells), 1)
    projected = None
    for d in range(2):
        rounded = total[d].astype(BF16)
        lam[d] = rounded
        back = rounded.astype(F32)
        well = jnp.zeros((1, cells), F32)
        for w in range(wells.shape[1]):
            well = well + jnp.where(spot == wells[d, w], gains[d, w], 0.0)
        grad = back[:, :cells] * (sens[d, 0:1, :] + well)
        for p in range(1, phases):
            grad = grad + back[:, p * cells : (p + 1) * cells] * sens[d, p : p + 1, :]
        term = dot(grad.astype(BF16), basis[d])
        projected = term if projected is None else projected + term
    if two:
        turned = projected.T
        modes, rows = turned.shape
        share, half = modes // columns, rows // 2
        for c in range(columns):
            top = turned[c * share : c * share + share // 2]
            low = turned[c * share + share // 2 : (c + 1) * share]
            for g in range(2):
                cut = slice(g * half, (g + 1) * half)
                pieces[2 * c + g] = jnp.concatenate([top[:, cut], low[:, cut]], axis=1)
    else:
        pieces[...] = projected


def sum_kernel(pieces, out):
    total = pieces[0]
    for i in range(1, pieces.shape[0]):
        total = total + pieces[i]
    half = total.shape[1] // 2
    joined = jnp.concatenate([total[:, :half], total[:, half:]], axis=0)
    out[...] = joined.T.astype(BF16)


def call(kernel, outs, ins, specs, scratch=(), flops=0, out_specs=None):
    return pl.pallas_call(
        kernel,
        out_shape=outs,
        in_specs=specs,
        out_specs=out_specs or [VMEM] * len(outs),
        scratch_shapes=list(scratch),
        compiler_params=pltpu.CompilerParams(vmem_limit_bytes=LIMIT),
        cost_estimate=pl.CostEstimate(flops=flops, bytes_accessed=flops // 200, transcendentals=0),
    )(*ins)


def shift(x, k):
    columns = lax.axis_size("areal")
    return held(lax.ppermute(x, "areal", [(i, (i - k) % columns) for i in range(columns)]))


def beside_layers(tiles, whole):
    groups = lax.axis_size("layer")
    if groups == 2:
        return [held(lax.ppermute(tiles[0], "layer", [(0, 1), (1, 0)]))]
    up = [(i, i + 1) for i in range(groups - 1)]
    down = [(i + 1, i) for i in range(groups - 1)]
    first, second = (tiles[0], tiles[0]) if whole else tiles
    return [held(lax.ppermute(first, "layer", up)), held(lax.ppermute(second, "layer", down))]


def on_device(
    rhs,
    areal_blocks,
    vertical_blocks,
    conn_src,
    conn_count,
    tile_map,
    well_cells,
    well_gain,
    sens,
    basis,
):
    columns = lax.axis_size("areal")
    groups = lax.axis_size("layer")
    two = groups == 2
    rows, width = rhs.shape[2:]
    modes = basis.shape[-1]
    number = conn_src.shape[-1]
    near, far = near_steps(number), far_steps(columns)
    steps = near + far
    rhs = rhs[0]
    me = lax.axis_index("areal").astype(jnp.int32).reshape(1)
    group = lax.axis_index("layer").astype(jnp.int32).reshape(1)

    tile = pltpu.VMEM((rows, width), BF16)
    pair = pltpu.VMEM((2, rows, width), BF16)
    ask = pltpu.VMEM((8, width), F32)
    part_type = pltpu.VMEM((2, rows, width), F32)
    scratch = [pltpu.VMEM((rows, number * width), BF16), pltpu.VMEM((2, rows, width), F32)]
    one = 2 * rows * width * width

    blocks = held(areal_blocks[0])
    vert = held(vertical_blocks[0])
    rhs_held = held(rhs)

    with jax.named_scope("plan"):
        meta, *asks = call(
            functools.partial(plan_kernel, columns, steps),
            [jax.ShapeDtypeStruct((3 * number,), jnp.int32)] + [ask] * number,
            (conn_src[0, 0], conn_count[0], tile_map, me),
            [SMEM] * 4,
            out_specs=[SMEM] + [VMEM] * number,
        )
        wanted = [shift(x, -k) for x, k in zip(asks, steps)]
        far_sends = call(
            functools.partial(pick_kernel, len(far)),
            [tile] * len(far),
            (rhs_held, *wanted[len(near) :]),
            [VMEM] * (1 + len(far)),
        )

    lam = rhs_held
    sends = [rhs] * len(near) + list(far_sends)
    outer = [rhs]
    pairs = [True] * len(near) + [False] * len(far)
    for step in range(ITERS):
        with jax.named_scope("apply"):
            arrived = [shift(x, k) for x, k in zip(sends, steps)]
            beside = beside_layers(outer, step == 0)
            (part,) = call(
                own_kernel, [part_type], (lam, rhs_held, vert), [VMEM] * 3, flops=2 * one
            )
            part = held(part)
            common = (number, pairs, two, step == 0)
            if step < ITERS - 1:
                lam, *rest = call(
                    functools.partial(apply_kernel, *common),
                    [pair] + [tile] * (number + len(beside)),
                    (meta, group, part, blocks, vert, *arrived, *beside, *wanted),
                    [SMEM] * 2 + [VMEM] * (3 + 2 * number + len(beside)),
                    scratch,
                    flops=2 * number * one,
                )
                lam = held(lam)
                sends, outer = rest[:number], rest[number:]
                pairs = [False] * number
            else:
                adjoint, pieces = call(
                    functools.partial(last_kernel, *common, columns, groups),
                    [
                        jax.ShapeDtypeStruct((2, rows, width), BF16),
                        pltpu.VMEM(
                            (2 * columns, modes // columns // 2, rows) if two else (rows, modes), F32
                        ),
                    ],
                    (meta, group, well_cells[0], well_gain[0], part, blocks, vert, held(sens[0]), held(basis[0]), *arrived, *beside),
                    [SMEM] * 4 + [VMEM] * (5 + number + len(beside)),
                    scratch,
                    flops=2 * number * one,
                )

    with jax.named_scope("project"):
        if two:
            landed = lax.all_to_all(pieces, ("areal", "layer"), 0, 0, tiled=True)
            (coefficients,) = call(
                sum_kernel,
                [jax.ShapeDtypeStruct((rows // 2, modes // columns), BF16)],
                (held(landed),),
                [VMEM],
            )
        else:
            cut = pieces.reshape(groups, rows // groups, columns, modes // columns)
            cut = cut.transpose(2, 0, 1, 3).reshape(columns * groups, rows // groups, modes // columns)
            landed = lax.all_to_all(cut, ("areal", "layer"), 0, 0, tiled=True)
            coefficients = jnp.sum(landed, axis=0).astype(BF16)
    return (adjoint[None], coefficients)


def solution(mesh):
    in_specs = (
        P("areal", "layer", None, None),
        P("areal", "layer", None, None, None),
        P("areal", "layer", None, None, None),
        P("areal", "layer", None),
        P("areal", "layer"),
        P(),
        P("areal", "layer", None),
        P("areal", "layer", None),
        P("areal", "layer", None, None),
        P("areal", "layer", None, None),
    )
    out_specs = (P("areal", "layer", None, None), P("layer", "areal"))
    return jax.shard_map(
        on_device, mesh=mesh, in_specs=in_specs, out_specs=out_specs, check_vma=False
    )
```

```python
import functools

import jax
import jax.numpy as jnp
from jax import lax
from jax.experimental import pallas as pl
from jax.experimental.pallas import tpu as pltpu
from jax.sharding import PartitionSpec as P

ITERS = 3
F32 = jnp.float32
BF16 = jnp.bfloat16
SMEM = pl.BlockSpec(memory_space=pltpu.SMEM)
VMEM = pl.BlockSpec(memory_space=pltpu.VMEM)
LIMIT = 32 * 1024 * 1024


def near_steps(count):
    near = list(range(1, count // 2))
    return near + [-k for k in near]


def far_steps(columns):
    return [columns // 2, columns // 2 + 1]


def held(x):
    return pltpu.with_memory_space_constraint(x, pltpu.VMEM)


def dot(a, b):
    return jnp.dot(a, b, preferred_element_type=F32)


def plan_kernel(columns, steps, near, src, count, tile_map, me, rhs, meta, payload, *asks):
    number = len(steps)
    rows = rhs.shape[1]
    conn = [0] * number
    slots = [0] * number
    for s in range(number):
        place = tile_map[src[s]]
        peer = lax.shift_right_logical(place, 1)
        slot = lax.bitwise_and(place, 1)
        away = peer - me[0]
        away = jnp.where(away < 0, away + columns, away)
        for i, k in enumerate(steps):
            hit = away == k % columns
            conn[i] = jnp.where(hit, s, conn[i])
            slots[i] = jnp.where(hit, slot, slots[i])
    line = lax.broadcasted_iota(jnp.int32, (16, rhs.shape[2]), 0)
    asked = jnp.zeros(line.shape, F32)
    for i in range(number):
        meta[i] = conn[i]
        meta[number + i] = slots[i]
        meta[2 * number + i] = jnp.where(conn[i] < count[0], 1, 0)
        asked = jnp.where(line == i, slots[i].astype(F32), asked)
    far = [i for i in range(number) if i not in near]
    for i, ask in zip(far, asks):
        ask[...] = jnp.full(ask.shape, slots[i], jnp.int32).astype(F32)
    payload[0:rows] = rhs[0]
    payload[rows : 2 * rows] = rhs[1]
    payload[2 * rows :] = asked.astype(BF16)


def load_kernel(blocks, vert, blocks_held, vert_held, sems):
    first = pltpu.make_async_copy(vert, vert_held, sems.at[0])
    second = pltpu.make_async_copy(blocks, blocks_held, sems.at[1])
    first.start()
    second.start()
    first.wait()
    second.wait()


def pick_kernel(number, payload, *refs):
    rows = refs[-1].shape[0]
    wanted, sends = refs[:number], refs[number:]
    low, high = payload[0:rows].astype(F32), payload[rows : 2 * rows].astype(F32)
    for mask, send in zip(wanted, sends):
        send[...] = jnp.where(mask[0:1, :] > 0.5, high, low).astype(BF16)


def own_kernel(lam, rhs, vert, part):
    part[0] = rhs[0].astype(F32) - dot(lam[1], vert[0, 1])
    part[1] = rhs[1].astype(F32) - dot(lam[0], vert[1, 0])


def tile_of(ref, slot, rows):
    if ref.shape[0] == rows:
        return ref[...]
    return ref[pl.ds(pl.multiple_of(slot * rows, 16), rows), :]


def updated(number, two, meta, group, part, blocks, vert, arrived, beside, joined, total):
    height, width = joined.shape[0], blocks.shape[-1]
    for i in range(number):
        tile = tile_of(arrived[i], meta[number + i], height)
        tile = jnp.where(meta[2 * number + i] > 0, tile, jnp.zeros_like(tile))
        joined[:, pl.ds(pl.multiple_of(meta[i] * width, 128), width)] = tile
    rows = joined[...]
    for d in range(2):
        total[d] = part[d] - dot(rows, blocks[d].reshape(rows.shape[1], width))
    if two:
        mine = group[0]
        d = 1 - mine
        total[d] = total[d] - dot(tile_of(beside[0], mine, height), vert[d, d])
    else:
        for d in range(2):
            total[d] = total[d] - dot(tile_of(beside[d], 1 - d, height), vert[d, d])


def apply_kernel(steps, near, two, first, meta, group, part, blocks, vert, *refs):
    number = len(steps)
    sides = 1 if two else 2
    arrived, refs = refs[:number], refs[number:]
    beside, refs = refs[:sides], refs[sides:]
    told = refs[: number - len(near)] if first else refs[:1]
    refs = refs[len(told) :]
    lam, sends, refs = refs[0], refs[1 : 1 + number], refs[1 + number :]
    outer, refs = refs[:sides], refs[sides:]
    masks, joined, total = refs if first else (told[0], *refs)
    updated(number, two, meta, group, part, blocks, vert, arrived, beside, joined, total)
    rows = joined.shape[0]
    if first:
        far = [i for i in range(number) if i not in near]
        for i, k in enumerate(steps):
            if i in near:
                source = arrived[steps.index(-k)]
                masks[i : i + 1, :] = source[2 * rows :, :].astype(F32)[i : i + 1, :]
            else:
                masks[i : i + 1, :] = told[far.index(i)][0:1, :]
    low, high = total[0], total[1]
    lam[0] = low.astype(BF16)
    lam[1] = high.astype(BF16)
    for i, send in enumerate(sends):
        send[...] = jnp.where(masks[i : i + 1, :] > 0.5, high, low).astype(BF16)
    if two:
        outer[0][...] = jnp.where(group[0] == 0, high, low).astype(BF16)
    else:
        outer[0][...] = high.astype(BF16)
        outer[1][...] = low.astype(BF16)


def last_kernel(number, two, columns, meta, group, wells, gains, part, blocks, vert, sens, basis, *refs):
    sides = 1 if two else 2
    arrived, refs = refs[:number], refs[number:]
    beside, refs = refs[:sides], refs[sides:]
    lam, pieces, joined, total = refs
    updated(number, two, meta, group, part, blocks, vert, arrived, beside, joined, total)
    phases, _, cells = sens.shape
    spot = lax.broadcasted_iota(jnp.int32, (1, cells), 1)
    projected = None
    for d in range(2):
        rounded = total[d].astype(BF16)
        lam[d] = rounded
        back = rounded.astype(F32)
        well = jnp.zeros((1, cells), F32)
        for w in range(wells.shape[1]):
            well = well + jnp.where(spot == wells[d, w], gains[d, w], 0.0)
        grad = back[:, :cells] * (sens[0, d : d + 1, :] + well)
        for p in range(1, phases):
            grad = grad + back[:, p * cells : (p + 1) * cells] * sens[p, d : d + 1, :]
        term = dot(grad.astype(BF16), basis[d])
        projected = term if projected is None else projected + term
    if two:
        turned = projected.T
        modes, rows = turned.shape
        share, half = modes // columns, rows // 2
        for c in range(columns):
            top = turned[c * share : c * share + share // 2]
            low = turned[c * share + share // 2 : (c + 1) * share]
            for g in range(2):
                cut = slice(g * half, (g + 1) * half)
                pieces[2 * c + g] = jnp.concatenate([top[:, cut], low[:, cut]], axis=1)
    else:
        pieces[...] = projected


def sum_kernel(pieces, out):
    total = pieces[0]
    for i in range(1, pieces.shape[0]):
        total = total + pieces[i]
    half = total.shape[1] // 2
    out[...] = jnp.concatenate([total[:, :half], total[:, half:]], axis=0).astype(BF16)


def call(kernel, outs, ins, specs, scratch=(), flops=0, moved=0, out_specs=None):
    return pl.pallas_call(
        kernel,
        out_shape=outs,
        in_specs=specs,
        out_specs=out_specs or [VMEM] * len(outs),
        scratch_shapes=list(scratch),
        compiler_params=pltpu.CompilerParams(vmem_limit_bytes=LIMIT),
        cost_estimate=pl.CostEstimate(
            flops=flops, bytes_accessed=moved or flops // 200, transcendentals=0
        ),
    )(*ins)


def shift(x, k):
    columns = lax.axis_size("areal")
    return held(lax.ppermute(x, "areal", [(i, (i - k) % columns) for i in range(columns)]))


def beside_layers(tiles):
    groups = lax.axis_size("layer")
    if groups == 2:
        return [held(lax.ppermute(tiles[0], "layer", [(0, 1), (1, 0)]))]
    up = [(i, i + 1) for i in range(groups - 1)]
    down = [(i + 1, i) for i in range(groups - 1)]
    return [held(lax.ppermute(tiles[0], "layer", up)), held(lax.ppermute(tiles[-1], "layer", down))]


def outside(x):
    return pltpu.with_memory_space_constraint(x, pltpu.HBM)


def on_device(
    rhs,
    areal_blocks,
    vertical_blocks,
    conn_src,
    conn_count,
    tile_map,
    well_cells,
    well_gain,
    sens,
    basis,
):
    columns = lax.axis_size("areal")
    groups = lax.axis_size("layer")
    two = groups == 2
    rows, width = rhs.shape[2:]
    modes = basis.shape[-1]
    number = conn_src.shape[-1]
    steps = far_steps(columns) + near_steps(number)
    near = list(range(2, number))
    rhs = rhs[0]
    me = lax.axis_index("areal").astype(jnp.int32).reshape(1)
    group = lax.axis_index("layer").astype(jnp.int32).reshape(1)

    tile = pltpu.VMEM((rows, width), BF16)
    pair = pltpu.VMEM((2, rows, width), BF16)
    ask = pltpu.VMEM((8, width), F32)
    part_type = pltpu.VMEM((2, rows, width), F32)
    scratch = [pltpu.VMEM((rows, number * width), BF16), pltpu.VMEM((2, rows, width), F32)]
    one = 2 * rows * width * width

    with jax.named_scope("plan"):
        meta, payload, *asks = call(
            functools.partial(plan_kernel, columns, steps, near),
            [jax.ShapeDtypeStruct((3 * number,), jnp.int32), pltpu.VMEM((2 * rows + 16, width), BF16)]
            + [ask] * 2,
            (outside(conn_src[0, 0]), conn_count[0], outside(tile_map), me, outside(rhs)),
            [SMEM] * 4 + [VMEM],
            out_specs=[SMEM] + [VMEM] * 3,
        )
        payload = held(payload)
        told = [shift(x, -k) for x, k in zip(asks, steps)]
        far_sends = call(
            functools.partial(pick_kernel, 2), [tile] * 2, (payload, *told), [VMEM] * 3
        )

    with jax.named_scope("load"):
        blocks, vert = call(
            load_kernel,
            [pltpu.VMEM(areal_blocks.shape[1:], BF16), pltpu.VMEM(vertical_blocks.shape[1:], BF16)],
            (outside(areal_blocks[0]), outside(vertical_blocks[0])),
            [pl.BlockSpec(memory_space=pltpu.HBM)] * 2,
            [pltpu.SemaphoreType.DMA((2,))],
            moved=areal_blocks.size * 2 + vertical_blocks.size * 2,
        )
        blocks, vert = held(blocks), held(vert)

    rhs_held = held(rhs)
    lam = rhs_held
    sends = list(far_sends) + [payload] * len(near)
    outer = [payload]
    for step in range(ITERS):
        with jax.named_scope("apply"):
            arrived = [shift(x, k) for x, k in zip(sends, steps)]
            beside = beside_layers(outer)
            (part,) = call(
                own_kernel, [part_type], (lam, rhs_held, vert), [VMEM] * 3, flops=2 * one
            )
            part = held(part)
            if step < ITERS - 1:
                first = step == 0
                outs = [pair] + [tile] * (number + len(beside)) + ([ask] if first else [])
                lam, *rest = call(
                    functools.partial(apply_kernel, steps, near, two, first),
                    outs,
                    (meta, group, part, blocks, vert, *arrived, *beside, *told),
                    [SMEM] * 2 + [VMEM] * (3 + number + len(beside) + len(told)),
                    scratch,
                    flops=2 * number * one,
                )
                lam = held(lam)
                if first:
                    told = [held(rest.pop())]
                sends, outer = rest[:number], rest[number:]
            else:
                adjoint, pieces = call(
                    functools.partial(last_kernel, number, two, columns),
                    [
                        jax.ShapeDtypeStruct((2, rows, width), BF16),
                        pltpu.VMEM(
                            (2 * columns, modes // columns // 2, rows) if two else (rows, modes), F32
                        ),
                    ],
                    (meta, group, well_cells[0], well_gain[0], part, blocks, vert, held(sens[0].transpose(1, 0, 2)), held(basis[0]), *arrived, *beside),
                    [SMEM] * 4 + [VMEM] * (5 + number + len(beside)),
                    scratch,
                    flops=2 * number * one,
                )

    with jax.named_scope("project"):
        if two:
            landed = lax.all_to_all(pieces, ("areal", "layer"), 0, 0, tiled=True)
            (coefficients,) = call(
                sum_kernel,
                [jax.ShapeDtypeStruct((modes // columns, rows // 2), BF16)],
                (held(landed),),
                [VMEM],
            )
            coefficients = coefficients.T
        else:
            cut = pieces.reshape(groups, rows // groups, columns, modes // columns)
            cut = cut.transpose(2, 0, 1, 3).reshape(columns * groups, rows // groups, modes // columns)
            landed = lax.all_to_all(cut, ("areal", "layer"), 0, 0, tiled=True)
            coefficients = jnp.sum(landed, axis=0).astype(BF16)
    return (adjoint[None], coefficients)


def solution(mesh):
    in_specs = (
        P("areal", "layer", None, None),
        P("areal", "layer", None, None, None),
        P("areal", "layer", None, None, None),
        P("areal", "layer", None),
        P("areal", "layer"),
        P(),
        P("areal", "layer", None),
        P("areal", "layer", None),
        P("areal", "layer", None, None),
        P("areal", "layer", None, None),
    )
    out_specs = (P("areal", "layer", None, None), P("layer", "areal"))
    return jax.shard_map(
        on_device, mesh=mesh, in_specs=in_specs, out_specs=out_specs, check_vma=False
    )
```

```python
import functools

import jax
import jax.numpy as jnp
from jax import lax
from jax.experimental import pallas as pl
from jax.experimental.pallas import tpu as pltpu
from jax.sharding import PartitionSpec as P

ITERS = 3
F32 = jnp.float32
BF16 = jnp.bfloat16
SMEM = pl.BlockSpec(memory_space=pltpu.SMEM)
VMEM = pl.BlockSpec(memory_space=pltpu.VMEM)
LIMIT = 32 * 1024 * 1024


def near_steps(count):
    near = list(range(1, count // 2))
    return near + [-k for k in near]


def far_steps(columns):
    return [columns // 2, columns // 2 + 1]


def held(x):
    return pltpu.with_memory_space_constraint(x, pltpu.VMEM)


def dot(a, b):
    return jnp.dot(a, b, preferred_element_type=F32)


def plan_kernel(columns, steps, src, count, tile_map, me, rhs, meta, payload):
    number = len(steps)
    rows = rhs.shape[0]
    conn = [0] * number
    slots = [0] * number
    for s in range(number):
        place = tile_map[src[s]]
        peer = lax.shift_right_logical(place, 1)
        slot = lax.bitwise_and(place, 1)
        away = peer - me[0]
        away = jnp.where(away < 0, away + columns, away)
        for i, k in enumerate(steps):
            hit = away == k % columns
            conn[i] = jnp.where(hit, s, conn[i])
            slots[i] = jnp.where(hit, slot, slots[i])
    line = lax.broadcasted_iota(jnp.int32, (16, rhs.shape[1]), 0)
    asked = jnp.zeros(line.shape, F32)
    for i in range(number):
        meta[i] = conn[i]
        meta[number + i] = slots[i]
        meta[2 * number + i] = jnp.where(conn[i] < count[0], 1, 0)
        asked = jnp.where(line == i, slots[i].astype(F32), asked)
    payload[0:rows] = rhs[...]
    payload[rows:] = asked.astype(BF16)


def load_kernel(blocks, vert, blocks_held, vert_held, sems):
    first = pltpu.make_async_copy(vert, vert_held, sems.at[0])
    second = pltpu.make_async_copy(blocks, blocks_held, sems.at[1])
    first.start()
    second.start()
    first.wait()
    second.wait()


def chosen(mask, low, high):
    return jnp.where(mask > 0.5, high, low).astype(BF16)


def asks_of(payload):
    return payload[payload.shape[0] - 16 :, :].astype(F32)


def pick_kernel(first, pair, told, tile):
    rows = tile.shape[0]
    mask = (asks_of(told) if first else told[...])[1:2, :]
    tile[...] = chosen(mask, pair[0:rows].astype(F32), pair[rows : 2 * rows].astype(F32))


def own_kernel(lam, rhs, vert, part):
    rows = rhs.shape[0] // 2
    part[0] = rhs[0:rows].astype(F32) - dot(lam[rows : 2 * rows], vert[0, 1])
    part[1] = rhs[rows:].astype(F32) - dot(lam[0:rows], vert[1, 0])


def tile_of(ref, slot, rows):
    if ref.shape[0] == rows:
        return ref[...]
    return ref[pl.ds(pl.multiple_of(slot * rows, 16), rows), :]


def less_sources(total, number, meta, blocks, numbered):
    rows = total[0].shape[0]
    for i, ref in numbered:
        tile = tile_of(ref, meta[number + i], rows)
        tile = jnp.where(meta[2 * number + i] > 0, tile, jnp.zeros_like(tile))
        total = [total[d] - dot(tile, blocks[d, meta[i]]) for d in range(2)]
    return total


def near_kernel(steps, two, first, meta, group, part, blocks, vert, *refs):
    number = len(steps)
    sides = 1 if two else 2
    arrived, refs = refs[: number - 2], refs[number - 2 :]
    beside, refs = refs[:sides], refs[sides:]
    total = refs[0]
    sums = less_sources([part[0], part[1]], number, meta, blocks, list(enumerate(arrived, 2)))
    total[0], total[1] = sums
    rows = total.shape[1]
    if two:
        mine = group[0]
        d = 1 - mine
        total[d] = total[d] - dot(tile_of(beside[0], mine, rows), vert[d, d])
    else:
        for d in range(2):
            total[d] = total[d] - dot(tile_of(beside[d], 1 - d, rows), vert[d, d])
    if first:
        masks = refs[1]
        for i, k in enumerate(steps):
            if i > 0:
                asking = steps.index(-1 if i == 1 else -k)
                masks[i : i + 1, :] = asks_of(arrived[asking - 2])[i : i + 1, :]


def far_kernel(steps, two, meta, group, total, blocks, pair, passed, masks, lam, *refs):
    number = len(steps)
    sends, outer = refs[: number - 2], refs[number - 2 :]
    low, high = less_sources([total[0], total[1]], number, meta, blocks, [(0, pair), (1, passed)])
    rows = low.shape[0]
    lam[0:rows] = low.astype(BF16)
    lam[rows:] = high.astype(BF16)
    for i, send in enumerate(sends, 2):
        send[...] = chosen(masks[i : i + 1, :], low, high)
    if two:
        outer[0][...] = jnp.where(group[0] == 0, high, low).astype(BF16)
    else:
        outer[0][...] = high.astype(BF16)
        outer[1][...] = low.astype(BF16)


def last_kernel(number, two, columns, meta, wells, gains, total, blocks, sens, basis, pair, passed, lam, pieces):
    sums = less_sources([total[0], total[1]], number, meta, blocks, [(0, pair), (1, passed)])
    phases, _, cells = sens.shape
    spot = lax.broadcasted_iota(jnp.int32, (1, cells), 1)
    projected = None
    for d in range(2):
        rounded = sums[d].astype(BF16)
        lam[d] = rounded
        back = rounded.astype(F32)
        well = jnp.zeros((1, cells), F32)
        for w in range(wells.shape[1]):
            well = well + jnp.where(spot == wells[d, w], gains[d, w], 0.0)
        grad = back[:, :cells] * (sens[0, d : d + 1, :] + well)
        for p in range(1, phases):
            grad = grad + back[:, p * cells : (p + 1) * cells] * sens[p, d : d + 1, :]
        term = dot(grad.astype(BF16), basis[d])
        projected = term if projected is None else projected + term
    if two:
        turned = projected.T
        modes, rows = turned.shape
        share, half = modes // columns, rows // 2
        for c in range(columns):
            top = turned[c * share : c * share + share // 2]
            low = turned[c * share + share // 2 : (c + 1) * share]
            for g in range(2):
                cut = slice(g * half, (g + 1) * half)
                pieces[2 * c + g] = jnp.concatenate([top[:, cut], low[:, cut]], axis=1)
    else:
        pieces[...] = projected


def sum_kernel(pieces, out):
    total = pieces[0]
    for i in range(1, pieces.shape[0]):
        total = total + pieces[i]
    half = total.shape[1] // 2
    out[...] = jnp.concatenate([total[:, :half], total[:, half:]], axis=0).astype(BF16)


def call(kernel, outs, ins, specs, scratch=(), flops=0, moved=0, out_specs=None):
    return pl.pallas_call(
        kernel,
        out_shape=outs,
        in_specs=specs,
        out_specs=out_specs or [VMEM] * len(outs),
        scratch_shapes=list(scratch),
        compiler_params=pltpu.CompilerParams(vmem_limit_bytes=LIMIT),
        cost_estimate=pl.CostEstimate(
            flops=flops, bytes_accessed=moved or flops // 200, transcendentals=0
        ),
    )(*ins)


def shift(x, k):
    columns = lax.axis_size("areal")
    return held(lax.ppermute(x, "areal", [(i, (i - k) % columns) for i in range(columns)]))


def beside_layers(tiles):
    groups = lax.axis_size("layer")
    if groups == 2:
        return [held(lax.ppermute(tiles[0], "layer", [(0, 1), (1, 0)]))]
    up = [(i, i + 1) for i in range(groups - 1)]
    down = [(i + 1, i) for i in range(groups - 1)]
    return [held(lax.ppermute(tiles[0], "layer", up)), held(lax.ppermute(tiles[-1], "layer", down))]


def outside(x):
    return pltpu.with_memory_space_constraint(x, pltpu.HBM)


def on_device(
    rhs,
    areal_blocks,
    vertical_blocks,
    conn_src,
    conn_count,
    tile_map,
    well_cells,
    well_gain,
    sens,
    basis,
):
    columns = lax.axis_size("areal")
    groups = lax.axis_size("layer")
    two = groups == 2
    rows, width = rhs.shape[2:]
    modes = basis.shape[-1]
    number = conn_src.shape[-1]
    steps = far_steps(columns) + near_steps(number)
    rhs = rhs[0].reshape(2 * rows, width)
    me = lax.axis_index("areal").astype(jnp.int32).reshape(1)
    group = lax.axis_index("layer").astype(jnp.int32).reshape(1)

    tile = pltpu.VMEM((rows, width), BF16)
    pair = pltpu.VMEM((2 * rows, width), BF16)
    sums = pltpu.VMEM((2, rows, width), F32)
    one = 2 * rows * width * width
    partial = functools.partial

    with jax.named_scope("plan"):
        meta, payload = call(
            partial(plan_kernel, columns, steps),
            [jax.ShapeDtypeStruct((3 * number,), jnp.int32), pltpu.VMEM((2 * rows + 16, width), BF16)],
            (outside(conn_src[0, 0]), conn_count[0], outside(tile_map), me, outside(rhs)),
            [SMEM] * 4 + [VMEM],
            out_specs=[SMEM, VMEM],
        )
        payload = held(payload)

    with jax.named_scope("load"):
        blocks, vert = call(
            load_kernel,
            [pltpu.VMEM(areal_blocks.shape[1:], BF16), pltpu.VMEM(vertical_blocks.shape[1:], BF16)],
            (outside(areal_blocks[0]), outside(vertical_blocks[0])),
            [pl.BlockSpec(memory_space=pltpu.HBM)] * 2,
            [pltpu.SemaphoreType.DMA((2,))],
            moved=areal_blocks.size * 2 + vertical_blocks.size * 2,
        )
        blocks, vert = held(blocks), held(vert)

    rhs_held = held(rhs)
    lam = rhs_held
    across = rhs
    sends = [payload] * (number - 2)
    outer = [payload]
    for step in range(ITERS):
        first = step == 0
        with jax.named_scope("apply"):
            far_pair = shift(across, steps[0])
            arrived = [shift(x, k) for x, k in zip(sends, steps[2:])]
            told = arrived[steps.index(-1) - 2] if first else masks
            (picked,) = call(partial(pick_kernel, first), [tile], (far_pair, told), [VMEM] * 2)
            passed = shift(picked, 1)
            beside = beside_layers(outer)
            (part,) = call(own_kernel, [sums], (lam, rhs_held, vert), [VMEM] * 3, flops=2 * one)
            total, *rest = call(
                partial(near_kernel, steps, two, first),
                [sums] + ([pltpu.VMEM((8, width), F32)] if first else []),
                (meta, group, held(part), blocks, vert, *arrived, *beside),
                [SMEM] * 2 + [VMEM] * (1 + number + len(beside)),
                flops=2 * (number - 1) * one,
            )
            if first:
                masks = held(rest[0])
            total = held(total)
            if step < ITERS - 1:
                lam, *rest = call(
                    partial(far_kernel, steps, two),
                    [pair] + [tile] * (number - 2 + len(beside)),
                    (meta, group, total, blocks, far_pair, passed, masks),
                    [SMEM] * 2 + [VMEM] * 5,
                    flops=4 * one,
                )
                lam = across = held(lam)
                sends, outer = rest[: number - 2], rest[number - 2 :]
            else:
                adjoint, pieces = call(
                    partial(last_kernel, number, two, columns),
                    [
                        jax.ShapeDtypeStruct((2, rows, width), BF16),
                        pltpu.VMEM(
                            (2 * columns, modes // columns // 2, rows) if two else (rows, modes), F32
                        ),
                    ],
                    (meta, well_cells[0], well_gain[0], total, blocks, held(sens[0].transpose(1, 0, 2)), held(basis[0]), far_pair, passed),
                    [SMEM] * 3 + [VMEM] * 6,
                    flops=5 * one,
                )

    with jax.named_scope("project"):
        if two:
            landed = lax.all_to_all(pieces, ("areal", "layer"), 0, 0, tiled=True)
            (coefficients,) = call(
                sum_kernel,
                [jax.ShapeDtypeStruct((modes // columns, rows // 2), BF16)],
                (held(landed),),
                [VMEM],
            )
            coefficients = coefficients.T
        else:
            cut = pieces.reshape(groups, rows // groups, columns, modes // columns)
            cut = cut.transpose(2, 0, 1, 3).reshape(columns * groups, rows // groups, modes // columns)
            landed = lax.all_to_all(cut, ("areal", "layer"), 0, 0, tiled=True)
            coefficients = jnp.sum(landed, axis=0).astype(BF16)
    return (adjoint[None], coefficients)


def solution(mesh):
    in_specs = (
        P("areal", "layer", None, None),
        P("areal", "layer", None, None, None),
        P("areal", "layer", None, None, None),
        P("areal", "layer", None),
        P("areal", "layer"),
        P(),
        P("areal", "layer", None),
        P("areal", "layer", None),
        P("areal", "layer", None, None),
        P("areal", "layer", None, None),
    )
    out_specs = (P("areal", "layer", None, None), P("layer", "areal"))
    return jax.shard_map(
        on_device, mesh=mesh, in_specs=in_specs, out_specs=out_specs, check_vma=False
    )
```

```python
import functools

import jax
import jax.numpy as jnp
from jax import lax
from jax.experimental import pallas as pl
from jax.experimental.pallas import tpu as pltpu
from jax.sharding import PartitionSpec as P

ITERS = 3
F32 = jnp.float32
BF16 = jnp.bfloat16
SMEM = pl.BlockSpec(memory_space=pltpu.SMEM)
VMEM = pl.BlockSpec(memory_space=pltpu.VMEM)
LIMIT = 32 * 1024 * 1024


def near_steps(count):
    near = list(range(1, count // 2))
    return near + [-k for k in near]


def far_steps(columns):
    return [columns // 2, columns // 2 + 1]


def held(x):
    return pltpu.with_memory_space_constraint(x, pltpu.VMEM)


def dot(a, b):
    return jnp.dot(a, b, preferred_element_type=F32)


def plan_kernel(columns, steps, src, count, tile_map, me, meta, asks):
    number = len(steps)
    conn = [0] * number
    slots = [0] * number
    for s in range(number):
        place = tile_map[src[s]]
        peer = lax.shift_right_logical(place, 1)
        slot = lax.bitwise_and(place, 1)
        away = peer - me[0]
        away = jnp.where(away < 0, away + columns, away)
        for i, k in enumerate(steps):
            hit = away == k % columns
            conn[i] = jnp.where(hit, s, conn[i])
            slots[i] = jnp.where(hit, slot, slots[i])
    line = lax.broadcasted_iota(jnp.int32, asks.shape, 0)
    asked = jnp.zeros(asks.shape, F32)
    for i in range(number):
        meta[i] = conn[i]
        meta[number + i] = slots[i]
        meta[2 * number + i] = jnp.where(conn[i] < count[0], 1, 0)
        asked = jnp.where(line == i, slots[i].astype(F32), asked)
    asks[...] = asked


def load_kernel(blocks, vert, blocks_held, vert_held, sems):
    first = pltpu.make_async_copy(vert, vert_held, sems.at[0])
    second = pltpu.make_async_copy(blocks, blocks_held, sems.at[1])
    first.start()
    second.start()
    first.wait()
    second.wait()


def chosen(mask, low, high):
    return jnp.where(mask > 0.5, high, low).astype(BF16)


def near_pick_kernel(pair, *refs):
    number = len(refs) // 2
    rows = pair.shape[0] // 2
    low, high = pair[0:rows].astype(F32), pair[rows:].astype(F32)
    for i in range(number):
        refs[number + i][...] = chosen(refs[i][i + 2 : i + 3, :], low, high)


def far_pick_kernel(pair, own, told, tile, relayed):
    rows = tile.shape[0]
    tile[...] = chosen(told[1:2, :], pair[0:rows].astype(F32), pair[rows:].astype(F32))
    line = lax.broadcasted_iota(jnp.int32, own.shape, 0)
    relayed[...] = jnp.where(line == 0, own[...], told[...])


def own_kernel(lam, rhs, vert, part):
    rows = rhs.shape[0] // 2
    part[0] = rhs[0:rows].astype(F32) - dot(lam[rows : 2 * rows], vert[0, 1])
    part[1] = rhs[rows:].astype(F32) - dot(lam[0:rows], vert[1, 0])


def tile_of(ref, slot, rows):
    if ref.shape[0] == rows:
        return ref[...]
    return ref[pl.ds(pl.multiple_of(slot * rows, 16), rows), :]


def less_sources(total, number, meta, blocks, numbered):
    rows = total[0].shape[0]
    for i, ref in numbered:
        tile = tile_of(ref, meta[number + i], rows)
        tile = jnp.where(meta[2 * number + i] > 0, tile, jnp.zeros_like(tile))
        total = [total[d] - dot(tile, blocks[d, meta[i]]) for d in range(2)]
    return total


def less_beside(total, two, group, vert, beside):
    if two:
        mine = group[0]
        term = dot(tile_of(beside[0], mine, total[0].shape[0]), vert[1 - mine, 1 - mine])
        none = jnp.zeros_like(term)
        return [
            total[0] - jnp.where(mine == 1, term, none),
            total[1] - jnp.where(mine == 0, term, none),
        ]
    return [
        total[d] - dot(tile_of(beside[d], 1 - d, total[d].shape[0]), vert[d, d]) for d in range(2)
    ]


def early_kernel(number, two, order, meta, group, part, blocks, vert, *refs):
    arrived, beside, out = refs[: len(order)], refs[len(order) : -1], refs[-1]
    sums = less_sources([part[0], part[1]], number, meta, blocks, list(zip(order, arrived)))
    if beside:
        sums = less_beside(sums, two, group, vert, beside)
    out[0], out[1] = sums


def late_kernel(number, two, order, first, meta, group, total, blocks, vert, *refs):
    sides = 0 if first else 1 if two else 2
    arrived, refs = refs[: len(order)], refs[len(order) :]
    beside, refs = refs[:sides], refs[sides:]
    sums = less_sources([total[0], total[1]], number, meta, blocks, list(zip(order, arrived)))
    if beside:
        sums = less_beside(sums, two, group, vert, beside)
    low, high = sums
    told = refs[: number - 1] if first else refs[:1]
    refs = refs[len(told) :]
    lam, sends, refs = refs[0], refs[1 : 1 + number], refs[1 + number :]
    outer, refs = refs[: 1 if two else 2], refs[1 if two else 2 :]
    masks = refs[0] if first else told[0]
    if first:
        masks[0:2, :] = told[0][0:2, :]
        for i in range(2, number):
            masks[i : i + 1, :] = told[i - 1][i : i + 1, :]
    rows = low.shape[0]
    lam[0:rows] = low.astype(BF16)
    lam[rows:] = high.astype(BF16)
    for i, send in enumerate(sends):
        send[...] = chosen(masks[i : i + 1, :], low, high)
    if two:
        outer[0][...] = jnp.where(group[0] == 0, high, low).astype(BF16)
    else:
        outer[0][...] = high.astype(BF16)
        outer[1][...] = low.astype(BF16)


def last_kernel(number, two, order, columns, meta, group, wells, gains, total, blocks, vert, sens, basis, *refs):
    arrived, beside, (lam, pieces) = refs[: len(order)], refs[len(order) : -2], refs[-2:]
    sums = less_sources([total[0], total[1]], number, meta, blocks, list(zip(order, arrived)))
    sums = less_beside(sums, two, group, vert, beside)
    phases, _, cells = sens.shape
    spot = lax.broadcasted_iota(jnp.int32, (1, cells), 1)
    projected = None
    for d in range(2):
        rounded = sums[d].astype(BF16)
        lam[d] = rounded
        back = rounded.astype(F32)
        well = jnp.zeros((1, cells), F32)
        for w in range(wells.shape[1]):
            well = well + jnp.where(spot == wells[d, w], gains[d, w], 0.0)
        grad = back[:, :cells] * (sens[0, d : d + 1, :] + well)
        for p in range(1, phases):
            grad = grad + back[:, p * cells : (p + 1) * cells] * sens[p, d : d + 1, :]
        term = dot(grad.astype(BF16), basis[d])
        projected = term if projected is None else projected + term
    if two:
        turned = projected.T
        modes, rows = turned.shape
        share, half = modes // columns, rows // 2
        for c in range(columns):
            top = turned[c * share : c * share + share // 2]
            low = turned[c * share + share // 2 : (c + 1) * share]
            for g in range(2):
                cut = slice(g * half, (g + 1) * half)
                pieces[2 * c + g] = jnp.concatenate([top[:, cut], low[:, cut]], axis=1)
    else:
        pieces[...] = projected


def sum_kernel(pieces, out):
    total = pieces[0]
    for i in range(1, pieces.shape[0]):
        total = total + pieces[i]
    half = total.shape[1] // 2
    out[...] = jnp.concatenate([total[:, :half], total[:, half:]], axis=0).astype(BF16)


def call(kernel, outs, ins, specs, scratch=(), flops=0, moved=0, out_specs=None):
    return pl.pallas_call(
        kernel,
        out_shape=outs,
        in_specs=specs,
        out_specs=out_specs or [VMEM] * len(outs),
        scratch_shapes=list(scratch),
        compiler_params=pltpu.CompilerParams(vmem_limit_bytes=LIMIT),
        cost_estimate=pl.CostEstimate(
            flops=flops, bytes_accessed=moved or flops // 200, transcendentals=0
        ),
    )(*ins)


def shift(x, k):
    columns = lax.axis_size("areal")
    return held(lax.ppermute(x, "areal", [(i, (i - k) % columns) for i in range(columns)]))


def beside_layers(tiles):
    groups = lax.axis_size("layer")
    if groups == 2:
        return [held(lax.ppermute(tiles[0], "layer", [(0, 1), (1, 0)]))]
    up = [(i, i + 1) for i in range(groups - 1)]
    down = [(i + 1, i) for i in range(groups - 1)]
    return [held(lax.ppermute(tiles[0], "layer", up)), held(lax.ppermute(tiles[-1], "layer", down))]


def outside(x):
    return pltpu.with_memory_space_constraint(x, pltpu.HBM)


def on_device(
    rhs,
    areal_blocks,
    vertical_blocks,
    conn_src,
    conn_count,
    tile_map,
    well_cells,
    well_gain,
    sens,
    basis,
):
    columns = lax.axis_size("areal")
    groups = lax.axis_size("layer")
    two = groups == 2
    rows, width = rhs.shape[2:]
    modes = basis.shape[-1]
    number = conn_src.shape[-1]
    steps = far_steps(columns) + near_steps(number)
    rhs = rhs[0].reshape(2 * rows, width)
    me = lax.axis_index("areal").astype(jnp.int32).reshape(1)
    group = lax.axis_index("layer").astype(jnp.int32).reshape(1)

    tile = pltpu.VMEM((rows, width), BF16)
    pair = pltpu.VMEM((2 * rows, width), BF16)
    sums = pltpu.VMEM((2, rows, width), F32)
    one = 2 * rows * width * width
    partial = functools.partial

    with jax.named_scope("plan"):
        far_pair = shift(rhs, steps[0])
        meta, asks = call(
            partial(plan_kernel, columns, steps),
            [jax.ShapeDtypeStruct((3 * number,), jnp.int32), pltpu.VMEM((8, width), F32)],
            (outside(conn_src[0, 0]), conn_count[0], outside(tile_map), me),
            [SMEM] * 4,
            out_specs=[SMEM, VMEM],
        )
        asks = held(asks)
        told = [shift(asks, -k) for k in steps[2:]]
        rhs_held = held(rhs)
        sends = call(near_pick_kernel, [tile] * (number - 2), (rhs_held, *told), [VMEM] * (number - 1))
        picked, relayed = call(
            far_pick_kernel,
            [tile, pltpu.VMEM((8, width), F32)],
            (far_pair, asks, told[steps.index(1) - 2]),
            [VMEM] * 3,
        )

    with jax.named_scope("load"):
        blocks, vert = call(
            load_kernel,
            [pltpu.VMEM(areal_blocks.shape[1:], BF16), pltpu.VMEM(vertical_blocks.shape[1:], BF16)],
            (outside(areal_blocks[0]), outside(vertical_blocks[0])),
            [pl.BlockSpec(memory_space=pltpu.HBM)] * 2,
            [pltpu.SemaphoreType.DMA((2,))],
            moved=areal_blocks.size * 2 + vertical_blocks.size * 2,
        )
        blocks, vert = held(blocks), held(vert)

    lam = rhs_held
    outer = [rhs]
    for step in range(ITERS):
        first = step == 0
        with jax.named_scope("apply"):
            if first:
                arrived = {i: shift(x, steps[i]) for i, x in enumerate(sends, 2)}
                arrived[0], arrived[1] = far_pair, shift(picked, 1)
                told = [shift(relayed, steps[0]), *told]
                early, late = list(range(2, number)), [0, 1]
            else:
                arrived = {i: shift(x, steps[i]) for i, x in enumerate(sends)}
                early, late = list(range(number - 1)), [number - 1]
            beside = beside_layers(outer)
            (part,) = call(own_kernel, [sums], (lam, rhs_held, vert), [VMEM] * 3, flops=2 * one)
            tiles = [arrived[i] for i in early] + (beside if first else [])
            (total,) = call(
                partial(early_kernel, number, two, early),
                [sums],
                (meta, group, held(part), blocks, vert, *tiles),
                [SMEM] * 2 + [VMEM] * (3 + len(tiles)),
                flops=2 * len(early) * one,
            )
            total = held(total)
            tiles = [arrived[i] for i in late] + ([] if first else beside)
            if step < ITERS - 1:
                lam, *rest = call(
                    partial(late_kernel, number, two, late, first),
                    [pair]
                    + [tile] * (number + len(beside))
                    + ([pltpu.VMEM((8, width), F32)] if first else []),
                    (meta, group, total, blocks, vert, *tiles, *told),
                    [SMEM] * 2 + [VMEM] * (3 + len(tiles) + len(told)),
                    flops=4 * one,
                )
                lam = held(lam)
                if first:
                    told = [held(rest.pop())]
                sends, outer = rest[:number], rest[number:]
            else:
                adjoint, pieces = call(
                    partial(last_kernel, number, two, late, columns),
                    [
                        jax.ShapeDtypeStruct((2, rows, width), BF16),
                        pltpu.VMEM(
                            (2 * columns, modes // columns // 2, rows) if two else (rows, modes), F32
                        ),
                    ],
                    (meta, group, well_cells[0], well_gain[0], total, blocks, vert, held(sens[0].transpose(1, 0, 2)), held(basis[0]), *tiles),
                    [SMEM] * 4 + [VMEM] * (5 + len(tiles)),
                    flops=5 * one,
                )

    with jax.named_scope("project"):
        if two:
            landed = lax.all_to_all(pieces, ("areal", "layer"), 0, 0, tiled=True)
            (coefficients,) = call(
                sum_kernel,
                [jax.ShapeDtypeStruct((modes // columns, rows // 2), BF16)],
                (held(landed),),
                [VMEM],
            )
            coefficients = coefficients.T
        else:
            cut = pieces.reshape(groups, rows // groups, columns, modes // columns)
            cut = cut.transpose(2, 0, 1, 3).reshape(columns * groups, rows // groups, modes // columns)
            landed = lax.all_to_all(cut, ("areal", "layer"), 0, 0, tiled=True)
            coefficients = jnp.sum(landed, axis=0).astype(BF16)
    return (adjoint[None], coefficients)


def solution(mesh):
    in_specs = (
        P("areal", "layer", None, None),
        P("areal", "layer", None, None, None),
        P("areal", "layer", None, None, None),
        P("areal", "layer", None),
        P("areal", "layer"),
        P(),
        P("areal", "layer", None),
        P("areal", "layer", None),
        P("areal", "layer", None, None),
        P("areal", "layer", None, None),
    )
    out_specs = (P("areal", "layer", None, None), P("layer", "areal"))
    return jax.shard_map(
        on_device, mesh=mesh, in_specs=in_specs, out_specs=out_specs, check_vma=False
    )
```

```python
import functools

import jax
import jax.numpy as jnp
from jax import lax
from jax.experimental import pallas as pl
from jax.experimental.pallas import tpu as pltpu
from jax.sharding import PartitionSpec as P

ITERS = 3
F32 = jnp.float32
BF16 = jnp.bfloat16
SMEM = pl.BlockSpec(memory_space=pltpu.SMEM)
VMEM = pl.BlockSpec(memory_space=pltpu.VMEM)
LIMIT = 32 * 1024 * 1024


def near_steps(count):
    return [sign * k for k in range(1, count // 2) for sign in (-1, 1)]


def far_steps(columns):
    return [columns // 2 + 1, columns // 2]


def held(x):
    return pltpu.with_memory_space_constraint(x, pltpu.VMEM)


def dot(a, b):
    return jnp.dot(a, b, preferred_element_type=F32)


def plan_kernel(columns, steps, src, count, tile_map, me, rhs, meta, payload):
    number = len(steps)
    conn = [0] * number
    slots = [0] * number
    for s in range(number):
        place = tile_map[src[s]]
        peer = lax.shift_right_logical(place, 1)
        slot = lax.bitwise_and(place, 1)
        away = peer - me[0]
        away = jnp.where(away < 0, away + columns, away)
        for i, k in enumerate(steps):
            hit = away == k % columns
            conn[i] = jnp.where(hit, s, conn[i])
            slots[i] = jnp.where(hit, slot, slots[i])
    rows = rhs.shape[0]
    line = lax.broadcasted_iota(jnp.int32, (16, rhs.shape[1]), 0)
    asked = jnp.zeros(line.shape, F32)
    for i in range(number):
        meta[i] = conn[i]
        meta[number + i] = slots[i]
        meta[2 * number + i] = jnp.where(conn[i] < count[0], 1, 0)
        asked = jnp.where(line == i, slots[i].astype(F32), asked)
    payload[0:rows] = rhs[...]
    payload[rows:] = asked.astype(BF16)


def load_kernel(blocks, vert, blocks_held, vert_held, sems):
    first = pltpu.make_async_copy(vert, vert_held, sems.at[0])
    second = pltpu.make_async_copy(blocks, blocks_held, sems.at[1])
    first.start()
    second.start()
    first.wait()
    second.wait()


def chosen(mask, low, high):
    return jnp.where(mask > 0.5, high, low).astype(BF16)


def asks_of(payload):
    return payload[payload.shape[0] - 16 :, :].astype(F32)


def far_pick_kernel(number, pair, own, told, tile, relayed):
    rows = tile.shape[0]
    mine, theirs = asks_of(own), asks_of(told)
    mask = theirs[number - 2 : number - 1, :]
    tile[...] = chosen(mask, pair[0:rows].astype(F32), pair[rows:].astype(F32))
    relayed[...] = mine[0:8, :]
    relayed[number - 2 : number - 1, :] = mask


def own_kernel(lam, rhs, vert, part):
    rows = rhs.shape[0] // 2
    part[0] = rhs[0:rows].astype(F32) - dot(lam[rows : 2 * rows], vert[0, 1])
    part[1] = rhs[rows:].astype(F32) - dot(lam[0:rows], vert[1, 0])


def tile_of(ref, slot, rows):
    if ref.shape[0] == rows:
        return ref[...]
    return ref[pl.ds(pl.multiple_of(slot * rows, 16), rows), :]


def less_sources(total, number, meta, blocks, numbered):
    rows = total[0].shape[0]
    for i, ref in numbered:
        tile = tile_of(ref, meta[number + i], rows)
        tile = jnp.where(meta[2 * number + i] > 0, tile, jnp.zeros_like(tile))
        total = [total[d] - dot(tile, blocks[d, meta[i]]) for d in range(2)]
    return total


def less_beside(total, two, group, vert, beside):
    if two:
        mine = group[0]
        term = dot(tile_of(beside[0], mine, total[0].shape[0]), vert[1 - mine, 1 - mine])
        none = jnp.zeros_like(term)
        return [
            total[0] - jnp.where(mine == 1, term, none),
            total[1] - jnp.where(mine == 0, term, none),
        ]
    return [
        total[d] - dot(tile_of(beside[d], 1 - d, total[d].shape[0]), vert[d, d]) for d in range(2)
    ]


def early_kernel(steps, two, first, meta, group, part, blocks, vert, *refs):
    near, number = len(steps) - 2, len(steps)
    arrived, refs = refs[:near], refs[near:]
    sums = less_sources([part[0], part[1]], number, meta, blocks, list(enumerate(arrived)))
    if first:
        beside, (out, masks) = refs[:-2], refs[-2:]
        sums = less_beside(sums, two, group, vert, beside)
        for i in range(near):
            asking = arrived[steps.index(-steps[i])]
            masks[i : i + 1, :] = asks_of(asking)[i : i + 1, :]
    else:
        (out,) = refs
    out[0], out[1] = sums


def late_kernel(number, two, first, meta, group, total, blocks, vert, *refs):
    sides = 0 if first else 1 if two else 2
    far, beside, refs = refs[:2], refs[2 : 2 + sides], refs[2 + sides :]
    numbered = list(enumerate(far, number - 2))
    sums = less_sources([total[0], total[1]], number, meta, blocks, numbered)
    if beside:
        sums = less_beside(sums, two, group, vert, beside)
    low, high = sums
    told, refs = refs[: 2 if first else 1], refs[2 if first else 1 :]
    lam, sends, refs = refs[0], refs[1 : 1 + number], refs[1 + number :]
    outer, refs = refs[: 1 if two else 2], refs[1 if two else 2 :]
    masks = told[0]
    if first:
        masks = refs[0]
        masks[0 : number - 2, :] = told[0][0 : number - 2, :]
        masks[number - 2 : number, :] = told[1][number - 2 : number, :]
    rows = low.shape[0]
    lam[0:rows] = low.astype(BF16)
    lam[rows:] = high.astype(BF16)
    for i, send in enumerate(sends):
        send[...] = chosen(masks[i : i + 1, :], low, high)
    if two:
        outer[0][...] = jnp.where(group[0] == 0, high, low).astype(BF16)
    else:
        outer[0][...] = high.astype(BF16)
        outer[1][...] = low.astype(BF16)


def last_kernel(number, two, columns, meta, group, wells, gains, total, blocks, vert, sens, basis, *refs):
    far, beside, (lam, pieces) = refs[:2], refs[2:-2], refs[-2:]
    numbered = list(enumerate(far, number - 2))
    sums = less_sources([total[0], total[1]], number, meta, blocks, numbered)
    sums = less_beside(sums, two, group, vert, beside)
    phases, _, cells = sens.shape
    spot = lax.broadcasted_iota(jnp.int32, (1, cells), 1)
    projected = None
    for d in range(2):
        rounded = sums[d].astype(BF16)
        lam[d] = rounded
        back = rounded.astype(F32)
        well = jnp.zeros((1, cells), F32)
        for w in range(wells.shape[1]):
            well = well + jnp.where(spot == wells[d, w], gains[d, w], 0.0)
        grad = back[:, :cells] * (sens[0, d : d + 1, :] + well)
        for p in range(1, phases):
            grad = grad + back[:, p * cells : (p + 1) * cells] * sens[p, d : d + 1, :]
        term = dot(grad.astype(BF16), basis[d])
        projected = term if projected is None else projected + term
    if two:
        turned = projected.T
        modes, rows = turned.shape
        share, half = modes // columns, rows // 2
        for c in range(columns):
            top = turned[c * share : c * share + share // 2]
            low = turned[c * share + share // 2 : (c + 1) * share]
            for g in range(2):
                cut = slice(g * half, (g + 1) * half)
                pieces[2 * c + g] = jnp.concatenate([top[:, cut], low[:, cut]], axis=1)
    else:
        pieces[...] = projected


def sum_kernel(pieces, out):
    total = pieces[0]
    for i in range(1, pieces.shape[0]):
        total = total + pieces[i]
    half = total.shape[1] // 2
    out[...] = jnp.concatenate([total[:, :half], total[:, half:]], axis=0).astype(BF16)


def call(kernel, outs, ins, specs, scratch=(), flops=0, moved=0, out_specs=None):
    return pl.pallas_call(
        kernel,
        out_shape=outs,
        in_specs=specs,
        out_specs=out_specs or [VMEM] * len(outs),
        scratch_shapes=list(scratch),
        compiler_params=pltpu.CompilerParams(vmem_limit_bytes=LIMIT),
        cost_estimate=pl.CostEstimate(
            flops=flops, bytes_accessed=moved or flops // 200, transcendentals=0
        ),
    )(*ins)


def shift(x, k):
    columns = lax.axis_size("areal")
    return held(lax.ppermute(x, "areal", [(i, (i - k) % columns) for i in range(columns)]))


def beside_layers(tiles):
    groups = lax.axis_size("layer")
    if groups == 2:
        return [held(lax.ppermute(tiles[0], "layer", [(0, 1), (1, 0)]))]
    up = [(i, i + 1) for i in range(groups - 1)]
    down = [(i + 1, i) for i in range(groups - 1)]
    return [held(lax.ppermute(tiles[0], "layer", up)), held(lax.ppermute(tiles[-1], "layer", down))]


def outside(x):
    return pltpu.with_memory_space_constraint(x, pltpu.HBM)


def on_device(
    rhs,
    areal_blocks,
    vertical_blocks,
    conn_src,
    conn_count,
    tile_map,
    well_cells,
    well_gain,
    sens,
    basis,
):
    columns = lax.axis_size("areal")
    groups = lax.axis_size("layer")
    two = groups == 2
    rows, width = rhs.shape[2:]
    modes = basis.shape[-1]
    number = conn_src.shape[-1]
    steps = near_steps(number) + far_steps(columns)
    rhs = rhs[0].reshape(2 * rows, width)
    me = lax.axis_index("areal").astype(jnp.int32).reshape(1)
    group = lax.axis_index("layer").astype(jnp.int32).reshape(1)

    tile = pltpu.VMEM((rows, width), BF16)
    pair = pltpu.VMEM((2 * rows, width), BF16)
    sums = pltpu.VMEM((2, rows, width), F32)
    one = 2 * rows * width * width
    partial = functools.partial

    with jax.named_scope("plan"):
        far_pair = shift(rhs, steps[-1])
        meta, payload = call(
            partial(plan_kernel, columns, steps),
            [jax.ShapeDtypeStruct((3 * number,), jnp.int32), pltpu.VMEM((2 * rows + 16, width), BF16)],
            (outside(conn_src[0, 0]), conn_count[0], outside(tile_map), me, outside(rhs)),
            [SMEM] * 4 + [VMEM],
            out_specs=[SMEM, VMEM],
        )
        payload = held(payload)

    with jax.named_scope("load"):
        blocks, vert = call(
            load_kernel,
            [pltpu.VMEM(areal_blocks.shape[1:], BF16), pltpu.VMEM(vertical_blocks.shape[1:], BF16)],
            (outside(areal_blocks[0]), outside(vertical_blocks[0])),
            [pl.BlockSpec(memory_space=pltpu.HBM)] * 2,
            [pltpu.SemaphoreType.DMA((2,))],
            moved=areal_blocks.size * 2 + vertical_blocks.size * 2,
        )
        blocks, vert = held(blocks), held(vert)

    rhs_held = held(rhs)
    lam = rhs_held
    sends = [payload] * (number - 2)
    outer = [payload]
    masks_type = pltpu.VMEM((8, width), F32)
    for step in range(ITERS):
        first = step == 0
        with jax.named_scope("apply"):
            arrived = [shift(x, k) for x, k in zip(sends, steps)]
            if first:
                picked, relayed = call(
                    partial(far_pick_kernel, number),
                    [tile, masks_type],
                    (far_pair, payload, arrived[steps.index(-1)]),
                    [VMEM] * 3,
                )
                arrived = [*arrived, shift(picked, 1), far_pair]
                told = shift(relayed, steps[-1])
            beside = beside_layers(outer)
            (part,) = call(own_kernel, [sums], (lam, rhs_held, vert), [VMEM] * 3, flops=2 * one)
            tiles = arrived[:-2] + (beside if first else [])
            total, *rest = call(
                partial(early_kernel, steps, two, first),
                [sums] + ([masks_type] if first else []),
                (meta, group, held(part), blocks, vert, *tiles),
                [SMEM] * 2 + [VMEM] * (3 + len(tiles)),
                flops=2 * (number - 2) * one,
            )
            total = held(total)
            told = [held(rest[0]), told] if first else [masks]
            tiles = arrived[-2:] + ([] if first else beside)
            if step < ITERS - 1:
                lam, *rest = call(
                    partial(late_kernel, number, two, first),
                    [pair] + [tile] * (number + len(beside)) + ([masks_type] if first else []),
                    (meta, group, total, blocks, vert, *tiles, *told),
                    [SMEM] * 2 + [VMEM] * (3 + len(tiles) + len(told)),
                    flops=4 * one,
                )
                lam = held(lam)
                if first:
                    masks = held(rest.pop())
                sends, outer = rest[:number], rest[number:]
            else:
                adjoint, pieces = call(
                    partial(last_kernel, number, two, columns),
                    [
                        jax.ShapeDtypeStruct((2, rows, width), BF16),
                        pltpu.VMEM(
                            (2 * columns, modes // columns // 2, rows) if two else (rows, modes), F32
                        ),
                    ],
                    (meta, group, well_cells[0], well_gain[0], total, blocks, vert, held(sens[0].transpose(1, 0, 2)), held(basis[0]), *tiles),
                    [SMEM] * 4 + [VMEM] * (5 + len(tiles)),
                    flops=5 * one,
                )

    with jax.named_scope("project"):
        if two:
            landed = lax.all_to_all(pieces, ("areal", "layer"), 0, 0, tiled=True)
            (coefficients,) = call(
                sum_kernel,
                [jax.ShapeDtypeStruct((modes // columns, rows // 2), BF16)],
                (held(landed),),
                [VMEM],
            )
            coefficients = coefficients.T
        else:
            cut = pieces.reshape(groups, rows // groups, columns, modes // columns)
            cut = cut.transpose(2, 0, 1, 3).reshape(columns * groups, rows // groups, modes // columns)
            landed = lax.all_to_all(cut, ("areal", "layer"), 0, 0, tiled=True)
            coefficients = jnp.sum(landed, axis=0).astype(BF16)
    return (adjoint[None], coefficients)


def solution(mesh):
    in_specs = (
        P("areal", "layer", None, None),
        P("areal", "layer", None, None, None),
        P("areal", "layer", None, None, None),
        P("areal", "layer", None),
        P("areal", "layer"),
        P(),
        P("areal", "layer", None),
        P("areal", "layer", None),
        P("areal", "layer", None, None),
        P("areal", "layer", None, None),
    )
    out_specs = (P("areal", "layer", None, None), P("layer", "areal"))
    return jax.shard_map(
        on_device, mesh=mesh, in_specs=in_specs, out_specs=out_specs, check_vma=False
    )
```

```python
import functools

import jax
import jax.numpy as jnp
from jax import lax
from jax.experimental import pallas as pl
from jax.experimental.pallas import tpu as pltpu
from jax.sharding import PartitionSpec as P

ITERS = 3
F32 = jnp.float32
BF16 = jnp.bfloat16
SMEM = pl.BlockSpec(memory_space=pltpu.SMEM)
VMEM = pl.BlockSpec(memory_space=pltpu.VMEM)
LIMIT = 32 * 1024 * 1024


def near_swaps(count):
    return [(k, color) for color in (1, 0) for k in range(count // 2 - 1, 0, -1)]


def swap_pairs(columns, k, color):
    return [
        (c, (c + k if (c // k) % 2 == color else c - k) % columns) for c in range(columns)
    ]


def held(x):
    return pltpu.with_memory_space_constraint(x, pltpu.VMEM)


def dot(a, b):
    return jnp.dot(a, b, preferred_element_type=F32)


def plan_kernel(columns, swaps, src, count, tile_map, me, rhs, meta, payload):
    steps = [
        jnp.where(lax.rem(lax.div(me[0], k), 2) == color, k, columns - k) for k, color in swaps
    ] + [columns // 2 + 1, columns // 2]
    number = len(steps)
    conn = [0] * number
    slots = [0] * number
    for s in range(number):
        place = tile_map[src[s]]
        peer = lax.shift_right_logical(place, 1)
        slot = lax.bitwise_and(place, 1)
        away = peer - me[0]
        away = jnp.where(away < 0, away + columns, away)
        for i, k in enumerate(steps):
            hit = away == k
            conn[i] = jnp.where(hit, s, conn[i])
            slots[i] = jnp.where(hit, slot, slots[i])
    rows = rhs.shape[0]
    line = lax.broadcasted_iota(jnp.int32, (16, rhs.shape[1]), 0)
    asked = jnp.zeros(line.shape, F32)
    for i in range(number):
        meta[i] = conn[i]
        meta[number + i] = slots[i]
        meta[2 * number + i] = jnp.where(conn[i] < count[0], 1, 0)
        asked = jnp.where(line == i, slots[i].astype(F32), asked)
    payload[0:rows] = rhs[...]
    payload[rows:] = asked.astype(BF16)


def load_kernel(blocks, vert, blocks_held, vert_held, sems):
    first = pltpu.make_async_copy(vert, vert_held, sems.at[0])
    second = pltpu.make_async_copy(blocks, blocks_held, sems.at[1])
    first.start()
    second.start()
    first.wait()
    second.wait()


def chosen(mask, low, high):
    return jnp.where(mask > 0.5, high, low).astype(BF16)


def asks_of(payload):
    return payload[payload.shape[0] - 16 :, :].astype(F32)


def far_pick_kernel(number, me, pair, own, even, odd, tile, relayed):
    rows = tile.shape[0]
    mine, theirs = asks_of(own), jnp.where(lax.rem(me[0], 2) == 0, asks_of(even), asks_of(odd))
    mask = theirs[number - 2 : number - 1, :]
    tile[...] = chosen(mask, pair[0:rows].astype(F32), pair[rows:].astype(F32))
    relayed[...] = mine[0:8, :]
    relayed[number - 2 : number - 1, :] = mask


def own_kernel(lam, rhs, vert, part):
    rows = rhs.shape[0] // 2
    part[0] = rhs[0:rows].astype(F32) - dot(lam[rows : 2 * rows], vert[0, 1])
    part[1] = rhs[rows:].astype(F32) - dot(lam[0:rows], vert[1, 0])


def tile_of(ref, slot, rows):
    if ref.shape[0] == rows:
        return ref[...]
    return ref[pl.ds(pl.multiple_of(slot * rows, 16), rows), :]


def less_sources(total, number, meta, blocks, numbered):
    rows = total[0].shape[0]
    for i, ref in numbered:
        tile = tile_of(ref, meta[number + i], rows)
        tile = jnp.where(meta[2 * number + i] > 0, tile, jnp.zeros_like(tile))
        total = [total[d] - dot(tile, blocks[d, meta[i]]) for d in range(2)]
    return total


def less_beside(total, two, group, vert, beside):
    if two:
        mine = group[0]
        term = dot(tile_of(beside[0], mine, total[0].shape[0]), vert[1 - mine, 1 - mine])
        none = jnp.zeros_like(term)
        return [
            total[0] - jnp.where(mine == 1, term, none),
            total[1] - jnp.where(mine == 0, term, none),
        ]
    return [
        total[d] - dot(tile_of(beside[d], 1 - d, total[d].shape[0]), vert[d, d]) for d in range(2)
    ]


def local_kernel(number, two, first_index, meta, group, part, blocks, vert, *refs):
    sides = 1 if two else 2
    arrived, beside, out = refs[: -sides - 1], refs[-sides - 1 : -1], refs[-1]
    numbered = list(enumerate(arrived, first_index))
    sums = less_sources([part[0], part[1]], number, meta, blocks, numbered)
    out[0], out[1] = less_beside(sums, two, group, vert, beside)


def cross_kernel(number, meta, blocks, *refs):
    arrived, out = refs[:-1], refs[-1]
    zero = jnp.zeros(out.shape[1:], F32)
    out[0], out[1] = less_sources([zero, zero], number, meta, blocks, list(enumerate(arrived)))


def far_kernel(number, meta, blocks, cross, passed, pair, out):
    numbered = list(enumerate([passed, pair], number - 2))
    out[0], out[1] = less_sources([cross[0], cross[1]], number, meta, blocks, numbered)


def update_kernel(number, two, first, group, total, far, *refs):
    low, high = total[0] + far[0], total[1] + far[1]
    count = number - 1 if first else 1
    told, refs = refs[:count], refs[count:]
    lam, sends, refs = refs[0], refs[1 : 1 + number], refs[1 + number :]
    outer, refs = refs[: 1 if two else 2], refs[1 if two else 2 :]
    masks = told[0]
    if first:
        masks = refs[0]
        for i in range(number - 2):
            masks[i : i + 1, :] = asks_of(told[i])[i : i + 1, :]
        masks[number - 2 : number, :] = told[-1][number - 2 : number, :]
    rows = low.shape[0]
    lam[0:rows] = low.astype(BF16)
    lam[rows:] = high.astype(BF16)
    for i, send in enumerate(sends):
        send[...] = chosen(masks[i : i + 1, :], low, high)
    if two:
        outer[0][...] = jnp.where(group[0] == 0, high, low).astype(BF16)
    else:
        outer[0][...] = high.astype(BF16)
        outer[1][...] = low.astype(BF16)


def last_kernel(columns, two, wells, gains, total, far, sens, basis, lam, pieces):
    sums = [total[0] + far[0], total[1] + far[1]]
    phases, _, cells = sens.shape
    spot = lax.broadcasted_iota(jnp.int32, (1, cells), 1)
    projected = None
    for d in range(2):
        rounded = sums[d].astype(BF16)
        lam[d] = rounded
        back = rounded.astype(F32)
        well = jnp.zeros((1, cells), F32)
        for w in range(wells.shape[1]):
            well = well + jnp.where(spot == wells[d, w], gains[d, w], 0.0)
        grad = back[:, :cells] * (sens[0, d : d + 1, :] + well)
        for p in range(1, phases):
            grad = grad + back[:, p * cells : (p + 1) * cells] * sens[p, d : d + 1, :]
        term = dot(grad.astype(BF16), basis[d])
        projected = term if projected is None else projected + term
    if two:
        turned = projected.T
        modes, rows = turned.shape
        share, half = modes // columns, rows // 2
        for c in range(columns):
            top = turned[c * share : c * share + share // 2]
            low = turned[c * share + share // 2 : (c + 1) * share]
            for g in range(2):
                cut = slice(g * half, (g + 1) * half)
                pieces[2 * c + g] = jnp.concatenate([top[:, cut], low[:, cut]], axis=1)
    else:
        pieces[...] = projected


def sum_kernel(pieces, out):
    total = pieces[0]
    for i in range(1, pieces.shape[0]):
        total = total + pieces[i]
    half = total.shape[1] // 2
    out[...] = jnp.concatenate([total[:, :half], total[:, half:]], axis=0).astype(BF16)


def call(kernel, outs, ins, specs, scratch=(), flops=0, moved=0, out_specs=None):
    return pl.pallas_call(
        kernel,
        out_shape=outs,
        in_specs=specs,
        out_specs=out_specs or [VMEM] * len(outs),
        scratch_shapes=list(scratch),
        compiler_params=pltpu.CompilerParams(vmem_limit_bytes=LIMIT),
        cost_estimate=pl.CostEstimate(
            flops=flops, bytes_accessed=moved or flops // 200, transcendentals=0
        ),
    )(*ins)


def moved_by(x, pairs):
    return held(lax.ppermute(x, "areal", pairs))


def shift_pairs(columns, k):
    return [(i, (i - k) % columns) for i in range(columns)]


def beside_layers(tiles):
    groups = lax.axis_size("layer")
    if groups == 2:
        return [held(lax.ppermute(tiles[0], "layer", [(0, 1), (1, 0)]))]
    up = [(i, i + 1) for i in range(groups - 1)]
    down = [(i + 1, i) for i in range(groups - 1)]
    return [held(lax.ppermute(tiles[0], "layer", up)), held(lax.ppermute(tiles[-1], "layer", down))]


def outside(x):
    return pltpu.with_memory_space_constraint(x, pltpu.HBM)


def on_device(
    rhs,
    areal_blocks,
    vertical_blocks,
    conn_src,
    conn_count,
    tile_map,
    well_cells,
    well_gain,
    sens,
    basis,
):
    columns = lax.axis_size("areal")
    groups = lax.axis_size("layer")
    two = groups == 2
    rows, width = rhs.shape[2:]
    modes = basis.shape[-1]
    number = conn_src.shape[-1]
    swaps = near_swaps(number)
    routes = [swap_pairs(columns, k, color) for k, color in swaps]
    routes += [shift_pairs(columns, columns // 2 + 1), shift_pairs(columns, columns // 2)]
    rhs = rhs[0].reshape(2 * rows, width)
    me = lax.axis_index("areal").astype(jnp.int32).reshape(1)
    group = lax.axis_index("layer").astype(jnp.int32).reshape(1)

    tile = pltpu.VMEM((rows, width), BF16)
    pair = pltpu.VMEM((2 * rows, width), BF16)
    sums = pltpu.VMEM((2, rows, width), F32)
    one = 2 * rows * width * width
    partial = functools.partial

    with jax.named_scope("plan"):
        far_pair = moved_by(rhs, routes[-1])
        meta, payload = call(
            partial(plan_kernel, columns, swaps),
            [jax.ShapeDtypeStruct((3 * number,), jnp.int32), pltpu.VMEM((2 * rows + 16, width), BF16)],
            (outside(conn_src[0, 0]), conn_count[0], outside(tile_map), me, outside(rhs)),
            [SMEM] * 4 + [VMEM],
            out_specs=[SMEM, VMEM],
        )
        payload = held(payload)

    with jax.named_scope("load"):
        blocks, vert = call(
            load_kernel,
            [pltpu.VMEM(areal_blocks.shape[1:], BF16), pltpu.VMEM(vertical_blocks.shape[1:], BF16)],
            (outside(areal_blocks[0]), outside(vertical_blocks[0])),
            [pl.BlockSpec(memory_space=pltpu.HBM)] * 2,
            [pltpu.SemaphoreType.DMA((2,))],
            moved=areal_blocks.size * 2 + vertical_blocks.size * 2,
        )
        blocks, vert = held(blocks), held(vert)

    rhs_held = held(rhs)
    lam = rhs_held
    sends = [payload] * (number - 2)
    outer = [payload]
    masks_type = pltpu.VMEM((8, width), F32)
    for step in range(ITERS):
        first = step == 0
        with jax.named_scope("apply"):
            arrived = [moved_by(x, pairs) for x, pairs in zip(sends, routes)]
            if first:
                even, odd = (arrived[swaps.index((1, color))] for color in (1, 0))
                picked, relayed = call(
                    partial(far_pick_kernel, number),
                    [tile, masks_type],
                    (me, far_pair, payload, even, odd),
                    [SMEM] + [VMEM] * 4,
                )
                arrived = [*arrived, moved_by(picked, shift_pairs(columns, 1)), far_pair]
                told = moved_by(relayed, routes[-1])
            beside = beside_layers(outer)
            (part,) = call(own_kernel, [sums], (lam, rhs_held, vert), [VMEM] * 3, flops=one)
            half = len(swaps) // 2
            tiles = arrived[half:-2] + beside
            (total,) = call(
                partial(local_kernel, number, two, half),
                [sums],
                (meta, group, held(part), blocks, vert, *tiles),
                [SMEM] * 2 + [VMEM] * (3 + len(tiles)),
                flops=one,
            )
            (cross,) = call(
                partial(cross_kernel, number),
                [sums],
                (meta, blocks, *arrived[:half]),
                [SMEM] + [VMEM] * (1 + half),
                flops=4 * one,
            )
            (far,) = call(
                partial(far_kernel, number),
                [sums],
                (meta, blocks, held(cross), *arrived[-2:]),
                [SMEM] + [VMEM] * 4,
                flops=4 * one,
            )
            total, far = held(total), held(far)
            told = [*arrived[:-2], told] if first else [masks]
            if step < ITERS - 1:
                lam, *rest = call(
                    partial(update_kernel, number, two, first),
                    [pair] + [tile] * (number + len(beside)) + ([masks_type] if first else []),
                    (group, total, far, *told),
                    [SMEM] + [VMEM] * (2 + len(told)),
                    flops=one,
                )
                lam = held(lam)
                if first:
                    masks = held(rest.pop())
                sends, outer = rest[:number], rest[number:]
            else:
                adjoint, pieces = call(
                    partial(last_kernel, columns, two),
                    [
                        jax.ShapeDtypeStruct((2, rows, width), BF16),
                        pltpu.VMEM(
                            (2 * columns, modes // columns // 2, rows) if two else (rows, modes), F32
                        ),
                    ],
                    (well_cells[0], well_gain[0], total, far, held(sens[0].transpose(1, 0, 2)), held(basis[0])),
                    [SMEM] * 2 + [VMEM] * 4,
                    flops=one,
                )

    with jax.named_scope("project"):
        if two:
            landed = lax.all_to_all(pieces, ("areal", "layer"), 0, 0, tiled=True)
            (coefficients,) = call(
                sum_kernel,
                [jax.ShapeDtypeStruct((modes // columns, rows // 2), BF16)],
                (held(landed),),
                [VMEM],
            )
            coefficients = coefficients.T
        else:
            cut = pieces.reshape(groups, rows // groups, columns, modes // columns)
            cut = cut.transpose(2, 0, 1, 3).reshape(columns * groups, rows // groups, modes // columns)
            landed = lax.all_to_all(cut, ("areal", "layer"), 0, 0, tiled=True)
            coefficients = jnp.sum(landed, axis=0).astype(BF16)
    return (adjoint[None], coefficients)


def solution(mesh):
    in_specs = (
        P("areal", "layer", None, None),
        P("areal", "layer", None, None, None),
        P("areal", "layer", None, None, None),
        P("areal", "layer", None),
        P("areal", "layer"),
        P(),
        P("areal", "layer", None),
        P("areal", "layer", None),
        P("areal", "layer", None, None),
        P("areal", "layer", None, None),
    )
    out_specs = (P("areal", "layer", None, None), P("layer", "areal"))
    return jax.shard_map(
        on_device, mesh=mesh, in_specs=in_specs, out_specs=out_specs, check_vma=False
    )
```

```python
import functools

import jax
import jax.numpy as jnp
from jax import lax
from jax.experimental import pallas as pl
from jax.experimental.pallas import tpu as pltpu
from jax.sharding import PartitionSpec as P

ITERS = 3
F32 = jnp.float32
BF16 = jnp.bfloat16
SMEM = pl.BlockSpec(memory_space=pltpu.SMEM)
VMEM = pl.BlockSpec(memory_space=pltpu.VMEM)
LIMIT = 32 * 1024 * 1024


def near_swaps(count):
    return [(k, color) for color in (1, 0) for k in range(count // 2 - 1, 0, -1)]


def swap_pairs(columns, k, color):
    return [
        (c, (c + k if (c // k) % 2 == color else c - k) % columns) for c in range(columns)
    ]


def held(x):
    return pltpu.with_memory_space_constraint(x, pltpu.VMEM)


def dot(a, b):
    return jnp.dot(a, b, preferred_element_type=F32)


def plan_kernel(columns, swaps, src, count, tile_map, me, meta, asks):
    steps = [
        jnp.where(lax.rem(lax.div(me[0], k), 2) == color, k, columns - k) for k, color in swaps
    ] + [columns // 2 + 1, columns // 2]
    number = len(steps)
    conn = [0] * number
    slots = [0] * number
    for s in range(number):
        place = tile_map[src[s]]
        peer = lax.shift_right_logical(place, 1)
        slot = lax.bitwise_and(place, 1)
        away = peer - me[0]
        away = jnp.where(away < 0, away + columns, away)
        for i, k in enumerate(steps):
            hit = away == k
            conn[i] = jnp.where(hit, s, conn[i])
            slots[i] = jnp.where(hit, slot, slots[i])
    line = lax.broadcasted_iota(jnp.int32, asks.shape, 0)
    asked = jnp.zeros(asks.shape, F32)
    for i in range(number):
        meta[i] = conn[i]
        meta[number + i] = jnp.where(conn[i] < count[0], 1, 0)
        asked = jnp.where(line == i, slots[i].astype(F32), asked)
    asks[...] = asked


def load_kernel(blocks, vert, blocks_held, vert_held, sems):
    first = pltpu.make_async_copy(vert, vert_held, sems.at[0])
    second = pltpu.make_async_copy(blocks, blocks_held, sems.at[1])
    first.start()
    second.start()
    first.wait()
    second.wait()


def pick(told, sends, low, high):
    for i, (ask, send) in enumerate(zip(told, sends)):
        mask = ask[i : i + 1, :]
        mask = jnp.concatenate([mask] * (send.shape[1] // mask.shape[1]), axis=1)
        send[...] = jnp.where(mask > 0.5, high, low).astype(BF16)


def pick_kernel(pair, *refs):
    number = len(refs) // 2
    rows = pair.shape[0] // 2
    low, high = pair[0:rows].astype(F32), pair[rows:].astype(F32)
    pick(refs[:number], refs[number:], low, high)


def own_kernel(lam, rhs, vert, part):
    rows = rhs.shape[0] // 2
    part[0] = rhs[0:rows].astype(F32) - dot(lam[rows : 2 * rows], vert[0, 1])
    part[1] = rhs[rows:].astype(F32) - dot(lam[0:rows], vert[1, 0])


def source_sums(number, meta, blocks, numbered):
    tiles, bands = [], []
    for i, ref in numbered:
        tile = ref[...]
        tiles.append(jnp.where(meta[number + i] > 0, tile, jnp.zeros_like(tile)))
        bands.append(jnp.concatenate([blocks[0, meta[i]], blocks[1, meta[i]]], axis=1))
    both = dot(jnp.concatenate(tiles, axis=1), jnp.concatenate(bands, axis=0))
    width = blocks.shape[-1]
    return both[:, :width], both[:, width:]


def tile_of(ref, slot, rows):
    if ref.shape[0] == rows:
        return ref[...]
    return ref[pl.ds(pl.multiple_of(slot * rows, 16), rows), :]


def beside_sums(two, group, vert, beside, rows):
    if two:
        mine = group[0]
        term = dot(tile_of(beside[0], mine, rows), vert[1 - mine, 1 - mine])
        none = jnp.zeros_like(term)
        return jnp.where(mine == 1, term, none), jnp.where(mine == 0, term, none)
    return [dot(tile_of(beside[d], 1 - d, rows), vert[d, d]) for d in range(2)]


def cross_kernel(number, meta, blocks, *refs):
    arrived, out = refs[:-1], refs[-1]
    out[0], out[1] = source_sums(number, meta, blocks, list(enumerate(arrived)))


def far_kernel(number, meta, blocks, cross, *refs):
    far, out = refs[:-1], refs[-1]
    low, high = source_sums(number, meta, blocks, list(enumerate(far, number - len(far))))
    out[0] = cross[0] + low
    out[1] = cross[1] + high


def updated(number, two, first_index, meta, group, part, far, blocks, vert, near, beside):
    numbered = list(enumerate(near, first_index))
    sums = source_sums(number, meta, blocks, numbered)
    terms = beside_sums(two, group, vert, beside, part.shape[1])
    return [part[d] - far[d] - sums[d] - terms[d] for d in range(2)]


def update_kernel(number, two, first_index, meta, group, part, far, blocks, vert, *refs):
    sides = 1 if two else 2
    here = number - 2 - first_index
    near, refs = refs[:here], refs[here:]
    beside, refs = refs[:sides], refs[sides:]
    told, refs = refs[:number], refs[number:]
    low, high = updated(
        number, two, first_index, meta, group, part, far, blocks, vert, near, beside
    )
    lam, sends, outer = refs[0], refs[1 : 1 + number], refs[1 + number :]
    rows = low.shape[0]
    lam[0:rows] = low.astype(BF16)
    lam[rows:] = high.astype(BF16)
    pick(told, sends, low, high)
    if two:
        outer[0][...] = jnp.where(group[0] == 0, high, low).astype(BF16)
    else:
        outer[0][...] = high.astype(BF16)
        outer[1][...] = low.astype(BF16)


def last_kernel(
    number, two, first_index, columns, meta, group, wells, gains, part, far, blocks, vert, sens, basis, *refs
):
    here = number - 2 - first_index
    near, beside, (lam, pieces) = refs[:here], refs[here:-2], refs[-2:]
    sums = updated(number, two, first_index, meta, group, part, far, blocks, vert, near, beside)
    phases, _, cells = sens.shape
    spot = lax.broadcasted_iota(jnp.int32, (1, cells), 1)
    projected = None
    for d in range(2):
        rounded = sums[d].astype(BF16)
        lam[d] = rounded
        back = rounded.astype(F32)
        well = jnp.zeros((1, cells), F32)
        for w in range(wells.shape[1]):
            well = well + jnp.where(spot == wells[d, w], gains[d, w], 0.0)
        grad = back[:, :cells] * (sens[0, d : d + 1, :] + well)
        for p in range(1, phases):
            grad = grad + back[:, p * cells : (p + 1) * cells] * sens[p, d : d + 1, :]
        term = dot(grad.astype(BF16), basis[d])
        projected = term if projected is None else projected + term
    if two:
        turned = projected.T
        modes, rows = turned.shape
        share, half = modes // columns, rows // 2
        for c in range(columns):
            top = turned[c * share : c * share + share // 2]
            low = turned[c * share + share // 2 : (c + 1) * share]
            for g in range(2):
                cut = slice(g * half, (g + 1) * half)
                pieces[2 * c + g] = jnp.concatenate([top[:, cut], low[:, cut]], axis=1)
    else:
        pieces[...] = projected


def sum_kernel(pieces, out):
    total = pieces[0]
    for i in range(1, pieces.shape[0]):
        total = total + pieces[i]
    half = total.shape[1] // 2
    out[...] = jnp.concatenate([total[:, :half], total[:, half:]], axis=0).astype(BF16)


def call(kernel, outs, ins, specs, scratch=(), flops=0, moved=0, out_specs=None):
    return pl.pallas_call(
        kernel,
        out_shape=outs,
        in_specs=specs,
        out_specs=out_specs or [VMEM] * len(outs),
        scratch_shapes=list(scratch),
        compiler_params=pltpu.CompilerParams(vmem_limit_bytes=LIMIT),
        cost_estimate=pl.CostEstimate(
            flops=flops, bytes_accessed=moved or flops // 200, transcendentals=0
        ),
    )(*ins)


def moved_by(x, pairs):
    return held(lax.ppermute(x, "areal", pairs))


def shift_pairs(columns, k):
    return [(i, (i - k) % columns) for i in range(columns)]


def beside_layers(tiles):
    groups = lax.axis_size("layer")
    if groups == 2:
        return [held(lax.ppermute(tiles[0], "layer", [(0, 1), (1, 0)]))]
    up = [(i, i + 1) for i in range(groups - 1)]
    down = [(i + 1, i) for i in range(groups - 1)]
    return [held(lax.ppermute(tiles[0], "layer", up)), held(lax.ppermute(tiles[-1], "layer", down))]


def outside(x):
    return pltpu.with_memory_space_constraint(x, pltpu.HBM)


def on_device(
    rhs,
    areal_blocks,
    vertical_blocks,
    conn_src,
    conn_count,
    tile_map,
    well_cells,
    well_gain,
    sens,
    basis,
):
    columns = lax.axis_size("areal")
    groups = lax.axis_size("layer")
    two = groups == 2
    rows, width = rhs.shape[2:]
    modes = basis.shape[-1]
    number = conn_src.shape[-1]
    swaps = near_swaps(number)
    routes = [swap_pairs(columns, k, color) for k, color in swaps]
    routes += [shift_pairs(columns, columns // 2 + 1), shift_pairs(columns, columns // 2)]
    rhs = rhs[0].reshape(2 * rows, width)
    me = lax.axis_index("areal").astype(jnp.int32).reshape(1)
    group = lax.axis_index("layer").astype(jnp.int32).reshape(1)

    tile = pltpu.VMEM((rows, width), BF16)
    pair = pltpu.VMEM((2 * rows, width), BF16)
    sums = pltpu.VMEM((2, rows, width), F32)
    one = 2 * rows * width * width
    partial = functools.partial

    with jax.named_scope("plan"):
        meta, asks = call(
            partial(plan_kernel, columns, swaps),
            [jax.ShapeDtypeStruct((2 * number,), jnp.int32), pltpu.VMEM((8, 128), F32)],
            (outside(conn_src[0, 0]), conn_count[0], outside(tile_map), me),
            [SMEM] * 4,
            out_specs=[SMEM, VMEM],
        )
        asks = held(asks)
        told = [moved_by(asks, [(to, at) for at, to in pairs]) for pairs in routes]
        rhs_held = held(rhs)
        sends = call(pick_kernel, [tile] * number, (rhs_held, *told), [VMEM] * (1 + number))

    with jax.named_scope("load"):
        blocks, vert = call(
            load_kernel,
            [pltpu.VMEM(areal_blocks.shape[1:], BF16), pltpu.VMEM(vertical_blocks.shape[1:], BF16)],
            (outside(areal_blocks[0]), outside(vertical_blocks[0])),
            [pl.BlockSpec(memory_space=pltpu.HBM)] * 2,
            [pltpu.SemaphoreType.DMA((2,))],
            moved=areal_blocks.size * 2 + vertical_blocks.size * 2,
        )
        blocks, vert = held(blocks), held(vert)

    lam = rhs_held
    outer = [rhs]
    half = len(swaps) // 2
    for step in range(ITERS):
        with jax.named_scope("apply"):
            arrived = [moved_by(x, pairs) for x, pairs in zip(sends, routes)]
            beside = beside_layers(outer)
            (part,) = call(own_kernel, [sums], (lam, rhs_held, vert), [VMEM] * 3, flops=one)
            (cross,) = call(
                partial(cross_kernel, number),
                [sums],
                (meta, blocks, *arrived[:half]),
                [SMEM] + [VMEM] * (1 + half),
                flops=4 * one,
            )
            (far,) = call(
                partial(far_kernel, number),
                [sums],
                (meta, blocks, held(cross), *arrived[-2:]),
                [SMEM] + [VMEM] * 4,
                flops=4 * one,
            )
            tiles = (held(part), held(far), blocks, vert)
            near = (*arrived[half:-2], *beside)
            if step < ITERS - 1:
                lam, *rest = call(
                    partial(update_kernel, number, two, half),
                    [pair] + [tile] * (number + len(beside)),
                    (meta, group, *tiles, *near, *told),
                    [SMEM] * 2 + [VMEM] * (4 + len(near) + number),
                    flops=one,
                )
                lam = held(lam)
                sends, outer = rest[:number], rest[number:]
            else:
                adjoint, pieces = call(
                    partial(last_kernel, number, two, half, columns),
                    [
                        jax.ShapeDtypeStruct((2, rows, width), BF16),
                        pltpu.VMEM(
                            (2 * columns, modes // columns // 2, rows) if two else (rows, modes), F32
                        ),
                    ],
                    (
                        meta,
                        group,
                        well_cells[0],
                        well_gain[0],
                        *tiles,
                        held(sens[0].transpose(1, 0, 2)),
                        held(basis[0]),
                        *near,
                    ),
                    [SMEM] * 4 + [VMEM] * (6 + len(near)),
                    flops=one,
                )

    with jax.named_scope("project"):
        if two:
            landed = lax.all_to_all(pieces, ("areal", "layer"), 0, 0, tiled=True)
            (coefficients,) = call(
                sum_kernel,
                [jax.ShapeDtypeStruct((modes // columns, rows // 2), BF16)],
                (held(landed),),
                [VMEM],
            )
            coefficients = coefficients.T
        else:
            cut = pieces.reshape(groups, rows // groups, columns, modes // columns)
            cut = cut.transpose(2, 0, 1, 3).reshape(columns * groups, rows // groups, modes // columns)
            landed = lax.all_to_all(cut, ("areal", "layer"), 0, 0, tiled=True)
            coefficients = jnp.sum(landed, axis=0).astype(BF16)
    return (adjoint[None], coefficients)


def solution(mesh):
    in_specs = (
        P("areal", "layer", None, None),
        P("areal", "layer", None, None, None),
        P("areal", "layer", None, None, None),
        P("areal", "layer", None),
        P("areal", "layer"),
        P(),
        P("areal", "layer", None),
        P("areal", "layer", None),
        P("areal", "layer", None, None),
        P("areal", "layer", None, None),
    )
    out_specs = (P("areal", "layer", None, None), P("layer", "areal"))
    return jax.shard_map(
        on_device, mesh=mesh, in_specs=in_specs, out_specs=out_specs, check_vma=False
    )
```

```python
import functools

import jax
import jax.numpy as jnp
from jax import lax
from jax.experimental import pallas as pl
from jax.experimental.pallas import tpu as pltpu
from jax.sharding import PartitionSpec as P

ITERS = 3
F32 = jnp.float32
BF16 = jnp.bfloat16
SMEM = pl.BlockSpec(memory_space=pltpu.SMEM)
VMEM = pl.BlockSpec(memory_space=pltpu.VMEM)
LIMIT = 32 * 1024 * 1024


def near_swaps(count):
    return [(k, color) for color in (1, 0) for k in range(count // 2 - 1, 0, -1)]


def swap_pairs(columns, k, color):
    return [
        (c, (c + k if (c // k) % 2 == color else c - k) % columns) for c in range(columns)
    ]


def held(x):
    return pltpu.with_memory_space_constraint(x, pltpu.VMEM)


def dot(a, b):
    return jnp.dot(a, b, preferred_element_type=F32)


def plan_kernel(columns, swaps, src, count, tile_map, me, rhs, table, asks, payload):
    steps = [
        jnp.where(lax.rem(lax.div(me[0], k), 2) == color, k, columns - k) for k, color in swaps
    ] + [columns // 2 + 1, columns // 2]
    number = len(steps)
    conn = [0] * number
    slots = [0] * number
    for s in range(number):
        place = tile_map[src[s]]
        peer = lax.shift_right_logical(place, 1)
        slot = lax.bitwise_and(place, 1)
        away = peer - me[0]
        away = jnp.where(away < 0, away + columns, away)
        for i, k in enumerate(steps):
            hit = away == k
            conn[i] = jnp.where(hit, s, conn[i])
            slots[i] = jnp.where(hit, slot, slots[i])
    rows, width = rhs.shape
    line = lax.broadcasted_iota(jnp.int32, (16, width), 0)
    asked = jnp.zeros(line.shape, F32)
    for i in range(number):
        table[i] = conn[i]
        table[number + i] = jnp.where(conn[i] < count[0], 1, 0)
        asked = jnp.where(line == i, slots[i].astype(F32), asked)
    asks[...] = asked[0:8, 0:128]
    payload[0:rows] = rhs[...]
    payload[rows:] = asked.astype(BF16)


def load_kernel(number, table, blocks, vert, bands, vert_held, sems):
    width = vert.shape[-1]
    side = pltpu.make_async_copy(vert, vert_held, sems.at[2 * number])
    side.start()

    def copies(i):
        return [
            pltpu.make_async_copy(
                blocks.at[d, table[i]],
                bands.at[i, :, pl.ds(d * width, width)],
                sems.at[2 * i + d],
            )
            for d in range(2)
        ]

    for i in range(number):

        @pl.when(table[number + i] > 0)
        def _():
            for copy in copies(i):
                copy.start()

        @pl.when(table[number + i] == 0)
        def _():
            bands[i] = jnp.zeros(bands.shape[1:], bands.dtype)

    for i in range(number):

        @pl.when(table[number + i] > 0)
        def _():
            for copy in copies(i):
                copy.wait()

    side.wait()


def wide(mask, width):
    return jnp.concatenate([mask] * (width // mask.shape[1]), axis=1)


def chosen(mask, low, high):
    return jnp.where(wide(mask, low.shape[1]) > 0.5, high, low).astype(BF16)


def asks_of(payload):
    return payload[payload.shape[0] - 16 :, 0:128].astype(F32)


def tile_of(ref, mask, rows):
    if ref.shape[0] == rows:
        return ref[...]
    return chosen(mask, ref[0:rows].astype(F32), ref[rows : 2 * rows].astype(F32))


def far_pick_kernel(number, me, pair, even, odd, told9, told8, tile, told):
    rows = tile.shape[0]
    theirs = jnp.where(lax.rem(me[0], 2) == 0, asks_of(even), asks_of(odd))
    tile[...] = tile_of(pair, theirs[number - 2 : number - 1, :], rows)
    line = lax.broadcasted_iota(jnp.int32, told.shape, 0)
    told[...] = jnp.where(line == number - 2, told9[...], told8[...])


def own_kernel(lam, rhs, vert, part):
    rows = rhs.shape[0] // 2
    part[0] = rhs[0:rows].astype(F32) - dot(lam[rows : 2 * rows], vert[0, 1])
    part[1] = rhs[rows:].astype(F32) - dot(lam[0:rows], vert[1, 0])


def source_sums(asks, bands, begin, refs, rows):
    tiles = [tile_of(ref, asks[i : i + 1, :], rows) for i, ref in enumerate(refs, begin)]
    count, width, both = len(refs), bands.shape[1], bands.shape[2]
    band = bands[begin : begin + count].reshape(count * width, both)
    sums = dot(jnp.concatenate(tiles, axis=1), band)
    return sums[:, :width], sums[:, width:]


def beside_sums(two, group, vert, beside, rows):
    def tile(ref, slot):
        if ref.shape[0] == rows:
            return ref[...]
        return ref[pl.ds(pl.multiple_of(slot * rows, 16), rows), :]

    if two:
        mine = group[0]
        term = dot(tile(beside[0], mine), vert[1 - mine, 1 - mine])
        none = jnp.zeros_like(term)
        return jnp.where(mine == 1, term, none), jnp.where(mine == 0, term, none)
    return [dot(tile(beside[d], 1 - d), vert[d, d]) for d in range(2)]


def cross_kernel(asks, bands, *refs):
    arrived, out = refs[:-1], refs[-1]
    out[0], out[1] = source_sums(asks, bands, 0, arrived, out.shape[1])


def far_kernel(asks, bands, cross, *refs):
    far, out = refs[:-1], refs[-1]
    low, high = source_sums(asks, bands, bands.shape[0] - len(far), far, out.shape[1])
    out[0] = cross[0] + low
    out[1] = cross[1] + high


def updated(two, begin, group, part, far, asks, bands, vert, near, beside):
    rows = part.shape[1]
    sums = source_sums(asks, bands, begin, near, rows)
    terms = beside_sums(two, group, vert, beside, rows)
    return [part[d] - far[d] - sums[d] - terms[d] for d in range(2)]


def update_kernel(number, two, begin, first, group, part, far, asks, bands, vert, *refs):
    sides = 1 if two else 2
    here = number - 2 - begin
    near, refs = refs[:here], refs[here:]
    beside, refs = refs[:sides], refs[sides:]
    count = number - 1 if first else 1
    told, refs = refs[:count], refs[count:]
    low, high = updated(two, begin, group, part, far, asks, bands, vert, near, beside)
    lam, sends, refs = refs[0], refs[1 : 1 + number], refs[1 + number :]
    outer, refs = refs[:sides], refs[sides:]
    masks = told[0]
    if first:
        masks = refs[0]
        masks[...] = told[-1][...]
        for i in range(number - 2):
            masks[i : i + 1, :] = asks_of(told[i])[i : i + 1, :]
    rows = low.shape[0]
    lam[0:rows] = low.astype(BF16)
    lam[rows:] = high.astype(BF16)
    for i, send in enumerate(sends):
        send[...] = chosen(masks[i : i + 1, :], low, high)
    if two:
        outer[0][...] = jnp.where(group[0] == 0, high, low).astype(BF16)
    else:
        outer[0][...] = high.astype(BF16)
        outer[1][...] = low.astype(BF16)


def last_kernel(number, two, begin, columns, group, wells, gains, part, far, asks, bands, vert, sens, basis, *refs):
    here = number - 2 - begin
    near, beside, (lam, pieces) = refs[:here], refs[here:-2], refs[-2:]
    sums = updated(two, begin, group, part, far, asks, bands, vert, near, beside)
    phases, _, cells = sens.shape
    spot = lax.broadcasted_iota(jnp.int32, (1, cells), 1)
    projected = None
    for d in range(2):
        rounded = sums[d].astype(BF16)
        lam[d] = rounded
        back = rounded.astype(F32)
        well = jnp.zeros((1, cells), F32)
        for w in range(wells.shape[1]):
            well = well + jnp.where(spot == wells[d, w], gains[d, w], 0.0)
        grad = back[:, :cells] * (sens[0, d : d + 1, :] + well)
        for p in range(1, phases):
            grad = grad + back[:, p * cells : (p + 1) * cells] * sens[p, d : d + 1, :]
        term = dot(grad.astype(BF16), basis[d])
        projected = term if projected is None else projected + term
    if two:
        turned = projected.T
        modes, rows = turned.shape
        share, half = modes // columns, rows // 2
        for c in range(columns):
            top = turned[c * share : c * share + share // 2]
            low = turned[c * share + share // 2 : (c + 1) * share]
            for g in range(2):
                cut = slice(g * half, (g + 1) * half)
                pieces[2 * c + g] = jnp.concatenate([top[:, cut], low[:, cut]], axis=1)
    else:
        pieces[...] = projected


def sum_kernel(pieces, out):
    total = pieces[0]
    for i in range(1, pieces.shape[0]):
        total = total + pieces[i]
    half = total.shape[1] // 2
    out[...] = jnp.concatenate([total[:, :half], total[:, half:]], axis=0).astype(BF16)


def call(kernel, outs, ins, specs, scratch=(), flops=0, moved=0, out_specs=None):
    return pl.pallas_call(
        kernel,
        out_shape=outs,
        in_specs=specs,
        out_specs=out_specs or [VMEM] * len(outs),
        scratch_shapes=list(scratch),
        compiler_params=pltpu.CompilerParams(vmem_limit_bytes=LIMIT),
        cost_estimate=pl.CostEstimate(
            flops=flops, bytes_accessed=moved or flops // 200, transcendentals=0
        ),
    )(*ins)


def moved_by(x, pairs):
    return held(lax.ppermute(x, "areal", pairs))


def shift_pairs(columns, k):
    return [(i, (i - k) % columns) for i in range(columns)]


def beside_layers(tiles):
    groups = lax.axis_size("layer")
    if groups == 2:
        return [held(lax.ppermute(tiles[0], "layer", [(0, 1), (1, 0)]))]
    up = [(i, i + 1) for i in range(groups - 1)]
    down = [(i + 1, i) for i in range(groups - 1)]
    return [held(lax.ppermute(tiles[0], "layer", up)), held(lax.ppermute(tiles[-1], "layer", down))]


def outside(x):
    return pltpu.with_memory_space_constraint(x, pltpu.HBM)


def on_device(
    rhs,
    areal_blocks,
    vertical_blocks,
    conn_src,
    conn_count,
    tile_map,
    well_cells,
    well_gain,
    sens,
    basis,
):
    columns = lax.axis_size("areal")
    groups = lax.axis_size("layer")
    two = groups == 2
    rows, width = rhs.shape[2:]
    modes = basis.shape[-1]
    number = conn_src.shape[-1]
    swaps = near_swaps(number)
    routes = [swap_pairs(columns, k, color) for k, color in swaps]
    routes += [shift_pairs(columns, columns // 2 + 1), shift_pairs(columns, columns // 2)]
    rhs = rhs[0].reshape(2 * rows, width)
    me = lax.axis_index("areal").astype(jnp.int32).reshape(1)
    group = lax.axis_index("layer").astype(jnp.int32).reshape(1)

    tile = pltpu.VMEM((rows, width), BF16)
    pair = pltpu.VMEM((2 * rows, width), BF16)
    sums = pltpu.VMEM((2, rows, width), F32)
    one = 2 * rows * width * width
    partial = functools.partial

    masks_type = pltpu.VMEM((8, 128), F32)
    with jax.named_scope("plan"):
        far_pair = moved_by(rhs, routes[-1])
        table, asks, payload = call(
            partial(plan_kernel, columns, swaps),
            [
                jax.ShapeDtypeStruct((2 * number,), jnp.int32),
                masks_type,
                pltpu.VMEM((2 * rows + 16, width), BF16),
            ],
            (outside(conn_src[0, 0]), conn_count[0], outside(tile_map), me, outside(rhs)),
            [SMEM] * 4 + [VMEM],
            out_specs=[SMEM] + [VMEM] * 2,
        )
        asks, payload = held(asks), held(payload)
        told9 = moved_by(asks, [(to, at) for at, to in routes[-2]])
        told8 = moved_by(asks, routes[-1])

    with jax.named_scope("load"):
        bands, vert = call(
            partial(load_kernel, number),
            [pltpu.VMEM((number, width, 2 * width), BF16), pltpu.VMEM(vertical_blocks.shape[1:], BF16)],
            (table, outside(areal_blocks[0]), outside(vertical_blocks[0])),
            [SMEM] + [pl.BlockSpec(memory_space=pltpu.HBM)] * 2,
            [pltpu.SemaphoreType.DMA((2 * number + 1,))],
            moved=areal_blocks.size * 2 + vertical_blocks.size * 2,
        )
        bands, vert = held(bands), held(vert)

    rhs_held = held(rhs)
    lam = rhs_held
    sends = [payload] * (number - 2)
    outer = [payload]
    half = len(swaps) // 2
    for step in range(ITERS):
        first = step == 0
        with jax.named_scope("apply"):
            arrived = [moved_by(x, pairs) for x, pairs in zip(sends, routes)]
            if first:
                even, odd = (arrived[swaps.index((1, color))] for color in (1, 0))
                picked, told = call(
                    partial(far_pick_kernel, number),
                    [tile, masks_type],
                    (me, far_pair, even, odd, told9, told8),
                    [SMEM] + [VMEM] * 5,
                )
                arrived = [*arrived, moved_by(picked, shift_pairs(columns, 1)), far_pair]
                told = [*arrived[:-2], held(told)]
            beside = beside_layers(outer)
            (part,) = call(own_kernel, [sums], (lam, rhs_held, vert), [VMEM] * 3, flops=one)
            (cross,) = call(
                cross_kernel,
                [sums],
                (asks, bands, *arrived[:half]),
                [VMEM] * (2 + half),
                flops=4 * one,
            )
            (far,) = call(
                far_kernel,
                [sums],
                (asks, bands, held(cross), *arrived[-2:]),
                [VMEM] * 5,
                flops=4 * one,
            )
            tiles = (held(part), held(far), asks, bands, vert)
            near = (*arrived[half:-2], *beside)
            if step < ITERS - 1:
                lam, *rest = call(
                    partial(update_kernel, number, two, half, first),
                    [pair] + [tile] * (number + len(beside)) + ([masks_type] if first else []),
                    (group, *tiles, *near, *told),
                    [SMEM] + [VMEM] * (5 + len(near) + len(told)),
                    flops=one,
                )
                lam = held(lam)
                if first:
                    told = [held(rest.pop())]
                sends, outer = rest[:number], rest[number:]
            else:
                adjoint, pieces = call(
                    partial(last_kernel, number, two, half, columns),
                    [
                        jax.ShapeDtypeStruct((2, rows, width), BF16),
                        pltpu.VMEM(
                            (2 * columns, modes // columns // 2, rows) if two else (rows, modes), F32
                        ),
                    ],
                    (
                        group,
                        well_cells[0],
                        well_gain[0],
                        *tiles,
                        held(sens[0].transpose(1, 0, 2)),
                        held(basis[0]),
                        *near,
                    ),
                    [SMEM] * 3 + [VMEM] * (7 + len(near)),
                    flops=one,
                )

    with jax.named_scope("project"):
        if two:
            landed = lax.all_to_all(pieces, ("areal", "layer"), 0, 0, tiled=True)
            (coefficients,) = call(
                sum_kernel,
                [jax.ShapeDtypeStruct((modes // columns, rows // 2), BF16)],
                (held(landed),),
                [VMEM],
            )
            coefficients = coefficients.T
        else:
            cut = pieces.reshape(groups, rows // groups, columns, modes // columns)
            cut = cut.transpose(2, 0, 1, 3).reshape(columns * groups, rows // groups, modes // columns)
            landed = lax.all_to_all(cut, ("areal", "layer"), 0, 0, tiled=True)
            coefficients = jnp.sum(landed, axis=0).astype(BF16)
    return (adjoint[None], coefficients)


def solution(mesh):
    in_specs = (
        P("areal", "layer", None, None),
        P("areal", "layer", None, None, None),
        P("areal", "layer", None, None, None),
        P("areal", "layer", None),
        P("areal", "layer"),
        P(),
        P("areal", "layer", None),
        P("areal", "layer", None),
        P("areal", "layer", None, None),
        P("areal", "layer", None, None),
    )
    out_specs = (P("areal", "layer", None, None), P("layer", "areal"))
    return jax.shard_map(
        on_device, mesh=mesh, in_specs=in_specs, out_specs=out_specs, check_vma=False
    )
```

```python
import functools

import jax
import jax.numpy as jnp
from jax import lax
from jax.experimental import pallas as pl
from jax.experimental.pallas import tpu as pltpu
from jax.sharding import PartitionSpec as P

ITERS = 3
F32 = jnp.float32
BF16 = jnp.bfloat16
SMEM = pl.BlockSpec(memory_space=pltpu.SMEM)
VMEM = pl.BlockSpec(memory_space=pltpu.VMEM)
LIMIT = 32 * 1024 * 1024


def near_swaps(count):
    return [(k, color) for color in (1, 0) for k in range(count // 2 - 1, 0, -1)]


def swap_pairs(columns, k, color):
    return [
        (c, (c + k if (c // k) % 2 == color else c - k) % columns) for c in range(columns)
    ]


AREAL = ("plane", "spot")
PLANE = 4


def held(x):
    return pltpu.with_memory_space_constraint(x, pltpu.VMEM)


def dot(a, b):
    return jnp.dot(a, b, preferred_element_type=F32)


def plan_kernel(columns, swaps, src, count, tile_map, me, rhs, table, asks, payload):
    steps = [
        jnp.where(lax.rem(lax.div(me[0], k), 2) == color, k, columns - k) for k, color in swaps
    ] + [columns // 2 + 1, columns // 2]
    number = len(steps)
    conn = [0] * number
    slots = [0] * number
    for s in range(number):
        place = tile_map[src[s]]
        peer = lax.shift_right_logical(place, 1)
        slot = lax.bitwise_and(place, 1)
        away = peer - me[0]
        away = jnp.where(away < 0, away + columns, away)
        for i, k in enumerate(steps):
            hit = away == k
            conn[i] = jnp.where(hit, s, conn[i])
            slots[i] = jnp.where(hit, slot, slots[i])
    rows, width = rhs.shape
    line = lax.broadcasted_iota(jnp.int32, (16, width), 0)
    asked = jnp.zeros(line.shape, F32)
    for i in range(number):
        table[i] = conn[i]
        table[number + i] = jnp.where(conn[i] < count[0], 1, 0)
        asked = jnp.where(line == i, slots[i].astype(F32), asked)
    asks[...] = asked[0:8, 0:128]
    payload[0:rows] = rhs[...]
    payload[rows:] = asked.astype(BF16)


def load_kernel(number, table, blocks, vert, bands, vert_held, sems):
    width = vert.shape[-1]
    side = pltpu.make_async_copy(vert, vert_held, sems.at[2 * number])
    side.start()

    def copies(i):
        return [
            pltpu.make_async_copy(
                blocks.at[d, table[i]],
                bands.at[i, :, pl.ds(d * width, width)],
                sems.at[2 * i + d],
            )
            for d in range(2)
        ]

    for i in range(number):

        @pl.when(table[number + i] > 0)
        def _():
            for copy in copies(i):
                copy.start()

        @pl.when(table[number + i] == 0)
        def _():
            bands[i] = jnp.zeros(bands.shape[1:], bands.dtype)

    for i in range(number):

        @pl.when(table[number + i] > 0)
        def _():
            for copy in copies(i):
                copy.wait()

    side.wait()


def wide(mask, width):
    return jnp.concatenate([mask] * (width // mask.shape[1]), axis=1)


def chosen(mask, low, high):
    return jnp.where(wide(mask, low.shape[1]) > 0.5, high, low).astype(BF16)


def asks_of(payload):
    return payload[payload.shape[0] - 16 :, 0:128].astype(F32)


def tile_of(ref, mask, rows):
    if ref.shape[0] == rows:
        return ref[...]
    return chosen(mask, ref[0:rows].astype(F32), ref[rows : 2 * rows].astype(F32))


def far_pick_kernel(number, me, pair, asks, even, odd, tile, relayed):
    rows = tile.shape[0]
    theirs = jnp.where(lax.rem(me[0], 2) == 0, asks_of(even), asks_of(odd))
    tile[...] = tile_of(pair, theirs[number - 2 : number - 1, :], rows)
    relayed[...] = asks[...]
    relayed[number - 2 : number - 1, :] = theirs[number - 2 : number - 1, :]


def own_kernel(lam, rhs, vert, part):
    rows = rhs.shape[0] // 2
    part[0] = rhs[0:rows].astype(F32) - dot(lam[rows : 2 * rows], vert[0, 1])
    part[1] = rhs[rows:].astype(F32) - dot(lam[0:rows], vert[1, 0])


def source_sums(asks, bands, begin, refs, rows):
    tiles = [tile_of(ref, asks[i : i + 1, :], rows) for i, ref in enumerate(refs, begin)]
    count, width, both = len(refs), bands.shape[1], bands.shape[2]
    band = bands[begin : begin + count].reshape(count * width, both)
    sums = dot(jnp.concatenate(tiles, axis=1), band)
    return sums[:, :width], sums[:, width:]


def beside_sums(two, group, vert, beside, rows):
    def tile(ref, slot):
        if ref.shape[0] == rows:
            return ref[...]
        return ref[pl.ds(pl.multiple_of(slot * rows, 16), rows), :]

    if two:
        mine = group[0]
        term = dot(tile(beside[0], mine), vert[1 - mine, 1 - mine])
        none = jnp.zeros_like(term)
        return jnp.where(mine == 1, term, none), jnp.where(mine == 0, term, none)
    return [dot(tile(beside[d], 1 - d), vert[d, d]) for d in range(2)]


def cross_kernel(asks, bands, *refs):
    arrived, out = refs[:-1], refs[-1]
    out[0], out[1] = source_sums(asks, bands, 0, arrived, out.shape[1])


def far_kernel(asks, bands, cross, *refs):
    far, out = refs[:-1], refs[-1]
    low, high = source_sums(asks, bands, bands.shape[0] - len(far), far, out.shape[1])
    out[0] = cross[0] + low
    out[1] = cross[1] + high


def updated(two, begin, group, part, far, asks, bands, vert, near, beside):
    rows = part.shape[1]
    sums = source_sums(asks, bands, begin, near, rows)
    terms = beside_sums(two, group, vert, beside, rows)
    return [part[d] - far[d] - sums[d] - terms[d] for d in range(2)]


def update_kernel(number, two, begin, first, group, part, far, asks, bands, vert, *refs):
    sides = 1 if two else 2
    here = number - 2 - begin
    near, refs = refs[:here], refs[here:]
    beside, refs = refs[:sides], refs[sides:]
    count = number - 1 if first else 1
    told, refs = refs[:count], refs[count:]
    low, high = updated(two, begin, group, part, far, asks, bands, vert, near, beside)
    lam, sends, refs = refs[0], refs[1 : 1 + number], refs[1 + number :]
    outer, refs = refs[:sides], refs[sides:]
    masks = told[0]
    if first:
        masks = refs[0]
        masks[...] = told[-1][...]
        for i in range(number - 2):
            masks[i : i + 1, :] = asks_of(told[i])[i : i + 1, :]
    rows = low.shape[0]
    lam[0:rows] = low.astype(BF16)
    lam[rows:] = high.astype(BF16)
    for i, send in enumerate(sends):
        send[...] = chosen(masks[i : i + 1, :], low, high)
    if two:
        outer[0][...] = jnp.where(group[0] == 0, high, low).astype(BF16)
    else:
        outer[0][...] = high.astype(BF16)
        outer[1][...] = low.astype(BF16)


def last_kernel(number, two, begin, columns, group, wells, gains, part, far, asks, bands, vert, sens, basis, *refs):
    here = number - 2 - begin
    near, beside, (lam, pieces) = refs[:here], refs[here:-2], refs[-2:]
    sums = updated(two, begin, group, part, far, asks, bands, vert, near, beside)
    phases, _, cells = sens.shape
    spot = lax.broadcasted_iota(jnp.int32, (1, cells), 1)
    projected = None
    for d in range(2):
        rounded = sums[d].astype(BF16)
        lam[d] = rounded
        back = rounded.astype(F32)
        well = jnp.zeros((1, cells), F32)
        for w in range(wells.shape[1]):
            well = well + jnp.where(spot == wells[d, w], gains[d, w], 0.0)
        grad = back[:, :cells] * (sens[0, d : d + 1, :] + well)
        for p in range(1, phases):
            grad = grad + back[:, p * cells : (p + 1) * cells] * sens[p, d : d + 1, :]
        term = dot(grad.astype(BF16), basis[d])
        projected = term if projected is None else projected + term
    if two:
        turned = projected.T
        modes, rows = turned.shape
        share, half = modes // columns, rows // 2
        spots = pieces.shape[0] // 2
        for c in range(columns):
            top = turned[c * share : c * share + share // 2]
            low = turned[c * share + share // 2 : (c + 1) * share]
            for g in range(2):
                cut = slice(g * half, (g + 1) * half)
                pieces[2 * (c % spots) + g, c // spots] = jnp.concatenate(
                    [top[:, cut], low[:, cut]], axis=1
                )
    else:
        pieces[...] = projected


def total_of(pieces):
    total = pieces[0]
    for i in range(1, pieces.shape[0]):
        total = total + pieces[i]
    return total


def plane_sum_kernel(pieces, out):
    out[...] = total_of(pieces)


def sum_kernel(pieces, out):
    total = total_of(pieces)
    half = total.shape[1] // 2
    out[...] = jnp.concatenate([total[:, :half], total[:, half:]], axis=0).astype(BF16)


def call(kernel, outs, ins, specs, scratch=(), flops=0, moved=0, out_specs=None):
    return pl.pallas_call(
        kernel,
        out_shape=outs,
        in_specs=specs,
        out_specs=out_specs or [VMEM] * len(outs),
        scratch_shapes=list(scratch),
        compiler_params=pltpu.CompilerParams(vmem_limit_bytes=LIMIT),
        cost_estimate=pl.CostEstimate(
            flops=flops, bytes_accessed=moved or flops // 200, transcendentals=0
        ),
    )(*ins)


def moved_by(x, pairs):
    return held(lax.ppermute(x, AREAL, pairs))


def shift_pairs(columns, k):
    return [(i, (i - k) % columns) for i in range(columns)]


def beside_layers(tiles):
    groups = lax.axis_size("layer")
    if groups == 2:
        return [held(lax.ppermute(tiles[0], "layer", [(0, 1), (1, 0)]))]
    up = [(i, i + 1) for i in range(groups - 1)]
    down = [(i + 1, i) for i in range(groups - 1)]
    return [held(lax.ppermute(tiles[0], "layer", up)), held(lax.ppermute(tiles[-1], "layer", down))]


def outside(x):
    return pltpu.with_memory_space_constraint(x, pltpu.HBM)


def on_device(
    rhs,
    areal_blocks,
    vertical_blocks,
    conn_src,
    conn_count,
    tile_map,
    well_cells,
    well_gain,
    sens,
    basis,
):
    planes, spots = lax.axis_size("plane"), lax.axis_size("spot")
    columns = planes * spots
    groups = lax.axis_size("layer")
    two = groups == 2
    rows, width = rhs.shape[2:]
    modes = basis.shape[-1]
    number = conn_src.shape[-1]
    swaps = near_swaps(number)
    routes = [swap_pairs(columns, k, color) for k, color in swaps]
    routes += [shift_pairs(columns, columns // 2 + 1), shift_pairs(columns, columns // 2)]
    rhs = rhs[0].reshape(2 * rows, width)
    me = lax.axis_index(AREAL).astype(jnp.int32).reshape(1)
    group = lax.axis_index("layer").astype(jnp.int32).reshape(1)

    tile = pltpu.VMEM((rows, width), BF16)
    pair = pltpu.VMEM((2 * rows, width), BF16)
    sums = pltpu.VMEM((2, rows, width), F32)
    one = 2 * rows * width * width
    partial = functools.partial

    masks_type = pltpu.VMEM((8, 128), F32)
    with jax.named_scope("plan"):
        far_pair = moved_by(rhs, routes[-1])
        table, asks, payload = call(
            partial(plan_kernel, columns, swaps),
            [
                jax.ShapeDtypeStruct((2 * number,), jnp.int32),
                masks_type,
                pltpu.VMEM((2 * rows + 16, width), BF16),
            ],
            (outside(conn_src[0, 0]), conn_count[0], outside(tile_map), me, outside(rhs)),
            [SMEM] * 4 + [VMEM],
            out_specs=[SMEM] + [VMEM] * 2,
        )
        asks, payload = held(asks), held(payload)

    with jax.named_scope("load"):
        bands, vert = call(
            partial(load_kernel, number),
            [pltpu.VMEM((number, width, 2 * width), BF16), pltpu.VMEM(vertical_blocks.shape[1:], BF16)],
            (table, outside(areal_blocks[0]), outside(vertical_blocks[0])),
            [SMEM] + [pl.BlockSpec(memory_space=pltpu.HBM)] * 2,
            [pltpu.SemaphoreType.DMA((2 * number + 1,))],
            moved=areal_blocks.size * 2 + vertical_blocks.size * 2,
        )
        bands, vert = held(bands), held(vert)

    rhs_held = held(rhs)
    lam = rhs_held
    sends = [payload] * (number - 2)
    outer = [payload]
    half = len(swaps) // 2
    for step in range(ITERS):
        first = step == 0
        with jax.named_scope("apply"):
            arrived = [moved_by(x, pairs) for x, pairs in zip(sends, routes)]
            if first:
                even, odd = (arrived[swaps.index((1, color))] for color in (1, 0))
                picked, relayed = call(
                    partial(far_pick_kernel, number),
                    [tile, masks_type],
                    (me, far_pair, asks, even, odd),
                    [SMEM] + [VMEM] * 4,
                )
                arrived = [*arrived, moved_by(picked, shift_pairs(columns, 1)), far_pair]
                told = [*arrived[:-2], moved_by(relayed, routes[-1])]
            beside = beside_layers(outer)
            (part,) = call(own_kernel, [sums], (lam, rhs_held, vert), [VMEM] * 3, flops=one)
            (cross,) = call(
                cross_kernel,
                [sums],
                (asks, bands, *arrived[:half]),
                [VMEM] * (2 + half),
                flops=4 * one,
            )
            (far,) = call(
                far_kernel,
                [sums],
                (asks, bands, held(cross), *arrived[-2:]),
                [VMEM] * 5,
                flops=4 * one,
            )
            tiles = (held(part), held(far), asks, bands, vert)
            near = (*arrived[half:-2], *beside)
            if step < ITERS - 1:
                lam, *rest = call(
                    partial(update_kernel, number, two, half, first),
                    [pair] + [tile] * (number + len(beside)) + ([masks_type] if first else []),
                    (group, *tiles, *near, *told),
                    [SMEM] + [VMEM] * (5 + len(near) + len(told)),
                    flops=one,
                )
                lam = held(lam)
                if first:
                    told = [held(rest.pop())]
                sends, outer = rest[:number], rest[number:]
            else:
                adjoint, pieces = call(
                    partial(last_kernel, number, two, half, columns),
                    [
                        jax.ShapeDtypeStruct((2, rows, width), BF16),
                        pltpu.VMEM(
                            (2 * spots, planes, modes // columns // 2, rows) if two else (rows, modes),
                            F32,
                        ),
                    ],
                    (
                        group,
                        well_cells[0],
                        well_gain[0],
                        *tiles,
                        held(sens[0].transpose(1, 0, 2)),
                        held(basis[0]),
                        *near,
                    ),
                    [SMEM] * 3 + [VMEM] * (7 + len(near)),
                    flops=one,
                )

    with jax.named_scope("project"):
        if two:
            landed = lax.all_to_all(pieces, ("spot", "layer"), 0, 0, tiled=True)
            (plane_sums,) = call(
                plane_sum_kernel, [pltpu.VMEM(pieces.shape[1:], F32)], (held(landed),), [VMEM]
            )
            landed = lax.all_to_all(plane_sums, "plane", 0, 0, tiled=True)
            (coefficients,) = call(
                sum_kernel,
                [jax.ShapeDtypeStruct((modes // columns, rows // 2), BF16)],
                (held(landed),),
                [VMEM],
            )
            coefficients = coefficients.T
        else:
            cut = pieces.reshape(groups, rows // groups, columns, modes // columns)
            cut = cut.transpose(2, 0, 1, 3).reshape(columns * groups, rows // groups, modes // columns)
            landed = lax.all_to_all(cut, (*AREAL, "layer"), 0, 0, tiled=True)
            coefficients = jnp.sum(landed, axis=0).astype(BF16)
    return (adjoint[None], coefficients)


def solution(mesh):
    columns, groups = mesh.devices.shape
    fine = jax.sharding.Mesh(
        mesh.devices.reshape(columns // PLANE, PLANE, groups), (*AREAL, "layer")
    )
    in_specs = (
        P(AREAL, "layer", None, None),
        P(AREAL, "layer", None, None, None),
        P(AREAL, "layer", None, None, None),
        P(AREAL, "layer", None),
        P(AREAL, "layer"),
        P(),
        P(AREAL, "layer", None),
        P(AREAL, "layer", None),
        P(AREAL, "layer", None, None),
        P(AREAL, "layer", None, None),
    )
    out_specs = (P(AREAL, "layer", None, None), P("layer", AREAL))
    return jax.shard_map(
        on_device, mesh=fine, in_specs=in_specs, out_specs=out_specs, check_vma=False
    )
```

```python
import functools

import jax
import jax.numpy as jnp
from jax import lax
from jax.experimental import pallas as pl
from jax.experimental.pallas import tpu as pltpu
from jax.sharding import PartitionSpec as P

ITERS = 3
F32 = jnp.float32
BF16 = jnp.bfloat16
SMEM = pl.BlockSpec(memory_space=pltpu.SMEM)
VMEM = pl.BlockSpec(memory_space=pltpu.VMEM)
LIMIT = 32 * 1024 * 1024


def near_swaps(count):
    return [(k, color) for color in (1, 0) for k in range(count // 2 - 1, 0, -1)]


def swap_pairs(columns, k, color):
    return [
        (c, (c + k if (c // k) % 2 == color else c - k) % columns) for c in range(columns)
    ]


def held(x):
    return pltpu.with_memory_space_constraint(x, pltpu.VMEM)


def dot(a, b):
    return jnp.dot(a, b, preferred_element_type=F32)


def plan_kernel(columns, swaps, src, count, tile_map, me, rhs, table, asks, payload):
    steps = [
        jnp.where(lax.rem(lax.div(me[0], k), 2) == color, k, columns - k) for k, color in swaps
    ] + [columns // 2 + 1, columns // 2]
    number = len(steps)
    conn = [0] * number
    slots = [0] * number
    for s in range(number):
        place = tile_map[src[s]]
        peer = lax.shift_right_logical(place, 1)
        slot = lax.bitwise_and(place, 1)
        away = peer - me[0]
        away = jnp.where(away < 0, away + columns, away)
        for i, k in enumerate(steps):
            hit = away == k
            conn[i] = jnp.where(hit, s, conn[i])
            slots[i] = jnp.where(hit, slot, slots[i])
    rows, width = rhs.shape
    line = lax.broadcasted_iota(jnp.int32, (16, width), 0)
    asked = jnp.zeros(line.shape, F32)
    for i in range(number):
        table[i] = conn[i]
        table[number + i] = jnp.where(conn[i] < count[0], 1, 0)
        asked = jnp.where(line == i, slots[i].astype(F32), asked)
    asks[...] = asked[0:8, 0:128]
    payload[0:rows] = rhs[...]
    payload[rows:] = asked.astype(BF16)


def load_kernel(number, table, blocks, vert, bands, vert_held, sems):
    width = vert.shape[-1]
    side = pltpu.make_async_copy(vert, vert_held, sems.at[2 * number])
    side.start()

    def copies(i):
        return [
            pltpu.make_async_copy(
                blocks.at[d, table[i]],
                bands.at[i, :, pl.ds(d * width, width)],
                sems.at[2 * i + d],
            )
            for d in range(2)
        ]

    for i in range(number):

        @pl.when(table[number + i] > 0)
        def _():
            for copy in copies(i):
                copy.start()

        @pl.when(table[number + i] == 0)
        def _():
            bands[i] = jnp.zeros(bands.shape[1:], bands.dtype)

    for i in range(number):

        @pl.when(table[number + i] > 0)
        def _():
            for copy in copies(i):
                copy.wait()

    side.wait()


def wide(mask, width):
    return jnp.concatenate([mask] * (width // mask.shape[1]), axis=1)


def chosen(mask, low, high):
    return jnp.where(wide(mask, low.shape[1]) > 0.5, high, low).astype(BF16)


def asks_of(payload):
    return payload[payload.shape[0] - 16 :, 0:128].astype(F32)


def tile_of(ref, mask, rows):
    if ref.shape[0] == rows:
        return ref[...]
    return chosen(mask, ref[0:rows].astype(F32), ref[rows : 2 * rows].astype(F32))


def far_pick_kernel(number, me, pair, asks, even, odd, part, tile, relayed):
    rows = tile.shape[0]
    theirs = jnp.where(lax.rem(me[0], 2) == 0, asks_of(even), asks_of(odd))
    tile[...] = tile_of(pair, theirs[number - 2 : number - 1, :], rows)
    relayed[...] = asks[...]
    relayed[number - 2 : number - 1, :] = theirs[number - 2 : number - 1, :]


def own_kernel(lam, rhs, vert, part):
    rows = rhs.shape[0] // 2
    part[0] = rhs[0:rows].astype(F32) - dot(lam[rows : 2 * rows], vert[0, 1])
    part[1] = rhs[rows:].astype(F32) - dot(lam[0:rows], vert[1, 0])


def source_sums(asks, bands, begin, refs, rows):
    tiles = [tile_of(ref, asks[i : i + 1, :], rows) for i, ref in enumerate(refs, begin)]
    count, width, both = len(refs), bands.shape[1], bands.shape[2]
    band = bands[begin : begin + count].reshape(count * width, both)
    sums = dot(jnp.concatenate(tiles, axis=1), band)
    return sums[:, :width], sums[:, width:]


def beside_sums(two, group, vert, beside, rows):
    def tile(ref, slot):
        if ref.shape[0] == rows:
            return ref[...]
        return ref[pl.ds(pl.multiple_of(slot * rows, 16), rows), :]

    if two:
        mine = group[0]
        term = dot(tile(beside[0], mine), vert[1 - mine, 1 - mine])
        none = jnp.zeros_like(term)
        return jnp.where(mine == 1, term, none), jnp.where(mine == 0, term, none)
    return [dot(tile(beside[d], 1 - d), vert[d, d]) for d in range(2)]


def cross_kernel(asks, bands, *refs):
    arrived, out = refs[:-1], refs[-1]
    out[0], out[1] = source_sums(asks, bands, 0, arrived, out.shape[1])


def far_kernel(asks, bands, cross, *refs):
    far, out = refs[:-1], refs[-1]
    low, high = source_sums(asks, bands, bands.shape[0] - len(far), far, out.shape[1])
    out[0] = cross[0] + low
    out[1] = cross[1] + high


def updated(two, begin, group, part, far, asks, bands, vert, near, beside):
    rows = part.shape[1]
    sums = source_sums(asks, bands, begin, near, rows)
    terms = beside_sums(two, group, vert, beside, rows)
    return [part[d] - far[d] - sums[d] - terms[d] for d in range(2)]


def update_kernel(number, two, begin, first, group, part, far, asks, bands, vert, *refs):
    sides = 1 if two else 2
    here = number - 2 - begin
    near, refs = refs[:here], refs[here:]
    beside, refs = refs[:sides], refs[sides:]
    count = number - 1 if first else 1
    told, refs = refs[:count], refs[count:]
    low, high = updated(two, begin, group, part, far, asks, bands, vert, near, beside)
    lam, sends, refs = refs[0], refs[1 : 1 + number], refs[1 + number :]
    outer, refs = refs[:sides], refs[sides:]
    masks = told[0]
    if first:
        masks = refs[0]
        masks[...] = told[-1][...]
        for i in range(number - 2):
            masks[i : i + 1, :] = asks_of(told[i])[i : i + 1, :]
    rows = low.shape[0]
    lam[0:rows] = low.astype(BF16)
    lam[rows:] = high.astype(BF16)
    for i, send in enumerate(sends):
        send[...] = chosen(masks[i : i + 1, :], low, high)
    if two:
        outer[0][...] = jnp.where(group[0] == 0, high, low).astype(BF16)
    else:
        outer[0][...] = high.astype(BF16)
        outer[1][...] = low.astype(BF16)


def last_kernel(number, two, begin, columns, group, wells, gains, part, far, asks, bands, vert, sens, basis, *refs):
    here = number - 2 - begin
    near, beside, (lam, pieces) = refs[:here], refs[here:-2], refs[-2:]
    sums = updated(two, begin, group, part, far, asks, bands, vert, near, beside)
    phases, _, cells = sens.shape
    spot = lax.broadcasted_iota(jnp.int32, (1, cells), 1)
    projected = None
    for d in range(2):
        rounded = sums[d].astype(BF16)
        lam[d] = rounded
        back = rounded.astype(F32)
        well = jnp.zeros((1, cells), F32)
        for w in range(wells.shape[1]):
            well = well + jnp.where(spot == wells[d, w], gains[d, w], 0.0)
        grad = back[:, :cells] * (sens[0, d : d + 1, :] + well)
        for p in range(1, phases):
            grad = grad + back[:, p * cells : (p + 1) * cells] * sens[p, d : d + 1, :]
        term = dot(grad.astype(BF16), basis[d])
        projected = term if projected is None else projected + term
    if two:
        turned = projected.T
        modes, rows = turned.shape
        share, half = modes // columns, rows // 2
        for c in range(columns):
            top = turned[c * share : c * share + share // 2]
            low = turned[c * share + share // 2 : (c + 1) * share]
            for g in range(2):
                cut = slice(g * half, (g + 1) * half)
                pieces[2 * c + g] = jnp.concatenate([top[:, cut], low[:, cut]], axis=1)
    else:
        pieces[...] = projected


def sum_kernel(pieces, out):
    total = pieces[0]
    for i in range(1, pieces.shape[0]):
        total = total + pieces[i]
    half = total.shape[1] // 2
    out[...] = jnp.concatenate([total[:, :half], total[:, half:]], axis=0).astype(BF16)


def call(kernel, outs, ins, specs, scratch=(), flops=0, moved=0, out_specs=None):
    return pl.pallas_call(
        kernel,
        out_shape=outs,
        in_specs=specs,
        out_specs=out_specs or [VMEM] * len(outs),
        scratch_shapes=list(scratch),
        compiler_params=pltpu.CompilerParams(vmem_limit_bytes=LIMIT),
        cost_estimate=pl.CostEstimate(
            flops=flops, bytes_accessed=moved or flops // 200, transcendentals=0
        ),
    )(*ins)


def moved_by(x, pairs):
    return held(lax.ppermute(x, "areal", pairs))


def shift_pairs(columns, k):
    return [(i, (i - k) % columns) for i in range(columns)]


def beside_layers(tiles):
    groups = lax.axis_size("layer")
    if groups == 2:
        return [held(lax.ppermute(tiles[0], "layer", [(0, 1), (1, 0)]))]
    up = [(i, i + 1) for i in range(groups - 1)]
    down = [(i + 1, i) for i in range(groups - 1)]
    return [held(lax.ppermute(tiles[0], "layer", up)), held(lax.ppermute(tiles[-1], "layer", down))]


def outside(x):
    return pltpu.with_memory_space_constraint(x, pltpu.HBM)


def on_device(
    rhs,
    areal_blocks,
    vertical_blocks,
    conn_src,
    conn_count,
    tile_map,
    well_cells,
    well_gain,
    sens,
    basis,
):
    columns = lax.axis_size("areal")
    groups = lax.axis_size("layer")
    two = groups == 2
    rows, width = rhs.shape[2:]
    modes = basis.shape[-1]
    number = conn_src.shape[-1]
    swaps = near_swaps(number)
    routes = [swap_pairs(columns, k, color) for k, color in swaps]
    routes += [shift_pairs(columns, columns // 2 + 1), shift_pairs(columns, columns // 2)]
    rhs = rhs[0].reshape(2 * rows, width)
    me = lax.axis_index("areal").astype(jnp.int32).reshape(1)
    group = lax.axis_index("layer").astype(jnp.int32).reshape(1)

    tile = pltpu.VMEM((rows, width), BF16)
    pair = pltpu.VMEM((2 * rows, width), BF16)
    sums = pltpu.VMEM((2, rows, width), F32)
    one = 2 * rows * width * width
    partial = functools.partial

    masks_type = pltpu.VMEM((8, 128), F32)
    with jax.named_scope("plan"):
        far_pair = moved_by(rhs, routes[-1])
        table, asks, payload = call(
            partial(plan_kernel, columns, swaps),
            [
                jax.ShapeDtypeStruct((2 * number,), jnp.int32),
                masks_type,
                pltpu.VMEM((2 * rows + 16, width), BF16),
            ],
            (outside(conn_src[0, 0]), conn_count[0], outside(tile_map), me, outside(rhs)),
            [SMEM] * 4 + [VMEM],
            out_specs=[SMEM] + [VMEM] * 2,
        )
        asks, payload = held(asks), held(payload)

    with jax.named_scope("load"):
        bands, vert = call(
            partial(load_kernel, number),
            [pltpu.VMEM((number, width, 2 * width), BF16), pltpu.VMEM(vertical_blocks.shape[1:], BF16)],
            (table, outside(areal_blocks[0]), outside(vertical_blocks[0])),
            [SMEM] + [pl.BlockSpec(memory_space=pltpu.HBM)] * 2,
            [pltpu.SemaphoreType.DMA((2 * number + 1,))],
            moved=areal_blocks.size * 2 + vertical_blocks.size * 2,
        )
        bands, vert = held(bands), held(vert)

    rhs_held = held(rhs)
    lam = rhs_held
    sends = [payload] * (number - 2)
    outer = [payload]
    half = len(swaps) // 2
    for step in range(ITERS):
        first = step == 0
        with jax.named_scope("apply"):
            arrived = [moved_by(x, pairs) for x, pairs in zip(sends, routes)]
            (part,) = call(own_kernel, [sums], (lam, rhs_held, vert), [VMEM] * 3, flops=one)
            part = held(part)
            if first:
                even, odd = (arrived[swaps.index((1, color))] for color in (1, 0))
                picked, relayed = call(
                    partial(far_pick_kernel, number),
                    [tile, masks_type],
                    (me, far_pair, asks, even, odd, part),
                    [SMEM] + [VMEM] * 5,
                )
                arrived = [*arrived, moved_by(picked, shift_pairs(columns, 1)), far_pair]
                told = [*arrived[:-2], moved_by(relayed, routes[-1])]
            beside = beside_layers(outer)
            (cross,) = call(
                cross_kernel,
                [sums],
                (asks, bands, *arrived[:half]),
                [VMEM] * (2 + half),
                flops=4 * one,
            )
            (far,) = call(
                far_kernel,
                [sums],
                (asks, bands, held(cross), *arrived[-2:]),
                [VMEM] * 5,
                flops=4 * one,
            )
            tiles = (part, held(far), asks, bands, vert)
            near = (*arrived[half:-2], *beside)
            if step < ITERS - 1:
                lam, *rest = call(
                    partial(update_kernel, number, two, half, first),
                    [pair] + [tile] * (number + len(beside)) + ([masks_type] if first else []),
                    (group, *tiles, *near, *told),
                    [SMEM] + [VMEM] * (5 + len(near) + len(told)),
                    flops=one,
                )
                lam = held(lam)
                if first:
                    told = [held(rest.pop())]
                sends, outer = rest[:number], rest[number:]
            else:
                adjoint, pieces = call(
                    partial(last_kernel, number, two, half, columns),
                    [
                        jax.ShapeDtypeStruct((2, rows, width), BF16),
                        pltpu.VMEM(
                            (2 * columns, modes // columns // 2, rows) if two else (rows, modes), F32
                        ),
                    ],
                    (
                        group,
                        well_cells[0],
                        well_gain[0],
                        *tiles,
                        held(sens[0].transpose(1, 0, 2)),
                        held(basis[0]),
                        *near,
                    ),
                    [SMEM] * 3 + [VMEM] * (7 + len(near)),
                    flops=one,
                )

    with jax.named_scope("project"):
        if two:
            landed = lax.all_to_all(pieces, ("areal", "layer"), 0, 0, tiled=True)
            (coefficients,) = call(
                sum_kernel,
                [jax.ShapeDtypeStruct((modes // columns, rows // 2), BF16)],
                (held(landed),),
                [VMEM],
            )
            coefficients = coefficients.T
        else:
            cut = pieces.reshape(groups, rows // groups, columns, modes // columns)
            cut = cut.transpose(2, 0, 1, 3).reshape(columns * groups, rows // groups, modes // columns)
            landed = lax.all_to_all(cut, ("areal", "layer"), 0, 0, tiled=True)
            coefficients = jnp.sum(landed, axis=0).astype(BF16)
    return (adjoint[None], coefficients)


def solution(mesh):
    in_specs = (
        P("areal", "layer", None, None),
        P("areal", "layer", None, None, None),
        P("areal", "layer", None, None, None),
        P("areal", "layer", None),
        P("areal", "layer"),
        P(),
        P("areal", "layer", None),
        P("areal", "layer", None),
        P("areal", "layer", None, None),
        P("areal", "layer", None, None),
    )
    out_specs = (P("areal", "layer", None, None), P("layer", "areal"))
    return jax.shard_map(
        on_device, mesh=mesh, in_specs=in_specs, out_specs=out_specs, check_vma=False
    )
```

```python
import functools

import jax
import jax.numpy as jnp
from jax import lax
from jax.experimental import pallas as pl
from jax.experimental.pallas import tpu as pltpu
from jax.sharding import PartitionSpec as P

ITERS = 3
F32 = jnp.float32
BF16 = jnp.bfloat16
SMEM = pl.BlockSpec(memory_space=pltpu.SMEM)
VMEM = pl.BlockSpec(memory_space=pltpu.VMEM)
LIMIT = 16 * 1024 * 1024


def near_swaps(count):
    return [(k, color) for color in (1, 0) for k in range(count // 2 - 1, 0, -1)]


def swap_pairs(columns, k, color):
    return [
        (c, (c + k if (c // k) % 2 == color else c - k) % columns) for c in range(columns)
    ]


def held(x):
    return pltpu.with_memory_space_constraint(x, pltpu.VMEM)


def dot(a, b):
    return jnp.dot(a, b, preferred_element_type=F32)


def plan_kernel(columns, swaps, src, count, tile_map, me, group, rhs, table, asks, payload):
    steps = [
        jnp.where(lax.rem(lax.div(me[0], k), 2) == color, k, columns - k) for k, color in swaps
    ] + [columns // 2 + 1, columns // 2]
    number = len(steps)
    conn = [0] * number
    slots = [0] * number
    for s in range(number):
        place = tile_map[src[s]]
        peer = lax.shift_right_logical(place, 1)
        slot = lax.bitwise_and(place, 1)
        away = peer - me[0]
        away = jnp.where(away < 0, away + columns, away)
        for i, k in enumerate(steps):
            hit = away == k
            conn[i] = jnp.where(hit, s, conn[i])
            slots[i] = jnp.where(hit, slot, slots[i])
    rows, width = rhs.shape
    line = lax.broadcasted_iota(jnp.int32, (16, width), 0)
    asked = jnp.zeros(line.shape, F32)
    for i in range(number):
        table[i] = conn[i]
        table[number + i] = jnp.where(conn[i] < count[0], 1, 0)
        asked = jnp.where(line == i, slots[i].astype(F32), asked)
    asked = jnp.where(line == number, group[0].astype(F32), asked)
    asked = jnp.where(line == number + 1, lax.rem(me[0], 2).astype(F32), asked)
    asks[...] = asked[0:8, 0:128]
    payload[0:rows] = rhs[...]
    payload[rows:] = asked.astype(BF16)


def load_kernel(number, two, table, group, blocks, vert, bands, sides, sems):
    width = vert.shape[-1]
    mine = group[0]
    ends = [(1 - mine, 1 - mine)] if two else [(0, 0), (1, 1)]
    beside = [
        pltpu.make_async_copy(vert.at[d, k], sides.at[i], sems.at[2 * number + i])
        for i, (d, k) in enumerate([(0, 1), (1, 0), *ends])
    ]
    for copy in beside:
        copy.start()

    def copies(i):
        return [
            pltpu.make_async_copy(
                blocks.at[d, table[i]],
                bands.at[i, :, pl.ds(d * width, width)],
                sems.at[2 * i + d],
            )
            for d in range(2)
        ]

    for i in range(number):

        @pl.when(table[number + i] > 0)
        def _():
            for copy in copies(i):
                copy.start()

        @pl.when(table[number + i] == 0)
        def _():
            bands[i] = jnp.zeros(bands.shape[1:], bands.dtype)

    for i in range(number):

        @pl.when(table[number + i] > 0)
        def _():
            for copy in copies(i):
                copy.wait()

    for copy in beside:
        copy.wait()


def turn_kernel(columns, basis, turned):
    _, cells, modes = basis.shape
    bands = []
    for d in range(2):
        by_mode = basis[d].astype(F32).T.reshape(columns, 2, modes // columns // 2, cells)
        bands += [by_mode[:, h].reshape(modes // 2, cells) for h in range(2)]
    turned[...] = jnp.concatenate(bands, axis=1).astype(BF16)


def weigh_kernel(wells, gains, sens, factors):
    cells = sens.shape[-1]
    spot = lax.broadcasted_iota(jnp.int32, (1, cells), 1)
    factors[...] = sens[...]
    for d in range(2):
        well = jnp.zeros((1, cells), F32)
        for w in range(wells.shape[1]):
            well = well + jnp.where(spot == wells[d, w], gains[d, w], 0.0)
        factors[0, d : d + 1, :] = sens[0, d : d + 1, :] + well


def wide(mask, width):
    return jnp.concatenate([mask] * (width // mask.shape[1]), axis=1)


def chosen(mask, low, high):
    return jnp.where(wide(mask, low.shape[1]) > 0.5, high, low).astype(BF16)


def asks_of(payload):
    return payload[payload.shape[0] - 16 :, 0:128].astype(F32)


def tile_of(ref, mask, rows):
    if ref.shape[0] == rows:
        return ref[...]
    return chosen(mask, ref[0:rows].astype(F32), ref[rows : 2 * rows].astype(F32))


def far_pick_kernel(number, pair, asks, even, odd, part, tile, relayed):
    rows = tile.shape[0]
    parity = asks[number + 1 : number + 2, :]
    ask = [asks_of(ref)[number - 2 : number - 1, :] for ref in (even, odd)]
    mask = jnp.where(parity > 0.5, ask[1], ask[0])
    tile[...] = tile_of(pair, mask, rows)
    relayed[...] = asks[...]
    relayed[number - 2 : number - 1, :] = mask


def own_kernel(lam, rhs, sides, part):
    rows = rhs.shape[0] // 2
    part[0] = rhs[0:rows].astype(F32) - dot(lam[rows : 2 * rows], sides[0])
    part[1] = rhs[rows:].astype(F32) - dot(lam[0:rows], sides[1])


def source_sums(asks, bands, begin, refs, rows):
    tiles = [tile_of(ref, asks[i : i + 1, :], rows) for i, ref in enumerate(refs, begin)]
    count, width, both = len(refs), bands.shape[1], bands.shape[2]
    band = bands[begin : begin + count].reshape(count * width, both)
    sums = dot(jnp.concatenate(tiles, axis=1), band)
    return sums[:, :width], sums[:, width:]


def beside_sums(number, two, asks, sides, beside, rows):
    if two:
        mine = asks[number : number + 1, :]
        term = dot(tile_of(beside[0], mine, rows), sides[2])
        above = wide(mine, term.shape[1]) > 0.5
        none = jnp.zeros_like(term)
        return jnp.where(above, term, none), jnp.where(above, none, term)
    return [
        dot(tile_of(beside[d], jnp.full((1, 128), 1.0 - d, F32), rows), sides[2 + d])
        for d in range(2)
    ]


def cross_kernel(asks, bands, *refs):
    arrived, out = refs[:-1], refs[-1]
    out[0], out[1] = source_sums(asks, bands, 0, arrived, out.shape[1])


def far_kernel(asks, bands, cross, *refs):
    far, out = refs[:-1], refs[-1]
    low, high = source_sums(asks, bands, bands.shape[0] - len(far), far, out.shape[1])
    out[0] = cross[0] + low
    out[1] = cross[1] + high


def updated(number, two, begin, part, far, asks, bands, sides, near, beside):
    rows = part.shape[1]
    sums = source_sums(asks, bands, begin, near, rows)
    terms = beside_sums(number, two, asks, sides, beside, rows)
    return [part[d] - far[d] - sums[d] - terms[d] for d in range(2)]


def update_kernel(number, two, begin, first, part, far, asks, bands, sides, *refs):
    ends = 1 if two else 2
    here = number - 2 - begin
    near, refs = refs[:here], refs[here:]
    beside, refs = refs[:ends], refs[ends:]
    count = number - 1 if first else 1
    told, refs = refs[:count], refs[count:]
    low, high = updated(number, two, begin, part, far, asks, bands, sides, near, beside)
    lam, sends, refs = refs[0], refs[1 : 1 + number], refs[1 + number :]
    outer, refs = refs[:ends], refs[ends:]
    masks = told[0]
    if first:
        masks = refs[0]
        masks[...] = told[-1][...]
        for i in range(number - 2):
            masks[i : i + 1, :] = asks_of(told[i])[i : i + 1, :]
    rows = low.shape[0]
    lam[0:rows] = low.astype(BF16)
    lam[rows:] = high.astype(BF16)
    for i, send in enumerate(sends):
        send[...] = chosen(masks[i : i + 1, :], low, high)
    if two:
        outer[0][...] = chosen(asks[number : number + 1, :], high, low)
    else:
        outer[0][...] = high.astype(BF16)
        outer[1][...] = low.astype(BF16)


def last_kernel(number, two, begin, part, far, asks, bands, sides, factors, basis, *refs):
    here = number - 2 - begin
    near, beside, (lam, pieces) = refs[:here], refs[here:-2], refs[-2:]
    sums = updated(number, two, begin, part, far, asks, bands, sides, near, beside)
    phases, _, cells = factors.shape
    grads = []
    for d in range(2):
        rounded = sums[d].astype(BF16)
        lam[d] = rounded
        back = rounded.astype(F32)
        grad = back[:, :cells] * factors[0, d : d + 1, :]
        for p in range(1, phases):
            grad = grad + back[:, p * cells : (p + 1) * cells] * factors[p, d : d + 1, :]
        grads.append(grad)
    if two:
        half = grads[0].shape[0] // 2
        none = jnp.zeros((half, cells), F32)
        band = pieces.shape[1]
        for g in range(2):
            cuts = [grad[g * half : (g + 1) * half] for grad in grads]
            top = jnp.concatenate([x for cut in cuts for x in (cut, none)], axis=1)
            low = jnp.concatenate([x for cut in cuts for x in (none, cut)], axis=1)
            wing = jnp.concatenate([top, low], axis=0).astype(BF16)
            share = lax.dot_general(
                basis[...], wing, (((1,), (1,)), ((), ())), preferred_element_type=F32
            )
            for c in range(pieces.shape[0] // 2):
                pieces[2 * c + g] = share[c * band : (c + 1) * band]
    else:
        terms = [dot(grad.astype(BF16), basis[d]) for d, grad in enumerate(grads)]
        pieces[...] = terms[0] + terms[1]


def sum_kernel(pieces, out):
    total = pieces[0]
    for i in range(1, pieces.shape[0]):
        total = total + pieces[i]
    half = total.shape[1] // 2
    out[...] = jnp.concatenate([total[:, :half], total[:, half:]], axis=0).astype(BF16)


def call(kernel, outs, ins, specs, scratch=(), flops=0, moved=0, out_specs=None):
    return pl.pallas_call(
        kernel,
        out_shape=outs,
        in_specs=specs,
        out_specs=out_specs or [VMEM] * len(outs),
        scratch_shapes=list(scratch),
        compiler_params=pltpu.CompilerParams(vmem_limit_bytes=LIMIT),
        cost_estimate=pl.CostEstimate(
            flops=flops, bytes_accessed=moved or flops // 200, transcendentals=0
        ),
    )(*ins)


def moved_by(x, pairs):
    return held(lax.ppermute(x, "areal", pairs))


def shift_pairs(columns, k):
    return [(i, (i - k) % columns) for i in range(columns)]


def beside_layers(tiles):
    groups = lax.axis_size("layer")
    if groups == 2:
        return [held(lax.ppermute(tiles[0], "layer", [(0, 1), (1, 0)]))]
    up = [(i, i + 1) for i in range(groups - 1)]
    down = [(i + 1, i) for i in range(groups - 1)]
    return [held(lax.ppermute(tiles[0], "layer", up)), held(lax.ppermute(tiles[-1], "layer", down))]


def outside(x):
    return pltpu.with_memory_space_constraint(x, pltpu.HBM)


def on_device(
    rhs,
    areal_blocks,
    vertical_blocks,
    conn_src,
    conn_count,
    tile_map,
    well_cells,
    well_gain,
    sens,
    basis,
):
    columns = lax.axis_size("areal")
    groups = lax.axis_size("layer")
    two = groups == 2
    rows, width = rhs.shape[2:]
    modes = basis.shape[-1]
    number = conn_src.shape[-1]
    swaps = near_swaps(number)
    routes = [swap_pairs(columns, k, color) for k, color in swaps]
    routes += [shift_pairs(columns, columns // 2 + 1), shift_pairs(columns, columns // 2)]
    rhs = rhs[0].reshape(2 * rows, width)
    me = lax.axis_index("areal").astype(jnp.int32).reshape(1)
    group = lax.axis_index("layer").astype(jnp.int32).reshape(1)

    tile = pltpu.VMEM((rows, width), BF16)
    pair = pltpu.VMEM((2 * rows, width), BF16)
    sums = pltpu.VMEM((2, rows, width), F32)
    one = 2 * rows * width * width
    partial = functools.partial

    masks_type = pltpu.VMEM((8, 128), F32)
    with jax.named_scope("plan"):
        far_pair = moved_by(rhs, routes[-1])
        table, asks, payload = call(
            partial(plan_kernel, columns, swaps),
            [
                jax.ShapeDtypeStruct((2 * number,), jnp.int32),
                masks_type,
                pltpu.VMEM((2 * rows + 16, width), BF16),
            ],
            (outside(conn_src[0, 0]), conn_count[0], outside(tile_map), me, group, outside(rhs)),
            [SMEM] * 5 + [VMEM],
            out_specs=[SMEM] + [VMEM] * 2,
        )
        asks, payload = held(asks), held(payload)

    with jax.named_scope("load"):
        bands, sides = call(
            partial(load_kernel, number, two),
            [
                pltpu.VMEM((number, width, 2 * width), BF16),
                pltpu.VMEM((3 if two else 4, width, width), BF16),
            ],
            (table, group, outside(areal_blocks[0]), outside(vertical_blocks[0])),
            [SMEM] * 2 + [pl.BlockSpec(memory_space=pltpu.HBM)] * 2,
            [pltpu.SemaphoreType.DMA((2 * number + 4,))],
            moved=areal_blocks.size * 2 + vertical_blocks.size * 2,
        )
        bands, sides = held(bands), held(sides)
        (factors,) = call(
            weigh_kernel,
            [pltpu.VMEM((sens.shape[2], 2, sens.shape[3]), F32)],
            (well_cells[0], well_gain[0], sens[0].transpose(1, 0, 2)),
            [SMEM] * 2 + [VMEM],
        )
        weights = held(basis[0])
        if two:
            (weights,) = call(
                partial(turn_kernel, columns),
                [pltpu.VMEM((modes // 2, 4 * sens.shape[3]), BF16)],
                (basis[0],),
                [VMEM],
            )
        factors, weights = held(factors), held(weights)

    rhs_held = held(rhs)
    lam = rhs_held
    sends = [payload] * (number - 2)
    outer = [payload]
    half = len(swaps) // 2
    for step in range(ITERS):
        first = step == 0
        with jax.named_scope("apply"):
            arrived = [moved_by(x, pairs) for x, pairs in zip(sends, routes)]
            (part,) = call(own_kernel, [sums], (lam, rhs_held, sides), [VMEM] * 3, flops=one)
            part = held(part)
            if first:
                even, odd = (arrived[swaps.index((1, color))] for color in (1, 0))
                picked, relayed = call(
                    partial(far_pick_kernel, number),
                    [tile, masks_type],
                    (far_pair, asks, even, odd, part),
                    [VMEM] * 5,
                )
                arrived = [*arrived, moved_by(picked, shift_pairs(columns, 1)), far_pair]
                told = [*arrived[:-2], moved_by(relayed, routes[-1])]
            beside = beside_layers(outer)
            (cross,) = call(
                cross_kernel,
                [sums],
                (asks, bands, *arrived[:half]),
                [VMEM] * (2 + half),
                flops=4 * one,
            )
            (far,) = call(
                far_kernel,
                [sums],
                (asks, bands, held(cross), *arrived[-2:]),
                [VMEM] * 5,
                flops=4 * one,
            )
            tiles = (part, held(far), asks, bands, sides)
            near = (*arrived[half:-2], *beside)
            if step < ITERS - 1:
                lam, *rest = call(
                    partial(update_kernel, number, two, half, first),
                    [pair] + [tile] * (number + len(beside)) + ([masks_type] if first else []),
                    (*tiles, *near, *told),
                    [VMEM] * (5 + len(near) + len(told)),
                    flops=one,
                )
                lam = held(lam)
                if first:
                    told = [held(rest.pop())]
                sends, outer = rest[:number], rest[number:]
            else:
                adjoint, pieces = call(
                    partial(last_kernel, number, two, half),
                    [
                        jax.ShapeDtypeStruct((2, rows, width), BF16),
                        pltpu.VMEM(
                            (2 * columns, modes // columns // 2, rows) if two else (rows, modes), F32
                        ),
                    ],
                    (*tiles, factors, weights, *near),
                    [VMEM] * (7 + len(near)),
                    flops=one,
                )

    with jax.named_scope("project"):
        if two:
            landed = lax.all_to_all(pieces, ("areal", "layer"), 0, 0, tiled=True)
            (coefficients,) = call(
                sum_kernel,
                [jax.ShapeDtypeStruct((modes // columns, rows // 2), BF16)],
                (held(landed),),
                [VMEM],
            )
            coefficients = coefficients.T
        else:
            cut = pieces.reshape(groups, rows // groups, columns, modes // columns)
            cut = cut.transpose(2, 0, 1, 3).reshape(columns * groups, rows // groups, modes // columns)
            landed = lax.all_to_all(cut, ("areal", "layer"), 0, 0, tiled=True)
            coefficients = jnp.sum(landed, axis=0).astype(BF16)
    return (adjoint[None], coefficients)


def solution(mesh):
    in_specs = (
        P("areal", "layer", None, None),
        P("areal", "layer", None, None, None),
        P("areal", "layer", None, None, None),
        P("areal", "layer", None),
        P("areal", "layer"),
        P(),
        P("areal", "layer", None),
        P("areal", "layer", None),
        P("areal", "layer", None, None),
        P("areal", "layer", None, None),
    )
    out_specs = (P("areal", "layer", None, None), P("layer", "areal"))
    return jax.shard_map(
        on_device, mesh=mesh, in_specs=in_specs, out_specs=out_specs, check_vma=False
    )
```

```python
import functools

import jax
import jax.numpy as jnp
from jax import lax
from jax.experimental import pallas as pl
from jax.experimental.pallas import tpu as pltpu
from jax.sharding import PartitionSpec as P

ITERS = 3
F32 = jnp.float32
BF16 = jnp.bfloat16
SMEM = pl.BlockSpec(memory_space=pltpu.SMEM)
VMEM = pl.BlockSpec(memory_space=pltpu.VMEM)
LIMIT = 16 * 1024 * 1024


def near_swaps(count):
    return [(k, color) for color in (1, 0) for k in range(count // 2 - 1, 0, -1)]


def swap_pairs(columns, k, color):
    return [
        (c, (c + k if (c // k) % 2 == color else c - k) % columns) for c in range(columns)
    ]


def held(x):
    return pltpu.with_memory_space_constraint(x, pltpu.VMEM)


def dot(a, b):
    return jnp.dot(a, b, preferred_element_type=F32)


def plan_kernel(columns, swaps, src, count, tile_map, me, group, rhs, table, asks, payload, pair):
    steps = [
        jnp.where(lax.rem(lax.div(me[0], k), 2) == color, k, columns - k) for k, color in swaps
    ] + [columns // 2 + 1, columns // 2]
    number = len(steps)
    conn = [0] * number
    slots = [0] * number
    for s in range(number):
        place = tile_map[src[s]]
        peer = lax.shift_right_logical(place, 1)
        slot = lax.bitwise_and(place, 1)
        away = peer - me[0]
        away = jnp.where(away < 0, away + columns, away)
        for i, k in enumerate(steps):
            hit = away == k
            conn[i] = jnp.where(hit, s, conn[i])
            slots[i] = jnp.where(hit, slot, slots[i])
    rows, width = rhs.shape
    line = lax.broadcasted_iota(jnp.int32, (16, width), 0)
    asked = jnp.zeros(line.shape, F32)
    for i in range(number):
        table[i] = conn[i]
        table[number + i] = jnp.where(conn[i] < count[0], 1, 0)
        asked = jnp.where(line == i, slots[i].astype(F32), asked)
    asked = jnp.where(line == number, group[0].astype(F32), asked)
    asked = jnp.where(line == number + 1, lax.rem(me[0], 2).astype(F32), asked)
    asks[...] = asked[0:8, 0:128]
    payload[0:rows] = rhs[...]
    payload[rows:] = asked.astype(BF16)
    pair[...] = rhs[...]


def load_kernel(number, two, table, group, blocks, vert, bands, sides, sems):
    width = vert.shape[-1]
    mine = group[0]
    ends = [(1 - mine, 1 - mine)] if two else [(0, 0), (1, 1)]
    beside = [
        pltpu.make_async_copy(vert.at[d, k], sides.at[i], sems.at[2 * number + i])
        for i, (d, k) in enumerate([(0, 1), (1, 0), *ends])
    ]
    for copy in beside:
        copy.start()

    def copies(i):
        return [
            pltpu.make_async_copy(
                blocks.at[d, table[i]],
                bands.at[i, :, pl.ds(d * width, width)],
                sems.at[2 * i + d],
            )
            for d in range(2)
        ]

    for i in range(number):

        @pl.when(table[number + i] > 0)
        def _():
            for copy in copies(i):
                copy.start()

        @pl.when(table[number + i] == 0)
        def _():
            bands[i] = jnp.zeros(bands.shape[1:], bands.dtype)

    for i in range(number):

        @pl.when(table[number + i] > 0)
        def _():
            for copy in copies(i):
                copy.wait()

    for copy in beside:
        copy.wait()


def turn_kernel(columns, basis, turned):
    _, cells, modes = basis.shape
    bands = []
    for d in range(2):
        by_mode = basis[d].astype(F32).T.reshape(columns, 2, modes // columns // 2, cells)
        bands += [by_mode[:, h].reshape(modes // 2, cells) for h in range(2)]
    turned[...] = jnp.concatenate(bands, axis=1).astype(BF16)


def weigh_kernel(wells, gains, sens, factors):
    cells = sens.shape[-1]
    spot = lax.broadcasted_iota(jnp.int32, (1, cells), 1)
    factors[...] = sens[...]
    for d in range(2):
        well = jnp.zeros((1, cells), F32)
        for w in range(wells.shape[1]):
            well = well + jnp.where(spot == wells[d, w], gains[d, w], 0.0)
        factors[0, d : d + 1, :] = sens[0, d : d + 1, :] + well


def wide(mask, width):
    return jnp.concatenate([mask] * (width // mask.shape[1]), axis=1)


def chosen(mask, low, high):
    return jnp.where(wide(mask, low.shape[1]) > 0.5, high, low).astype(BF16)


def asks_of(payload):
    return payload[payload.shape[0] - 16 :, 0:128].astype(F32)


def tile_of(ref, mask, rows):
    if ref.shape[0] == rows:
        return ref[...]
    return chosen(mask, ref[0:rows].astype(F32), ref[rows : 2 * rows].astype(F32))


def relay_ask_kernel(number, even, odd, asks, relayed):
    parity = asks[number + 1 : number + 2, :]
    ask = [asks_of(ref)[number - 2 : number - 1, :] for ref in (even, odd)]
    relayed[...] = asks[...]
    relayed[number - 2 : number - 1, :] = jnp.where(parity > 0.5, ask[1], ask[0])


def far_pick_kernel(number, pair, relayed, part, tile):
    tile[...] = tile_of(pair, relayed[number - 2 : number - 1, :], tile.shape[0])


def own_kernel(lam, rhs, sides, part):
    rows = rhs.shape[0] // 2
    part[0] = rhs[0:rows].astype(F32) - dot(lam[rows : 2 * rows], sides[0])
    part[1] = rhs[rows:].astype(F32) - dot(lam[0:rows], sides[1])


def source_sums(asks, bands, begin, refs, rows):
    tiles = [tile_of(ref, asks[i : i + 1, :], rows) for i, ref in enumerate(refs, begin)]
    count, width, both = len(refs), bands.shape[1], bands.shape[2]
    band = bands[begin : begin + count].reshape(count * width, both)
    sums = dot(jnp.concatenate(tiles, axis=1), band)
    return sums[:, :width], sums[:, width:]


def beside_sums(number, two, asks, sides, beside, rows):
    if two:
        mine = asks[number : number + 1, :]
        term = dot(tile_of(beside[0], mine, rows), sides[2])
        above = wide(mine, term.shape[1]) > 0.5
        none = jnp.zeros_like(term)
        return jnp.where(above, term, none), jnp.where(above, none, term)
    return [
        dot(tile_of(beside[d], jnp.full((1, 128), 1.0 - d, F32), rows), sides[2 + d])
        for d in range(2)
    ]


def cross_kernel(asks, bands, *refs):
    arrived, out = refs[:-1], refs[-1]
    out[0], out[1] = source_sums(asks, bands, 0, arrived, out.shape[1])


def far_kernel(asks, bands, cross, *refs):
    far, out = refs[:-1], refs[-1]
    low, high = source_sums(asks, bands, bands.shape[0] - len(far), far, out.shape[1])
    out[0] = cross[0] + low
    out[1] = cross[1] + high


def updated(number, two, begin, part, far, asks, bands, sides, near, beside):
    rows = part.shape[1]
    sums = source_sums(asks, bands, begin, near, rows)
    terms = beside_sums(number, two, asks, sides, beside, rows)
    return [part[d] - far[d] - sums[d] - terms[d] for d in range(2)]


def update_kernel(number, two, begin, first, part, far, asks, bands, sides, *refs):
    ends = 1 if two else 2
    here = number - 2 - begin
    near, refs = refs[:here], refs[here:]
    beside, refs = refs[:ends], refs[ends:]
    count = number - 1 if first else 1
    told, refs = refs[:count], refs[count:]
    low, high = updated(number, two, begin, part, far, asks, bands, sides, near, beside)
    lam, sends, refs = refs[0], refs[1 : 1 + number], refs[1 + number :]
    outer, refs = refs[:ends], refs[ends:]
    masks = told[0]
    if first:
        masks = refs[0]
        masks[...] = told[-1][...]
        for i in range(number - 2):
            masks[i : i + 1, :] = asks_of(told[i])[i : i + 1, :]
    rows = low.shape[0]
    lam[0:rows] = low.astype(BF16)
    lam[rows:] = high.astype(BF16)
    for i, send in enumerate(sends):
        send[...] = chosen(masks[i : i + 1, :], low, high)
    if two:
        outer[0][...] = chosen(asks[number : number + 1, :], high, low)
    else:
        outer[0][...] = high.astype(BF16)
        outer[1][...] = low.astype(BF16)


def last_kernel(number, two, begin, part, far, asks, bands, sides, factors, basis, *refs):
    here = number - 2 - begin
    near, beside, (lam, pieces) = refs[:here], refs[here:-2], refs[-2:]
    sums = updated(number, two, begin, part, far, asks, bands, sides, near, beside)
    phases, _, cells = factors.shape
    grads = []
    for d in range(2):
        rounded = sums[d].astype(BF16)
        lam[d] = rounded
        back = rounded.astype(F32)
        grad = back[:, :cells] * factors[0, d : d + 1, :]
        for p in range(1, phases):
            grad = grad + back[:, p * cells : (p + 1) * cells] * factors[p, d : d + 1, :]
        grads.append(grad)
    if two:
        half = grads[0].shape[0] // 2
        none = jnp.zeros((half, cells), F32)
        band = pieces.shape[1]
        for g in range(2):
            cuts = [grad[g * half : (g + 1) * half] for grad in grads]
            top = jnp.concatenate([x for cut in cuts for x in (cut, none)], axis=1)
            low = jnp.concatenate([x for cut in cuts for x in (none, cut)], axis=1)
            wing = jnp.concatenate([top, low], axis=0).astype(BF16)
            share = lax.dot_general(
                basis[...], wing, (((1,), (1,)), ((), ())), preferred_element_type=F32
            )
            for c in range(pieces.shape[0] // 2):
                pieces[2 * c + g] = share[c * band : (c + 1) * band]
    else:
        terms = [dot(grad.astype(BF16), basis[d]) for d, grad in enumerate(grads)]
        pieces[...] = terms[0] + terms[1]


def sum_kernel(pieces, out):
    total = pieces[0]
    for i in range(1, pieces.shape[0]):
        total = total + pieces[i]
    half = total.shape[1] // 2
    out[...] = jnp.concatenate([total[:, :half], total[:, half:]], axis=0).astype(BF16)


def call(kernel, outs, ins, specs, scratch=(), flops=0, moved=0, out_specs=None):
    return pl.pallas_call(
        kernel,
        out_shape=outs,
        in_specs=specs,
        out_specs=out_specs or [VMEM] * len(outs),
        scratch_shapes=list(scratch),
        compiler_params=pltpu.CompilerParams(vmem_limit_bytes=LIMIT),
        cost_estimate=pl.CostEstimate(
            flops=flops, bytes_accessed=moved or flops // 200, transcendentals=0
        ),
    )(*ins)


def moved_by(x, pairs):
    return held(lax.ppermute(x, "areal", pairs))


def shift_pairs(columns, k):
    return [(i, (i - k) % columns) for i in range(columns)]


def beside_layers(tiles):
    groups = lax.axis_size("layer")
    if groups == 2:
        return [held(lax.ppermute(tiles[0], "layer", [(0, 1), (1, 0)]))]
    up = [(i, i + 1) for i in range(groups - 1)]
    down = [(i + 1, i) for i in range(groups - 1)]
    return [held(lax.ppermute(tiles[0], "layer", up)), held(lax.ppermute(tiles[-1], "layer", down))]


def outside(x):
    return pltpu.with_memory_space_constraint(x, pltpu.HBM)


def on_device(
    rhs,
    areal_blocks,
    vertical_blocks,
    conn_src,
    conn_count,
    tile_map,
    well_cells,
    well_gain,
    sens,
    basis,
):
    columns = lax.axis_size("areal")
    groups = lax.axis_size("layer")
    two = groups == 2
    rows, width = rhs.shape[2:]
    modes = basis.shape[-1]
    number = conn_src.shape[-1]
    swaps = near_swaps(number)
    routes = [swap_pairs(columns, k, color) for k, color in swaps]
    routes += [shift_pairs(columns, columns // 2 + 1), shift_pairs(columns, columns // 2)]
    rhs = rhs[0].reshape(2 * rows, width)
    me = lax.axis_index("areal").astype(jnp.int32).reshape(1)
    group = lax.axis_index("layer").astype(jnp.int32).reshape(1)

    tile = pltpu.VMEM((rows, width), BF16)
    pair = pltpu.VMEM((2 * rows, width), BF16)
    sums = pltpu.VMEM((2, rows, width), F32)
    one = 2 * rows * width * width
    partial = functools.partial

    masks_type = pltpu.VMEM((8, 128), F32)
    with jax.named_scope("plan"):
        table, asks, payload, both = call(
            partial(plan_kernel, columns, swaps),
            [
                jax.ShapeDtypeStruct((2 * number,), jnp.int32),
                masks_type,
                pltpu.VMEM((2 * rows + 16, width), BF16),
                pair,
            ],
            (outside(conn_src[0, 0]), conn_count[0], outside(tile_map), me, group, outside(rhs)),
            [SMEM] * 5 + [VMEM],
            out_specs=[SMEM] + [VMEM] * 3,
        )
        asks, payload, both = held(asks), held(payload), held(both)
        far_pair = moved_by(both, routes[-1])

    with jax.named_scope("load"):
        bands, sides = call(
            partial(load_kernel, number, two),
            [
                pltpu.VMEM((number, width, 2 * width), BF16),
                pltpu.VMEM((3 if two else 4, width, width), BF16),
            ],
            (table, group, outside(areal_blocks[0]), outside(vertical_blocks[0])),
            [SMEM] * 2 + [pl.BlockSpec(memory_space=pltpu.HBM)] * 2,
            [pltpu.SemaphoreType.DMA((2 * number + 4,))],
            moved=areal_blocks.size * 2 + vertical_blocks.size * 2,
        )
        bands, sides = held(bands), held(sides)
        (factors,) = call(
            weigh_kernel,
            [pltpu.VMEM((sens.shape[2], 2, sens.shape[3]), F32)],
            (well_cells[0], well_gain[0], sens[0].transpose(1, 0, 2)),
            [SMEM] * 2 + [VMEM],
        )
        weights = held(basis[0])
        if two:
            (weights,) = call(
                partial(turn_kernel, columns),
                [pltpu.VMEM((modes // 2, 4 * sens.shape[3]), BF16)],
                (basis[0],),
                [VMEM],
            )
        factors, weights = held(factors), held(weights)

    rhs_held = lam = both
    sends = [payload] * (number - 2)
    outer = [payload]
    half = len(swaps) // 2
    for step in range(ITERS):
        first = step == 0
        with jax.named_scope("apply"):
            arrived = [moved_by(x, pairs) for x, pairs in zip(sends, routes)]
            (part,) = call(own_kernel, [sums], (lam, rhs_held, sides), [VMEM] * 3, flops=one)
            part = held(part)
            if first:
                even, odd = (arrived[swaps.index((1, color))] for color in (1, 0))
                (relayed,) = call(
                    partial(relay_ask_kernel, number),
                    [masks_type],
                    (even, odd, asks),
                    [VMEM] * 3,
                    flops=4 * one,
                )
                relayed = held(relayed)
                (picked,) = call(
                    partial(far_pick_kernel, number),
                    [tile],
                    (far_pair, relayed, part),
                    [VMEM] * 3,
                )
                arrived = [*arrived, moved_by(picked, shift_pairs(columns, 1)), far_pair]
                told = [*arrived[:-2], moved_by(relayed, routes[-1])]
            beside = beside_layers(outer)
            (cross,) = call(
                cross_kernel,
                [sums],
                (asks, bands, *arrived[:half]),
                [VMEM] * (2 + half),
                flops=4 * one,
            )
            (far,) = call(
                far_kernel,
                [sums],
                (asks, bands, held(cross), *arrived[-2:]),
                [VMEM] * 5,
                flops=4 * one,
            )
            tiles = (part, held(far), asks, bands, sides)
            near = (*arrived[half:-2], *beside)
            if step < ITERS - 1:
                lam, *rest = call(
                    partial(update_kernel, number, two, half, first),
                    [pair] + [tile] * (number + len(beside)) + ([masks_type] if first else []),
                    (*tiles, *near, *told),
                    [VMEM] * (5 + len(near) + len(told)),
                    flops=one,
                )
                lam = held(lam)
                if first:
                    told = [held(rest.pop())]
                sends, outer = rest[:number], rest[number:]
            else:
                adjoint, pieces = call(
                    partial(last_kernel, number, two, half),
                    [
                        jax.ShapeDtypeStruct((2, rows, width), BF16),
                        pltpu.VMEM(
                            (2 * columns, modes // columns // 2, rows) if two else (rows, modes), F32
                        ),
                    ],
                    (*tiles, factors, weights, *near),
                    [VMEM] * (7 + len(near)),
                    flops=one,
                )

    with jax.named_scope("project"):
        if two:
            landed = lax.all_to_all(pieces, ("areal", "layer"), 0, 0, tiled=True)
            (coefficients,) = call(
                sum_kernel,
                [jax.ShapeDtypeStruct((modes // columns, rows // 2), BF16)],
                (held(landed),),
                [VMEM],
            )
            coefficients = coefficients.T
        else:
            cut = pieces.reshape(groups, rows // groups, columns, modes // columns)
            cut = cut.transpose(2, 0, 1, 3).reshape(columns * groups, rows // groups, modes // columns)
            landed = lax.all_to_all(cut, ("areal", "layer"), 0, 0, tiled=True)
            coefficients = jnp.sum(landed, axis=0).astype(BF16)
    return (adjoint[None], coefficients)


def solution(mesh):
    in_specs = (
        P("areal", "layer", None, None),
        P("areal", "layer", None, None, None),
        P("areal", "layer", None, None, None),
        P("areal", "layer", None),
        P("areal", "layer"),
        P(),
        P("areal", "layer", None),
        P("areal", "layer", None),
        P("areal", "layer", None, None),
        P("areal", "layer", None, None),
    )
    out_specs = (P("areal", "layer", None, None), P("layer", "areal"))
    return jax.shard_map(
        on_device, mesh=mesh, in_specs=in_specs, out_specs=out_specs, check_vma=False
    )
```

```python
import functools

import jax
import jax.numpy as jnp
from jax import lax
from jax.experimental import pallas as pl
from jax.experimental.pallas import tpu as pltpu
from jax.sharding import PartitionSpec as P

ITERS = 3
F32 = jnp.float32
BF16 = jnp.bfloat16
SMEM = pl.BlockSpec(memory_space=pltpu.SMEM)
VMEM = pl.BlockSpec(memory_space=pltpu.VMEM)
LIMIT = 16 * 1024 * 1024


def near_swaps(count):
    return [(k, color) for color in (1, 0) for k in range(count // 2 - 1, 0, -1)]


def swap_pairs(columns, k, color):
    return [
        (c, (c + k if (c // k) % 2 == color else c - k) % columns) for c in range(columns)
    ]


def held(x):
    return pltpu.with_memory_space_constraint(x, pltpu.VMEM)


def dot(a, b):
    return jnp.dot(a, b, preferred_element_type=F32)


def plan_kernel(columns, swaps, src, count, tile_map, me, group, rhs, table, asks, payload, pair):
    steps = [
        jnp.where(lax.rem(lax.div(me[0], k), 2) == color, k, columns - k) for k, color in swaps
    ] + [columns // 2 + 1, columns // 2]
    number = len(steps)
    conn = [0] * number
    slots = [0] * number
    for s in range(number):
        place = tile_map[src[s]]
        peer = lax.shift_right_logical(place, 1)
        slot = lax.bitwise_and(place, 1)
        away = peer - me[0]
        away = jnp.where(away < 0, away + columns, away)
        for i, k in enumerate(steps):
            hit = away == k
            conn[i] = jnp.where(hit, s, conn[i])
            slots[i] = jnp.where(hit, slot, slots[i])
    rows, width = rhs.shape
    line = lax.broadcasted_iota(jnp.int32, (16, width), 0)
    asked = jnp.zeros(line.shape, F32)
    for i in range(number):
        table[i] = conn[i]
        table[number + i] = jnp.where(conn[i] < count[0], 1, 0)
        asked = jnp.where(line == i, slots[i].astype(F32), asked)
    asked = jnp.where(line == number, group[0].astype(F32), asked)
    asked = jnp.where(line == number + 1, lax.rem(me[0], 2).astype(F32), asked)
    asks[...] = asked[0:8, 0:128]
    payload[0:rows] = rhs[...]
    payload[rows:] = asked.astype(BF16)
    pair[...] = rhs[...]


def load_kernel(number, two, table, group, blocks, vert, bands, sides, sems):
    width = vert.shape[-1]
    mine = group[0]
    ends = [(1 - mine, 1 - mine)] if two else [(0, 0), (1, 1)]
    beside = [
        pltpu.make_async_copy(vert.at[d, k], sides.at[i], sems.at[2 * number + i])
        for i, (d, k) in enumerate([(0, 1), (1, 0), *ends])
    ]
    for copy in beside:
        copy.start()

    def copies(i):
        return [
            pltpu.make_async_copy(
                blocks.at[d, table[i]],
                bands.at[i, :, pl.ds(d * width, width)],
                sems.at[2 * i + d],
            )
            for d in range(2)
        ]

    for i in range(number):

        @pl.when(table[number + i] > 0)
        def _():
            for copy in copies(i):
                copy.start()

        @pl.when(table[number + i] == 0)
        def _():
            bands[i] = jnp.zeros(bands.shape[1:], bands.dtype)

    for i in range(number):

        @pl.when(table[number + i] > 0)
        def _():
            for copy in copies(i):
                copy.wait()

    for copy in beside:
        copy.wait()


def turn_kernel(columns, basis, turned):
    _, cells, modes = basis.shape
    bands = []
    for d in range(2):
        by_mode = basis[d].astype(F32).T.reshape(columns, 2, modes // columns // 2, cells)
        bands += [by_mode[:, h].reshape(modes // 2, cells) for h in range(2)]
    turned[...] = jnp.concatenate(bands, axis=1).astype(BF16)


def weigh_kernel(wells, gains, sens, factors):
    cells = sens.shape[-1]
    spot = lax.broadcasted_iota(jnp.int32, (1, cells), 1)
    factors[...] = sens[...]
    for d in range(2):
        well = jnp.zeros((1, cells), F32)
        for w in range(wells.shape[1]):
            well = well + jnp.where(spot == wells[d, w], gains[d, w], 0.0)
        factors[0, d : d + 1, :] = sens[0, d : d + 1, :] + well


def wide(mask, width):
    return jnp.concatenate([mask] * (width // mask.shape[1]), axis=1)


def chosen(mask, low, high):
    return jnp.where(wide(mask, low.shape[1]) > 0.5, high, low).astype(BF16)


def asks_of(payload):
    return payload[payload.shape[0] - 16 :, 0:128].astype(F32)


def tile_of(ref, mask, rows):
    if ref.shape[0] == rows:
        return ref[...]
    return chosen(mask, ref[0:rows].astype(F32), ref[rows : 2 * rows].astype(F32))


def relay_ask_kernel(number, even, odd, asks, relayed):
    parity = asks[number + 1 : number + 2, :]
    ask = [asks_of(ref)[number - 2 : number - 1, :] for ref in (even, odd)]
    relayed[...] = asks[...]
    relayed[number - 2 : number - 1, :] = jnp.where(parity > 0.5, ask[1], ask[0])


def far_pick_kernel(number, pair, relayed, part, tile):
    tile[...] = tile_of(pair, relayed[number - 2 : number - 1, :], tile.shape[0])


def own_kernel(lam, rhs, sides, part):
    rows = rhs.shape[0] // 2
    part[0] = rhs[0:rows].astype(F32) - dot(lam[rows : 2 * rows], sides[0])
    part[1] = rhs[rows:].astype(F32) - dot(lam[0:rows], sides[1])


def source_sums(asks, bands, begin, refs, rows):
    tiles = [tile_of(ref, asks[i : i + 1, :], rows) for i, ref in enumerate(refs, begin)]
    count, width, both = len(refs), bands.shape[1], bands.shape[2]
    band = bands[begin : begin + count].reshape(count * width, both)
    sums = dot(jnp.concatenate(tiles, axis=1), band)
    return sums[:, :width], sums[:, width:]


def beside_sums(number, two, asks, sides, beside, rows):
    if two:
        mine = asks[number : number + 1, :]
        term = dot(tile_of(beside[0], mine, rows), sides[2])
        above = wide(mine, term.shape[1]) > 0.5
        none = jnp.zeros_like(term)
        return jnp.where(above, term, none), jnp.where(above, none, term)
    return [
        dot(tile_of(beside[d], jnp.full((1, 128), 1.0 - d, F32), rows), sides[2 + d])
        for d in range(2)
    ]


def cross_kernel(asks, bands, *refs):
    arrived, out = refs[:-1], refs[-1]
    out[0], out[1] = source_sums(asks, bands, 0, arrived, out.shape[1])


def far_kernel(asks, bands, cross, *refs):
    far, out = refs[:-1], refs[-1]
    low, high = source_sums(asks, bands, bands.shape[0] - len(far), far, out.shape[1])
    out[0] = cross[0] + low
    out[1] = cross[1] + high


def updated(number, two, begin, part, far, asks, bands, sides, near, beside):
    rows = part.shape[1]
    sums = source_sums(asks, bands, begin, near, rows)
    terms = beside_sums(number, two, asks, sides, beside, rows)
    return [part[d] - far[d] - sums[d] - terms[d] for d in range(2)]


def update_kernel(number, two, begin, first, part, far, asks, bands, sides, *refs):
    ends = 1 if two else 2
    here = number - 2 - begin
    near, refs = refs[:here], refs[here:]
    beside, refs = refs[:ends], refs[ends:]
    count = number - 1 if first else 1
    told, refs = refs[:count], refs[count:]
    low, high = updated(number, two, begin, part, far, asks, bands, sides, near, beside)
    lam, sends, refs = refs[0], refs[1 : 1 + number], refs[1 + number :]
    outer, refs = refs[:ends], refs[ends:]
    masks = told[0]
    if first:
        masks = refs[0]
        masks[...] = told[-1][...]
        for i in range(number - 2):
            masks[i : i + 1, :] = asks_of(told[i])[i : i + 1, :]
    rows = low.shape[0]
    lam[0:rows] = low.astype(BF16)
    lam[rows:] = high.astype(BF16)
    for i, send in enumerate(sends):
        send[...] = chosen(masks[i : i + 1, :], low, high)
    if two:
        outer[0][...] = chosen(asks[number : number + 1, :], high, low)
    else:
        outer[0][...] = high.astype(BF16)
        outer[1][...] = low.astype(BF16)


def last_kernel(number, two, begin, part, far, asks, bands, sides, factors, basis, *refs):
    here = number - 2 - begin
    near, beside, (lam, pieces) = refs[:here], refs[here:-2], refs[-2:]
    sums = updated(number, two, begin, part, far, asks, bands, sides, near, beside)
    phases, _, cells = factors.shape
    grads = []
    for d in range(2):
        rounded = sums[d].astype(BF16)
        lam[d] = rounded
        back = rounded.astype(F32)
        grad = back[:, :cells] * factors[0, d : d + 1, :]
        for p in range(1, phases):
            grad = grad + back[:, p * cells : (p + 1) * cells] * factors[p, d : d + 1, :]
        grads.append(grad)
    if two:
        half = grads[0].shape[0] // 2
        none = jnp.zeros((half, cells), F32)
        band = pieces.shape[1]
        for g in range(2):
            cuts = [grad[g * half : (g + 1) * half] for grad in grads]
            top = jnp.concatenate([x for cut in cuts for x in (cut, none)], axis=1)
            low = jnp.concatenate([x for cut in cuts for x in (none, cut)], axis=1)
            wing = jnp.concatenate([top, low], axis=0).astype(BF16)
            share = lax.dot_general(
                basis[...], wing, (((1,), (1,)), ((), ())), preferred_element_type=F32
            )
            for c in range(pieces.shape[0] // 2):
                pieces[2 * c + g] = share[c * band : (c + 1) * band].astype(BF16)
    else:
        terms = [dot(grad.astype(BF16), basis[d]) for d, grad in enumerate(grads)]
        pieces[...] = terms[0] + terms[1]


def sum_kernel(pieces, out):
    total = pieces[0].astype(F32)
    for i in range(1, pieces.shape[0]):
        total = total + pieces[i].astype(F32)
    half = total.shape[1] // 2
    out[...] = jnp.concatenate([total[:, :half], total[:, half:]], axis=0).astype(BF16)


def call(kernel, outs, ins, specs, scratch=(), flops=0, moved=0, out_specs=None):
    return pl.pallas_call(
        kernel,
        out_shape=outs,
        in_specs=specs,
        out_specs=out_specs or [VMEM] * len(outs),
        scratch_shapes=list(scratch),
        compiler_params=pltpu.CompilerParams(vmem_limit_bytes=LIMIT),
        cost_estimate=pl.CostEstimate(
            flops=flops, bytes_accessed=moved or flops // 200, transcendentals=0
        ),
    )(*ins)


def moved_by(x, pairs):
    return held(lax.ppermute(x, "areal", pairs))


def shift_pairs(columns, k):
    return [(i, (i - k) % columns) for i in range(columns)]


def beside_layers(tiles):
    groups = lax.axis_size("layer")
    if groups == 2:
        return [held(lax.ppermute(tiles[0], "layer", [(0, 1), (1, 0)]))]
    up = [(i, i + 1) for i in range(groups - 1)]
    down = [(i + 1, i) for i in range(groups - 1)]
    return [held(lax.ppermute(tiles[0], "layer", up)), held(lax.ppermute(tiles[-1], "layer", down))]


def outside(x):
    return pltpu.with_memory_space_constraint(x, pltpu.HBM)


def on_device(
    rhs,
    areal_blocks,
    vertical_blocks,
    conn_src,
    conn_count,
    tile_map,
    well_cells,
    well_gain,
    sens,
    basis,
):
    columns = lax.axis_size("areal")
    groups = lax.axis_size("layer")
    two = groups == 2
    rows, width = rhs.shape[2:]
    modes = basis.shape[-1]
    number = conn_src.shape[-1]
    swaps = near_swaps(number)
    routes = [swap_pairs(columns, k, color) for k, color in swaps]
    routes += [shift_pairs(columns, columns // 2 + 1), shift_pairs(columns, columns // 2)]
    rhs = rhs[0].reshape(2 * rows, width)
    me = lax.axis_index("areal").astype(jnp.int32).reshape(1)
    group = lax.axis_index("layer").astype(jnp.int32).reshape(1)

    tile = pltpu.VMEM((rows, width), BF16)
    pair = pltpu.VMEM((2 * rows, width), BF16)
    sums = pltpu.VMEM((2, rows, width), F32)
    one = 2 * rows * width * width
    partial = functools.partial

    masks_type = pltpu.VMEM((8, 128), F32)
    with jax.named_scope("plan"):
        table, asks, payload, both = call(
            partial(plan_kernel, columns, swaps),
            [
                jax.ShapeDtypeStruct((2 * number,), jnp.int32),
                masks_type,
                pltpu.VMEM((2 * rows + 16, width), BF16),
                pair,
            ],
            (outside(conn_src[0, 0]), conn_count[0], outside(tile_map), me, group, outside(rhs)),
            [SMEM] * 5 + [VMEM],
            out_specs=[SMEM] + [VMEM] * 3,
        )
        asks, payload, both = held(asks), held(payload), held(both)
        far_pair = moved_by(both, routes[-1])

    with jax.named_scope("load"):
        bands, sides = call(
            partial(load_kernel, number, two),
            [
                pltpu.VMEM((number, width, 2 * width), BF16),
                pltpu.VMEM((3 if two else 4, width, width), BF16),
            ],
            (table, group, outside(areal_blocks[0]), outside(vertical_blocks[0])),
            [SMEM] * 2 + [pl.BlockSpec(memory_space=pltpu.HBM)] * 2,
            [pltpu.SemaphoreType.DMA((2 * number + 4,))],
            moved=areal_blocks.size * 2 + vertical_blocks.size * 2,
        )
        bands, sides = held(bands), held(sides)
        (factors,) = call(
            weigh_kernel,
            [pltpu.VMEM((sens.shape[2], 2, sens.shape[3]), F32)],
            (well_cells[0], well_gain[0], sens[0].transpose(1, 0, 2)),
            [SMEM] * 2 + [VMEM],
        )
        weights = held(basis[0])
        if two:
            (weights,) = call(
                partial(turn_kernel, columns),
                [pltpu.VMEM((modes // 2, 4 * sens.shape[3]), BF16)],
                (basis[0],),
                [VMEM],
            )
        factors, weights = held(factors), held(weights)

    rhs_held = lam = both
    sends = [payload] * (number - 2)
    outer = [payload]
    half = len(swaps) // 2
    for step in range(ITERS):
        first = step == 0
        with jax.named_scope("apply"):
            arrived = [moved_by(x, pairs) for x, pairs in zip(sends, routes)]
            (part,) = call(own_kernel, [sums], (lam, rhs_held, sides), [VMEM] * 3, flops=one)
            part = held(part)
            if first:
                even, odd = (arrived[swaps.index((1, color))] for color in (1, 0))
                (relayed,) = call(
                    partial(relay_ask_kernel, number),
                    [masks_type],
                    (even, odd, asks),
                    [VMEM] * 3,
                    flops=4 * one,
                )
                relayed = held(relayed)
                (picked,) = call(
                    partial(far_pick_kernel, number),
                    [tile],
                    (far_pair, relayed, part),
                    [VMEM] * 3,
                )
                arrived = [*arrived, moved_by(picked, shift_pairs(columns, 1)), far_pair]
                told = [*arrived[:-2], moved_by(relayed, routes[-1])]
            beside = beside_layers(outer)
            (cross,) = call(
                cross_kernel,
                [sums],
                (asks, bands, *arrived[:half]),
                [VMEM] * (2 + half),
                flops=4 * one,
            )
            (far,) = call(
                far_kernel,
                [sums],
                (asks, bands, held(cross), *arrived[-2:]),
                [VMEM] * 5,
                flops=4 * one,
            )
            tiles = (part, held(far), asks, bands, sides)
            near = (*arrived[half:-2], *beside)
            if step < ITERS - 1:
                lam, *rest = call(
                    partial(update_kernel, number, two, half, first),
                    [pair] + [tile] * (number + len(beside)) + ([masks_type] if first else []),
                    (*tiles, *near, *told),
                    [VMEM] * (5 + len(near) + len(told)),
                    flops=one,
                )
                lam = held(lam)
                if first:
                    told = [held(rest.pop())]
                sends, outer = rest[:number], rest[number:]
            else:
                adjoint, pieces = call(
                    partial(last_kernel, number, two, half),
                    [
                        jax.ShapeDtypeStruct((2, rows, width), BF16),
                        pltpu.VMEM((2 * columns, modes // columns // 2, rows), BF16)
                        if two
                        else pltpu.VMEM((rows, modes), F32),
                    ],
                    (*tiles, factors, weights, *near),
                    [VMEM] * (7 + len(near)),
                    flops=one,
                )

    with jax.named_scope("project"):
        if two:
            landed = lax.all_to_all(pieces, ("areal", "layer"), 0, 0, tiled=True)
            (coefficients,) = call(
                sum_kernel,
                [jax.ShapeDtypeStruct((modes // columns, rows // 2), BF16)],
                (held(landed),),
                [VMEM],
            )
            coefficients = coefficients.T
        else:
            cut = pieces.reshape(groups, rows // groups, columns, modes // columns)
            cut = cut.transpose(2, 0, 1, 3).reshape(columns * groups, rows // groups, modes // columns)
            landed = lax.all_to_all(cut, ("areal", "layer"), 0, 0, tiled=True)
            coefficients = jnp.sum(landed, axis=0).astype(BF16)
    return (adjoint[None], coefficients)


def solution(mesh):
    in_specs = (
        P("areal", "layer", None, None),
        P("areal", "layer", None, None, None),
        P("areal", "layer", None, None, None),
        P("areal", "layer", None),
        P("areal", "layer"),
        P(),
        P("areal", "layer", None),
        P("areal", "layer", None),
        P("areal", "layer", None, None),
        P("areal", "layer", None, None),
    )
    out_specs = (P("areal", "layer", None, None), P("layer", "areal"))
    return jax.shard_map(
        on_device, mesh=mesh, in_specs=in_specs, out_specs=out_specs, check_vma=False
    )
```

```python
import functools

import jax
import jax.numpy as jnp
from jax import lax
from jax.experimental import pallas as pl
from jax.experimental.pallas import tpu as pltpu
from jax.sharding import PartitionSpec as P

ITERS = 3
F32 = jnp.float32
BF16 = jnp.bfloat16
SMEM = pl.BlockSpec(memory_space=pltpu.SMEM)
VMEM = pl.BlockSpec(memory_space=pltpu.VMEM)
LIMIT = 16 * 1024 * 1024


def near_swaps(count):
    return [(k, color) for color in (1, 0) for k in range(count // 2 - 1, 0, -1)]


def swap_pairs(columns, k, color):
    return [
        (c, (c + k if (c // k) % 2 == color else c - k) % columns) for c in range(columns)
    ]


def kept_pairs(pairs):
    half = len(pairs) // 2
    return [(at, to) for at, to in pairs if at // half == to // half]


def mirrored_pairs(pairs):
    columns, half = len(pairs), len(pairs) // 2
    return [((at + half) % columns, to) for at, to in pairs if at // half != to // half]


def held(x):
    return pltpu.with_memory_space_constraint(x, pltpu.VMEM)


def dot(a, b):
    return jnp.dot(a, b, preferred_element_type=F32)


def plan_kernel(columns, swaps, src, count, tile_map, me, group, rhs, table, asks, payload, pair):
    steps = [
        jnp.where(lax.rem(lax.div(me[0], k), 2) == color, k, columns - k) for k, color in swaps
    ] + [columns // 2 + 1, columns // 2]
    number = len(steps)
    conn = [0] * number
    slots = [0] * number
    for s in range(number):
        place = tile_map[src[s]]
        peer = lax.shift_right_logical(place, 1)
        slot = lax.bitwise_and(place, 1)
        away = peer - me[0]
        away = jnp.where(away < 0, away + columns, away)
        for i, k in enumerate(steps):
            hit = away == k
            conn[i] = jnp.where(hit, s, conn[i])
            slots[i] = jnp.where(hit, slot, slots[i])
    rows, width = rhs.shape
    line = lax.broadcasted_iota(jnp.int32, (16, width), 0)
    asked = jnp.zeros(line.shape, F32)
    for i in range(number):
        table[i] = conn[i]
        table[number + i] = jnp.where(conn[i] < count[0], 1, 0)
        asked = jnp.where(line == i, slots[i].astype(F32), asked)
    asked = jnp.where(line == number, group[0].astype(F32), asked)
    asked = jnp.where(line == number + 1, lax.rem(me[0], 2).astype(F32), asked)
    asks[...] = asked[0:8, 0:128]
    payload[0:rows] = rhs[...]
    payload[rows:] = asked.astype(BF16)
    pair[...] = rhs[...]


def load_kernel(number, two, table, group, blocks, vert, bands, sides, sems):
    width = vert.shape[-1]
    mine = group[0]
    ends = [(1 - mine, 1 - mine)] if two else [(0, 0), (1, 1)]
    beside = [
        pltpu.make_async_copy(vert.at[d, k], sides.at[i], sems.at[2 * number + i])
        for i, (d, k) in enumerate([(0, 1), (1, 0), *ends])
    ]
    for copy in beside:
        copy.start()

    def copies(i):
        return [
            pltpu.make_async_copy(
                blocks.at[d, table[i]],
                bands.at[i, :, pl.ds(d * width, width)],
                sems.at[2 * i + d],
            )
            for d in range(2)
        ]

    for i in range(number):

        @pl.when(table[number + i] > 0)
        def _():
            for copy in copies(i):
                copy.start()

        @pl.when(table[number + i] == 0)
        def _():
            bands[i] = jnp.zeros(bands.shape[1:], bands.dtype)

    for i in range(number):

        @pl.when(table[number + i] > 0)
        def _():
            for copy in copies(i):
                copy.wait()

    for copy in beside:
        copy.wait()


def turn_kernel(columns, basis, turned):
    _, cells, modes = basis.shape
    bands = []
    for d in range(2):
        by_mode = basis[d].astype(F32).T.reshape(columns, 2, modes // columns // 2, cells)
        bands += [by_mode[:, h].reshape(modes // 2, cells) for h in range(2)]
    turned[...] = jnp.concatenate(bands, axis=1).astype(BF16)


def weigh_kernel(wells, gains, sens, factors):
    cells = sens.shape[-1]
    spot = lax.broadcasted_iota(jnp.int32, (1, cells), 1)
    factors[...] = sens[...]
    for d in range(2):
        well = jnp.zeros((1, cells), F32)
        for w in range(wells.shape[1]):
            well = well + jnp.where(spot == wells[d, w], gains[d, w], 0.0)
        factors[0, d : d + 1, :] = sens[0, d : d + 1, :] + well


def wide(mask, width):
    return jnp.concatenate([mask] * (width // mask.shape[1]), axis=1)


def chosen(mask, low, high):
    return jnp.where(wide(mask, low.shape[1]) > 0.5, high, low).astype(BF16)


def asks_of(payload):
    return payload[payload.shape[0] - 16 :, 0:128].astype(F32)


def tile_of(ref, mask, rows):
    if ref.shape[0] == rows:
        return ref[...]
    return chosen(mask, ref[0:rows].astype(F32), ref[rows : 2 * rows].astype(F32))


def relay_ask_kernel(number, even, odd, asks, relayed):
    parity = asks[number + 1 : number + 2, :]
    ask = [asks_of(ref)[number - 2 : number - 1, :] for ref in (even, odd)]
    relayed[...] = asks[...]
    relayed[number - 2 : number - 1, :] = jnp.where(parity > 0.5, ask[1], ask[0])


def far_pick_kernel(number, pair, relayed, part, tile):
    tile[...] = tile_of(pair, relayed[number - 2 : number - 1, :], tile.shape[0])


def own_kernel(lam, rhs, sides, part):
    rows = rhs.shape[0] // 2
    part[0] = rhs[0:rows].astype(F32) - dot(lam[rows : 2 * rows], sides[0])
    part[1] = rhs[rows:].astype(F32) - dot(lam[0:rows], sides[1])


def source_sums(asks, bands, begin, refs, rows):
    tiles = [tile_of(ref, asks[i : i + 1, :], rows) for i, ref in enumerate(refs, begin)]
    count, width, both = len(refs), bands.shape[1], bands.shape[2]
    band = bands[begin : begin + count].reshape(count * width, both)
    sums = dot(jnp.concatenate(tiles, axis=1), band)
    return sums[:, :width], sums[:, width:]


def beside_sums(number, two, asks, sides, beside, rows):
    if two:
        mine = asks[number : number + 1, :]
        term = dot(tile_of(beside[0], mine, rows), sides[2])
        above = wide(mine, term.shape[1]) > 0.5
        none = jnp.zeros_like(term)
        return jnp.where(above, term, none), jnp.where(above, none, term)
    return [
        dot(tile_of(beside[d], jnp.full((1, 128), 1.0 - d, F32), rows), sides[2 + d])
        for d in range(2)
    ]


def merge_kernel(kept, mirrored, merged):
    merged[...] = (kept[...].astype(F32) + mirrored[...].astype(F32)).astype(BF16)


def cross_kernel(asks, bands, *refs):
    arrived, out = refs[:-1], refs[-1]
    out[0], out[1] = source_sums(asks, bands, 0, arrived, out.shape[1])


def far_kernel(asks, bands, cross, *refs):
    far, out = refs[:-1], refs[-1]
    low, high = source_sums(asks, bands, bands.shape[0] - len(far), far, out.shape[1])
    out[0] = cross[0] + low
    out[1] = cross[1] + high


def updated(number, two, begin, part, far, asks, bands, sides, near, beside):
    rows = part.shape[1]
    sums = source_sums(asks, bands, begin, near, rows)
    terms = beside_sums(number, two, asks, sides, beside, rows)
    return [part[d] - far[d] - sums[d] - terms[d] for d in range(2)]


def update_kernel(number, two, begin, first, part, far, asks, bands, sides, *refs):
    ends = 1 if two else 2
    here = number - 2 - begin
    near, refs = refs[:here], refs[here:]
    beside, refs = refs[:ends], refs[ends:]
    count = number - 1 if first else 1
    told, refs = refs[:count], refs[count:]
    low, high = updated(number, two, begin, part, far, asks, bands, sides, near, beside)
    lam, sends, refs = refs[0], refs[1 : 1 + number], refs[1 + number :]
    outer, refs = refs[:ends], refs[ends:]
    masks = told[0]
    if first:
        masks = refs[0]
        masks[...] = told[-1][...]
        for i in range(number - 2):
            masks[i : i + 1, :] = asks_of(told[i])[i : i + 1, :]
    rows = low.shape[0]
    lam[0:rows] = low.astype(BF16)
    lam[rows:] = high.astype(BF16)
    for i, send in enumerate(sends):
        send[...] = chosen(masks[i : i + 1, :], low, high)
    if two:
        outer[0][...] = chosen(asks[number : number + 1, :], high, low)
    else:
        outer[0][...] = high.astype(BF16)
        outer[1][...] = low.astype(BF16)


def last_kernel(number, two, begin, part, far, asks, bands, sides, factors, basis, *refs):
    here = number - 2 - begin
    near, beside, (lam, pieces) = refs[:here], refs[here:-2], refs[-2:]
    sums = updated(number, two, begin, part, far, asks, bands, sides, near, beside)
    phases, _, cells = factors.shape
    grads = []
    for d in range(2):
        rounded = sums[d].astype(BF16)
        lam[d] = rounded
        back = rounded.astype(F32)
        grad = back[:, :cells] * factors[0, d : d + 1, :]
        for p in range(1, phases):
            grad = grad + back[:, p * cells : (p + 1) * cells] * factors[p, d : d + 1, :]
        grads.append(grad)
    if two:
        half = grads[0].shape[0] // 2
        none = jnp.zeros((half, cells), F32)
        band = pieces.shape[1]
        for g in range(2):
            cuts = [grad[g * half : (g + 1) * half] for grad in grads]
            top = jnp.concatenate([x for cut in cuts for x in (cut, none)], axis=1)
            low = jnp.concatenate([x for cut in cuts for x in (none, cut)], axis=1)
            wing = jnp.concatenate([top, low], axis=0).astype(BF16)
            share = lax.dot_general(
                basis[...], wing, (((1,), (1,)), ((), ())), preferred_element_type=F32
            )
            for c in range(pieces.shape[0] // 2):
                pieces[2 * c + g] = share[c * band : (c + 1) * band].astype(BF16)
    else:
        terms = [dot(grad.astype(BF16), basis[d]) for d, grad in enumerate(grads)]
        pieces[...] = terms[0] + terms[1]


def sum_kernel(pieces, out):
    total = pieces[0].astype(F32)
    for i in range(1, pieces.shape[0]):
        total = total + pieces[i].astype(F32)
    half = total.shape[1] // 2
    out[...] = jnp.concatenate([total[:, :half], total[:, half:]], axis=0).astype(BF16)


def call(kernel, outs, ins, specs, scratch=(), flops=0, moved=0, out_specs=None):
    return pl.pallas_call(
        kernel,
        out_shape=outs,
        in_specs=specs,
        out_specs=out_specs or [VMEM] * len(outs),
        scratch_shapes=list(scratch),
        compiler_params=pltpu.CompilerParams(vmem_limit_bytes=LIMIT),
        cost_estimate=pl.CostEstimate(
            flops=flops, bytes_accessed=moved or flops // 200, transcendentals=0
        ),
    )(*ins)


def moved_by(x, pairs):
    return held(lax.ppermute(x, "areal", pairs))


def shift_pairs(columns, k):
    return [(i, (i - k) % columns) for i in range(columns)]


def beside_layers(tiles):
    groups = lax.axis_size("layer")
    if groups == 2:
        return [held(lax.ppermute(tiles[0], "layer", [(0, 1), (1, 0)]))]
    up = [(i, i + 1) for i in range(groups - 1)]
    down = [(i + 1, i) for i in range(groups - 1)]
    return [held(lax.ppermute(tiles[0], "layer", up)), held(lax.ppermute(tiles[-1], "layer", down))]


def outside(x):
    return pltpu.with_memory_space_constraint(x, pltpu.HBM)


def on_device(
    rhs,
    areal_blocks,
    vertical_blocks,
    conn_src,
    conn_count,
    tile_map,
    well_cells,
    well_gain,
    sens,
    basis,
):
    columns = lax.axis_size("areal")
    groups = lax.axis_size("layer")
    two = groups == 2
    rows, width = rhs.shape[2:]
    modes = basis.shape[-1]
    number = conn_src.shape[-1]
    swaps = near_swaps(number)
    routes = [swap_pairs(columns, k, color) for k, color in swaps]
    routes += [shift_pairs(columns, columns // 2 + 1), shift_pairs(columns, columns // 2)]
    rhs = rhs[0].reshape(2 * rows, width)
    me = lax.axis_index("areal").astype(jnp.int32).reshape(1)
    group = lax.axis_index("layer").astype(jnp.int32).reshape(1)

    tile = pltpu.VMEM((rows, width), BF16)
    pair = pltpu.VMEM((2 * rows, width), BF16)
    sums = pltpu.VMEM((2, rows, width), F32)
    one = 2 * rows * width * width
    partial = functools.partial

    masks_type = pltpu.VMEM((8, 128), F32)
    with jax.named_scope("plan"):
        table, asks, payload, both = call(
            partial(plan_kernel, columns, swaps),
            [
                jax.ShapeDtypeStruct((2 * number,), jnp.int32),
                masks_type,
                pltpu.VMEM((2 * rows + 16, width), BF16),
                pair,
            ],
            (outside(conn_src[0, 0]), conn_count[0], outside(tile_map), me, group, outside(rhs)),
            [SMEM] * 5 + [VMEM],
            out_specs=[SMEM] + [VMEM] * 3,
        )
        asks, payload, both = held(asks), held(payload), held(both)
        far_pair = moved_by(payload, routes[-1])

    with jax.named_scope("load"):
        bands, sides = call(
            partial(load_kernel, number, two),
            [
                pltpu.VMEM((number, width, 2 * width), BF16),
                pltpu.VMEM((3 if two else 4, width, width), BF16),
            ],
            (table, group, outside(areal_blocks[0]), outside(vertical_blocks[0])),
            [SMEM] * 2 + [pl.BlockSpec(memory_space=pltpu.HBM)] * 2,
            [pltpu.SemaphoreType.DMA((2 * number + 4,))],
            moved=areal_blocks.size * 2 + vertical_blocks.size * 2,
        )
        bands, sides = held(bands), held(sides)
        (factors,) = call(
            weigh_kernel,
            [pltpu.VMEM((sens.shape[2], 2, sens.shape[3]), F32)],
            (well_cells[0], well_gain[0], sens[0].transpose(1, 0, 2)),
            [SMEM] * 2 + [VMEM],
        )
        weights = held(basis[0])
        if two:
            (weights,) = call(
                partial(turn_kernel, columns),
                [pltpu.VMEM((modes // 2, 4 * sens.shape[3]), BF16)],
                (basis[0],),
                [VMEM],
            )
        factors, weights = held(factors), held(weights)

    rhs_held = lam = both
    sends = [payload] * (number - 2)
    outer = [payload]
    half = len(swaps) // 2
    for step in range(ITERS):
        first = step == 0
        with jax.named_scope("apply"):
            if first:
                arrived = [moved_by(x, pairs) for x, pairs in zip(sends[1:], routes[1:-2])]
                (merged,) = call(
                    merge_kernel,
                    [pltpu.VMEM(payload.shape, BF16)],
                    (
                        moved_by(sends[0], kept_pairs(routes[0])),
                        moved_by(far_pair, mirrored_pairs(routes[0])),
                    ),
                    [VMEM] * 2,
                )
                arrived = [held(merged), *arrived]
            else:
                arrived = [moved_by(x, pairs) for x, pairs in zip(sends, routes)]
            (part,) = call(own_kernel, [sums], (lam, rhs_held, sides), [VMEM] * 3, flops=one)
            part = held(part)
            if first:
                even, odd = (arrived[swaps.index((1, color))] for color in (1, 0))
                (relayed,) = call(
                    partial(relay_ask_kernel, number),
                    [masks_type],
                    (even, odd, asks),
                    [VMEM] * 3,
                    flops=4 * one,
                )
                relayed = held(relayed)
                (picked,) = call(
                    partial(far_pick_kernel, number),
                    [tile],
                    (far_pair, relayed, part),
                    [VMEM] * 3,
                )
                arrived = [*arrived, moved_by(picked, shift_pairs(columns, 1)), far_pair]
                told = [*arrived[:-2], moved_by(relayed, routes[-1])]
            beside = beside_layers(outer)
            (cross,) = call(
                cross_kernel,
                [sums],
                (asks, bands, *arrived[:half]),
                [VMEM] * (2 + half),
                flops=4 * one,
            )
            (far,) = call(
                far_kernel,
                [sums],
                (asks, bands, held(cross), *arrived[-2:]),
                [VMEM] * 5,
                flops=4 * one,
            )
            tiles = (part, held(far), asks, bands, sides)
            near = (*arrived[half:-2], *beside)
            if step < ITERS - 1:
                lam, *rest = call(
                    partial(update_kernel, number, two, half, first),
                    [pair] + [tile] * (number + len(beside)) + ([masks_type] if first else []),
                    (*tiles, *near, *told),
                    [VMEM] * (5 + len(near) + len(told)),
                    flops=one,
                )
                lam = held(lam)
                if first:
                    told = [held(rest.pop())]
                sends, outer = rest[:number], rest[number:]
            else:
                adjoint, pieces = call(
                    partial(last_kernel, number, two, half),
                    [
                        jax.ShapeDtypeStruct((2, rows, width), BF16),
                        pltpu.VMEM((2 * columns, modes // columns // 2, rows), BF16)
                        if two
                        else pltpu.VMEM((rows, modes), F32),
                    ],
                    (*tiles, factors, weights, *near),
                    [VMEM] * (7 + len(near)),
                    flops=one,
                )

    with jax.named_scope("project"):
        if two:
            landed = lax.all_to_all(pieces, ("areal", "layer"), 0, 0, tiled=True)
            (coefficients,) = call(
                sum_kernel,
                [jax.ShapeDtypeStruct((modes // columns, rows // 2), BF16)],
                (held(landed),),
                [VMEM],
            )
            coefficients = coefficients.T
        else:
            cut = pieces.reshape(groups, rows // groups, columns, modes // columns)
            cut = cut.transpose(2, 0, 1, 3).reshape(columns * groups, rows // groups, modes // columns)
            landed = lax.all_to_all(cut, ("areal", "layer"), 0, 0, tiled=True)
            coefficients = jnp.sum(landed, axis=0).astype(BF16)
    return (adjoint[None], coefficients)


def solution(mesh):
    in_specs = (
        P("areal", "layer", None, None),
        P("areal", "layer", None, None, None),
        P("areal", "layer", None, None, None),
        P("areal", "layer", None),
        P("areal", "layer"),
        P(),
        P("areal", "layer", None),
        P("areal", "layer", None),
        P("areal", "layer", None, None),
        P("areal", "layer", None, None),
    )
    out_specs = (P("areal", "layer", None, None), P("layer", "areal"))
    return jax.shard_map(
        on_device, mesh=mesh, in_specs=in_specs, out_specs=out_specs, check_vma=False
    )
```

```python
import functools

import jax
import jax.numpy as jnp
from jax import lax
from jax.experimental import pallas as pl
from jax.experimental.pallas import tpu as pltpu
from jax.sharding import PartitionSpec as P

ITERS = 3
F32 = jnp.float32
BF16 = jnp.bfloat16
SMEM = pl.BlockSpec(memory_space=pltpu.SMEM)
VMEM = pl.BlockSpec(memory_space=pltpu.VMEM)
LIMIT = 16 * 1024 * 1024


def near_swaps(count):
    return [(k, color) for color in (1, 0) for k in range(count // 2 - 1, 0, -1)]


def swap_pairs(columns, k, color):
    return [
        (c, (c + k if (c // k) % 2 == color else c - k) % columns) for c in range(columns)
    ]


def held(x):
    return pltpu.with_memory_space_constraint(x, pltpu.VMEM)


def dot(a, b):
    return jnp.dot(a, b, preferred_element_type=F32)


def plan_kernel(columns, swaps, src, count, tile_map, me, group, table, asks):
    steps = [
        jnp.where(lax.rem(lax.div(me[0], k), 2) == color, k, columns - k) for k, color in swaps
    ] + [columns // 2 + 1, columns // 2]
    number = len(steps)
    conn = [0] * number
    slots = [0] * number
    for s in range(number):
        place = tile_map[src[s]]
        peer = lax.shift_right_logical(place, 1)
        slot = lax.bitwise_and(place, 1)
        away = peer - me[0]
        away = jnp.where(away < 0, away + columns, away)
        for i, k in enumerate(steps):
            hit = away == k
            conn[i] = jnp.where(hit, s, conn[i])
            slots[i] = jnp.where(hit, slot, slots[i])
    line = lax.broadcasted_iota(jnp.int32, asks.shape, 0)
    asked = jnp.zeros(line.shape, F32)
    for i in range(number):
        table[i] = conn[i]
        table[number + i] = jnp.where(conn[i] < count[0], 1, 0)
        asked = jnp.where(line == i, slots[i].astype(F32), asked)
    asked = jnp.where(line == number, group[0].astype(F32), asked)
    asked = jnp.where(line == number + 1, lax.rem(me[0], 2).astype(F32), asked)
    asks[...] = asked


def load_kernel(number, two, table, group, blocks, vert, bands, sides, sems):
    width = vert.shape[-1]
    mine = group[0]
    ends = [(1 - mine, 1 - mine)] if two else [(0, 0), (1, 1)]
    beside = [
        pltpu.make_async_copy(vert.at[d, k], sides.at[i], sems.at[2 * number + i])
        for i, (d, k) in enumerate([(0, 1), (1, 0), *ends])
    ]
    for copy in beside:
        copy.start()

    def copies(i):
        return [
            pltpu.make_async_copy(
                blocks.at[d, table[i]],
                bands.at[i, :, pl.ds(d * width, width)],
                sems.at[2 * i + d],
            )
            for d in range(2)
        ]

    for i in range(number):

        @pl.when(table[number + i] > 0)
        def _():
            for copy in copies(i):
                copy.start()

        @pl.when(table[number + i] == 0)
        def _():
            bands[i] = jnp.zeros(bands.shape[1:], bands.dtype)

    for i in range(number):

        @pl.when(table[number + i] > 0)
        def _():
            for copy in copies(i):
                copy.wait()

    for copy in beside:
        copy.wait()


def turn_kernel(columns, basis, turned):
    _, cells, modes = basis.shape
    bands = []
    for d in range(2):
        by_mode = basis[d].astype(F32).T.reshape(columns, 2, modes // columns // 2, cells)
        bands += [by_mode[:, h].reshape(modes // 2, cells) for h in range(2)]
    turned[...] = jnp.concatenate(bands, axis=1).astype(BF16)


def weigh_kernel(wells, gains, sens, factors):
    cells = sens.shape[-1]
    spot = lax.broadcasted_iota(jnp.int32, (1, cells), 1)
    factors[...] = sens[...]
    for d in range(2):
        well = jnp.zeros((1, cells), F32)
        for w in range(wells.shape[1]):
            well = well + jnp.where(spot == wells[d, w], gains[d, w], 0.0)
        factors[0, d : d + 1, :] = sens[0, d : d + 1, :] + well


def wide(mask, width):
    return jnp.concatenate([mask] * (width // mask.shape[1]), axis=1)


def chosen(mask, low, high):
    return jnp.where(wide(mask, low.shape[1]) > 0.5, high, low).astype(BF16)


def asks_of(payload):
    return payload[payload.shape[0] - 16 :, 0:128].astype(F32)


def tile_of(ref, mask, rows):
    if ref.shape[0] == rows:
        return ref[...]
    return chosen(mask, ref[0:rows].astype(F32), ref[rows : 2 * rows].astype(F32))


def cross_pick_kernel(columns, me, tile_map, *refs):
    count = (len(refs) - 5) // 2
    tables, (rhs, asks), refs = refs[:count], refs[count : count + 2], refs[count + 2 :]
    (known, payload, pair), tiles = refs[:3], refs[3:]
    rows = rhs.shape[0] // 2
    ahead = me[0] + columns // 2
    ahead = jnp.where(ahead >= columns, ahead - columns, ahead)
    wanted, passed = [], []
    for table in tables:
        here, there = 0, 0
        for s in range(table.shape[-1]):
            place = tile_map[table[s]]
            peer = lax.shift_right_logical(place, 1)
            slot = lax.bitwise_and(place, 1)
            here = jnp.where(peer == me[0], slot, here)
            there = jnp.where(peer == ahead, slot, there)
        wanted.append(here.astype(F32))
        passed.append(there.astype(F32))
    line = lax.broadcasted_iota(jnp.int32, known.shape, 0)
    rows_of = jnp.zeros(known.shape, F32)
    for i, value in enumerate([*wanted, *passed]):
        rows_of = jnp.where(line == i, value, rows_of)
    known[...] = rows_of
    payload[0 : 2 * rows] = rhs[...]
    payload[2 * rows :] = jnp.zeros((16, rhs.shape[1]), BF16)
    none = jnp.zeros((8, 128), F32)
    payload[2 * rows :, 0:128] = jnp.concatenate([asks[...], none], axis=0).astype(BF16)
    pair[...] = rhs[...]
    low, high = rhs[0:rows].astype(F32), rhs[rows:].astype(F32)
    for i, tile in enumerate(tiles):
        tile[...] = chosen(rows_of[i : i + 1, :], low, high)


def relay_ask_kernel(number, known, odd, asks, relayed):
    parity = asks[number + 1 : number + 2, :]
    last = number // 2 - 2
    even = known[last + number // 2 - 1 : last + number // 2, :]
    ask = asks_of(odd)[number - 2 : number - 1, :]
    relayed[...] = asks[...]
    relayed[number - 2 : number - 1, :] = jnp.where(parity > 0.5, ask, even)


def far_pick_kernel(number, pair, relayed, part, tile):
    tile[...] = tile_of(pair, relayed[number - 2 : number - 1, :], tile.shape[0])


def own_kernel(lam, rhs, sides, part):
    rows = rhs.shape[0] // 2
    part[0] = rhs[0:rows].astype(F32) - dot(lam[rows : 2 * rows], sides[0])
    part[1] = rhs[rows:].astype(F32) - dot(lam[0:rows], sides[1])


def source_sums(asks, bands, begin, refs, rows):
    tiles = [tile_of(ref, asks[i : i + 1, :], rows) for i, ref in enumerate(refs, begin)]
    count, width, both = len(refs), bands.shape[1], bands.shape[2]
    band = bands[begin : begin + count].reshape(count * width, both)
    sums = dot(jnp.concatenate(tiles, axis=1), band)
    return sums[:, :width], sums[:, width:]


def beside_sums(number, two, asks, sides, beside, rows):
    if two:
        mine = asks[number : number + 1, :]
        term = dot(tile_of(beside[0], mine, rows), sides[2])
        above = wide(mine, term.shape[1]) > 0.5
        none = jnp.zeros_like(term)
        return jnp.where(above, term, none), jnp.where(above, none, term)
    return [
        dot(tile_of(beside[d], jnp.full((1, 128), 1.0 - d, F32), rows), sides[2 + d])
        for d in range(2)
    ]


def cross_kernel(asks, bands, *refs):
    arrived, out = refs[:-1], refs[-1]
    out[0], out[1] = source_sums(asks, bands, 0, arrived, out.shape[1])


def far_kernel(asks, bands, cross, *refs):
    far, out = refs[:-1], refs[-1]
    low, high = source_sums(asks, bands, bands.shape[0] - len(far), far, out.shape[1])
    out[0] = cross[0] + low
    out[1] = cross[1] + high


def updated(number, two, begin, part, far, asks, bands, sides, near, beside):
    rows = part.shape[1]
    sums = source_sums(asks, bands, begin, near, rows)
    terms = beside_sums(number, two, asks, sides, beside, rows)
    return [part[d] - far[d] - sums[d] - terms[d] for d in range(2)]


def update_kernel(number, two, begin, first, part, far, asks, bands, sides, *refs):
    ends = 1 if two else 2
    here = number - 2 - begin
    near, refs = refs[:here], refs[here:]
    beside, refs = refs[:ends], refs[ends:]
    count = number - 1 if first else 1
    told, refs = refs[:count], refs[count:]
    low, high = updated(number, two, begin, part, far, asks, bands, sides, near, beside)
    lam, sends, refs = refs[0], refs[1 : 1 + number], refs[1 + number :]
    outer, refs = refs[:ends], refs[ends:]
    masks = told[0]
    if first:
        masks = refs[0]
        masks[...] = told[-1][...]
        for i in range(number - 2):
            masks[i : i + 1, :] = asks_of(told[i])[i : i + 1, :]
    rows = low.shape[0]
    lam[0:rows] = low.astype(BF16)
    lam[rows:] = high.astype(BF16)
    for i, send in enumerate(sends):
        send[...] = chosen(masks[i : i + 1, :], low, high)
    if two:
        outer[0][...] = chosen(asks[number : number + 1, :], high, low)
    else:
        outer[0][...] = high.astype(BF16)
        outer[1][...] = low.astype(BF16)


def last_kernel(number, two, begin, part, far, asks, bands, sides, factors, basis, *refs):
    here = number - 2 - begin
    near, beside, (lam, pieces) = refs[:here], refs[here:-2], refs[-2:]
    sums = updated(number, two, begin, part, far, asks, bands, sides, near, beside)
    phases, _, cells = factors.shape
    grads = []
    for d in range(2):
        rounded = sums[d].astype(BF16)
        lam[d] = rounded
        back = rounded.astype(F32)
        grad = back[:, :cells] * factors[0, d : d + 1, :]
        for p in range(1, phases):
            grad = grad + back[:, p * cells : (p + 1) * cells] * factors[p, d : d + 1, :]
        grads.append(grad)
    if two:
        half = grads[0].shape[0] // 2
        none = jnp.zeros((half, cells), F32)
        band = pieces.shape[1]
        for g in range(2):
            cuts = [grad[g * half : (g + 1) * half] for grad in grads]
            top = jnp.concatenate([x for cut in cuts for x in (cut, none)], axis=1)
            low = jnp.concatenate([x for cut in cuts for x in (none, cut)], axis=1)
            wing = jnp.concatenate([top, low], axis=0).astype(BF16)
            share = lax.dot_general(
                basis[...], wing, (((1,), (1,)), ((), ())), preferred_element_type=F32
            )
            for c in range(pieces.shape[0] // 2):
                pieces[2 * c + g] = share[c * band : (c + 1) * band].astype(BF16)
    else:
        terms = [dot(grad.astype(BF16), basis[d]) for d, grad in enumerate(grads)]
        pieces[...] = terms[0] + terms[1]


def sum_kernel(pieces, out):
    total = pieces[0].astype(F32)
    for i in range(1, pieces.shape[0]):
        total = total + pieces[i].astype(F32)
    half = total.shape[1] // 2
    out[...] = jnp.concatenate([total[:, :half], total[:, half:]], axis=0).astype(BF16)


def call(kernel, outs, ins, specs, scratch=(), flops=0, moved=0, out_specs=None):
    return pl.pallas_call(
        kernel,
        out_shape=outs,
        in_specs=specs,
        out_specs=out_specs or [VMEM] * len(outs),
        scratch_shapes=list(scratch),
        compiler_params=pltpu.CompilerParams(vmem_limit_bytes=LIMIT),
        cost_estimate=pl.CostEstimate(
            flops=flops, bytes_accessed=moved or flops // 200, transcendentals=0
        ),
    )(*ins)


def moved_by(x, pairs):
    return held(lax.ppermute(x, "areal", pairs))


def shift_pairs(columns, k):
    return [(i, (i - k) % columns) for i in range(columns)]


def beside_layers(tiles):
    groups = lax.axis_size("layer")
    if groups == 2:
        return [held(lax.ppermute(tiles[0], "layer", [(0, 1), (1, 0)]))]
    up = [(i, i + 1) for i in range(groups - 1)]
    down = [(i + 1, i) for i in range(groups - 1)]
    return [held(lax.ppermute(tiles[0], "layer", up)), held(lax.ppermute(tiles[-1], "layer", down))]


def outside(x):
    return pltpu.with_memory_space_constraint(x, pltpu.HBM)


def on_device(
    rhs,
    areal_blocks,
    vertical_blocks,
    conn_src,
    conn_count,
    tile_map,
    well_cells,
    well_gain,
    sens,
    basis,
):
    columns = lax.axis_size("areal")
    groups = lax.axis_size("layer")
    two = groups == 2
    rows, width = rhs.shape[2:]
    modes = basis.shape[-1]
    number = conn_src.shape[-1]
    swaps = near_swaps(number)
    routes = [swap_pairs(columns, k, color) for k, color in swaps]
    routes += [shift_pairs(columns, columns // 2 + 1), shift_pairs(columns, columns // 2)]
    rhs = rhs[0].reshape(2 * rows, width)
    me = lax.axis_index("areal").astype(jnp.int32).reshape(1)
    group = lax.axis_index("layer").astype(jnp.int32).reshape(1)

    tile = pltpu.VMEM((rows, width), BF16)
    pair = pltpu.VMEM((2 * rows, width), BF16)
    sums = pltpu.VMEM((2, rows, width), F32)
    one = 2 * rows * width * width
    partial = functools.partial

    masks_type = pltpu.VMEM((8, 128), F32)
    with jax.named_scope("plan"):
        half = len(swaps) // 2
        tables = [lax.ppermute(conn_src, "areal", pairs) for pairs in routes[:half]]
        table, asks = call(
            partial(plan_kernel, columns, swaps),
            [jax.ShapeDtypeStruct((2 * number,), jnp.int32), masks_type],
            (outside(conn_src[0, 0]), conn_count[0], outside(tile_map), me, group),
            [SMEM] * 5,
            out_specs=[SMEM, VMEM],
        )
        asks = held(asks)
        known, payload, both, *crossing = call(
            partial(cross_pick_kernel, columns),
            [masks_type, pltpu.VMEM((2 * rows + 16, width), BF16), pair] + [tile] * half,
            (me, outside(tile_map), *[x[0, 0] for x in tables], outside(rhs), asks),
            [SMEM] * (2 + half) + [VMEM] * 2,
        )
        known, payload, both = held(known), held(payload), held(both)
        far_pair = moved_by(both, routes[-1])

    with jax.named_scope("load"):
        bands, sides = call(
            partial(load_kernel, number, two),
            [
                pltpu.VMEM((number, width, 2 * width), BF16),
                pltpu.VMEM((3 if two else 4, width, width), BF16),
            ],
            (table, group, outside(areal_blocks[0]), outside(vertical_blocks[0])),
            [SMEM] * 2 + [pl.BlockSpec(memory_space=pltpu.HBM)] * 2,
            [pltpu.SemaphoreType.DMA((2 * number + 4,))],
            moved=areal_blocks.size * 2 + vertical_blocks.size * 2,
        )
        bands, sides = held(bands), held(sides)
        (factors,) = call(
            weigh_kernel,
            [pltpu.VMEM((sens.shape[2], 2, sens.shape[3]), F32)],
            (well_cells[0], well_gain[0], sens[0].transpose(1, 0, 2)),
            [SMEM] * 2 + [VMEM],
        )
        weights = held(basis[0])
        if two:
            (weights,) = call(
                partial(turn_kernel, columns),
                [pltpu.VMEM((modes // 2, 4 * sens.shape[3]), BF16)],
                (basis[0],),
                [VMEM],
            )
        factors, weights = held(factors), held(weights)

    rhs_held = lam = both
    sends = [*crossing, *[payload] * half]
    outer = [payload]
    for step in range(ITERS):
        first = step == 0
        with jax.named_scope("apply"):
            arrived = [moved_by(x, pairs) for x, pairs in zip(sends, routes)]
            (part,) = call(own_kernel, [sums], (lam, rhs_held, sides), [VMEM] * 3, flops=one)
            part = held(part)
            if first:
                odd = arrived[swaps.index((1, 0))]
                (relayed,) = call(
                    partial(relay_ask_kernel, number),
                    [masks_type],
                    (known, odd, asks),
                    [VMEM] * 3,
                )
                relayed = held(relayed)
                (picked,) = call(
                    partial(far_pick_kernel, number),
                    [tile],
                    (far_pair, relayed, part),
                    [VMEM] * 3,
                )
                arrived = [*arrived, moved_by(picked, shift_pairs(columns, 1)), far_pair]
                told = [*[known] * half, *arrived[half:-2], moved_by(relayed, routes[-1])]
            beside = beside_layers(outer)
            (cross,) = call(
                cross_kernel,
                [sums],
                (asks, bands, *arrived[:half]),
                [VMEM] * (2 + half),
                flops=(64 if first else 4) * one,
            )
            (far,) = call(
                far_kernel,
                [sums],
                (asks, bands, held(cross), *arrived[-2:]),
                [VMEM] * 5,
                flops=4 * one,
            )
            tiles = (part, held(far), asks, bands, sides)
            near = (*arrived[half:-2], *beside)
            if step < ITERS - 1:
                lam, *rest = call(
                    partial(update_kernel, number, two, half, first),
                    [pair] + [tile] * (number + len(beside)) + ([masks_type] if first else []),
                    (*tiles, *near, *told),
                    [VMEM] * (5 + len(near) + len(told)),
                    flops=one,
                )
                lam = held(lam)
                if first:
                    told = [held(rest.pop())]
                sends, outer = rest[:number], rest[number:]
            else:
                adjoint, pieces = call(
                    partial(last_kernel, number, two, half),
                    [
                        jax.ShapeDtypeStruct((2, rows, width), BF16),
                        pltpu.VMEM((2 * columns, modes // columns // 2, rows), BF16)
                        if two
                        else pltpu.VMEM((rows, modes), F32),
                    ],
                    (*tiles, factors, weights, *near),
                    [VMEM] * (7 + len(near)),
                    flops=one,
                )

    with jax.named_scope("project"):
        if two:
            landed = lax.all_to_all(pieces, ("areal", "layer"), 0, 0, tiled=True)
            (coefficients,) = call(
                sum_kernel,
                [jax.ShapeDtypeStruct((modes // columns, rows // 2), BF16)],
                (held(landed),),
                [VMEM],
            )
            coefficients = coefficients.T
        else:
            cut = pieces.reshape(groups, rows // groups, columns, modes // columns)
            cut = cut.transpose(2, 0, 1, 3).reshape(columns * groups, rows // groups, modes // columns)
            landed = lax.all_to_all(cut, ("areal", "layer"), 0, 0, tiled=True)
            coefficients = jnp.sum(landed, axis=0).astype(BF16)
    return (adjoint[None], coefficients)


def solution(mesh):
    in_specs = (
        P("areal", "layer", None, None),
        P("areal", "layer", None, None, None),
        P("areal", "layer", None, None, None),
        P("areal", "layer", None),
        P("areal", "layer"),
        P(),
        P("areal", "layer", None),
        P("areal", "layer", None),
        P("areal", "layer", None, None),
        P("areal", "layer", None, None),
    )
    out_specs = (P("areal", "layer", None, None), P("layer", "areal"))
    return jax.shard_map(
        on_device, mesh=mesh, in_specs=in_specs, out_specs=out_specs, check_vma=False
    )
```

```python
import functools

import jax
import jax.numpy as jnp
from jax import lax
from jax.experimental import pallas as pl
from jax.experimental.pallas import tpu as pltpu
from jax.sharding import PartitionSpec as P

ITERS = 3
F32 = jnp.float32
BF16 = jnp.bfloat16
SMEM = pl.BlockSpec(memory_space=pltpu.SMEM)
VMEM = pl.BlockSpec(memory_space=pltpu.VMEM)
LIMIT = 16 * 1024 * 1024


def near_swaps(count):
    return [(k, color) for color in (1, 0) for k in range(count // 2 - 1, 0, -1)]


def swap_pairs(columns, k, color):
    return [
        (c, (c + k if (c // k) % 2 == color else c - k) % columns) for c in range(columns)
    ]


def held(x):
    return pltpu.with_memory_space_constraint(x, pltpu.VMEM)


def dot(a, b):
    return jnp.dot(a, b, preferred_element_type=F32)


def plan_kernel(columns, swaps, src, count, tile_map, me, group, table, asks):
    steps = [
        jnp.where(lax.rem(lax.div(me[0], k), 2) == color, k, columns - k) for k, color in swaps
    ] + [columns // 2 + 1, columns // 2]
    number = len(steps)
    conn = [0] * number
    slots = [0] * number
    for s in range(number):
        place = tile_map[src[s]]
        peer = lax.shift_right_logical(place, 1)
        slot = lax.bitwise_and(place, 1)
        away = peer - me[0]
        away = jnp.where(away < 0, away + columns, away)
        for i, k in enumerate(steps):
            hit = away == k
            conn[i] = jnp.where(hit, s, conn[i])
            slots[i] = jnp.where(hit, slot, slots[i])
    line = lax.broadcasted_iota(jnp.int32, asks.shape, 0)
    asked = jnp.zeros(line.shape, F32)
    for i in range(number):
        table[i] = conn[i]
        table[number + i] = jnp.where(conn[i] < count[0], 1, 0)
        asked = jnp.where(line == i, slots[i].astype(F32), asked)
    asked = jnp.where(line == number, group[0].astype(F32), asked)
    asked = jnp.where(line == number + 1, lax.rem(me[0], 2).astype(F32), asked)
    asks[...] = asked


def load_kernel(number, two, table, group, blocks, vert, bands, sides, sems):
    width = vert.shape[-1]
    mine = group[0]
    ends = [(1 - mine, 1 - mine)] if two else [(0, 0), (1, 1)]
    beside = [
        pltpu.make_async_copy(vert.at[d, k], sides.at[i], sems.at[2 * number + i])
        for i, (d, k) in enumerate([(0, 1), (1, 0), *ends])
    ]
    for copy in beside:
        copy.start()

    def copies(i):
        return [
            pltpu.make_async_copy(
                blocks.at[d, table[i]],
                bands.at[i, :, pl.ds(d * width, width)],
                sems.at[2 * i + d],
            )
            for d in range(2)
        ]

    for i in range(number):

        @pl.when(table[number + i] > 0)
        def _():
            for copy in copies(i):
                copy.start()

        @pl.when(table[number + i] == 0)
        def _():
            bands[i] = jnp.zeros(bands.shape[1:], bands.dtype)

    for i in range(number):

        @pl.when(table[number + i] > 0)
        def _():
            for copy in copies(i):
                copy.wait()

    for copy in beside:
        copy.wait()


def turn_kernel(columns, basis, turned):
    _, cells, modes = basis.shape
    bands = []
    for d in range(2):
        by_mode = basis[d].astype(F32).T.reshape(columns, 2, modes // columns // 2, cells)
        bands += [by_mode[:, h].reshape(modes // 2, cells) for h in range(2)]
    turned[...] = jnp.concatenate(bands, axis=1).astype(BF16)


def weigh_kernel(wells, gains, sens, factors):
    cells = sens.shape[-1]
    spot = lax.broadcasted_iota(jnp.int32, (1, cells), 1)
    factors[...] = sens[...]
    for d in range(2):
        well = jnp.zeros((1, cells), F32)
        for w in range(wells.shape[1]):
            well = well + jnp.where(spot == wells[d, w], gains[d, w], 0.0)
        factors[0, d : d + 1, :] = sens[0, d : d + 1, :] + well


def wide(mask, width):
    return jnp.concatenate([mask] * (width // mask.shape[1]), axis=1)


def chosen(mask, low, high):
    return jnp.where(wide(mask, low.shape[1]) > 0.5, high, low).astype(BF16)


def asks_of(payload):
    return payload[payload.shape[0] - 16 :, 0:128].astype(F32)


def tile_of(ref, mask, rows):
    if ref.shape[0] == rows:
        return ref[...]
    return chosen(mask, ref[0:rows].astype(F32), ref[rows : 2 * rows].astype(F32))


def cross_pick_kernel(columns, me, tile_map, *refs):
    count = (len(refs) - 5) // 2
    tables, (rhs, asks), refs = refs[:count], refs[count : count + 2], refs[count + 2 :]
    (known, payload, pair), tiles = refs[:3], refs[3:]
    rows = rhs.shape[0] // 2
    ahead = me[0] + columns // 2
    ahead = jnp.where(ahead >= columns, ahead - columns, ahead)
    wanted, passed = [], []
    for table in tables:
        here, there = 0, 0
        for s in range(table.shape[-1]):
            place = tile_map[table[s]]
            peer = lax.shift_right_logical(place, 1)
            slot = lax.bitwise_and(place, 1)
            here = jnp.where(peer == me[0], slot, here)
            there = jnp.where(peer == ahead, slot, there)
        wanted.append(here.astype(F32))
        passed.append(there.astype(F32))
    line = lax.broadcasted_iota(jnp.int32, known.shape, 0)
    rows_of = jnp.zeros(known.shape, F32)
    for i, value in enumerate([*wanted, *passed]):
        rows_of = jnp.where(line == i, value, rows_of)
    known[...] = rows_of
    payload[0 : 2 * rows] = rhs[...]
    payload[2 * rows :] = jnp.zeros((16, rhs.shape[1]), BF16)
    none = jnp.zeros((8, 128), F32)
    payload[2 * rows :, 0:128] = jnp.concatenate([asks[...], none], axis=0).astype(BF16)
    pair[...] = rhs[...]
    low, high = rhs[0:rows].astype(F32), rhs[rows:].astype(F32)
    for i, tile in enumerate(tiles):
        tile[...] = chosen(rows_of[i : i + 1, :], low, high)


def relay_ask_kernel(number, known, odd, asks, relayed):
    parity = asks[number + 1 : number + 2, :]
    last = number // 2 - 2
    even = known[last + number // 2 - 1 : last + number // 2, :]
    ask = asks_of(odd)[number - 2 : number - 1, :]
    relayed[...] = asks[...]
    relayed[number - 2 : number - 1, :] = jnp.where(parity > 0.5, ask, even)


def far_pick_kernel(number, pair, relayed, nearer, tile):
    tile[...] = tile_of(pair, relayed[number - 2 : number - 1, :], tile.shape[0])


def own_kernel(lam, rhs, sides, part):
    rows = rhs.shape[0] // 2
    part[0] = rhs[0:rows].astype(F32) - dot(lam[rows : 2 * rows], sides[0])
    part[1] = rhs[rows:].astype(F32) - dot(lam[0:rows], sides[1])


def source_sums(asks, bands, begin, refs, rows):
    tiles = [tile_of(ref, asks[i : i + 1, :], rows) for i, ref in enumerate(refs, begin)]
    count, width, both = len(refs), bands.shape[1], bands.shape[2]
    band = bands[begin : begin + count].reshape(count * width, both)
    sums = dot(jnp.concatenate(tiles, axis=1), band)
    return sums[:, :width], sums[:, width:]


def beside_sums(number, two, asks, sides, beside, rows):
    if two:
        mine = asks[number : number + 1, :]
        term = dot(tile_of(beside[0], mine, rows), sides[2])
        above = wide(mine, term.shape[1]) > 0.5
        none = jnp.zeros_like(term)
        return jnp.where(above, term, none), jnp.where(above, none, term)
    return [
        dot(tile_of(beside[d], jnp.full((1, 128), 1.0 - d, F32), rows), sides[2 + d])
        for d in range(2)
    ]


def cross_kernel(asks, bands, *refs):
    arrived, out = refs[:-1], refs[-1]
    out[0], out[1] = source_sums(asks, bands, 0, arrived, out.shape[1])


def nearer_kernel(asks, bands, pair, out):
    out[0], out[1] = source_sums(asks, bands, bands.shape[0] - 1, [pair], out.shape[1])


def farther_kernel(asks, bands, cross, nearer, passed, out):
    sums = source_sums(asks, bands, bands.shape[0] - 2, [passed], out.shape[1])
    for d in range(2):
        out[d] = cross[d] + nearer[d] + sums[d]


def far_kernel(asks, bands, cross, *refs):
    far, out = refs[:-1], refs[-1]
    low, high = source_sums(asks, bands, bands.shape[0] - len(far), far, out.shape[1])
    out[0] = cross[0] + low
    out[1] = cross[1] + high


def updated(number, two, begin, part, far, asks, bands, sides, near, beside):
    rows = part.shape[1]
    sums = source_sums(asks, bands, begin, near, rows)
    terms = beside_sums(number, two, asks, sides, beside, rows)
    return [part[d] - far[d] - sums[d] - terms[d] for d in range(2)]


def update_kernel(number, two, begin, first, part, far, asks, bands, sides, *refs):
    ends = 1 if two else 2
    here = number - 2 - begin
    near, refs = refs[:here], refs[here:]
    beside, refs = refs[:ends], refs[ends:]
    count = number - 1 if first else 1
    told, refs = refs[:count], refs[count:]
    low, high = updated(number, two, begin, part, far, asks, bands, sides, near, beside)
    lam, sends, refs = refs[0], refs[1 : 1 + number], refs[1 + number :]
    outer, refs = refs[:ends], refs[ends:]
    masks = told[0]
    if first:
        masks = refs[0]
        masks[...] = told[-1][...]
        for i in range(number - 2):
            masks[i : i + 1, :] = asks_of(told[i])[i : i + 1, :]
    rows = low.shape[0]
    lam[0:rows] = low.astype(BF16)
    lam[rows:] = high.astype(BF16)
    for i, send in enumerate(sends):
        send[...] = chosen(masks[i : i + 1, :], low, high)
    if two:
        outer[0][...] = chosen(asks[number : number + 1, :], high, low)
    else:
        outer[0][...] = high.astype(BF16)
        outer[1][...] = low.astype(BF16)


def last_kernel(number, two, begin, part, far, asks, bands, sides, factors, basis, *refs):
    here = number - 2 - begin
    near, beside, (lam, pieces) = refs[:here], refs[here:-2], refs[-2:]
    sums = updated(number, two, begin, part, far, asks, bands, sides, near, beside)
    phases, _, cells = factors.shape
    grads = []
    for d in range(2):
        rounded = sums[d].astype(BF16)
        lam[d] = rounded
        back = rounded.astype(F32)
        grad = back[:, :cells] * factors[0, d : d + 1, :]
        for p in range(1, phases):
            grad = grad + back[:, p * cells : (p + 1) * cells] * factors[p, d : d + 1, :]
        grads.append(grad)
    if two:
        half = grads[0].shape[0] // 2
        none = jnp.zeros((half, cells), F32)
        band = pieces.shape[1]
        for g in range(2):
            cuts = [grad[g * half : (g + 1) * half] for grad in grads]
            top = jnp.concatenate([x for cut in cuts for x in (cut, none)], axis=1)
            low = jnp.concatenate([x for cut in cuts for x in (none, cut)], axis=1)
            wing = jnp.concatenate([top, low], axis=0).astype(BF16)
            share = lax.dot_general(
                basis[...], wing, (((1,), (1,)), ((), ())), preferred_element_type=F32
            )
            for c in range(pieces.shape[0] // 2):
                pieces[2 * c + g] = share[c * band : (c + 1) * band].astype(BF16)
    else:
        terms = [dot(grad.astype(BF16), basis[d]) for d, grad in enumerate(grads)]
        pieces[...] = terms[0] + terms[1]


def sum_kernel(pieces, out):
    total = pieces[0].astype(F32)
    for i in range(1, pieces.shape[0]):
        total = total + pieces[i].astype(F32)
    half = total.shape[1] // 2
    out[...] = jnp.concatenate([total[:, :half], total[:, half:]], axis=0).astype(BF16)


def call(kernel, outs, ins, specs, scratch=(), flops=0, moved=0, out_specs=None):
    return pl.pallas_call(
        kernel,
        out_shape=outs,
        in_specs=specs,
        out_specs=out_specs or [VMEM] * len(outs),
        scratch_shapes=list(scratch),
        compiler_params=pltpu.CompilerParams(vmem_limit_bytes=LIMIT),
        cost_estimate=pl.CostEstimate(
            flops=flops, bytes_accessed=moved or flops // 200, transcendentals=0
        ),
    )(*ins)


def moved_by(x, pairs):
    return held(lax.ppermute(x, "areal", pairs))


def shift_pairs(columns, k):
    return [(i, (i - k) % columns) for i in range(columns)]


def beside_layers(tiles):
    groups = lax.axis_size("layer")
    if groups == 2:
        return [held(lax.ppermute(tiles[0], "layer", [(0, 1), (1, 0)]))]
    up = [(i, i + 1) for i in range(groups - 1)]
    down = [(i + 1, i) for i in range(groups - 1)]
    return [held(lax.ppermute(tiles[0], "layer", up)), held(lax.ppermute(tiles[-1], "layer", down))]


def outside(x):
    return pltpu.with_memory_space_constraint(x, pltpu.HBM)


def on_device(
    rhs,
    areal_blocks,
    vertical_blocks,
    conn_src,
    conn_count,
    tile_map,
    well_cells,
    well_gain,
    sens,
    basis,
):
    columns = lax.axis_size("areal")
    groups = lax.axis_size("layer")
    two = groups == 2
    rows, width = rhs.shape[2:]
    modes = basis.shape[-1]
    number = conn_src.shape[-1]
    swaps = near_swaps(number)
    routes = [swap_pairs(columns, k, color) for k, color in swaps]
    routes += [shift_pairs(columns, columns // 2 + 1), shift_pairs(columns, columns // 2)]
    rhs = rhs[0].reshape(2 * rows, width)
    me = lax.axis_index("areal").astype(jnp.int32).reshape(1)
    group = lax.axis_index("layer").astype(jnp.int32).reshape(1)

    tile = pltpu.VMEM((rows, width), BF16)
    pair = pltpu.VMEM((2 * rows, width), BF16)
    sums = pltpu.VMEM((2, rows, width), F32)
    one = 2 * rows * width * width
    partial = functools.partial

    masks_type = pltpu.VMEM((8, 128), F32)
    with jax.named_scope("plan"):
        half = len(swaps) // 2
        tables = [lax.ppermute(conn_src, "areal", pairs) for pairs in routes[:half]]
        table, asks = call(
            partial(plan_kernel, columns, swaps),
            [jax.ShapeDtypeStruct((2 * number,), jnp.int32), masks_type],
            (outside(conn_src[0, 0]), conn_count[0], outside(tile_map), me, group),
            [SMEM] * 5,
            out_specs=[SMEM, VMEM],
        )
        asks = held(asks)
        known, payload, both, *crossing = call(
            partial(cross_pick_kernel, columns),
            [masks_type, pltpu.VMEM((2 * rows + 16, width), BF16), pair] + [tile] * half,
            (me, outside(tile_map), *[x[0, 0] for x in tables], outside(rhs), asks),
            [SMEM] * (2 + half) + [VMEM] * 2,
            flops=64 * one,
        )
        known, payload, both = held(known), held(payload), held(both)
        far_pair = moved_by(rhs, routes[-1])

    with jax.named_scope("load"):
        bands, sides = call(
            partial(load_kernel, number, two),
            [
                pltpu.VMEM((number, width, 2 * width), BF16),
                pltpu.VMEM((3 if two else 4, width, width), BF16),
            ],
            (table, group, outside(areal_blocks[0]), outside(vertical_blocks[0])),
            [SMEM] * 2 + [pl.BlockSpec(memory_space=pltpu.HBM)] * 2,
            [pltpu.SemaphoreType.DMA((2 * number + 4,))],
            moved=areal_blocks.size * 2 + vertical_blocks.size * 2,
        )
        bands, sides = held(bands), held(sides)
        (factors,) = call(
            weigh_kernel,
            [pltpu.VMEM((sens.shape[2], 2, sens.shape[3]), F32)],
            (well_cells[0], well_gain[0], sens[0].transpose(1, 0, 2)),
            [SMEM] * 2 + [VMEM],
        )
        weights = held(basis[0])
        if two:
            (weights,) = call(
                partial(turn_kernel, columns),
                [pltpu.VMEM((modes // 2, 4 * sens.shape[3]), BF16)],
                (basis[0],),
                [VMEM],
            )
        factors, weights = held(factors), held(weights)

    rhs_held = lam = both
    sends = [*crossing, *[payload] * half]
    outer = [payload]
    for step in range(ITERS):
        first = step == 0
        with jax.named_scope("apply"):
            arrived = [moved_by(x, pairs) for x, pairs in zip(sends, routes)]
            (part,) = call(own_kernel, [sums], (lam, rhs_held, sides), [VMEM] * 3, flops=one)
            part = held(part)
            if first:
                odd = arrived[swaps.index((1, 0))]
                (relayed,) = call(
                    partial(relay_ask_kernel, number),
                    [masks_type],
                    (known, odd, asks),
                    [VMEM] * 3,
                )
                relayed = held(relayed)
                (nearer,) = call(
                    nearer_kernel,
                    [sums],
                    (asks, bands, far_pair),
                    [VMEM] * 3,
                    flops=16 * one,
                )
                nearer = held(nearer)
                (picked,) = call(
                    partial(far_pick_kernel, number),
                    [tile],
                    (far_pair, relayed, nearer),
                    [VMEM] * 3,
                )
                arrived = [*arrived, moved_by(picked, shift_pairs(columns, 1)), far_pair]
                told = [*[known] * half, *arrived[half:-2], moved_by(relayed, routes[-1])]
            beside = beside_layers(outer)
            (cross,) = call(
                cross_kernel,
                [sums],
                (asks, bands, *arrived[:half]),
                [VMEM] * (2 + half),
                flops=(64 if first else 4) * one,
            )
            if first:
                tiles = (asks, bands, held(cross), nearer, arrived[-2])
                adding = farther_kernel
            else:
                tiles = (asks, bands, held(cross), *arrived[-2:])
                adding = far_kernel
            (far,) = call(adding, [sums], tiles, [VMEM] * 5, flops=4 * one)
            tiles = (part, held(far), asks, bands, sides)
            near = (*arrived[half:-2], *beside)
            if step < ITERS - 1:
                lam, *rest = call(
                    partial(update_kernel, number, two, half, first),
                    [pair] + [tile] * (number + len(beside)) + ([masks_type] if first else []),
                    (*tiles, *near, *told),
                    [VMEM] * (5 + len(near) + len(told)),
                    flops=one,
                )
                lam = held(lam)
                if first:
                    told = [held(rest.pop())]
                sends, outer = rest[:number], rest[number:]
            else:
                adjoint, pieces = call(
                    partial(last_kernel, number, two, half),
                    [
                        jax.ShapeDtypeStruct((2, rows, width), BF16),
                        pltpu.VMEM((2 * columns, modes // columns // 2, rows), BF16)
                        if two
                        else pltpu.VMEM((rows, modes), F32),
                    ],
                    (*tiles, factors, weights, *near),
                    [VMEM] * (7 + len(near)),
                    flops=one,
                )

    with jax.named_scope("project"):
        if two:
            landed = lax.all_to_all(pieces, ("areal", "layer"), 0, 0, tiled=True)
            (coefficients,) = call(
                sum_kernel,
                [jax.ShapeDtypeStruct((modes // columns, rows // 2), BF16)],
                (held(landed),),
                [VMEM],
            )
            coefficients = coefficients.T
        else:
            cut = pieces.reshape(groups, rows // groups, columns, modes // columns)
            cut = cut.transpose(2, 0, 1, 3).reshape(columns * groups, rows // groups, modes // columns)
            landed = lax.all_to_all(cut, ("areal", "layer"), 0, 0, tiled=True)
            coefficients = jnp.sum(landed, axis=0).astype(BF16)
    return (adjoint[None], coefficients)


def solution(mesh):
    in_specs = (
        P("areal", "layer", None, None),
        P("areal", "layer", None, None, None),
        P("areal", "layer", None, None, None),
        P("areal", "layer", None),
        P("areal", "layer"),
        P(),
        P("areal", "layer", None),
        P("areal", "layer", None),
        P("areal", "layer", None, None),
        P("areal", "layer", None, None),
    )
    out_specs = (P("areal", "layer", None, None), P("layer", "areal"))
    return jax.shard_map(
        on_device, mesh=mesh, in_specs=in_specs, out_specs=out_specs, check_vma=False
    )
```

```python
import functools

import jax
import jax.numpy as jnp
from jax import lax
from jax.experimental import pallas as pl
from jax.experimental.pallas import tpu as pltpu
from jax.sharding import PartitionSpec as P

ITERS = 3
F32 = jnp.float32
BF16 = jnp.bfloat16
SMEM = pl.BlockSpec(memory_space=pltpu.SMEM)
VMEM = pl.BlockSpec(memory_space=pltpu.VMEM)
LIMIT = 16 * 1024 * 1024


def near_swaps(count):
    return [(k, color) for color in (1, 0) for k in range(count // 2 - 1, 0, -1)]


def swap_pairs(columns, k, color):
    return [
        (c, (c + k if (c // k) % 2 == color else c - k) % columns) for c in range(columns)
    ]


def held(x):
    return pltpu.with_memory_space_constraint(x, pltpu.VMEM)


def dot(a, b):
    return jnp.dot(a, b, preferred_element_type=F32)


def plan_kernel(columns, swaps, src, count, tile_map, me, group, rhs, table, asks, payload):
    steps = [
        jnp.where(lax.rem(lax.div(me[0], k), 2) == color, k, columns - k) for k, color in swaps
    ] + [columns // 2 + 1, columns // 2]
    number = len(steps)
    conn = [0] * number
    slots = [0] * number
    for s in range(number):
        place = tile_map[src[s]]
        peer = lax.shift_right_logical(place, 1)
        slot = lax.bitwise_and(place, 1)
        away = peer - me[0]
        away = jnp.where(away < 0, away + columns, away)
        for i, k in enumerate(steps):
            hit = away == k
            conn[i] = jnp.where(hit, s, conn[i])
            slots[i] = jnp.where(hit, slot, slots[i])
    rows, width = rhs.shape
    line = lax.broadcasted_iota(jnp.int32, (16, width), 0)
    asked = jnp.zeros(line.shape, F32)
    for i in range(number):
        table[i] = conn[i]
        table[number + i] = jnp.where(conn[i] < count[0], 1, 0)
        asked = jnp.where(line == i, slots[i].astype(F32), asked)
    asked = jnp.where(line == number, group[0].astype(F32), asked)
    asked = jnp.where(line == number + 1, lax.rem(me[0], 2).astype(F32), asked)
    asks[...] = asked[0:8, 0:128]
    payload[0:rows] = rhs[...]
    payload[rows:] = asked.astype(BF16)


def load_kernel(number, two, table, group, blocks, vert, bands, sides, sems):
    width = vert.shape[-1]
    mine = group[0]
    ends = [(1 - mine, 1 - mine)] if two else [(0, 0), (1, 1)]
    beside = [
        pltpu.make_async_copy(vert.at[d, k], sides.at[i], sems.at[2 * number + i])
        for i, (d, k) in enumerate([(0, 1), (1, 0), *ends])
    ]
    for copy in beside:
        copy.start()

    def copies(i):
        return [
            pltpu.make_async_copy(
                blocks.at[d, table[i]],
                bands.at[i, :, pl.ds(d * width, width)],
                sems.at[2 * i + d],
            )
            for d in range(2)
        ]

    for i in range(number):

        @pl.when(table[number + i] > 0)
        def _():
            for copy in copies(i):
                copy.start()

        @pl.when(table[number + i] == 0)
        def _():
            bands[i] = jnp.zeros(bands.shape[1:], bands.dtype)

    for i in range(number):

        @pl.when(table[number + i] > 0)
        def _():
            for copy in copies(i):
                copy.wait()

    for copy in beside:
        copy.wait()


def turn_kernel(columns, basis, turned):
    _, cells, modes = basis.shape
    bands = []
    for d in range(2):
        by_mode = basis[d].astype(F32).T.reshape(columns, 2, modes // columns // 2, cells)
        bands += [by_mode[:, h].reshape(modes // 2, cells) for h in range(2)]
    turned[...] = jnp.concatenate(bands, axis=1).astype(BF16)


def weigh_kernel(wells, gains, sens, factors):
    cells = sens.shape[-1]
    spot = lax.broadcasted_iota(jnp.int32, (1, cells), 1)
    factors[...] = sens[...]
    for d in range(2):
        well = jnp.zeros((1, cells), F32)
        for w in range(wells.shape[1]):
            well = well + jnp.where(spot == wells[d, w], gains[d, w], 0.0)
        factors[0, d : d + 1, :] = sens[0, d : d + 1, :] + well


def wide(mask, width):
    return jnp.concatenate([mask] * (width // mask.shape[1]), axis=1)


def chosen(mask, low, high):
    return jnp.where(wide(mask, low.shape[1]) > 0.5, high, low).astype(BF16)


def asks_of(payload):
    return payload[payload.shape[0] - 16 :, 0:128].astype(F32)


def tile_of(ref, mask, rows):
    if ref.shape[0] == rows:
        return ref[...]
    return chosen(mask, ref[0:rows].astype(F32), ref[rows : 2 * rows].astype(F32))


def far_pick_kernel(number, pair, asks, even, odd, part, tile, relayed):
    rows = tile.shape[0]
    parity = asks[number + 1 : number + 2, :]
    ask = [asks_of(ref)[number - 2 : number - 1, :] for ref in (even, odd)]
    mask = jnp.where(parity > 0.5, ask[1], ask[0])
    tile[...] = tile_of(pair, mask, rows)
    relayed[...] = asks[...]
    relayed[number - 2 : number - 1, :] = mask


def own_kernel(lam, rhs, sides, part):
    rows = rhs.shape[0] // 2
    part[0] = rhs[0:rows].astype(F32) - dot(lam[rows : 2 * rows], sides[0])
    part[1] = rhs[rows:].astype(F32) - dot(lam[0:rows], sides[1])


def source_sums(asks, bands, begin, refs, rows):
    tiles = [tile_of(ref, asks[i : i + 1, :], rows) for i, ref in enumerate(refs, begin)]
    count, width, both = len(refs), bands.shape[1], bands.shape[2]
    band = bands[begin : begin + count].reshape(count * width, both)
    sums = dot(jnp.concatenate(tiles, axis=1), band)
    return sums[:, :width], sums[:, width:]


def beside_sums(number, two, asks, sides, beside, rows):
    if two:
        mine = asks[number : number + 1, :]
        term = dot(tile_of(beside[0], mine, rows), sides[2])
        above = wide(mine, term.shape[1]) > 0.5
        none = jnp.zeros_like(term)
        return jnp.where(above, term, none), jnp.where(above, none, term)
    return [
        dot(tile_of(beside[d], jnp.full((1, 128), 1.0 - d, F32), rows), sides[2 + d])
        for d in range(2)
    ]


def cross_kernel(asks, bands, *refs):
    arrived, out = refs[:-1], refs[-1]
    out[0], out[1] = source_sums(asks, bands, 0, arrived, out.shape[1])


def far_kernel(asks, bands, cross, nearer, farther, out):
    begin = bands.shape[0] - 2
    low, high = source_sums(asks, bands, begin, [farther, nearer], out.shape[1])
    out[0] = cross[0] + low
    out[1] = cross[1] + high


def updated(number, two, begin, part, far, asks, bands, sides, near, beside):
    rows = part.shape[1]
    sums = source_sums(asks, bands, begin, near, rows)
    terms = beside_sums(number, two, asks, sides, beside, rows)
    return [part[d] - far[d] - sums[d] - terms[d] for d in range(2)]


def update_kernel(number, two, begin, first, part, far, asks, bands, sides, *refs):
    ends = 1 if two else 2
    here = number - 2 - begin
    near, refs = refs[:here], refs[here:]
    beside, refs = refs[:ends], refs[ends:]
    count = number - 1 if first else 1
    told, refs = refs[:count], refs[count:]
    low, high = updated(number, two, begin, part, far, asks, bands, sides, near, beside)
    lam, sends, refs = refs[0], refs[1 : 1 + number], refs[1 + number :]
    outer, refs = refs[:ends], refs[ends:]
    masks = told[0]
    if first:
        masks = refs[0]
        masks[...] = told[-1][...]
        for i in range(number - 2):
            masks[i : i + 1, :] = asks_of(told[i])[i : i + 1, :]
    rows = low.shape[0]
    lam[0:rows] = low.astype(BF16)
    lam[rows:] = high.astype(BF16)
    for i, send in enumerate(sends):
        send[...] = chosen(masks[i : i + 1, :], low, high)
    if two:
        outer[0][...] = chosen(asks[number : number + 1, :], high, low)
    else:
        outer[0][...] = high.astype(BF16)
        outer[1][...] = low.astype(BF16)


def last_kernel(number, two, begin, part, far, asks, bands, sides, factors, basis, *refs):
    here = number - 2 - begin
    near, beside, (lam, pieces) = refs[:here], refs[here:-2], refs[-2:]
    sums = updated(number, two, begin, part, far, asks, bands, sides, near, beside)
    phases, _, cells = factors.shape
    grads = []
    for d in range(2):
        rounded = sums[d].astype(BF16)
        lam[d] = rounded
        back = rounded.astype(F32)
        grad = back[:, :cells] * factors[0, d : d + 1, :]
        for p in range(1, phases):
            grad = grad + back[:, p * cells : (p + 1) * cells] * factors[p, d : d + 1, :]
        grads.append(grad)
    if two:
        half = grads[0].shape[0] // 2
        none = jnp.zeros((half, cells), F32)
        band = pieces.shape[1]
        for g in range(2):
            cuts = [grad[g * half : (g + 1) * half] for grad in grads]
            top = jnp.concatenate([x for cut in cuts for x in (cut, none)], axis=1)
            low = jnp.concatenate([x for cut in cuts for x in (none, cut)], axis=1)
            wing = jnp.concatenate([top, low], axis=0).astype(BF16)
            share = lax.dot_general(
                basis[...], wing, (((1,), (1,)), ((), ())), preferred_element_type=F32
            )
            for c in range(pieces.shape[0] // 2):
                pieces[2 * c + g] = share[c * band : (c + 1) * band].astype(BF16)
    else:
        terms = [dot(grad.astype(BF16), basis[d]) for d, grad in enumerate(grads)]
        pieces[...] = terms[0] + terms[1]


def sum_kernel(pieces, out):
    total = pieces[0].astype(F32)
    for i in range(1, pieces.shape[0]):
        total = total + pieces[i].astype(F32)
    half = total.shape[1] // 2
    out[...] = jnp.concatenate([total[:, :half], total[:, half:]], axis=0).astype(BF16)


def call(kernel, outs, ins, specs, scratch=(), flops=0, moved=0, out_specs=None):
    return pl.pallas_call(
        kernel,
        out_shape=outs,
        in_specs=specs,
        out_specs=out_specs or [VMEM] * len(outs),
        scratch_shapes=list(scratch),
        compiler_params=pltpu.CompilerParams(vmem_limit_bytes=LIMIT),
        cost_estimate=pl.CostEstimate(
            flops=flops, bytes_accessed=moved or flops // 200, transcendentals=0
        ),
    )(*ins)


def moved_by(x, pairs):
    return held(lax.ppermute(x, "areal", pairs))


def shift_pairs(columns, k):
    return [(i, (i - k) % columns) for i in range(columns)]


def beside_layers(tiles):
    groups = lax.axis_size("layer")
    if groups == 2:
        return [held(lax.ppermute(tiles[0], "layer", [(0, 1), (1, 0)]))]
    up = [(i, i + 1) for i in range(groups - 1)]
    down = [(i + 1, i) for i in range(groups - 1)]
    return [held(lax.ppermute(tiles[0], "layer", up)), held(lax.ppermute(tiles[-1], "layer", down))]


def outside(x):
    return pltpu.with_memory_space_constraint(x, pltpu.HBM)


def on_device(
    rhs,
    areal_blocks,
    vertical_blocks,
    conn_src,
    conn_count,
    tile_map,
    well_cells,
    well_gain,
    sens,
    basis,
):
    columns = lax.axis_size("areal")
    groups = lax.axis_size("layer")
    two = groups == 2
    rows, width = rhs.shape[2:]
    modes = basis.shape[-1]
    number = conn_src.shape[-1]
    swaps = near_swaps(number)
    routes = [swap_pairs(columns, k, color) for k, color in swaps]
    routes += [shift_pairs(columns, columns // 2 + 1), shift_pairs(columns, columns // 2)]
    rhs = rhs[0].reshape(2 * rows, width)
    me = lax.axis_index("areal").astype(jnp.int32).reshape(1)
    group = lax.axis_index("layer").astype(jnp.int32).reshape(1)

    tile = pltpu.VMEM((rows, width), BF16)
    pair = pltpu.VMEM((2 * rows, width), BF16)
    sums = pltpu.VMEM((2, rows, width), F32)
    one = 2 * rows * width * width
    partial = functools.partial

    masks_type = pltpu.VMEM((8, 128), F32)
    with jax.named_scope("plan"):
        far_pair = moved_by(rhs, routes[-1])
        table, asks, payload = call(
            partial(plan_kernel, columns, swaps),
            [
                jax.ShapeDtypeStruct((2 * number,), jnp.int32),
                masks_type,
                pltpu.VMEM((2 * rows + 16, width), BF16),
            ],
            (outside(conn_src[0, 0]), conn_count[0], outside(tile_map), me, group, outside(rhs)),
            [SMEM] * 5 + [VMEM],
            out_specs=[SMEM] + [VMEM] * 2,
        )
        asks, payload = held(asks), held(payload)

    with jax.named_scope("load"):
        bands, sides = call(
            partial(load_kernel, number, two),
            [
                pltpu.VMEM((number, width, 2 * width), BF16),
                pltpu.VMEM((3 if two else 4, width, width), BF16),
            ],
            (table, group, outside(areal_blocks[0]), outside(vertical_blocks[0])),
            [SMEM] * 2 + [pl.BlockSpec(memory_space=pltpu.HBM)] * 2,
            [pltpu.SemaphoreType.DMA((2 * number + 4,))],
            moved=areal_blocks.size * 2 + vertical_blocks.size * 2,
        )
        bands, sides = held(bands), held(sides)
        (factors,) = call(
            weigh_kernel,
            [pltpu.VMEM((sens.shape[2], 2, sens.shape[3]), F32)],
            (well_cells[0], well_gain[0], sens[0].transpose(1, 0, 2)),
            [SMEM] * 2 + [VMEM],
        )
        weights = held(basis[0])
        if two:
            (weights,) = call(
                partial(turn_kernel, columns),
                [pltpu.VMEM((modes // 2, 4 * sens.shape[3]), BF16)],
                (basis[0],),
                [VMEM],
            )
        factors, weights = held(factors), held(weights)

    rhs_held = held(rhs)
    lam = rhs_held
    sends = [payload] * (number - 2)
    outer = [payload]
    half = len(swaps) // 2
    for step in range(ITERS):
        first = step == 0
        with jax.named_scope("apply"):
            arrived = [moved_by(x, pairs) for x, pairs in zip(sends, routes)]
            (part,) = call(own_kernel, [sums], (lam, rhs_held, sides), [VMEM] * 3, flops=one)
            part = held(part)
            if first:
                even, odd = (arrived[swaps.index((1, color))] for color in (1, 0))
                picked, relayed = call(
                    partial(far_pick_kernel, number),
                    [tile, masks_type],
                    (far_pair, asks, even, odd, part),
                    [VMEM] * 5,
                )
                arrived = [*arrived, moved_by(picked, shift_pairs(columns, 1)), far_pair]
                told = [*arrived[:-2], moved_by(relayed, routes[-1])]
            beside = beside_layers(outer)
            (cross,) = call(
                cross_kernel,
                [sums],
                (asks, bands, *arrived[:half]),
                [VMEM] * (2 + half),
                flops=4 * one,
            )
            (far,) = call(
                far_kernel,
                [sums],
                (asks, bands, held(cross), arrived[-1], arrived[-2]),
                [VMEM] * 5,
                flops=4 * one,
            )
            tiles = (part, held(far), asks, bands, sides)
            near = (*arrived[half:-2], *beside)
            if step < ITERS - 1:
                lam, *rest = call(
                    partial(update_kernel, number, two, half, first),
                    [pair] + [tile] * (number + len(beside)) + ([masks_type] if first else []),
                    (*tiles, *near, *told),
                    [VMEM] * (5 + len(near) + len(told)),
                    flops=one,
                )
                lam = held(lam)
                if first:
                    told = [held(rest.pop())]
                sends, outer = rest[:number], rest[number:]
            else:
                adjoint, pieces = call(
                    partial(last_kernel, number, two, half),
                    [
                        jax.ShapeDtypeStruct((2, rows, width), BF16),
                        pltpu.VMEM((2 * columns, modes // columns // 2, rows), BF16)
                        if two
                        else pltpu.VMEM((rows, modes), F32),
                    ],
                    (*tiles, factors, weights, *near),
                    [VMEM] * (7 + len(near)),
                    flops=one,
                )

    with jax.named_scope("project"):
        if two:
            landed = lax.all_to_all(pieces, ("areal", "layer"), 0, 0, tiled=True)
            (coefficients,) = call(
                sum_kernel,
                [jax.ShapeDtypeStruct((modes // columns, rows // 2), BF16)],
                (held(landed),),
                [VMEM],
            )
            coefficients = coefficients.T
        else:
            cut = pieces.reshape(groups, rows // groups, columns, modes // columns)
            cut = cut.transpose(2, 0, 1, 3).reshape(columns * groups, rows // groups, modes // columns)
            landed = lax.all_to_all(cut, ("areal", "layer"), 0, 0, tiled=True)
            coefficients = jnp.sum(landed, axis=0).astype(BF16)
    return (adjoint[None], coefficients)


def solution(mesh):
    in_specs = (
        P("areal", "layer", None, None),
        P("areal", "layer", None, None, None),
        P("areal", "layer", None, None, None),
        P("areal", "layer", None),
        P("areal", "layer"),
        P(),
        P("areal", "layer", None),
        P("areal", "layer", None),
        P("areal", "layer", None, None),
        P("areal", "layer", None, None),
    )
    out_specs = (P("areal", "layer", None, None), P("layer", "areal"))
    return jax.shard_map(
        on_device, mesh=mesh, in_specs=in_specs, out_specs=out_specs, check_vma=False
    )
```

```python
import functools

import jax
import jax.numpy as jnp
from jax import lax
from jax.experimental import pallas as pl
from jax.experimental.pallas import tpu as pltpu
from jax.sharding import PartitionSpec as P

ITERS = 3
F32 = jnp.float32
BF16 = jnp.bfloat16
SMEM = pl.BlockSpec(memory_space=pltpu.SMEM)
VMEM = pl.BlockSpec(memory_space=pltpu.VMEM)
LIMIT = 16 * 1024 * 1024


def near_swaps(count):
    return [(k, color) for color in (1, 0) for k in range(count // 2 - 1, 0, -1)]


def swap_pairs(columns, k, color):
    return [
        (c, (c + k if (c // k) % 2 == color else c - k) % columns) for c in range(columns)
    ]


def held(x):
    return pltpu.with_memory_space_constraint(x, pltpu.VMEM)


def dot(a, b):
    return jnp.dot(a, b, preferred_element_type=F32)


def plan_kernel(columns, swaps, src, count, tile_map, me, group, table, asks):
    steps = [
        jnp.where(lax.rem(lax.div(me[0], k), 2) == color, k, columns - k) for k, color in swaps
    ] + [columns // 2 + 1, columns // 2]
    number = len(steps)
    conn = [0] * number
    slots = [0] * number
    for s in range(number):
        place = tile_map[src[s]]
        peer = lax.shift_right_logical(place, 1)
        slot = lax.bitwise_and(place, 1)
        away = peer - me[0]
        away = jnp.where(away < 0, away + columns, away)
        for i, k in enumerate(steps):
            hit = away == k
            conn[i] = jnp.where(hit, s, conn[i])
            slots[i] = jnp.where(hit, slot, slots[i])
    line = lax.broadcasted_iota(jnp.int32, asks.shape, 0)
    asked = jnp.zeros(line.shape, F32)
    for i in range(number):
        table[i] = conn[i]
        table[number + i] = jnp.where(conn[i] < count[0], 1, 0)
        asked = jnp.where(line == i, slots[i].astype(F32), asked)
    asked = jnp.where(line == number, group[0].astype(F32), asked)
    asked = jnp.where(line == number + 1, lax.rem(me[0], 2).astype(F32), asked)
    asks[...] = asked


def load_kernel(number, two, table, group, blocks, vert, bands, sides, sems):
    width = vert.shape[-1]
    mine = group[0]
    ends = [(1 - mine, 1 - mine)] if two else [(0, 0), (1, 1)]
    beside = [
        pltpu.make_async_copy(vert.at[d, k], sides.at[i], sems.at[2 * number + i])
        for i, (d, k) in enumerate([(0, 1), (1, 0), *ends])
    ]
    for copy in beside:
        copy.start()

    def copies(i):
        return [
            pltpu.make_async_copy(
                blocks.at[d, table[i]],
                bands.at[i, :, pl.ds(d * width, width)],
                sems.at[2 * i + d],
            )
            for d in range(2)
        ]

    for i in range(number):

        @pl.when(table[number + i] > 0)
        def _():
            for copy in copies(i):
                copy.start()

        @pl.when(table[number + i] == 0)
        def _():
            bands[i] = jnp.zeros(bands.shape[1:], bands.dtype)

    for i in range(number):

        @pl.when(table[number + i] > 0)
        def _():
            for copy in copies(i):
                copy.wait()

    for copy in beside:
        copy.wait()


def turn_kernel(columns, basis, turned):
    _, cells, modes = basis.shape
    bands = []
    for d in range(2):
        by_mode = basis[d].astype(F32).T.reshape(columns, 2, modes // columns // 2, cells)
        bands += [by_mode[:, h].reshape(modes // 2, cells) for h in range(2)]
    turned[...] = jnp.concatenate(bands, axis=1).astype(BF16)


def weigh_kernel(wells, gains, sens, factors):
    cells = sens.shape[-1]
    spot = lax.broadcasted_iota(jnp.int32, (1, cells), 1)
    factors[...] = sens[...]
    for d in range(2):
        well = jnp.zeros((1, cells), F32)
        for w in range(wells.shape[1]):
            well = well + jnp.where(spot == wells[d, w], gains[d, w], 0.0)
        factors[0, d : d + 1, :] = sens[0, d : d + 1, :] + well


def wide(mask, width):
    return jnp.concatenate([mask] * (width // mask.shape[1]), axis=1)


def chosen(mask, low, high):
    return jnp.where(wide(mask, low.shape[1]) > 0.5, high, low).astype(BF16)


def asks_of(payload):
    return payload[payload.shape[0] - 16 :, 0:128].astype(F32)


def tile_of(ref, mask, rows):
    if ref.shape[0] == rows:
        return ref[...]
    return chosen(mask, ref[0:rows].astype(F32), ref[rows : 2 * rows].astype(F32))


def cross_pick_kernel(lines, me, tile_map, *refs):
    count = len(lines)
    tables, (rhs, asks), refs = refs[:count], refs[count : count + 2], refs[count + 2 :]
    (known, payload, pair), tiles = refs[:3], refs[3:]
    rows = rhs.shape[0] // 2
    line = lax.broadcasted_iota(jnp.int32, known.shape, 0)
    masks = jnp.zeros(known.shape, F32)
    for i, table in zip(lines, tables):
        wanted = 0
        for s in range(table.shape[-1]):
            place = tile_map[table[s]]
            peer = lax.shift_right_logical(place, 1)
            wanted = jnp.where(peer == me[0], lax.bitwise_and(place, 1), wanted)
        masks = jnp.where(line == i, wanted.astype(F32), masks)
    known[...] = masks
    payload[0 : 2 * rows] = rhs[...]
    payload[2 * rows :] = jnp.zeros((16, rhs.shape[1]), BF16)
    none = jnp.zeros((8, 128), F32)
    payload[2 * rows :, 0:128] = jnp.concatenate([asks[...], none], axis=0).astype(BF16)
    pair[...] = rhs[...]
    low, high = rhs[0:rows].astype(F32), rhs[rows:].astype(F32)
    for i, tile in zip(lines, tiles):
        tile[...] = chosen(masks[i : i + 1, :], low, high)


def own_kernel(lam, rhs, sides, part):
    rows = rhs.shape[0] // 2
    part[0] = rhs[0:rows].astype(F32) - dot(lam[rows : 2 * rows], sides[0])
    part[1] = rhs[rows:].astype(F32) - dot(lam[0:rows], sides[1])


def source_sums(asks, bands, begin, refs, rows):
    tiles = [tile_of(ref, asks[i : i + 1, :], rows) for i, ref in enumerate(refs, begin)]
    count, width, both = len(refs), bands.shape[1], bands.shape[2]
    band = bands[begin : begin + count].reshape(count * width, both)
    sums = dot(jnp.concatenate(tiles, axis=1), band)
    return sums[:, :width], sums[:, width:]


def beside_sums(number, two, asks, sides, beside, rows):
    if two:
        mine = asks[number : number + 1, :]
        term = dot(tile_of(beside[0], mine, rows), sides[2])
        above = wide(mine, term.shape[1]) > 0.5
        none = jnp.zeros_like(term)
        return jnp.where(above, term, none), jnp.where(above, none, term)
    return [
        dot(tile_of(beside[d], jnp.full((1, 128), 1.0 - d, F32), rows), sides[2 + d])
        for d in range(2)
    ]


def cross_kernel(asks, bands, *refs):
    arrived, out = refs[:-1], refs[-1]
    out[0], out[1] = source_sums(asks, bands, 0, arrived, out.shape[1])


def far_kernel(asks, bands, cross, *refs):
    far, out = refs[:-1], refs[-1]
    low, high = source_sums(asks, bands, bands.shape[0] - len(far), far, out.shape[1])
    out[0] = cross[0] + low
    out[1] = cross[1] + high


def updated(number, two, begin, part, far, asks, bands, sides, near, beside):
    rows = part.shape[1]
    sums = source_sums(asks, bands, begin, near, rows)
    terms = beside_sums(number, two, asks, sides, beside, rows)
    return [part[d] - far[d] - sums[d] - terms[d] for d in range(2)]


def update_kernel(number, two, begin, first, part, far, asks, bands, sides, *refs):
    ends = 1 if two else 2
    here = number - 2 - begin
    near, refs = refs[:here], refs[here:]
    beside, refs = refs[:ends], refs[ends:]
    count = 1 + here if first else 1
    told, refs = refs[:count], refs[count:]
    low, high = updated(number, two, begin, part, far, asks, bands, sides, near, beside)
    lam, sends, refs = refs[0], refs[1 : 1 + number], refs[1 + number :]
    outer, refs = refs[:ends], refs[ends:]
    masks = told[0]
    if first:
        masks = refs[0]
        masks[...] = told[0][...]
        for i, ref in enumerate(told[1:], begin):
            masks[i : i + 1, :] = asks_of(ref)[i : i + 1, :]
    rows = low.shape[0]
    lam[0:rows] = low.astype(BF16)
    lam[rows:] = high.astype(BF16)
    for i, send in enumerate(sends):
        send[...] = chosen(masks[i : i + 1, :], low, high)
    if two:
        outer[0][...] = chosen(asks[number : number + 1, :], high, low)
    else:
        outer[0][...] = high.astype(BF16)
        outer[1][...] = low.astype(BF16)


def last_kernel(number, two, begin, part, far, asks, bands, sides, factors, basis, *refs):
    here = number - 2 - begin
    near, beside, (lam, pieces) = refs[:here], refs[here:-2], refs[-2:]
    sums = updated(number, two, begin, part, far, asks, bands, sides, near, beside)
    phases, _, cells = factors.shape
    grads = []
    for d in range(2):
        rounded = sums[d].astype(BF16)
        lam[d] = rounded
        back = rounded.astype(F32)
        grad = back[:, :cells] * factors[0, d : d + 1, :]
        for p in range(1, phases):
            grad = grad + back[:, p * cells : (p + 1) * cells] * factors[p, d : d + 1, :]
        grads.append(grad)
    if two:
        half = grads[0].shape[0] // 2
        none = jnp.zeros((half, cells), F32)
        band = pieces.shape[1]
        for g in range(2):
            cuts = [grad[g * half : (g + 1) * half] for grad in grads]
            top = jnp.concatenate([x for cut in cuts for x in (cut, none)], axis=1)
            low = jnp.concatenate([x for cut in cuts for x in (none, cut)], axis=1)
            wing = jnp.concatenate([top, low], axis=0).astype(BF16)
            share = lax.dot_general(
                basis[...], wing, (((1,), (1,)), ((), ())), preferred_element_type=F32
            )
            for c in range(pieces.shape[0] // 2):
                pieces[2 * c + g] = share[c * band : (c + 1) * band].astype(BF16)
    else:
        terms = [dot(grad.astype(BF16), basis[d]) for d, grad in enumerate(grads)]
        pieces[...] = terms[0] + terms[1]


def sum_kernel(pieces, out):
    total = pieces[0].astype(F32)
    for i in range(1, pieces.shape[0]):
        total = total + pieces[i].astype(F32)
    half = total.shape[1] // 2
    out[...] = jnp.concatenate([total[:, :half], total[:, half:]], axis=0).astype(BF16)


def call(kernel, outs, ins, specs, scratch=(), flops=0, moved=0, out_specs=None):
    return pl.pallas_call(
        kernel,
        out_shape=outs,
        in_specs=specs,
        out_specs=out_specs or [VMEM] * len(outs),
        scratch_shapes=list(scratch),
        compiler_params=pltpu.CompilerParams(vmem_limit_bytes=LIMIT),
        cost_estimate=pl.CostEstimate(
            flops=flops, bytes_accessed=moved or flops // 200, transcendentals=0
        ),
    )(*ins)


def moved_by(x, pairs):
    return held(lax.ppermute(x, "areal", pairs))


def shift_pairs(columns, k):
    return [(i, (i - k) % columns) for i in range(columns)]


def beside_layers(tiles):
    groups = lax.axis_size("layer")
    if groups == 2:
        return [held(lax.ppermute(tiles[0], "layer", [(0, 1), (1, 0)]))]
    up = [(i, i + 1) for i in range(groups - 1)]
    down = [(i + 1, i) for i in range(groups - 1)]
    return [held(lax.ppermute(tiles[0], "layer", up)), held(lax.ppermute(tiles[-1], "layer", down))]


def outside(x):
    return pltpu.with_memory_space_constraint(x, pltpu.HBM)


def on_device(
    rhs,
    areal_blocks,
    vertical_blocks,
    conn_src,
    conn_count,
    tile_map,
    well_cells,
    well_gain,
    sens,
    basis,
):
    columns = lax.axis_size("areal")
    groups = lax.axis_size("layer")
    two = groups == 2
    rows, width = rhs.shape[2:]
    modes = basis.shape[-1]
    number = conn_src.shape[-1]
    swaps = near_swaps(number)
    routes = [swap_pairs(columns, k, color) for k, color in swaps]
    routes += [shift_pairs(columns, columns // 2 + 1), shift_pairs(columns, columns // 2)]
    rhs = rhs[0].reshape(2 * rows, width)
    me = lax.axis_index("areal").astype(jnp.int32).reshape(1)
    group = lax.axis_index("layer").astype(jnp.int32).reshape(1)

    tile = pltpu.VMEM((rows, width), BF16)
    pair = pltpu.VMEM((2 * rows, width), BF16)
    sums = pltpu.VMEM((2, rows, width), F32)
    one = 2 * rows * width * width
    partial = functools.partial

    masks_type = pltpu.VMEM((8, 128), F32)
    with jax.named_scope("plan"):
        half = len(swaps) // 2
        lines = [*range(half), number - 2, number - 1]
        tables = [
            lax.ppermute(conn_src, "areal", [(to, at) for at, to in routes[i]]) for i in lines
        ]
        table, asks = call(
            partial(plan_kernel, columns, swaps),
            [jax.ShapeDtypeStruct((2 * number,), jnp.int32), masks_type],
            (outside(conn_src[0, 0]), conn_count[0], outside(tile_map), me, group),
            [SMEM] * 5,
            out_specs=[SMEM, VMEM],
        )
        asks = held(asks)
        known, payload, both, *crossing = call(
            partial(cross_pick_kernel, lines),
            [masks_type, pltpu.VMEM((2 * rows + 16, width), BF16), pair] + [tile] * len(lines),
            (me, outside(tile_map), *[x[0, 0] for x in tables], outside(rhs), asks),
            [SMEM] * (2 + len(lines)) + [VMEM] * 2,
        )
        known, payload, both = held(known), held(payload), held(both)

    with jax.named_scope("load"):
        bands, sides = call(
            partial(load_kernel, number, two),
            [
                pltpu.VMEM((number, width, 2 * width), BF16),
                pltpu.VMEM((3 if two else 4, width, width), BF16),
            ],
            (table, group, outside(areal_blocks[0]), outside(vertical_blocks[0])),
            [SMEM] * 2 + [pl.BlockSpec(memory_space=pltpu.HBM)] * 2,
            [pltpu.SemaphoreType.DMA((2 * number + 4,))],
            moved=areal_blocks.size * 2 + vertical_blocks.size * 2,
        )
        bands, sides = held(bands), held(sides)
        (factors,) = call(
            weigh_kernel,
            [pltpu.VMEM((sens.shape[2], 2, sens.shape[3]), F32)],
            (well_cells[0], well_gain[0], sens[0].transpose(1, 0, 2)),
            [SMEM] * 2 + [VMEM],
        )
        weights = held(basis[0])
        if two:
            (weights,) = call(
                partial(turn_kernel, columns),
                [pltpu.VMEM((modes // 2, 4 * sens.shape[3]), BF16)],
                (basis[0],),
                [VMEM],
            )
        factors, weights = held(factors), held(weights)

    rhs_held = lam = both
    sends = [*crossing[:half], *[payload] * half, *crossing[half:]]
    outer = [payload]
    for step in range(ITERS):
        first = step == 0
        with jax.named_scope("apply"):
            arrived = [moved_by(x, pairs) for x, pairs in zip(sends, routes)]
            (part,) = call(own_kernel, [sums], (lam, rhs_held, sides), [VMEM] * 3, flops=one)
            part = held(part)
            if first:
                told = [known, *arrived[half:-2]]
            beside = beside_layers(outer)
            (cross,) = call(
                cross_kernel,
                [sums],
                (asks, bands, *arrived[:half]),
                [VMEM] * (2 + half),
                flops=4 * one,
            )
            (far,) = call(
                far_kernel,
                [sums],
                (asks, bands, held(cross), *arrived[-2:]),
                [VMEM] * 5,
                flops=(64 if first else 4) * one,
            )
            tiles = (part, held(far), asks, bands, sides)
            near = (*arrived[half:-2], *beside)
            if step < ITERS - 1:
                lam, *rest = call(
                    partial(update_kernel, number, two, half, first),
                    [pair] + [tile] * (number + len(beside)) + ([masks_type] if first else []),
                    (*tiles, *near, *told),
                    [VMEM] * (5 + len(near) + len(told)),
                    flops=one,
                )
                lam = held(lam)
                if first:
                    told = [held(rest.pop())]
                sends, outer = rest[:number], rest[number:]
            else:
                adjoint, pieces = call(
                    partial(last_kernel, number, two, half),
                    [
                        jax.ShapeDtypeStruct((2, rows, width), BF16),
                        pltpu.VMEM((2 * columns, modes // columns // 2, rows), BF16)
                        if two
                        else pltpu.VMEM((rows, modes), F32),
                    ],
                    (*tiles, factors, weights, *near),
                    [VMEM] * (7 + len(near)),
                    flops=one,
                )

    with jax.named_scope("project"):
        if two:
            landed = lax.all_to_all(pieces, ("areal", "layer"), 0, 0, tiled=True)
            (coefficients,) = call(
                sum_kernel,
                [jax.ShapeDtypeStruct((modes // columns, rows // 2), BF16)],
                (held(landed),),
                [VMEM],
            )
            coefficients = coefficients.T
        else:
            cut = pieces.reshape(groups, rows // groups, columns, modes // columns)
            cut = cut.transpose(2, 0, 1, 3).reshape(columns * groups, rows // groups, modes // columns)
            landed = lax.all_to_all(cut, ("areal", "layer"), 0, 0, tiled=True)
            coefficients = jnp.sum(landed, axis=0).astype(BF16)
    return (adjoint[None], coefficients)


def solution(mesh):
    in_specs = (
        P("areal", "layer", None, None),
        P("areal", "layer", None, None, None),
        P("areal", "layer", None, None, None),
        P("areal", "layer", None),
        P("areal", "layer"),
        P(),
        P("areal", "layer", None),
        P("areal", "layer", None),
        P("areal", "layer", None, None),
        P("areal", "layer", None, None),
    )
    out_specs = (P("areal", "layer", None, None), P("layer", "areal"))
    return jax.shard_map(
        on_device, mesh=mesh, in_specs=in_specs, out_specs=out_specs, check_vma=False
    )
```

```python
import functools

import jax
import jax.numpy as jnp
from jax import lax
from jax.experimental import pallas as pl
from jax.experimental.pallas import tpu as pltpu
from jax.sharding import PartitionSpec as P

ITERS = 3
F32 = jnp.float32
BF16 = jnp.bfloat16
SMEM = pl.BlockSpec(memory_space=pltpu.SMEM)
VMEM = pl.BlockSpec(memory_space=pltpu.VMEM)
LIMIT = 16 * 1024 * 1024


def near_swaps(count):
    return [(k, color) for color in (1, 0) for k in range(count // 2 - 1, 0, -1)]


def swap_pairs(columns, k, color):
    return [
        (c, (c + k if (c // k) % 2 == color else c - k) % columns) for c in range(columns)
    ]


def held(x):
    return pltpu.with_memory_space_constraint(x, pltpu.VMEM)


def dot(a, b):
    return jnp.dot(a, b, preferred_element_type=F32)


def plan_kernel(columns, swaps, src, count, tile_map, me, group, rhs, table, asks, payload):
    steps = [
        jnp.where(lax.rem(lax.div(me[0], k), 2) == color, k, columns - k) for k, color in swaps
    ] + [columns // 2 + 1, columns // 2]
    number = len(steps)
    conn = [0] * number
    slots = [0] * number
    for s in range(number):
        place = tile_map[src[s]]
        peer = lax.shift_right_logical(place, 1)
        slot = lax.bitwise_and(place, 1)
        away = peer - me[0]
        away = jnp.where(away < 0, away + columns, away)
        for i, k in enumerate(steps):
            hit = away == k
            conn[i] = jnp.where(hit, s, conn[i])
            slots[i] = jnp.where(hit, slot, slots[i])
    line = lax.broadcasted_iota(jnp.int32, asks.shape, 0)
    asked = jnp.zeros(line.shape, F32)
    for i in range(number):
        table[i] = conn[i]
        table[number + i] = jnp.where(conn[i] < count[0], 1, 0)
        asked = jnp.where(line == i, slots[i].astype(F32), asked)
    asked = jnp.where(line == number, group[0].astype(F32), asked)
    asked = jnp.where(line == number + 1, lax.rem(me[0], 2).astype(F32), asked)
    asks[...] = asked
    rows, width = rhs.shape
    payload[0:rows] = rhs[...]
    payload[rows:] = jnp.zeros((16, width), BF16)
    none = jnp.zeros(asked.shape, F32)
    payload[rows:, 0:128] = jnp.concatenate([asked, none], axis=0).astype(BF16)


def load_kernel(number, two, table, group, blocks, vert, bands, sides, sems):
    width = vert.shape[-1]
    mine = group[0]
    ends = [(1 - mine, 1 - mine)] if two else [(0, 0), (1, 1)]
    beside = [
        pltpu.make_async_copy(vert.at[d, k], sides.at[i], sems.at[2 * number + i])
        for i, (d, k) in enumerate([(0, 1), (1, 0), *ends])
    ]
    for copy in beside:
        copy.start()

    def copies(i):
        return [
            pltpu.make_async_copy(
                blocks.at[d, table[i]],
                bands.at[i, :, pl.ds(d * width, width)],
                sems.at[2 * i + d],
            )
            for d in range(2)
        ]

    for i in range(number):

        @pl.when(table[number + i] > 0)
        def _():
            for copy in copies(i):
                copy.start()

        @pl.when(table[number + i] == 0)
        def _():
            bands[i] = jnp.zeros(bands.shape[1:], bands.dtype)

    for i in range(number):

        @pl.when(table[number + i] > 0)
        def _():
            for copy in copies(i):
                copy.wait()

    for copy in beside:
        copy.wait()


def turn_kernel(columns, basis, turned):
    _, cells, modes = basis.shape
    bands = []
    for d in range(2):
        by_mode = basis[d].astype(F32).T.reshape(columns, 2, modes // columns // 2, cells)
        bands += [by_mode[:, h].reshape(modes // 2, cells) for h in range(2)]
    turned[...] = jnp.concatenate(bands, axis=1).astype(BF16)


def weigh_kernel(wells, gains, sens, factors):
    cells = sens.shape[-1]
    spot = lax.broadcasted_iota(jnp.int32, (1, cells), 1)
    factors[...] = sens[...]
    for d in range(2):
        well = jnp.zeros((1, cells), F32)
        for w in range(wells.shape[1]):
            well = well + jnp.where(spot == wells[d, w], gains[d, w], 0.0)
        factors[0, d : d + 1, :] = sens[0, d : d + 1, :] + well


def wide(mask, width):
    return jnp.concatenate([mask] * (width // mask.shape[1]), axis=1)


def chosen(mask, low, high):
    return jnp.where(wide(mask, low.shape[1]) > 0.5, high, low).astype(BF16)


def asks_of(payload):
    return payload[payload.shape[0] - 16 :, 0:128].astype(F32)


def tile_of(ref, mask, rows):
    if ref.shape[0] == rows:
        return ref[...]
    return chosen(mask, ref[0:rows].astype(F32), ref[rows : 2 * rows].astype(F32))


def cross_pick_kernel(lines, me, tile_map, *refs):
    count = len(lines)
    tables, payload, known, tiles = refs[:count], refs[count], refs[count + 1], refs[count + 2 :]
    rows = tiles[0].shape[0]
    line = lax.broadcasted_iota(jnp.int32, known.shape, 0)
    masks = jnp.zeros(known.shape, F32)
    for i, table in zip(lines, tables):
        wanted = 0
        for s in range(table.shape[-1]):
            place = tile_map[table[s]]
            peer = lax.shift_right_logical(place, 1)
            wanted = jnp.where(peer == me[0], lax.bitwise_and(place, 1), wanted)
        masks = jnp.where(line == i, wanted.astype(F32), masks)
    known[...] = masks
    low, high = payload[0:rows].astype(F32), payload[rows : 2 * rows].astype(F32)
    for i, tile in zip(lines, tiles):
        tile[...] = chosen(masks[i : i + 1, :], low, high)


def own_kernel(lam, rhs, sides, part):
    rows = rhs.shape[0] // 2
    part[0] = rhs[0:rows].astype(F32) - dot(lam[rows : 2 * rows], sides[0])
    part[1] = rhs[rows:].astype(F32) - dot(lam[0:rows], sides[1])


def source_sums(asks, bands, begin, refs, rows):
    tiles = [tile_of(ref, asks[i : i + 1, :], rows) for i, ref in enumerate(refs, begin)]
    count, width, both = len(refs), bands.shape[1], bands.shape[2]
    band = bands[begin : begin + count].reshape(count * width, both)
    sums = dot(jnp.concatenate(tiles, axis=1), band)
    return sums[:, :width], sums[:, width:]


def beside_sums(number, two, asks, sides, beside, rows):
    if two:
        mine = asks[number : number + 1, :]
        term = dot(tile_of(beside[0], mine, rows), sides[2])
        above = wide(mine, term.shape[1]) > 0.5
        none = jnp.zeros_like(term)
        return jnp.where(above, term, none), jnp.where(above, none, term)
    return [
        dot(tile_of(beside[d], jnp.full((1, 128), 1.0 - d, F32), rows), sides[2 + d])
        for d in range(2)
    ]


def cross_kernel(asks, bands, *refs):
    arrived, out = refs[:-1], refs[-1]
    out[0], out[1] = source_sums(asks, bands, 0, arrived, out.shape[1])


def far_kernel(asks, bands, cross, *refs):
    far, out = refs[:-1], refs[-1]
    low, high = source_sums(asks, bands, bands.shape[0] - len(far), far, out.shape[1])
    out[0] = cross[0] + low
    out[1] = cross[1] + high


def local_kernel(number, two, begin, asks, bands, sides, *refs):
    here = number - 2 - begin
    near, beside, out = refs[:here], refs[here:-1], refs[-1]
    rows = out.shape[1]
    sums = source_sums(asks, bands, begin, near, rows)
    terms = beside_sums(number, two, asks, sides, beside, rows)
    for d in range(2):
        out[d] = sums[d] + terms[d]


def updated(number, two, begin, part, far, asks, bands, sides, near, beside):
    rows = part.shape[1]
    sums = source_sums(asks, bands, begin, near, rows)
    terms = beside_sums(number, two, asks, sides, beside, rows)
    return [part[d] - far[d] - sums[d] - terms[d] for d in range(2)]


def update_kernel(number, two, begin, first, part, far, asks, *refs):
    ends = 1 if two else 2
    here = number - 2 - begin
    if first:
        local, refs = refs[0], refs[1:]
        low, high = [part[d] - far[d] - local[d] for d in range(2)]
    else:
        (bands, sides), refs = refs[:2], refs[2:]
        near, refs = refs[:here], refs[here:]
        beside, refs = refs[:ends], refs[ends:]
        low, high = updated(number, two, begin, part, far, asks, bands, sides, near, beside)
    count = 1 + here if first else 1
    told, refs = refs[:count], refs[count:]
    lam, sends, refs = refs[0], refs[1 : 1 + number], refs[1 + number :]
    outer, refs = refs[:ends], refs[ends:]
    masks = told[0]
    if first:
        masks = refs[0]
        masks[...] = told[0][...]
        for i, ref in enumerate(told[1:], begin):
            masks[i : i + 1, :] = asks_of(ref)[i : i + 1, :]
    rows = low.shape[0]
    lam[0:rows] = low.astype(BF16)
    lam[rows:] = high.astype(BF16)
    for i, send in enumerate(sends):
        send[...] = chosen(masks[i : i + 1, :], low, high)
    if two:
        outer[0][...] = chosen(asks[number : number + 1, :], high, low)
    else:
        outer[0][...] = high.astype(BF16)
        outer[1][...] = low.astype(BF16)


def last_kernel(number, two, begin, part, far, asks, bands, sides, factors, basis, *refs):
    here = number - 2 - begin
    near, beside, (lam, pieces) = refs[:here], refs[here:-2], refs[-2:]
    sums = updated(number, two, begin, part, far, asks, bands, sides, near, beside)
    phases, _, cells = factors.shape
    grads = []
    for d in range(2):
        rounded = sums[d].astype(BF16)
        lam[d] = rounded
        back = rounded.astype(F32)
        grad = back[:, :cells] * factors[0, d : d + 1, :]
        for p in range(1, phases):
            grad = grad + back[:, p * cells : (p + 1) * cells] * factors[p, d : d + 1, :]
        grads.append(grad)
    if two:
        half = grads[0].shape[0] // 2
        none = jnp.zeros((half, cells), F32)
        band = pieces.shape[1]
        for g in range(2):
            cuts = [grad[g * half : (g + 1) * half] for grad in grads]
            top = jnp.concatenate([x for cut in cuts for x in (cut, none)], axis=1)
            low = jnp.concatenate([x for cut in cuts for x in (none, cut)], axis=1)
            wing = jnp.concatenate([top, low], axis=0).astype(BF16)
            share = lax.dot_general(
                basis[...], wing, (((1,), (1,)), ((), ())), preferred_element_type=F32
            )
            for c in range(pieces.shape[0] // 2):
                pieces[2 * c + g] = share[c * band : (c + 1) * band].astype(BF16)
    else:
        terms = [dot(grad.astype(BF16), basis[d]) for d, grad in enumerate(grads)]
        pieces[...] = terms[0] + terms[1]


def sum_kernel(pieces, out):
    total = pieces[0].astype(F32)
    for i in range(1, pieces.shape[0]):
        total = total + pieces[i].astype(F32)
    half = total.shape[1] // 2
    out[...] = jnp.concatenate([total[:, :half], total[:, half:]], axis=0).astype(BF16)


def call(kernel, outs, ins, specs, scratch=(), flops=0, moved=0, out_specs=None):
    return pl.pallas_call(
        kernel,
        out_shape=outs,
        in_specs=specs,
        out_specs=out_specs or [VMEM] * len(outs),
        scratch_shapes=list(scratch),
        compiler_params=pltpu.CompilerParams(vmem_limit_bytes=LIMIT),
        cost_estimate=pl.CostEstimate(
            flops=flops, bytes_accessed=moved or flops // 200, transcendentals=0
        ),
    )(*ins)


def moved_by(x, pairs):
    return held(lax.ppermute(x, "areal", pairs))


def shift_pairs(columns, k):
    return [(i, (i - k) % columns) for i in range(columns)]


def beside_layers(tiles):
    groups = lax.axis_size("layer")
    if groups == 2:
        return [held(lax.ppermute(tiles[0], "layer", [(0, 1), (1, 0)]))]
    up = [(i, i + 1) for i in range(groups - 1)]
    down = [(i + 1, i) for i in range(groups - 1)]
    return [held(lax.ppermute(tiles[0], "layer", up)), held(lax.ppermute(tiles[-1], "layer", down))]


def outside(x):
    return pltpu.with_memory_space_constraint(x, pltpu.HBM)


def on_device(
    rhs,
    areal_blocks,
    vertical_blocks,
    conn_src,
    conn_count,
    tile_map,
    well_cells,
    well_gain,
    sens,
    basis,
):
    columns = lax.axis_size("areal")
    groups = lax.axis_size("layer")
    two = groups == 2
    rows, width = rhs.shape[2:]
    modes = basis.shape[-1]
    number = conn_src.shape[-1]
    swaps = near_swaps(number)
    routes = [swap_pairs(columns, k, color) for k, color in swaps]
    routes += [shift_pairs(columns, columns // 2 + 1), shift_pairs(columns, columns // 2)]
    rhs = rhs[0].reshape(2 * rows, width)
    me = lax.axis_index("areal").astype(jnp.int32).reshape(1)
    group = lax.axis_index("layer").astype(jnp.int32).reshape(1)

    tile = pltpu.VMEM((rows, width), BF16)
    pair = pltpu.VMEM((2 * rows, width), BF16)
    sums = pltpu.VMEM((2, rows, width), F32)
    one = 2 * rows * width * width
    partial = functools.partial

    masks_type = pltpu.VMEM((8, 128), F32)
    with jax.named_scope("plan"):
        half = len(swaps) // 2
        lines = [*range(half), number - 2, number - 1]
        tables = [
            lax.ppermute(conn_src, "areal", [(to, at) for at, to in routes[i]]) for i in lines
        ]
        table, asks, payload = call(
            partial(plan_kernel, columns, swaps),
            [
                jax.ShapeDtypeStruct((2 * number,), jnp.int32),
                masks_type,
                pltpu.VMEM((2 * rows + 16, width), BF16),
            ],
            (outside(conn_src[0, 0]), conn_count[0], outside(tile_map), me, group, outside(rhs)),
            [SMEM] * 5 + [VMEM],
            out_specs=[SMEM] + [VMEM] * 2,
        )
        asks, payload = held(asks), held(payload)
        known, *crossing = call(
            partial(cross_pick_kernel, lines),
            [masks_type] + [tile] * len(lines),
            (me, outside(tile_map), *[x[0, 0] for x in tables], payload),
            [SMEM] * (2 + len(lines)) + [VMEM],
        )
        known = held(known)

    with jax.named_scope("load"):
        bands, sides = call(
            partial(load_kernel, number, two),
            [
                pltpu.VMEM((number, width, 2 * width), BF16),
                pltpu.VMEM((3 if two else 4, width, width), BF16),
            ],
            (table, group, outside(areal_blocks[0]), outside(vertical_blocks[0])),
            [SMEM] * 2 + [pl.BlockSpec(memory_space=pltpu.HBM)] * 2,
            [pltpu.SemaphoreType.DMA((2 * number + 4,))],
            moved=areal_blocks.size * 2 + vertical_blocks.size * 2,
        )
        bands, sides = held(bands), held(sides)
        (factors,) = call(
            weigh_kernel,
            [pltpu.VMEM((sens.shape[2], 2, sens.shape[3]), F32)],
            (well_cells[0], well_gain[0], sens[0].transpose(1, 0, 2)),
            [SMEM] * 2 + [VMEM],
        )
        weights = held(basis[0])
        if two:
            (weights,) = call(
                partial(turn_kernel, columns),
                [pltpu.VMEM((modes // 2, 4 * sens.shape[3]), BF16)],
                (basis[0],),
                [VMEM],
            )
        factors, weights = held(factors), held(weights)

    rhs_held = lam = held(rhs)
    sends = [*crossing[:half], *[payload] * half, *crossing[half:]]
    outer = [payload]
    for step in range(ITERS):
        first = step == 0
        with jax.named_scope("apply"):
            arrived = [moved_by(x, pairs) for x, pairs in zip(sends, routes)]
            (part,) = call(own_kernel, [sums], (lam, rhs_held, sides), [VMEM] * 3, flops=one)
            part = held(part)
            if first:
                told = [known, *arrived[half:-2]]
            beside = beside_layers(outer)
            (cross,) = call(
                cross_kernel,
                [sums],
                (asks, bands, *arrived[:half]),
                [VMEM] * (2 + half),
                flops=4 * one,
            )
            (far,) = call(
                far_kernel,
                [sums],
                (asks, bands, held(cross), *arrived[-2:]),
                [VMEM] * 5,
                flops=(64 if first else 4) * one,
            )
            tiles = (part, held(far), asks, bands, sides)
            near = (*arrived[half:-2], *beside)
            if step < ITERS - 1:
                if first:
                    (local,) = call(
                        partial(local_kernel, number, two, half),
                        [sums],
                        (asks, bands, sides, *near),
                        [VMEM] * (3 + len(near)),
                        flops=96 * one,
                    )
                    given = (part, held(far), asks, held(local))
                else:
                    given = (*tiles, *near)
                lam, *rest = call(
                    partial(update_kernel, number, two, half, first),
                    [pair] + [tile] * (number + len(beside)) + ([masks_type] if first else []),
                    (*given, *told),
                    [VMEM] * (len(given) + len(told)),
                    flops=one,
                )
                lam = held(lam)
                if first:
                    told = [held(rest.pop())]
                sends, outer = rest[:number], rest[number:]
            else:
                adjoint, pieces = call(
                    partial(last_kernel, number, two, half),
                    [
                        jax.ShapeDtypeStruct((2, rows, width), BF16),
                        pltpu.VMEM((2 * columns, modes // columns // 2, rows), BF16)
                        if two
                        else pltpu.VMEM((rows, modes), F32),
                    ],
                    (*tiles, factors, weights, *near),
                    [VMEM] * (7 + len(near)),
                    flops=one,
                )

    with jax.named_scope("project"):
        if two:
            landed = lax.all_to_all(pieces, ("areal", "layer"), 0, 0, tiled=True)
            (coefficients,) = call(
                sum_kernel,
                [jax.ShapeDtypeStruct((modes // columns, rows // 2), BF16)],
                (held(landed),),
                [VMEM],
            )
            coefficients = coefficients.T
        else:
            cut = pieces.reshape(groups, rows // groups, columns, modes // columns)
            cut = cut.transpose(2, 0, 1, 3).reshape(columns * groups, rows // groups, modes // columns)
            landed = lax.all_to_all(cut, ("areal", "layer"), 0, 0, tiled=True)
            coefficients = jnp.sum(landed, axis=0).astype(BF16)
    return (adjoint[None], coefficients)


def solution(mesh):
    in_specs = (
        P("areal", "layer", None, None),
        P("areal", "layer", None, None, None),
        P("areal", "layer", None, None, None),
        P("areal", "layer", None),
        P("areal", "layer"),
        P(),
        P("areal", "layer", None),
        P("areal", "layer", None),
        P("areal", "layer", None, None),
        P("areal", "layer", None, None),
    )
    out_specs = (P("areal", "layer", None, None), P("layer", "areal"))
    return jax.shard_map(
        on_device, mesh=mesh, in_specs=in_specs, out_specs=out_specs, check_vma=False
    )
```

```python
import functools

import jax
import jax.numpy as jnp
from jax import lax
from jax.experimental import pallas as pl
from jax.experimental.pallas import tpu as pltpu
from jax.sharding import PartitionSpec as P

ITERS = 3
F32 = jnp.float32
BF16 = jnp.bfloat16
SMEM = pl.BlockSpec(memory_space=pltpu.SMEM)
VMEM = pl.BlockSpec(memory_space=pltpu.VMEM)
LIMIT = 16 * 1024 * 1024


def near_swaps(count):
    return [(k, color) for color in (1, 0) for k in range(count // 2 - 1, 0, -1)]


def swap_pairs(columns, k, color):
    return [
        (c, (c + k if (c // k) % 2 == color else c - k) % columns) for c in range(columns)
    ]


def held(x):
    return pltpu.with_memory_space_constraint(x, pltpu.VMEM)


def dot(a, b):
    return jnp.dot(a, b, preferred_element_type=F32)


def plan_kernel(columns, swaps, src, count, tile_map, me, group, rhs, table, asks, payload):
    steps = [
        jnp.where(lax.rem(lax.div(me[0], k), 2) == color, k, columns - k) for k, color in swaps
    ] + [columns // 2 + 1, columns // 2]
    number = len(steps)
    conn = [0] * number
    slots = [0] * number
    for s in range(number):
        place = tile_map[src[s]]
        peer = lax.shift_right_logical(place, 1)
        slot = lax.bitwise_and(place, 1)
        away = peer - me[0]
        away = jnp.where(away < 0, away + columns, away)
        for i, k in enumerate(steps):
            hit = away == k
            conn[i] = jnp.where(hit, s, conn[i])
            slots[i] = jnp.where(hit, slot, slots[i])
    line = lax.broadcasted_iota(jnp.int32, asks.shape, 0)
    asked = jnp.zeros(line.shape, F32)
    for i in range(number):
        table[i] = conn[i]
        table[number + i] = jnp.where(conn[i] < count[0], 1, 0)
        asked = jnp.where(line == i, slots[i].astype(F32), asked)
    asked = jnp.where(line == number, group[0].astype(F32), asked)
    asked = jnp.where(line == number + 1, lax.rem(me[0], 2).astype(F32), asked)
    asks[...] = asked
    rows, width = rhs.shape
    payload[0:rows] = rhs[...]
    payload[rows:] = jnp.zeros((16, width), BF16)
    none = jnp.zeros(asked.shape, F32)
    payload[rows:, 0:128] = jnp.concatenate([asked, none], axis=0).astype(BF16)


def load_kernel(number, two, table, group, blocks, vert, bands, sides, sems):
    width = vert.shape[-1]
    mine = group[0]
    ends = [(1 - mine, 1 - mine)] if two else [(0, 0), (1, 1)]
    beside = [
        pltpu.make_async_copy(vert.at[d, k], sides.at[i], sems.at[2 * number + i])
        for i, (d, k) in enumerate([(0, 1), (1, 0), *ends])
    ]
    for copy in beside:
        copy.start()

    def copies(i):
        return [
            pltpu.make_async_copy(
                blocks.at[d, table[i]],
                bands.at[i, :, pl.ds(d * width, width)],
                sems.at[2 * i + d],
            )
            for d in range(2)
        ]

    for i in range(number):

        @pl.when(table[number + i] > 0)
        def _():
            for copy in copies(i):
                copy.start()

        @pl.when(table[number + i] == 0)
        def _():
            bands[i] = jnp.zeros(bands.shape[1:], bands.dtype)

    for i in range(number):

        @pl.when(table[number + i] > 0)
        def _():
            for copy in copies(i):
                copy.wait()

    for copy in beside:
        copy.wait()


def turn_kernel(columns, basis, turned):
    _, cells, modes = basis.shape
    bands = []
    for d in range(2):
        by_mode = basis[d].astype(F32).T.reshape(columns, 2, modes // columns // 2, cells)
        bands += [by_mode[:, h].reshape(modes // 2, cells) for h in range(2)]
    turned[...] = jnp.concatenate(bands, axis=1).astype(BF16)


def weigh_kernel(wells, gains, sens, factors):
    cells = sens.shape[-1]
    spot = lax.broadcasted_iota(jnp.int32, (1, cells), 1)
    factors[...] = sens[...]
    for d in range(2):
        well = jnp.zeros((1, cells), F32)
        for w in range(wells.shape[1]):
            well = well + jnp.where(spot == wells[d, w], gains[d, w], 0.0)
        factors[0, d : d + 1, :] = sens[0, d : d + 1, :] + well


def wide(mask, width):
    return jnp.concatenate([mask] * (width // mask.shape[1]), axis=1)


def chosen(mask, low, high):
    return jnp.where(wide(mask, low.shape[1]) > 0.5, high, low).astype(BF16)


def asks_of(payload):
    return payload[payload.shape[0] - 16 :, 0:128].astype(F32)


def tile_of(ref, mask, rows):
    if ref.shape[0] == rows:
        return ref[...]
    return chosen(mask, ref[0:rows].astype(F32), ref[rows : 2 * rows].astype(F32))


def cross_pick_kernel(lines, me, tile_map, *refs):
    count = len(lines)
    tables, (payload, _, known), tiles = refs[:count], refs[count : count + 3], refs[count + 3 :]
    rows = tiles[0].shape[0]
    line = lax.broadcasted_iota(jnp.int32, known.shape, 0)
    masks = jnp.zeros(known.shape, F32)
    for i, table in zip(lines, tables):
        wanted = 0
        for s in range(table.shape[-1]):
            place = tile_map[table[s]]
            peer = lax.shift_right_logical(place, 1)
            wanted = jnp.where(peer == me[0], lax.bitwise_and(place, 1), wanted)
        masks = jnp.where(line == i, wanted.astype(F32), masks)
    known[...] = masks
    low, high = payload[0:rows].astype(F32), payload[rows : 2 * rows].astype(F32)
    for i, tile in zip(lines, tiles):
        tile[...] = chosen(masks[i : i + 1, :], low, high)


def own_kernel(lam, rhs, sides, part):
    rows = rhs.shape[0] // 2
    part[0] = rhs[0:rows].astype(F32) - dot(lam[rows : 2 * rows], sides[0])
    part[1] = rhs[rows:].astype(F32) - dot(lam[0:rows], sides[1])


def source_sums(asks, bands, begin, refs, rows):
    tiles = [tile_of(ref, asks[i : i + 1, :], rows) for i, ref in enumerate(refs, begin)]
    count, width, both = len(refs), bands.shape[1], bands.shape[2]
    band = bands[begin : begin + count].reshape(count * width, both)
    sums = dot(jnp.concatenate(tiles, axis=1), band)
    return sums[:, :width], sums[:, width:]


def beside_sums(number, two, asks, sides, beside, rows):
    if two:
        mine = asks[number : number + 1, :]
        term = dot(tile_of(beside[0], mine, rows), sides[2])
        above = wide(mine, term.shape[1]) > 0.5
        none = jnp.zeros_like(term)
        return jnp.where(above, term, none), jnp.where(above, none, term)
    return [
        dot(tile_of(beside[d], jnp.full((1, 128), 1.0 - d, F32), rows), sides[2 + d])
        for d in range(2)
    ]


def cross_kernel(asks, bands, *refs):
    arrived, out = refs[:-1], refs[-1]
    out[0], out[1] = source_sums(asks, bands, 0, arrived, out.shape[1])


def far_kernel(asks, bands, cross, *refs):
    far, out = refs[:-1], refs[-1]
    low, high = source_sums(asks, bands, bands.shape[0] - len(far), far, out.shape[1])
    out[0] = cross[0] + low
    out[1] = cross[1] + high


def local_kernel(number, two, begin, asks, bands, sides, *refs):
    here = number - 2 - begin
    near, beside, out = refs[:here], refs[here:-1], refs[-1]
    rows = out.shape[1]
    sums = source_sums(asks, bands, begin, near, rows)
    terms = beside_sums(number, two, asks, sides, beside, rows)
    for d in range(2):
        out[d] = sums[d] + terms[d]


def updated(number, two, begin, part, far, asks, bands, sides, near, beside):
    rows = part.shape[1]
    sums = source_sums(asks, bands, begin, near, rows)
    terms = beside_sums(number, two, asks, sides, beside, rows)
    return [part[d] - far[d] - sums[d] - terms[d] for d in range(2)]


def update_kernel(number, two, begin, first, part, far, asks, *refs):
    ends = 1 if two else 2
    here = number - 2 - begin
    if first:
        local, refs = refs[0], refs[1:]
        low, high = [part[d] - far[d] - local[d] for d in range(2)]
    else:
        (bands, sides), refs = refs[:2], refs[2:]
        near, refs = refs[:here], refs[here:]
        beside, refs = refs[:ends], refs[ends:]
        low, high = updated(number, two, begin, part, far, asks, bands, sides, near, beside)
    count = 1 + here if first else 1
    told, refs = refs[:count], refs[count:]
    lam, sends, refs = refs[0], refs[1 : 1 + number], refs[1 + number :]
    outer, refs = refs[:ends], refs[ends:]
    masks = told[0]
    if first:
        masks = refs[0]
        masks[...] = told[0][...]
        for i, ref in enumerate(told[1:], begin):
            masks[i : i + 1, :] = asks_of(ref)[i : i + 1, :]
    rows = low.shape[0]
    lam[0:rows] = low.astype(BF16)
    lam[rows:] = high.astype(BF16)
    for i, send in enumerate(sends):
        send[...] = chosen(masks[i : i + 1, :], low, high)
    if two:
        outer[0][...] = chosen(asks[number : number + 1, :], high, low)
    else:
        outer[0][...] = high.astype(BF16)
        outer[1][...] = low.astype(BF16)


def last_kernel(number, two, begin, part, far, asks, bands, sides, factors, basis, *refs):
    here = number - 2 - begin
    near, beside, (lam, pieces) = refs[:here], refs[here:-2], refs[-2:]
    sums = updated(number, two, begin, part, far, asks, bands, sides, near, beside)
    phases, _, cells = factors.shape
    grads = []
    for d in range(2):
        rounded = sums[d].astype(BF16)
        lam[d] = rounded
        back = rounded.astype(F32)
        grad = back[:, :cells] * factors[0, d : d + 1, :]
        for p in range(1, phases):
            grad = grad + back[:, p * cells : (p + 1) * cells] * factors[p, d : d + 1, :]
        grads.append(grad)
    if two:
        half = grads[0].shape[0] // 2
        none = jnp.zeros((half, cells), F32)
        band = pieces.shape[1]
        for g in range(2):
            cuts = [grad[g * half : (g + 1) * half] for grad in grads]
            top = jnp.concatenate([x for cut in cuts for x in (cut, none)], axis=1)
            low = jnp.concatenate([x for cut in cuts for x in (none, cut)], axis=1)
            wing = jnp.concatenate([top, low], axis=0).astype(BF16)
            share = lax.dot_general(
                basis[...], wing, (((1,), (1,)), ((), ())), preferred_element_type=F32
            )
            for c in range(pieces.shape[0] // 2):
                pieces[2 * c + g] = share[c * band : (c + 1) * band].astype(BF16)
    else:
        terms = [dot(grad.astype(BF16), basis[d]) for d, grad in enumerate(grads)]
        pieces[...] = terms[0] + terms[1]


def sum_kernel(pieces, out):
    total = pieces[0].astype(F32)
    for i in range(1, pieces.shape[0]):
        total = total + pieces[i].astype(F32)
    half = total.shape[1] // 2
    out[...] = jnp.concatenate([total[:, :half], total[:, half:]], axis=0).astype(BF16)


def call(kernel, outs, ins, specs, scratch=(), flops=0, moved=0, out_specs=None):
    return pl.pallas_call(
        kernel,
        out_shape=outs,
        in_specs=specs,
        out_specs=out_specs or [VMEM] * len(outs),
        scratch_shapes=list(scratch),
        compiler_params=pltpu.CompilerParams(vmem_limit_bytes=LIMIT),
        cost_estimate=pl.CostEstimate(
            flops=flops, bytes_accessed=moved or flops // 200, transcendentals=0
        ),
    )(*ins)


def moved_by(x, pairs):
    return held(lax.ppermute(x, "areal", pairs))


def shift_pairs(columns, k):
    return [(i, (i - k) % columns) for i in range(columns)]


def beside_layers(tiles):
    groups = lax.axis_size("layer")
    if groups == 2:
        return [held(lax.ppermute(tiles[0], "layer", [(0, 1), (1, 0)]))]
    up = [(i, i + 1) for i in range(groups - 1)]
    down = [(i + 1, i) for i in range(groups - 1)]
    return [held(lax.ppermute(tiles[0], "layer", up)), held(lax.ppermute(tiles[-1], "layer", down))]


def outside(x):
    return pltpu.with_memory_space_constraint(x, pltpu.HBM)


def on_device(
    rhs,
    areal_blocks,
    vertical_blocks,
    conn_src,
    conn_count,
    tile_map,
    well_cells,
    well_gain,
    sens,
    basis,
):
    columns = lax.axis_size("areal")
    groups = lax.axis_size("layer")
    two = groups == 2
    rows, width = rhs.shape[2:]
    modes = basis.shape[-1]
    number = conn_src.shape[-1]
    swaps = near_swaps(number)
    routes = [swap_pairs(columns, k, color) for k, color in swaps]
    routes += [shift_pairs(columns, columns // 2 + 1), shift_pairs(columns, columns // 2)]
    rhs = rhs[0].reshape(2 * rows, width)
    me = lax.axis_index("areal").astype(jnp.int32).reshape(1)
    group = lax.axis_index("layer").astype(jnp.int32).reshape(1)

    tile = pltpu.VMEM((rows, width), BF16)
    pair = pltpu.VMEM((2 * rows, width), BF16)
    sums = pltpu.VMEM((2, rows, width), F32)
    one = 2 * rows * width * width
    partial = functools.partial

    masks_type = pltpu.VMEM((8, 128), F32)
    with jax.named_scope("plan"):
        half = len(swaps) // 2
        lines = [*range(half), number - 2, number - 1]
        tables = [
            lax.ppermute(conn_src, "areal", [(to, at) for at, to in routes[i]]) for i in lines
        ]
        table, asks, payload = call(
            partial(plan_kernel, columns, swaps),
            [
                jax.ShapeDtypeStruct((2 * number,), jnp.int32),
                masks_type,
                pltpu.VMEM((2 * rows + 16, width), BF16),
            ],
            (outside(conn_src[0, 0]), conn_count[0], outside(tile_map), me, group, outside(rhs)),
            [SMEM] * 5 + [VMEM],
            out_specs=[SMEM] + [VMEM] * 2,
        )
        asks, payload = held(asks), held(payload)

    with jax.named_scope("load"):
        bands, sides = call(
            partial(load_kernel, number, two),
            [
                pltpu.VMEM((number, width, 2 * width), BF16),
                pltpu.VMEM((3 if two else 4, width, width), BF16),
            ],
            (table, group, outside(areal_blocks[0]), outside(vertical_blocks[0])),
            [SMEM] * 2 + [pl.BlockSpec(memory_space=pltpu.HBM)] * 2,
            [pltpu.SemaphoreType.DMA((2 * number + 4,))],
            moved=areal_blocks.size * 2 + vertical_blocks.size * 2,
        )
        bands, sides = held(bands), held(sides)
        known, *crossing = call(
            partial(cross_pick_kernel, lines),
            [masks_type] + [tile] * len(lines),
            (me, outside(tile_map), *[x[0, 0] for x in tables], payload, sides),
            [SMEM] * (2 + len(lines)) + [VMEM] * 2,
        )
        known = held(known)
        (factors,) = call(
            weigh_kernel,
            [pltpu.VMEM((sens.shape[2], 2, sens.shape[3]), F32)],
            (well_cells[0], well_gain[0], sens[0].transpose(1, 0, 2)),
            [SMEM] * 2 + [VMEM],
        )
        weights = held(basis[0])
        if two:
            (weights,) = call(
                partial(turn_kernel, columns),
                [pltpu.VMEM((modes // 2, 4 * sens.shape[3]), BF16)],
                (basis[0],),
                [VMEM],
            )
        factors, weights = held(factors), held(weights)

    rhs_held = lam = held(rhs)
    sends = [*crossing[:half], *[payload] * half, *crossing[half:]]
    outer = [payload]
    for step in range(ITERS):
        first = step == 0
        with jax.named_scope("apply"):
            arrived = [moved_by(x, pairs) for x, pairs in zip(sends, routes)]
            (part,) = call(own_kernel, [sums], (lam, rhs_held, sides), [VMEM] * 3, flops=one)
            part = held(part)
            if first:
                told = [known, *arrived[half:-2]]
            beside = beside_layers(outer)
            (cross,) = call(
                cross_kernel,
                [sums],
                (asks, bands, *arrived[:half]),
                [VMEM] * (2 + half),
                flops=4 * one,
            )
            (far,) = call(
                far_kernel,
                [sums],
                (asks, bands, held(cross), *arrived[-2:]),
                [VMEM] * 5,
                flops=(64 if first else 4) * one,
            )
            tiles = (part, held(far), asks, bands, sides)
            near = (*arrived[half:-2], *beside)
            if step < ITERS - 1:
                if first:
                    (local,) = call(
                        partial(local_kernel, number, two, half),
                        [sums],
                        (asks, bands, sides, *near),
                        [VMEM] * (3 + len(near)),
                        flops=96 * one,
                    )
                    given = (part, held(far), asks, held(local))
                else:
                    given = (*tiles, *near)
                lam, *rest = call(
                    partial(update_kernel, number, two, half, first),
                    [pair] + [tile] * (number + len(beside)) + ([masks_type] if first else []),
                    (*given, *told),
                    [VMEM] * (len(given) + len(told)),
                    flops=one,
                )
                lam = held(lam)
                if first:
                    told = [held(rest.pop())]
                sends, outer = rest[:number], rest[number:]
            else:
                adjoint, pieces = call(
                    partial(last_kernel, number, two, half),
                    [
                        jax.ShapeDtypeStruct((2, rows, width), BF16),
                        pltpu.VMEM((2 * columns, modes // columns // 2, rows), BF16)
                        if two
                        else pltpu.VMEM((rows, modes), F32),
                    ],
                    (*tiles, factors, weights, *near),
                    [VMEM] * (7 + len(near)),
                    flops=one,
                )

    with jax.named_scope("project"):
        if two:
            landed = lax.all_to_all(pieces, ("areal", "layer"), 0, 0, tiled=True)
            (coefficients,) = call(
                sum_kernel,
                [jax.ShapeDtypeStruct((modes // columns, rows // 2), BF16)],
                (held(landed),),
                [VMEM],
            )
            coefficients = coefficients.T
        else:
            cut = pieces.reshape(groups, rows // groups, columns, modes // columns)
            cut = cut.transpose(2, 0, 1, 3).reshape(columns * groups, rows // groups, modes // columns)
            landed = lax.all_to_all(cut, ("areal", "layer"), 0, 0, tiled=True)
            coefficients = jnp.sum(landed, axis=0).astype(BF16)
    return (adjoint[None], coefficients)


def solution(mesh):
    in_specs = (
        P("areal", "layer", None, None),
        P("areal", "layer", None, None, None),
        P("areal", "layer", None, None, None),
        P("areal", "layer", None),
        P("areal", "layer"),
        P(),
        P("areal", "layer", None),
        P("areal", "layer", None),
        P("areal", "layer", None, None),
        P("areal", "layer", None, None),
    )
    out_specs = (P("areal", "layer", None, None), P("layer", "areal"))
    return jax.shard_map(
        on_device, mesh=mesh, in_specs=in_specs, out_specs=out_specs, check_vma=False
    )
```

```python
import functools

import jax
import jax.numpy as jnp
from jax import lax
from jax.experimental import pallas as pl
from jax.experimental.pallas import tpu as pltpu
from jax.sharding import PartitionSpec as P

ITERS = 3
F32 = jnp.float32
BF16 = jnp.bfloat16
SMEM = pl.BlockSpec(memory_space=pltpu.SMEM)
VMEM = pl.BlockSpec(memory_space=pltpu.VMEM)
LIMIT = 16 * 1024 * 1024


def near_swaps(count):
    return [(k, color) for color in (1, 0) for k in range(count // 2 - 1, 0, -1)]


def swap_pairs(columns, k, color):
    return [
        (c, (c + k if (c // k) % 2 == color else c - k) % columns) for c in range(columns)
    ]


def held(x):
    return pltpu.with_memory_space_constraint(x, pltpu.VMEM)


def dot(a, b):
    return jnp.dot(a, b, preferred_element_type=F32)


def plan_kernel(columns, swaps, src, count, tile_map, me, group, rhs, table, asks, payload, pair):
    steps = [
        jnp.where(lax.rem(lax.div(me[0], k), 2) == color, k, columns - k) for k, color in swaps
    ] + [columns // 2 + 1, columns // 2]
    number = len(steps)
    conn = [0] * number
    slots = [0] * number
    for s in range(number):
        place = tile_map[src[s]]
        peer = lax.shift_right_logical(place, 1)
        slot = lax.bitwise_and(place, 1)
        away = peer - me[0]
        away = jnp.where(away < 0, away + columns, away)
        for i, k in enumerate(steps):
            hit = away == k
            conn[i] = jnp.where(hit, s, conn[i])
            slots[i] = jnp.where(hit, slot, slots[i])
    rows, width = rhs.shape
    line = lax.broadcasted_iota(jnp.int32, (16, width), 0)
    asked = jnp.zeros(line.shape, F32)
    for i in range(number):
        table[i] = conn[i]
        table[number + i] = jnp.where(conn[i] < count[0], 1, 0)
        asked = jnp.where(line == i, slots[i].astype(F32), asked)
    asked = jnp.where(line == number, group[0].astype(F32), asked)
    asked = jnp.where(line == number + 1, lax.rem(me[0], 2).astype(F32), asked)
    asks[...] = asked[0:8, 0:128]
    payload[0:rows] = rhs[...]
    payload[rows:] = asked.astype(BF16)
    pair[...] = rhs[...]


def load_kernel(number, two, table, group, blocks, vert, bands, sides, sems):
    width = vert.shape[-1]
    mine = group[0]
    ends = [(1 - mine, 1 - mine)] if two else [(0, 0), (1, 1)]
    beside = [
        pltpu.make_async_copy(vert.at[d, k], sides.at[i], sems.at[2 * number + i])
        for i, (d, k) in enumerate([(0, 1), (1, 0), *ends])
    ]
    for copy in beside:
        copy.start()

    def copies(i):
        return [
            pltpu.make_async_copy(
                blocks.at[d, table[i]],
                bands.at[i, :, pl.ds(d * width, width)],
                sems.at[2 * i + d],
            )
            for d in range(2)
        ]

    for i in range(number):

        @pl.when(table[number + i] > 0)
        def _():
            for copy in copies(i):
                copy.start()

        @pl.when(table[number + i] == 0)
        def _():
            bands[i] = jnp.zeros(bands.shape[1:], bands.dtype)

    for i in range(number):

        @pl.when(table[number + i] > 0)
        def _():
            for copy in copies(i):
                copy.wait()

    for copy in beside:
        copy.wait()


def turn_kernel(columns, basis, turned):
    _, cells, modes = basis.shape
    bands = []
    for d in range(2):
        by_mode = basis[d].astype(F32).T.reshape(columns, 2, modes // columns // 2, cells)
        bands += [by_mode[:, h].reshape(modes // 2, cells) for h in range(2)]
    turned[...] = jnp.concatenate(bands, axis=1).astype(BF16)


def weigh_kernel(wells, gains, sens, factors):
    cells = sens.shape[-1]
    spot = lax.broadcasted_iota(jnp.int32, (1, cells), 1)
    factors[...] = sens[...]
    for d in range(2):
        well = jnp.zeros((1, cells), F32)
        for w in range(wells.shape[1]):
            well = well + jnp.where(spot == wells[d, w], gains[d, w], 0.0)
        factors[0, d : d + 1, :] = sens[0, d : d + 1, :] + well


def wide(mask, width):
    return jnp.concatenate([mask] * (width // mask.shape[1]), axis=1)


def chosen(mask, low, high):
    return jnp.where(wide(mask, low.shape[1]) > 0.5, high, low).astype(BF16)


def asks_of(payload):
    return payload[payload.shape[0] - 16 :, 0:128].astype(F32)


def tile_of(ref, mask, rows):
    if ref.shape[0] == rows:
        return ref[...]
    return chosen(mask, ref[0:rows].astype(F32), ref[rows : 2 * rows].astype(F32))


def relay_ask_kernel(number, even, odd, asks, relayed):
    parity = asks[number + 1 : number + 2, :]
    ask = [asks_of(ref)[number - 2 : number - 1, :] for ref in (even, odd)]
    relayed[...] = asks[...]
    relayed[number - 2 : number - 1, :] = jnp.where(parity > 0.5, ask[1], ask[0])


def far_pick_kernel(number, pair, relayed, part, tile):
    tile[...] = tile_of(pair, relayed[number - 2 : number - 1, :], tile.shape[0])


def own_kernel(lam, rhs, sides, part):
    rows = rhs.shape[0] // 2
    part[0] = rhs[0:rows].astype(F32) - dot(lam[rows : 2 * rows], sides[0])
    part[1] = rhs[rows:].astype(F32) - dot(lam[0:rows], sides[1])


def source_sums(asks, bands, begin, refs, rows):
    tiles = [tile_of(ref, asks[i : i + 1, :], rows) for i, ref in enumerate(refs, begin)]
    count, width, both = len(refs), bands.shape[1], bands.shape[2]
    band = bands[begin : begin + count].reshape(count * width, both)
    sums = dot(jnp.concatenate(tiles, axis=1), band)
    return sums[:, :width], sums[:, width:]


def beside_sums(number, two, asks, sides, beside, rows):
    if two:
        mine = asks[number : number + 1, :]
        term = dot(tile_of(beside[0], mine, rows), sides[2])
        above = wide(mine, term.shape[1]) > 0.5
        none = jnp.zeros_like(term)
        return jnp.where(above, term, none), jnp.where(above, none, term)
    return [
        dot(tile_of(beside[d], jnp.full((1, 128), 1.0 - d, F32), rows), sides[2 + d])
        for d in range(2)
    ]


def cross_kernel(asks, bands, *refs):
    arrived, out = refs[:-1], refs[-1]
    out[0], out[1] = source_sums(asks, bands, 0, arrived, out.shape[1])


def nearer_kernel(asks, bands, pair, out):
    out[0], out[1] = source_sums(asks, bands, bands.shape[0] - 1, [pair], out.shape[1])


def farther_kernel(asks, bands, cross, nearer, passed, out):
    sums = source_sums(asks, bands, bands.shape[0] - 2, [passed], out.shape[1])
    for d in range(2):
        out[d] = cross[d] + nearer[d] + sums[d]


def far_kernel(asks, bands, cross, *refs):
    far, out = refs[:-1], refs[-1]
    low, high = source_sums(asks, bands, bands.shape[0] - len(far), far, out.shape[1])
    out[0] = cross[0] + low
    out[1] = cross[1] + high


def updated(number, two, begin, part, far, asks, bands, sides, near, beside):
    rows = part.shape[1]
    sums = source_sums(asks, bands, begin, near, rows)
    terms = beside_sums(number, two, asks, sides, beside, rows)
    return [part[d] - far[d] - sums[d] - terms[d] for d in range(2)]


def update_kernel(number, two, begin, first, part, far, asks, bands, sides, *refs):
    ends = 1 if two else 2
    here = number - 2 - begin
    near, refs = refs[:here], refs[here:]
    beside, refs = refs[:ends], refs[ends:]
    count = number - 1 if first else 1
    told, refs = refs[:count], refs[count:]
    low, high = updated(number, two, begin, part, far, asks, bands, sides, near, beside)
    lam, sends, refs = refs[0], refs[1 : 1 + number], refs[1 + number :]
    outer, refs = refs[:ends], refs[ends:]
    masks = told[0]
    if first:
        masks = refs[0]
        masks[...] = told[-1][...]
        for i in range(number - 2):
            masks[i : i + 1, :] = asks_of(told[i])[i : i + 1, :]
    rows = low.shape[0]
    lam[0:rows] = low.astype(BF16)
    lam[rows:] = high.astype(BF16)
    for i, send in enumerate(sends):
        send[...] = chosen(masks[i : i + 1, :], low, high)
    if two:
        outer[0][...] = chosen(asks[number : number + 1, :], high, low)
    else:
        outer[0][...] = high.astype(BF16)
        outer[1][...] = low.astype(BF16)


def last_kernel(number, two, begin, part, far, asks, bands, sides, factors, basis, *refs):
    here = number - 2 - begin
    near, beside, (lam, pieces) = refs[:here], refs[here:-2], refs[-2:]
    sums = updated(number, two, begin, part, far, asks, bands, sides, near, beside)
    phases, _, cells = factors.shape
    grads = []
    for d in range(2):
        rounded = sums[d].astype(BF16)
        lam[d] = rounded
        back = rounded.astype(F32)
        grad = back[:, :cells] * factors[0, d : d + 1, :]
        for p in range(1, phases):
            grad = grad + back[:, p * cells : (p + 1) * cells] * factors[p, d : d + 1, :]
        grads.append(grad)
    if two:
        half = grads[0].shape[0] // 2
        none = jnp.zeros((half, cells), F32)
        band = pieces.shape[1]
        for g in range(2):
            cuts = [grad[g * half : (g + 1) * half] for grad in grads]
            top = jnp.concatenate([x for cut in cuts for x in (cut, none)], axis=1)
            low = jnp.concatenate([x for cut in cuts for x in (none, cut)], axis=1)
            wing = jnp.concatenate([top, low], axis=0).astype(BF16)
            share = lax.dot_general(
                basis[...], wing, (((1,), (1,)), ((), ())), preferred_element_type=F32
            )
            for c in range(pieces.shape[0] // 2):
                pieces[2 * c + g] = share[c * band : (c + 1) * band].astype(BF16)
    else:
        terms = [dot(grad.astype(BF16), basis[d]) for d, grad in enumerate(grads)]
        pieces[...] = terms[0] + terms[1]


def sum_kernel(pieces, out):
    total = pieces[0].astype(F32)
    for i in range(1, pieces.shape[0]):
        total = total + pieces[i].astype(F32)
    half = total.shape[1] // 2
    out[...] = jnp.concatenate([total[:, :half], total[:, half:]], axis=0).astype(BF16)


def call(kernel, outs, ins, specs, scratch=(), flops=0, moved=0, out_specs=None):
    return pl.pallas_call(
        kernel,
        out_shape=outs,
        in_specs=specs,
        out_specs=out_specs or [VMEM] * len(outs),
        scratch_shapes=list(scratch),
        compiler_params=pltpu.CompilerParams(vmem_limit_bytes=LIMIT),
        cost_estimate=pl.CostEstimate(
            flops=flops, bytes_accessed=moved or flops // 200, transcendentals=0
        ),
    )(*ins)


def moved_by(x, pairs):
    return held(lax.ppermute(x, "areal", pairs))


def shift_pairs(columns, k):
    return [(i, (i - k) % columns) for i in range(columns)]


def beside_layers(tiles):
    groups = lax.axis_size("layer")
    if groups == 2:
        return [held(lax.ppermute(tiles[0], "layer", [(0, 1), (1, 0)]))]
    up = [(i, i + 1) for i in range(groups - 1)]
    down = [(i + 1, i) for i in range(groups - 1)]
    return [held(lax.ppermute(tiles[0], "layer", up)), held(lax.ppermute(tiles[-1], "layer", down))]


def outside(x):
    return pltpu.with_memory_space_constraint(x, pltpu.HBM)


def on_device(
    rhs,
    areal_blocks,
    vertical_blocks,
    conn_src,
    conn_count,
    tile_map,
    well_cells,
    well_gain,
    sens,
    basis,
):
    columns = lax.axis_size("areal")
    groups = lax.axis_size("layer")
    two = groups == 2
    rows, width = rhs.shape[2:]
    modes = basis.shape[-1]
    number = conn_src.shape[-1]
    swaps = near_swaps(number)
    routes = [swap_pairs(columns, k, color) for k, color in swaps]
    routes += [shift_pairs(columns, columns // 2 + 1), shift_pairs(columns, columns // 2)]
    rhs = rhs[0].reshape(2 * rows, width)
    me = lax.axis_index("areal").astype(jnp.int32).reshape(1)
    group = lax.axis_index("layer").astype(jnp.int32).reshape(1)

    tile = pltpu.VMEM((rows, width), BF16)
    pair = pltpu.VMEM((2 * rows, width), BF16)
    sums = pltpu.VMEM((2, rows, width), F32)
    one = 2 * rows * width * width
    partial = functools.partial

    masks_type = pltpu.VMEM((8, 128), F32)
    with jax.named_scope("plan"):
        table, asks, payload, both = call(
            partial(plan_kernel, columns, swaps),
            [
                jax.ShapeDtypeStruct((2 * number,), jnp.int32),
                masks_type,
                pltpu.VMEM((2 * rows + 16, width), BF16),
                pair,
            ],
            (outside(conn_src[0, 0]), conn_count[0], outside(tile_map), me, group, outside(rhs)),
            [SMEM] * 5 + [VMEM],
            out_specs=[SMEM] + [VMEM] * 3,
        )
        asks, payload, both = held(asks), held(payload), held(both)
        far_pair = moved_by(both, routes[-1])

    with jax.named_scope("load"):
        bands, sides = call(
            partial(load_kernel, number, two),
            [
                pltpu.VMEM((number, width, 2 * width), BF16),
                pltpu.VMEM((3 if two else 4, width, width), BF16),
            ],
            (table, group, outside(areal_blocks[0]), outside(vertical_blocks[0])),
            [SMEM] * 2 + [pl.BlockSpec(memory_space=pltpu.HBM)] * 2,
            [pltpu.SemaphoreType.DMA((2 * number + 4,))],
            moved=areal_blocks.size * 2 + vertical_blocks.size * 2,
        )
        bands, sides = held(bands), held(sides)
        (factors,) = call(
            weigh_kernel,
            [pltpu.VMEM((sens.shape[2], 2, sens.shape[3]), F32)],
            (well_cells[0], well_gain[0], sens[0].transpose(1, 0, 2)),
            [SMEM] * 2 + [VMEM],
        )
        weights = held(basis[0])
        if two:
            (weights,) = call(
                partial(turn_kernel, columns),
                [pltpu.VMEM((modes // 2, 4 * sens.shape[3]), BF16)],
                (basis[0],),
                [VMEM],
            )
        factors, weights = held(factors), held(weights)

    rhs_held = lam = both
    sends = [payload] * (number - 2)
    outer = [payload]
    half = len(swaps) // 2
    for step in range(ITERS):
        first = step == 0
        with jax.named_scope("apply"):
            arrived = [moved_by(x, pairs) for x, pairs in zip(sends, routes)]
            (part,) = call(own_kernel, [sums], (lam, rhs_held, sides), [VMEM] * 3, flops=one)
            part = held(part)
            if first:
                even, odd = (arrived[swaps.index((1, color))] for color in (1, 0))
                (relayed,) = call(
                    partial(relay_ask_kernel, number),
                    [masks_type],
                    (even, odd, asks),
                    [VMEM] * 3,
                    flops=4 * one,
                )
                relayed = held(relayed)
                (picked,) = call(
                    partial(far_pick_kernel, number),
                    [tile],
                    (far_pair, relayed, part),
                    [VMEM] * 3,
                )
                arrived = [*arrived, moved_by(picked, shift_pairs(columns, 1)), far_pair]
                told = [*arrived[:-2], moved_by(relayed, routes[-1])]
            beside = beside_layers(outer)
            (cross,) = call(
                cross_kernel,
                [sums],
                (asks, bands, *arrived[:half]),
                [VMEM] * (2 + half),
                flops=4 * one,
            )
            if first:
                (far,) = call(
                    far_kernel,
                    [sums],
                    (asks, bands, held(cross), *arrived[-2:]),
                    [VMEM] * 5,
                    flops=4 * one,
                )
            else:
                (nearer,) = call(
                    nearer_kernel,
                    [sums],
                    (asks, bands, arrived[-1]),
                    [VMEM] * 3,
                    flops=64 * one,
                )
                (far,) = call(
                    farther_kernel,
                    [sums],
                    (asks, bands, held(cross), held(nearer), arrived[-2]),
                    [VMEM] * 5,
                    flops=4 * one,
                )
            tiles = (part, held(far), asks, bands, sides)
            near = (*arrived[half:-2], *beside)
            if step < ITERS - 1:
                lam, *rest = call(
                    partial(update_kernel, number, two, half, first),
                    [pair] + [tile] * (number + len(beside)) + ([masks_type] if first else []),
                    (*tiles, *near, *told),
                    [VMEM] * (5 + len(near) + len(told)),
                    flops=one,
                )
                lam = held(lam)
                if first:
                    told = [held(rest.pop())]
                sends, outer = rest[:number], rest[number:]
            else:
                adjoint, pieces = call(
                    partial(last_kernel, number, two, half),
                    [
                        jax.ShapeDtypeStruct((2, rows, width), BF16),
                        pltpu.VMEM((2 * columns, modes // columns // 2, rows), BF16)
                        if two
                        else pltpu.VMEM((rows, modes), F32),
                    ],
                    (*tiles, factors, weights, *near),
                    [VMEM] * (7 + len(near)),
                    flops=one,
                )

    with jax.named_scope("project"):
        if two:
            landed = lax.all_to_all(pieces, ("areal", "layer"), 0, 0, tiled=True)
            (coefficients,) = call(
                sum_kernel,
                [jax.ShapeDtypeStruct((modes // columns, rows // 2), BF16)],
                (held(landed),),
                [VMEM],
            )
            coefficients = coefficients.T
        else:
            cut = pieces.reshape(groups, rows // groups, columns, modes // columns)
            cut = cut.transpose(2, 0, 1, 3).reshape(columns * groups, rows // groups, modes // columns)
            landed = lax.all_to_all(cut, ("areal", "layer"), 0, 0, tiled=True)
            coefficients = jnp.sum(landed, axis=0).astype(BF16)
    return (adjoint[None], coefficients)


def solution(mesh):
    in_specs = (
        P("areal", "layer", None, None),
        P("areal", "layer", None, None, None),
        P("areal", "layer", None, None, None),
        P("areal", "layer", None),
        P("areal", "layer"),
        P(),
        P("areal", "layer", None),
        P("areal", "layer", None),
        P("areal", "layer", None, None),
        P("areal", "layer", None, None),
    )
    out_specs = (P("areal", "layer", None, None), P("layer", "areal"))
    return jax.shard_map(
        on_device, mesh=mesh, in_specs=in_specs, out_specs=out_specs, check_vma=False
    )
```

```python
import functools

import jax
import jax.numpy as jnp
from jax import lax
from jax.experimental import pallas as pl
from jax.experimental.pallas import tpu as pltpu
from jax.sharding import PartitionSpec as P

ITERS = 3
F32 = jnp.float32
BF16 = jnp.bfloat16
SMEM = pl.BlockSpec(memory_space=pltpu.SMEM)
VMEM = pl.BlockSpec(memory_space=pltpu.VMEM)
LIMIT = 16 * 1024 * 1024


def near_swaps(count):
    return [(k, color) for color in (1, 0) for k in range(count // 2 - 1, 0, -1)]


def swap_pairs(columns, k, color):
    return [
        (c, (c + k if (c // k) % 2 == color else c - k) % columns) for c in range(columns)
    ]


def held(x):
    return pltpu.with_memory_space_constraint(x, pltpu.VMEM)


def dot(a, b):
    return jnp.dot(a, b, preferred_element_type=F32)


def plan_kernel(columns, swaps, src, count, tile_map, me, group, rhs, table, asks, payload, pair):
    steps = [
        jnp.where(lax.rem(lax.div(me[0], k), 2) == color, k, columns - k) for k, color in swaps
    ] + [columns // 2 + 1, columns // 2]
    number = len(steps)
    conn = [0] * number
    slots = [0] * number
    for s in range(number):
        place = tile_map[src[s]]
        peer = lax.shift_right_logical(place, 1)
        slot = lax.bitwise_and(place, 1)
        away = peer - me[0]
        away = jnp.where(away < 0, away + columns, away)
        for i, k in enumerate(steps):
            hit = away == k
            conn[i] = jnp.where(hit, s, conn[i])
            slots[i] = jnp.where(hit, slot, slots[i])
    rows, width = rhs.shape
    line = lax.broadcasted_iota(jnp.int32, (16, width), 0)
    asked = jnp.zeros(line.shape, F32)
    for i in range(number):
        table[i] = conn[i]
        table[number + i] = jnp.where(conn[i] < count[0], 1, 0)
        asked = jnp.where(line == i, slots[i].astype(F32), asked)
    asked = jnp.where(line == number, group[0].astype(F32), asked)
    asked = jnp.where(line == number + 1, lax.rem(me[0], 2).astype(F32), asked)
    asks[...] = asked[0:8, 0:128]
    payload[0:rows] = rhs[...]
    payload[rows:] = asked.astype(BF16)
    pair[...] = rhs[...]


def load_kernel(number, two, table, group, blocks, vert, bands, sides, sems):
    width = vert.shape[-1]
    mine = group[0]
    ends = [(1 - mine, 1 - mine)] if two else [(0, 0), (1, 1)]
    beside = [
        pltpu.make_async_copy(vert.at[d, k], sides.at[i], sems.at[2 * number + i])
        for i, (d, k) in enumerate([(0, 1), (1, 0), *ends])
    ]
    for copy in beside:
        copy.start()

    def copies(i):
        return [
            pltpu.make_async_copy(
                blocks.at[d, table[i]],
                bands.at[i, :, pl.ds(d * width, width)],
                sems.at[2 * i + d],
            )
            for d in range(2)
        ]

    for i in range(number):

        @pl.when(table[number + i] > 0)
        def _():
            for copy in copies(i):
                copy.start()

        @pl.when(table[number + i] == 0)
        def _():
            bands[i] = jnp.zeros(bands.shape[1:], bands.dtype)

    for i in range(number):

        @pl.when(table[number + i] > 0)
        def _():
            for copy in copies(i):
                copy.wait()

    for copy in beside:
        copy.wait()


def turn_kernel(columns, basis, turned):
    _, cells, modes = basis.shape
    bands = []
    for d in range(2):
        by_mode = basis[d].astype(F32).T.reshape(columns, 2, modes // columns // 2, cells)
        bands += [by_mode[:, h].reshape(modes // 2, cells) for h in range(2)]
    turned[...] = jnp.concatenate(bands, axis=1).astype(BF16)


def weigh_kernel(wells, gains, sens, factors):
    cells = sens.shape[-1]
    spot = lax.broadcasted_iota(jnp.int32, (1, cells), 1)
    factors[...] = sens[...]
    for d in range(2):
        well = jnp.zeros((1, cells), F32)
        for w in range(wells.shape[1]):
            well = well + jnp.where(spot == wells[d, w], gains[d, w], 0.0)
        factors[0, d : d + 1, :] = sens[0, d : d + 1, :] + well


def wide(mask, width):
    return jnp.concatenate([mask] * (width // mask.shape[1]), axis=1)


def chosen(mask, low, high):
    return jnp.where(wide(mask, low.shape[1]) > 0.5, high, low).astype(BF16)


def asks_of(payload):
    return payload[payload.shape[0] - 16 :, 0:128].astype(F32)


def tile_of(ref, mask, rows):
    if ref.shape[0] == rows:
        return ref[...]
    return chosen(mask, ref[0:rows].astype(F32), ref[rows : 2 * rows].astype(F32))


def relay_ask_kernel(number, even, odd, asks, relayed):
    parity = asks[number + 1 : number + 2, :]
    ask = [asks_of(ref)[number - 2 : number - 1, :] for ref in (even, odd)]
    relayed[...] = asks[...]
    relayed[number - 2 : number - 1, :] = jnp.where(parity > 0.5, ask[1], ask[0])


def far_pick_kernel(number, pair, relayed, part, factors, weights, tile):
    tile[...] = tile_of(pair, relayed[number - 2 : number - 1, :], tile.shape[0])


def own_kernel(lam, rhs, sides, part):
    rows = rhs.shape[0] // 2
    part[0] = rhs[0:rows].astype(F32) - dot(lam[rows : 2 * rows], sides[0])
    part[1] = rhs[rows:].astype(F32) - dot(lam[0:rows], sides[1])


def source_sums(asks, bands, begin, refs, rows):
    tiles = [tile_of(ref, asks[i : i + 1, :], rows) for i, ref in enumerate(refs, begin)]
    count, width, both = len(refs), bands.shape[1], bands.shape[2]
    band = bands[begin : begin + count].reshape(count * width, both)
    sums = dot(jnp.concatenate(tiles, axis=1), band)
    return sums[:, :width], sums[:, width:]


def beside_sums(number, two, asks, sides, beside, rows):
    if two:
        mine = asks[number : number + 1, :]
        term = dot(tile_of(beside[0], mine, rows), sides[2])
        above = wide(mine, term.shape[1]) > 0.5
        none = jnp.zeros_like(term)
        return jnp.where(above, term, none), jnp.where(above, none, term)
    return [
        dot(tile_of(beside[d], jnp.full((1, 128), 1.0 - d, F32), rows), sides[2 + d])
        for d in range(2)
    ]


def cross_kernel(asks, bands, *refs):
    arrived, out = refs[:-1], refs[-1]
    out[0], out[1] = source_sums(asks, bands, 0, arrived, out.shape[1])


def nearer_kernel(asks, bands, pair, out):
    out[0], out[1] = source_sums(asks, bands, bands.shape[0] - 1, [pair], out.shape[1])


def farther_kernel(asks, bands, cross, nearer, passed, out):
    sums = source_sums(asks, bands, bands.shape[0] - 2, [passed], out.shape[1])
    for d in range(2):
        out[d] = cross[d] + nearer[d] + sums[d]


def far_kernel(asks, bands, cross, *refs):
    far, out = refs[:-1], refs[-1]
    low, high = source_sums(asks, bands, bands.shape[0] - len(far), far, out.shape[1])
    out[0] = cross[0] + low
    out[1] = cross[1] + high


def updated(number, two, begin, part, far, asks, bands, sides, near, beside):
    rows = part.shape[1]
    sums = source_sums(asks, bands, begin, near, rows)
    terms = beside_sums(number, two, asks, sides, beside, rows)
    return [part[d] - far[d] - sums[d] - terms[d] for d in range(2)]


def update_kernel(number, two, begin, first, part, far, asks, bands, sides, *refs):
    ends = 1 if two else 2
    here = number - 2 - begin
    near, refs = refs[:here], refs[here:]
    beside, refs = refs[:ends], refs[ends:]
    count = number - 1 if first else 1
    told, refs = refs[:count], refs[count:]
    low, high = updated(number, two, begin, part, far, asks, bands, sides, near, beside)
    lam, sends, refs = refs[0], refs[1 : 1 + number], refs[1 + number :]
    outer, refs = refs[:ends], refs[ends:]
    masks = told[0]
    if first:
        masks = refs[0]
        masks[...] = told[-1][...]
        for i in range(number - 2):
            masks[i : i + 1, :] = asks_of(told[i])[i : i + 1, :]
    rows = low.shape[0]
    lam[0:rows] = low.astype(BF16)
    lam[rows:] = high.astype(BF16)
    for i, send in enumerate(sends):
        send[...] = chosen(masks[i : i + 1, :], low, high)
    if two:
        outer[0][...] = chosen(asks[number : number + 1, :], high, low)
    else:
        outer[0][...] = high.astype(BF16)
        outer[1][...] = low.astype(BF16)


def last_kernel(number, two, begin, part, far, asks, bands, sides, factors, basis, *refs):
    here = number - 2 - begin
    near, beside, (lam, pieces) = refs[:here], refs[here:-2], refs[-2:]
    sums = updated(number, two, begin, part, far, asks, bands, sides, near, beside)
    phases, _, cells = factors.shape
    grads = []
    for d in range(2):
        rounded = sums[d].astype(BF16)
        lam[d] = rounded
        back = rounded.astype(F32)
        grad = back[:, :cells] * factors[0, d : d + 1, :]
        for p in range(1, phases):
            grad = grad + back[:, p * cells : (p + 1) * cells] * factors[p, d : d + 1, :]
        grads.append(grad)
    if two:
        half = grads[0].shape[0] // 2
        none = jnp.zeros((half, cells), F32)
        band = pieces.shape[1]
        for g in range(2):
            cuts = [grad[g * half : (g + 1) * half] for grad in grads]
            top = jnp.concatenate([x for cut in cuts for x in (cut, none)], axis=1)
            low = jnp.concatenate([x for cut in cuts for x in (none, cut)], axis=1)
            wing = jnp.concatenate([top, low], axis=0).astype(BF16)
            share = lax.dot_general(
                basis[...], wing, (((1,), (1,)), ((), ())), preferred_element_type=F32
            )
            for c in range(pieces.shape[0] // 2):
                pieces[2 * c + g] = share[c * band : (c + 1) * band].astype(BF16)
    else:
        terms = [dot(grad.astype(BF16), basis[d]) for d, grad in enumerate(grads)]
        pieces[...] = terms[0] + terms[1]


def sum_kernel(pieces, out):
    total = pieces[0].astype(F32)
    for i in range(1, pieces.shape[0]):
        total = total + pieces[i].astype(F32)
    half = total.shape[1] // 2
    out[...] = jnp.concatenate([total[:, :half], total[:, half:]], axis=0).astype(BF16)


def call(kernel, outs, ins, specs, scratch=(), flops=0, moved=0, out_specs=None):
    return pl.pallas_call(
        kernel,
        out_shape=outs,
        in_specs=specs,
        out_specs=out_specs or [VMEM] * len(outs),
        scratch_shapes=list(scratch),
        compiler_params=pltpu.CompilerParams(vmem_limit_bytes=LIMIT),
        cost_estimate=pl.CostEstimate(
            flops=flops, bytes_accessed=moved or flops // 200, transcendentals=0
        ),
    )(*ins)


def moved_by(x, pairs):
    return held(lax.ppermute(x, "areal", pairs))


def shift_pairs(columns, k):
    return [(i, (i - k) % columns) for i in range(columns)]


def beside_layers(tiles):
    groups = lax.axis_size("layer")
    if groups == 2:
        return [held(lax.ppermute(tiles[0], "layer", [(0, 1), (1, 0)]))]
    up = [(i, i + 1) for i in range(groups - 1)]
    down = [(i + 1, i) for i in range(groups - 1)]
    return [held(lax.ppermute(tiles[0], "layer", up)), held(lax.ppermute(tiles[-1], "layer", down))]


def outside(x):
    return pltpu.with_memory_space_constraint(x, pltpu.HBM)


def on_device(
    rhs,
    areal_blocks,
    vertical_blocks,
    conn_src,
    conn_count,
    tile_map,
    well_cells,
    well_gain,
    sens,
    basis,
):
    columns = lax.axis_size("areal")
    groups = lax.axis_size("layer")
    two = groups == 2
    rows, width = rhs.shape[2:]
    modes = basis.shape[-1]
    number = conn_src.shape[-1]
    swaps = near_swaps(number)
    routes = [swap_pairs(columns, k, color) for k, color in swaps]
    routes += [shift_pairs(columns, columns // 2 + 1), shift_pairs(columns, columns // 2)]
    rhs = rhs[0].reshape(2 * rows, width)
    me = lax.axis_index("areal").astype(jnp.int32).reshape(1)
    group = lax.axis_index("layer").astype(jnp.int32).reshape(1)

    tile = pltpu.VMEM((rows, width), BF16)
    pair = pltpu.VMEM((2 * rows, width), BF16)
    sums = pltpu.VMEM((2, rows, width), F32)
    one = 2 * rows * width * width
    partial = functools.partial

    masks_type = pltpu.VMEM((8, 128), F32)
    with jax.named_scope("plan"):
        table, asks, payload, both = call(
            partial(plan_kernel, columns, swaps),
            [
                jax.ShapeDtypeStruct((2 * number,), jnp.int32),
                masks_type,
                pltpu.VMEM((2 * rows + 16, width), BF16),
                pair,
            ],
            (outside(conn_src[0, 0]), conn_count[0], outside(tile_map), me, group, outside(rhs)),
            [SMEM] * 5 + [VMEM],
            out_specs=[SMEM] + [VMEM] * 3,
        )
        asks, payload, both = held(asks), held(payload), held(both)
        far_pair = moved_by(both, routes[-1])

    with jax.named_scope("load"):
        bands, sides = call(
            partial(load_kernel, number, two),
            [
                pltpu.VMEM((number, width, 2 * width), BF16),
                pltpu.VMEM((3 if two else 4, width, width), BF16),
            ],
            (table, group, outside(areal_blocks[0]), outside(vertical_blocks[0])),
            [SMEM] * 2 + [pl.BlockSpec(memory_space=pltpu.HBM)] * 2,
            [pltpu.SemaphoreType.DMA((2 * number + 4,))],
            moved=areal_blocks.size * 2 + vertical_blocks.size * 2,
        )
        bands, sides = held(bands), held(sides)
        (factors,) = call(
            weigh_kernel,
            [pltpu.VMEM((sens.shape[2], 2, sens.shape[3]), F32)],
            (well_cells[0], well_gain[0], sens[0].transpose(1, 0, 2)),
            [SMEM] * 2 + [VMEM],
        )
        weights = held(basis[0])
        if two:
            (weights,) = call(
                partial(turn_kernel, columns),
                [pltpu.VMEM((modes // 2, 4 * sens.shape[3]), BF16)],
                (basis[0],),
                [VMEM],
            )
        factors, weights = held(factors), held(weights)

    rhs_held = lam = both
    sends = [payload] * (number - 2)
    outer = [payload]
    half = len(swaps) // 2
    for step in range(ITERS):
        first = step == 0
        with jax.named_scope("apply"):
            arrived = [moved_by(x, pairs) for x, pairs in zip(sends, routes)]
            (part,) = call(own_kernel, [sums], (lam, rhs_held, sides), [VMEM] * 3, flops=one)
            part = held(part)
            if first:
                even, odd = (arrived[swaps.index((1, color))] for color in (1, 0))
                (relayed,) = call(
                    partial(relay_ask_kernel, number),
                    [masks_type],
                    (even, odd, asks),
                    [VMEM] * 3,
                    flops=4 * one,
                )
                relayed = held(relayed)
                (picked,) = call(
                    partial(far_pick_kernel, number),
                    [tile],
                    (far_pair, relayed, part, factors, weights),
                    [VMEM] * 5,
                )
                arrived = [*arrived, moved_by(picked, shift_pairs(columns, 1)), far_pair]
                told = [*arrived[:-2], moved_by(relayed, routes[-1])]
            beside = beside_layers(outer)
            (cross,) = call(
                cross_kernel,
                [sums],
                (asks, bands, *arrived[:half]),
                [VMEM] * (2 + half),
                flops=4 * one,
            )
            if first:
                (far,) = call(
                    far_kernel,
                    [sums],
                    (asks, bands, held(cross), *arrived[-2:]),
                    [VMEM] * 5,
                    flops=4 * one,
                )
            else:
                (nearer,) = call(
                    nearer_kernel,
                    [sums],
                    (asks, bands, arrived[-1]),
                    [VMEM] * 3,
                    flops=64 * one,
                )
                (far,) = call(
                    farther_kernel,
                    [sums],
                    (asks, bands, held(cross), held(nearer), arrived[-2]),
                    [VMEM] * 5,
                    flops=4 * one,
                )
            tiles = (part, held(far), asks, bands, sides)
            near = (*arrived[half:-2], *beside)
            if step < ITERS - 1:
                lam, *rest = call(
                    partial(update_kernel, number, two, half, first),
                    [pair] + [tile] * (number + len(beside)) + ([masks_type] if first else []),
                    (*tiles, *near, *told),
                    [VMEM] * (5 + len(near) + len(told)),
                    flops=one,
                )
                lam = held(lam)
                if first:
                    told = [held(rest.pop())]
                sends, outer = rest[:number], rest[number:]
            else:
                adjoint, pieces = call(
                    partial(last_kernel, number, two, half),
                    [
                        jax.ShapeDtypeStruct((2, rows, width), BF16),
                        pltpu.VMEM((2 * columns, modes // columns // 2, rows), BF16)
                        if two
                        else pltpu.VMEM((rows, modes), F32),
                    ],
                    (*tiles, factors, weights, *near),
                    [VMEM] * (7 + len(near)),
                    flops=one,
                )

    with jax.named_scope("project"):
        if two:
            landed = lax.all_to_all(pieces, ("areal", "layer"), 0, 0, tiled=True)
            (coefficients,) = call(
                sum_kernel,
                [jax.ShapeDtypeStruct((modes // columns, rows // 2), BF16)],
                (held(landed),),
                [VMEM],
            )
            coefficients = coefficients.T
        else:
            cut = pieces.reshape(groups, rows // groups, columns, modes // columns)
            cut = cut.transpose(2, 0, 1, 3).reshape(columns * groups, rows // groups, modes // columns)
            landed = lax.all_to_all(cut, ("areal", "layer"), 0, 0, tiled=True)
            coefficients = jnp.sum(landed, axis=0).astype(BF16)
    return (adjoint[None], coefficients)


def solution(mesh):
    in_specs = (
        P("areal", "layer", None, None),
        P("areal", "layer", None, None, None),
        P("areal", "layer", None, None, None),
        P("areal", "layer", None),
        P("areal", "layer"),
        P(),
        P("areal", "layer", None),
        P("areal", "layer", None),
        P("areal", "layer", None, None),
        P("areal", "layer", None, None),
    )
    out_specs = (P("areal", "layer", None, None), P("layer", "areal"))
    return jax.shard_map(
        on_device, mesh=mesh, in_specs=in_specs, out_specs=out_specs, check_vma=False
    )
```

```python
import functools

import jax
import jax.numpy as jnp
from jax import lax
from jax.experimental import pallas as pl
from jax.experimental.pallas import tpu as pltpu
from jax.sharding import PartitionSpec as P

ITERS = 3
F32 = jnp.float32
BF16 = jnp.bfloat16
SMEM = pl.BlockSpec(memory_space=pltpu.SMEM)
VMEM = pl.BlockSpec(memory_space=pltpu.VMEM)
LIMIT = 16 * 1024 * 1024


def near_swaps(count):
    return [(k, color) for color in (1, 0) for k in range(count // 2 - 1, 0, -1)]


def swap_pairs(columns, k, color):
    return [
        (c, (c + k if (c // k) % 2 == color else c - k) % columns) for c in range(columns)
    ]


def held(x):
    return pltpu.with_memory_space_constraint(x, pltpu.VMEM)


def dot(a, b):
    return jnp.dot(a, b, preferred_element_type=F32)


def plan_kernel(columns, swaps, src, count, tile_map, me, group, rhs, table, asks, payload, pair):
    steps = [
        jnp.where(lax.rem(lax.div(me[0], k), 2) == color, k, columns - k) for k, color in swaps
    ] + [columns // 2 + 1, columns // 2]
    number = len(steps)
    conn = [0] * number
    slots = [0] * number
    for s in range(number):
        place = tile_map[src[s]]
        peer = lax.shift_right_logical(place, 1)
        slot = lax.bitwise_and(place, 1)
        away = peer - me[0]
        away = jnp.where(away < 0, away + columns, away)
        for i, k in enumerate(steps):
            hit = away == k
            conn[i] = jnp.where(hit, s, conn[i])
            slots[i] = jnp.where(hit, slot, slots[i])
    rows, width = rhs.shape
    line = lax.broadcasted_iota(jnp.int32, (16, width), 0)
    asked = jnp.zeros(line.shape, F32)
    for i in range(number):
        table[i] = conn[i]
        table[number + i] = jnp.where(conn[i] < count[0], 1, 0)
        asked = jnp.where(line == i, slots[i].astype(F32), asked)
    asked = jnp.where(line == number, group[0].astype(F32), asked)
    asked = jnp.where(line == number + 1, lax.rem(me[0], 2).astype(F32), asked)
    asks[...] = asked[0:8, 0:128]
    payload[0:rows] = rhs[...]
    payload[rows:] = asked.astype(BF16)
    pair[...] = rhs[...]


def load_kernel(number, two, columns, table, group, wells, gains, blocks, vert, sens, basis, bands, sides, factors, turned, sems):
    width = vert.shape[-1]
    mine = group[0]
    ends = [(1 - mine, 1 - mine)] if two else [(0, 0), (1, 1)]
    beside = [
        pltpu.make_async_copy(vert.at[d, k], sides.at[i], sems.at[2 * number + i])
        for i, (d, k) in enumerate([(0, 1), (1, 0), *ends])
    ]
    for copy in beside:
        copy.start()

    def copies(i):
        return [
            pltpu.make_async_copy(
                blocks.at[d, table[i]],
                bands.at[i, :, pl.ds(d * width, width)],
                sems.at[2 * i + d],
            )
            for d in range(2)
        ]

    for i in range(number):

        @pl.when(table[number + i] > 0)
        def _():
            for copy in copies(i):
                copy.start()

        @pl.when(table[number + i] == 0)
        def _():
            bands[i] = jnp.zeros(bands.shape[1:], bands.dtype)

    weigh_kernel(wells, gains, sens, factors)
    if two:
        turn_kernel(columns, basis, turned)
    else:
        turned[...] = basis[...]

    for i in range(number):

        @pl.when(table[number + i] > 0)
        def _():
            for copy in copies(i):
                copy.wait()

    for copy in beside:
        copy.wait()


def turn_kernel(columns, basis, turned):
    _, cells, modes = basis.shape
    bands = []
    for d in range(2):
        by_mode = basis[d].astype(F32).T.reshape(columns, 2, modes // columns // 2, cells)
        bands += [by_mode[:, h].reshape(modes // 2, cells) for h in range(2)]
    turned[...] = jnp.concatenate(bands, axis=1).astype(BF16)


def weigh_kernel(wells, gains, sens, factors):
    cells = sens.shape[-1]
    spot = lax.broadcasted_iota(jnp.int32, (1, cells), 1)
    factors[...] = sens[...]
    for d in range(2):
        well = jnp.zeros((1, cells), F32)
        for w in range(wells.shape[1]):
            well = well + jnp.where(spot == wells[d, w], gains[d, w], 0.0)
        factors[0, d : d + 1, :] = sens[0, d : d + 1, :] + well


def wide(mask, width):
    return jnp.concatenate([mask] * (width // mask.shape[1]), axis=1)


def chosen(mask, low, high):
    return jnp.where(wide(mask, low.shape[1]) > 0.5, high, low).astype(BF16)


def asks_of(payload):
    return payload[payload.shape[0] - 16 :, 0:128].astype(F32)


def tile_of(ref, mask, rows):
    if ref.shape[0] == rows:
        return ref[...]
    return chosen(mask, ref[0:rows].astype(F32), ref[rows : 2 * rows].astype(F32))


def relay_ask_kernel(number, even, odd, asks, relayed):
    parity = asks[number + 1 : number + 2, :]
    ask = [asks_of(ref)[number - 2 : number - 1, :] for ref in (even, odd)]
    relayed[...] = asks[...]
    relayed[number - 2 : number - 1, :] = jnp.where(parity > 0.5, ask[1], ask[0])


def far_pick_kernel(number, pair, relayed, part, tile):
    tile[...] = tile_of(pair, relayed[number - 2 : number - 1, :], tile.shape[0])


def own_kernel(lam, rhs, sides, part):
    rows = rhs.shape[0] // 2
    part[0] = rhs[0:rows].astype(F32) - dot(lam[rows : 2 * rows], sides[0])
    part[1] = rhs[rows:].astype(F32) - dot(lam[0:rows], sides[1])


def source_sums(asks, bands, begin, refs, rows):
    tiles = [tile_of(ref, asks[i : i + 1, :], rows) for i, ref in enumerate(refs, begin)]
    count, width, both = len(refs), bands.shape[1], bands.shape[2]
    band = bands[begin : begin + count].reshape(count * width, both)
    sums = dot(jnp.concatenate(tiles, axis=1), band)
    return sums[:, :width], sums[:, width:]


def beside_sums(number, two, asks, sides, beside, rows):
    if two:
        mine = asks[number : number + 1, :]
        term = dot(tile_of(beside[0], mine, rows), sides[2])
        above = wide(mine, term.shape[1]) > 0.5
        none = jnp.zeros_like(term)
        return jnp.where(above, term, none), jnp.where(above, none, term)
    return [
        dot(tile_of(beside[d], jnp.full((1, 128), 1.0 - d, F32), rows), sides[2 + d])
        for d in range(2)
    ]


def cross_kernel(asks, bands, *refs):
    arrived, out = refs[:-1], refs[-1]
    out[0], out[1] = source_sums(asks, bands, 0, arrived, out.shape[1])


def nearer_kernel(asks, bands, pair, out):
    out[0], out[1] = source_sums(asks, bands, bands.shape[0] - 1, [pair], out.shape[1])


def farther_kernel(asks, bands, cross, nearer, passed, out):
    sums = source_sums(asks, bands, bands.shape[0] - 2, [passed], out.shape[1])
    for d in range(2):
        out[d] = cross[d] + nearer[d] + sums[d]


def far_kernel(asks, bands, cross, *refs):
    far, out = refs[:-1], refs[-1]
    low, high = source_sums(asks, bands, bands.shape[0] - len(far), far, out.shape[1])
    out[0] = cross[0] + low
    out[1] = cross[1] + high


def updated(number, two, begin, part, far, asks, bands, sides, near, beside):
    rows = part.shape[1]
    sums = source_sums(asks, bands, begin, near, rows)
    terms = beside_sums(number, two, asks, sides, beside, rows)
    return [part[d] - far[d] - sums[d] - terms[d] for d in range(2)]


def update_kernel(number, two, begin, first, part, far, asks, bands, sides, *refs):
    ends = 1 if two else 2
    here = number - 2 - begin
    near, refs = refs[:here], refs[here:]
    beside, refs = refs[:ends], refs[ends:]
    count = number - 1 if first else 1
    told, refs = refs[:count], refs[count:]
    low, high = updated(number, two, begin, part, far, asks, bands, sides, near, beside)
    lam, sends, refs = refs[0], refs[1 : 1 + number], refs[1 + number :]
    outer, refs = refs[:ends], refs[ends:]
    masks = told[0]
    if first:
        masks = refs[0]
        masks[...] = told[-1][...]
        for i in range(number - 2):
            masks[i : i + 1, :] = asks_of(told[i])[i : i + 1, :]
    rows = low.shape[0]
    lam[0:rows] = low.astype(BF16)
    lam[rows:] = high.astype(BF16)
    for i, send in enumerate(sends):
        send[...] = chosen(masks[i : i + 1, :], low, high)
    if two:
        outer[0][...] = chosen(asks[number : number + 1, :], high, low)
    else:
        outer[0][...] = high.astype(BF16)
        outer[1][...] = low.astype(BF16)


def last_kernel(number, two, begin, part, far, asks, bands, sides, factors, basis, *refs):
    here = number - 2 - begin
    near, beside, (lam, pieces) = refs[:here], refs[here:-2], refs[-2:]
    sums = updated(number, two, begin, part, far, asks, bands, sides, near, beside)
    phases, _, cells = factors.shape
    grads = []
    for d in range(2):
        rounded = sums[d].astype(BF16)
        lam[d] = rounded
        back = rounded.astype(F32)
        grad = back[:, :cells] * factors[0, d : d + 1, :]
        for p in range(1, phases):
            grad = grad + back[:, p * cells : (p + 1) * cells] * factors[p, d : d + 1, :]
        grads.append(grad)
    if two:
        half = grads[0].shape[0] // 2
        none = jnp.zeros((half, cells), F32)
        band = pieces.shape[1]
        for g in range(2):
            cuts = [grad[g * half : (g + 1) * half] for grad in grads]
            top = jnp.concatenate([x for cut in cuts for x in (cut, none)], axis=1)
            low = jnp.concatenate([x for cut in cuts for x in (none, cut)], axis=1)
            wing = jnp.concatenate([top, low], axis=0).astype(BF16)
            share = lax.dot_general(
                basis[...], wing, (((1,), (1,)), ((), ())), preferred_element_type=F32
            )
            for c in range(pieces.shape[0] // 2):
                pieces[2 * c + g] = share[c * band : (c + 1) * band].astype(BF16)
    else:
        terms = [dot(grad.astype(BF16), basis[d]) for d, grad in enumerate(grads)]
        pieces[...] = terms[0] + terms[1]


def sum_kernel(pieces, out):
    total = pieces[0].astype(F32)
    for i in range(1, pieces.shape[0]):
        total = total + pieces[i].astype(F32)
    half = total.shape[1] // 2
    out[...] = jnp.concatenate([total[:, :half], total[:, half:]], axis=0).astype(BF16)


def call(kernel, outs, ins, specs, scratch=(), flops=0, moved=0, out_specs=None):
    return pl.pallas_call(
        kernel,
        out_shape=outs,
        in_specs=specs,
        out_specs=out_specs or [VMEM] * len(outs),
        scratch_shapes=list(scratch),
        compiler_params=pltpu.CompilerParams(vmem_limit_bytes=LIMIT),
        cost_estimate=pl.CostEstimate(
            flops=flops, bytes_accessed=moved or flops // 200, transcendentals=0
        ),
    )(*ins)


def moved_by(x, pairs):
    return held(lax.ppermute(x, "areal", pairs))


def shift_pairs(columns, k):
    return [(i, (i - k) % columns) for i in range(columns)]


def beside_layers(tiles):
    groups = lax.axis_size("layer")
    if groups == 2:
        return [held(lax.ppermute(tiles[0], "layer", [(0, 1), (1, 0)]))]
    up = [(i, i + 1) for i in range(groups - 1)]
    down = [(i + 1, i) for i in range(groups - 1)]
    return [held(lax.ppermute(tiles[0], "layer", up)), held(lax.ppermute(tiles[-1], "layer", down))]


def outside(x):
    return pltpu.with_memory_space_constraint(x, pltpu.HBM)


def on_device(
    rhs,
    areal_blocks,
    vertical_blocks,
    conn_src,
    conn_count,
    tile_map,
    well_cells,
    well_gain,
    sens,
    basis,
):
    columns = lax.axis_size("areal")
    groups = lax.axis_size("layer")
    two = groups == 2
    rows, width = rhs.shape[2:]
    modes = basis.shape[-1]
    number = conn_src.shape[-1]
    swaps = near_swaps(number)
    routes = [swap_pairs(columns, k, color) for k, color in swaps]
    routes += [shift_pairs(columns, columns // 2 + 1), shift_pairs(columns, columns // 2)]
    rhs = rhs[0].reshape(2 * rows, width)
    me = lax.axis_index("areal").astype(jnp.int32).reshape(1)
    group = lax.axis_index("layer").astype(jnp.int32).reshape(1)

    tile = pltpu.VMEM((rows, width), BF16)
    pair = pltpu.VMEM((2 * rows, width), BF16)
    sums = pltpu.VMEM((2, rows, width), F32)
    one = 2 * rows * width * width
    partial = functools.partial

    masks_type = pltpu.VMEM((8, 128), F32)
    with jax.named_scope("plan"):
        table, asks, payload, both = call(
            partial(plan_kernel, columns, swaps),
            [
                jax.ShapeDtypeStruct((2 * number,), jnp.int32),
                masks_type,
                pltpu.VMEM((2 * rows + 16, width), BF16),
                pair,
            ],
            (outside(conn_src[0, 0]), conn_count[0], outside(tile_map), me, group, outside(rhs)),
            [SMEM] * 5 + [VMEM],
            out_specs=[SMEM] + [VMEM] * 3,
        )
        asks, payload, both = held(asks), held(payload), held(both)
        far_pair = moved_by(both, routes[-1])

    with jax.named_scope("load"):
        cells = sens.shape[-1]
        bands, sides, factors, weights = call(
            partial(load_kernel, number, two, columns),
            [
                pltpu.VMEM((number, width, 2 * width), BF16),
                pltpu.VMEM((3 if two else 4, width, width), BF16),
                pltpu.VMEM((sens.shape[2], 2, cells), F32),
                pltpu.VMEM((modes // 2, 4 * cells) if two else basis.shape[1:], BF16),
            ],
            (
                table,
                group,
                well_cells[0],
                well_gain[0],
                outside(areal_blocks[0]),
                outside(vertical_blocks[0]),
                sens[0].transpose(1, 0, 2),
                basis[0],
            ),
            [SMEM] * 4 + [pl.BlockSpec(memory_space=pltpu.HBM)] * 2 + [VMEM] * 2,
            [pltpu.SemaphoreType.DMA((2 * number + 4,))],
            moved=areal_blocks.size * 2 + vertical_blocks.size * 2,
        )
        bands, sides = held(bands), held(sides)
        factors, weights = held(factors), held(weights)

    rhs_held = lam = both
    sends = [payload] * (number - 2)
    outer = [payload]
    half = len(swaps) // 2
    for step in range(ITERS):
        first = step == 0
        with jax.named_scope("apply"):
            arrived = [moved_by(x, pairs) for x, pairs in zip(sends, routes)]
            (part,) = call(own_kernel, [sums], (lam, rhs_held, sides), [VMEM] * 3, flops=one)
            part = held(part)
            if first:
                even, odd = (arrived[swaps.index((1, color))] for color in (1, 0))
                (relayed,) = call(
                    partial(relay_ask_kernel, number),
                    [masks_type],
                    (even, odd, asks),
                    [VMEM] * 3,
                    flops=4 * one,
                )
                relayed = held(relayed)
                (picked,) = call(
                    partial(far_pick_kernel, number),
                    [tile],
                    (far_pair, relayed, part),
                    [VMEM] * 3,
                )
                arrived = [*arrived, moved_by(picked, shift_pairs(columns, 1)), far_pair]
                told = [*arrived[:-2], moved_by(relayed, routes[-1])]
            beside = beside_layers(outer)
            (cross,) = call(
                cross_kernel,
                [sums],
                (asks, bands, *arrived[:half]),
                [VMEM] * (2 + half),
                flops=4 * one,
            )
            if first:
                (far,) = call(
                    far_kernel,
                    [sums],
                    (asks, bands, held(cross), *arrived[-2:]),
                    [VMEM] * 5,
                    flops=4 * one,
                )
            else:
                (nearer,) = call(
                    nearer_kernel,
                    [sums],
                    (asks, bands, arrived[-1]),
                    [VMEM] * 3,
                    flops=64 * one,
                )
                (far,) = call(
                    farther_kernel,
                    [sums],
                    (asks, bands, held(cross), held(nearer), arrived[-2]),
                    [VMEM] * 5,
                    flops=4 * one,
                )
            tiles = (part, held(far), asks, bands, sides)
            near = (*arrived[half:-2], *beside)
            if step < ITERS - 1:
                lam, *rest = call(
                    partial(update_kernel, number, two, half, first),
                    [pair] + [tile] * (number + len(beside)) + ([masks_type] if first else []),
                    (*tiles, *near, *told),
                    [VMEM] * (5 + len(near) + len(told)),
                    flops=one,
                )
                lam = held(lam)
                if first:
                    told = [held(rest.pop())]
                sends, outer = rest[:number], rest[number:]
            else:
                adjoint, pieces = call(
                    partial(last_kernel, number, two, half),
                    [
                        jax.ShapeDtypeStruct((2, rows, width), BF16),
                        pltpu.VMEM((2 * columns, modes // columns // 2, rows), BF16)
                        if two
                        else pltpu.VMEM((rows, modes), F32),
                    ],
                    (*tiles, factors, weights, *near),
                    [VMEM] * (7 + len(near)),
                    flops=one,
                )

    with jax.named_scope("project"):
        if two:
            landed = lax.all_to_all(pieces, ("areal", "layer"), 0, 0, tiled=True)
            (coefficients,) = call(
                sum_kernel,
                [jax.ShapeDtypeStruct((modes // columns, rows // 2), BF16)],
                (held(landed),),
                [VMEM],
            )
            coefficients = coefficients.T
        else:
            cut = pieces.reshape(groups, rows // groups, columns, modes // columns)
            cut = cut.transpose(2, 0, 1, 3).reshape(columns * groups, rows // groups, modes // columns)
            landed = lax.all_to_all(cut, ("areal", "layer"), 0, 0, tiled=True)
            coefficients = jnp.sum(landed, axis=0).astype(BF16)
    return (adjoint[None], coefficients)


def solution(mesh):
    in_specs = (
        P("areal", "layer", None, None),
        P("areal", "layer", None, None, None),
        P("areal", "layer", None, None, None),
        P("areal", "layer", None),
        P("areal", "layer"),
        P(),
        P("areal", "layer", None),
        P("areal", "layer", None),
        P("areal", "layer", None, None),
        P("areal", "layer", None, None),
    )
    out_specs = (P("areal", "layer", None, None), P("layer", "areal"))
    return jax.shard_map(
        on_device, mesh=mesh, in_specs=in_specs, out_specs=out_specs, check_vma=False
    )
```

```python
import functools

import jax
import jax.numpy as jnp
from jax import lax
from jax.experimental import pallas as pl
from jax.experimental.pallas import tpu as pltpu
from jax.sharding import PartitionSpec as P

ITERS = 3
F32 = jnp.float32
BF16 = jnp.bfloat16
SMEM = pl.BlockSpec(memory_space=pltpu.SMEM)
VMEM = pl.BlockSpec(memory_space=pltpu.VMEM)
LIMIT = 16 * 1024 * 1024


def near_swaps(count):
    return [(k, color) for color in (1, 0) for k in range(count // 2 - 1, 0, -1)]


def swap_pairs(columns, k, color):
    return [
        (c, (c + k if (c // k) % 2 == color else c - k) % columns) for c in range(columns)
    ]


def held(x):
    return pltpu.with_memory_space_constraint(x, pltpu.VMEM)


def dot(a, b):
    return jnp.dot(a, b, preferred_element_type=F32)


def plan_kernel(columns, swaps, src, count, tile_map, me, group, rhs, table, asks, payload, pair):
    steps = [
        jnp.where(lax.rem(lax.div(me[0], k), 2) == color, k, columns - k) for k, color in swaps
    ] + [columns // 2 + 1, columns // 2]
    number = len(steps)
    conn = [0] * number
    slots = [0] * number
    for s in range(number):
        place = tile_map[src[s]]
        peer = lax.shift_right_logical(place, 1)
        slot = lax.bitwise_and(place, 1)
        away = peer - me[0]
        away = jnp.where(away < 0, away + columns, away)
        for i, k in enumerate(steps):
            hit = away == k
            conn[i] = jnp.where(hit, s, conn[i])
            slots[i] = jnp.where(hit, slot, slots[i])
    rows, width = rhs.shape
    line = lax.broadcasted_iota(jnp.int32, (16, width), 0)
    asked = jnp.zeros(line.shape, F32)
    for i in range(number):
        table[i] = conn[i]
        table[number + i] = jnp.where(conn[i] < count[0], 1, 0)
        asked = jnp.where(line == i, slots[i].astype(F32), asked)
    asked = jnp.where(line == number, group[0].astype(F32), asked)
    asked = jnp.where(line == number + 1, lax.rem(me[0], 2).astype(F32), asked)
    asks[...] = asked[0:8, 0:128]
    payload[0:rows] = rhs[...]
    payload[rows:] = asked.astype(BF16)
    pair[...] = rhs[...]


def load_kernel(number, two, table, group, blocks, vert, bands, sides, sems):
    width = vert.shape[-1]
    mine = group[0]
    ends = [(1 - mine, 1 - mine)] if two else [(0, 0), (1, 1)]
    beside = [
        pltpu.make_async_copy(vert.at[d, k], sides.at[i], sems.at[2 * number + i])
        for i, (d, k) in enumerate([(0, 1), (1, 0), *ends])
    ]
    for copy in beside:
        copy.start()

    def copies(i):
        return [
            pltpu.make_async_copy(
                blocks.at[d, table[i]],
                bands.at[i, :, pl.ds(d * width, width)],
                sems.at[2 * i + d],
            )
            for d in range(2)
        ]

    for i in range(number):

        @pl.when(table[number + i] > 0)
        def _():
            for copy in copies(i):
                copy.start()

        @pl.when(table[number + i] == 0)
        def _():
            bands[i] = jnp.zeros(bands.shape[1:], bands.dtype)

    for i in range(number):

        @pl.when(table[number + i] > 0)
        def _():
            for copy in copies(i):
                copy.wait()

    for copy in beside:
        copy.wait()


def turn_kernel(columns, basis, turned):
    _, cells, modes = basis.shape
    bands = []
    for d in range(2):
        by_mode = basis[d].astype(F32).T.reshape(columns, 2, modes // columns // 2, cells)
        bands += [by_mode[:, h].reshape(modes // 2, cells) for h in range(2)]
    turned[...] = jnp.concatenate(bands, axis=1).astype(BF16)


def weigh_kernel(wells, gains, sens, factors):
    cells = sens.shape[-1]
    spot = lax.broadcasted_iota(jnp.int32, (1, cells), 1)
    factors[...] = sens[...]
    for d in range(2):
        well = jnp.zeros((1, cells), F32)
        for w in range(wells.shape[1]):
            well = well + jnp.where(spot == wells[d, w], gains[d, w], 0.0)
        factors[0, d : d + 1, :] = sens[0, d : d + 1, :] + well


def wide(mask, width):
    return jnp.concatenate([mask] * (width // mask.shape[1]), axis=1)


def chosen(mask, low, high):
    return jnp.where(wide(mask, low.shape[1]) > 0.5, high, low).astype(BF16)


def asks_of(payload):
    return payload[payload.shape[0] - 16 :, 0:128].astype(F32)


def tile_of(ref, mask, rows):
    if ref.shape[0] == rows:
        return ref[...]
    return chosen(mask, ref[0:rows].astype(F32), ref[rows : 2 * rows].astype(F32))


def relay_ask_kernel(number, even, odd, asks, relayed):
    parity = asks[number + 1 : number + 2, :]
    ask = [asks_of(ref)[number - 2 : number - 1, :] for ref in (even, odd)]
    relayed[...] = asks[...]
    relayed[number - 2 : number - 1, :] = jnp.where(parity > 0.5, ask[1], ask[0])


def far_pick_kernel(number, pair, relayed, part, tile):
    tile[...] = tile_of(pair, relayed[number - 2 : number - 1, :], tile.shape[0])


def own_kernel(lam, rhs, sides, part):
    rows = rhs.shape[0] // 2
    part[0] = rhs[0:rows].astype(F32) - dot(lam[rows : 2 * rows], sides[0])
    part[1] = rhs[rows:].astype(F32) - dot(lam[0:rows], sides[1])


def source_sums(asks, bands, begin, refs, rows):
    tiles = [tile_of(ref, asks[i : i + 1, :], rows) for i, ref in enumerate(refs, begin)]
    count, width, both = len(refs), bands.shape[1], bands.shape[2]
    band = bands[begin : begin + count].reshape(count * width, both)
    sums = dot(jnp.concatenate(tiles, axis=1), band)
    return sums[:, :width], sums[:, width:]


def beside_sums(number, two, asks, sides, beside, rows):
    if two:
        mine = asks[number : number + 1, :]
        term = dot(tile_of(beside[0], mine, rows), sides[2])
        above = wide(mine, term.shape[1]) > 0.5
        none = jnp.zeros_like(term)
        return jnp.where(above, term, none), jnp.where(above, none, term)
    return [
        dot(tile_of(beside[d], jnp.full((1, 128), 1.0 - d, F32), rows), sides[2 + d])
        for d in range(2)
    ]


def cross_kernel(asks, bands, factors, weights, *refs):
    arrived, out = refs[:-1], refs[-1]
    out[0], out[1] = source_sums(asks, bands, 0, arrived, out.shape[1])


def nearer_kernel(asks, bands, pair, out):
    out[0], out[1] = source_sums(asks, bands, bands.shape[0] - 1, [pair], out.shape[1])


def farther_kernel(asks, bands, cross, nearer, passed, out):
    sums = source_sums(asks, bands, bands.shape[0] - 2, [passed], out.shape[1])
    for d in range(2):
        out[d] = cross[d] + nearer[d] + sums[d]


def far_kernel(asks, bands, cross, *refs):
    far, out = refs[:-1], refs[-1]
    low, high = source_sums(asks, bands, bands.shape[0] - len(far), far, out.shape[1])
    out[0] = cross[0] + low
    out[1] = cross[1] + high


def updated(number, two, begin, part, far, asks, bands, sides, near, beside):
    rows = part.shape[1]
    sums = source_sums(asks, bands, begin, near, rows)
    terms = beside_sums(number, two, asks, sides, beside, rows)
    return [part[d] - far[d] - sums[d] - terms[d] for d in range(2)]


def update_kernel(number, two, begin, first, part, far, asks, bands, sides, *refs):
    ends = 1 if two else 2
    here = number - 2 - begin
    near, refs = refs[:here], refs[here:]
    beside, refs = refs[:ends], refs[ends:]
    count = number - 1 if first else 1
    told, refs = refs[:count], refs[count:]
    low, high = updated(number, two, begin, part, far, asks, bands, sides, near, beside)
    lam, sends, refs = refs[0], refs[1 : 1 + number], refs[1 + number :]
    outer, refs = refs[:ends], refs[ends:]
    masks = told[0]
    if first:
        masks = refs[0]
        masks[...] = told[-1][...]
        for i in range(number - 2):
            masks[i : i + 1, :] = asks_of(told[i])[i : i + 1, :]
    rows = low.shape[0]
    lam[0:rows] = low.astype(BF16)
    lam[rows:] = high.astype(BF16)
    for i, send in enumerate(sends):
        send[...] = chosen(masks[i : i + 1, :], low, high)
    if two:
        outer[0][...] = chosen(asks[number : number + 1, :], high, low)
    else:
        outer[0][...] = high.astype(BF16)
        outer[1][...] = low.astype(BF16)


def last_kernel(number, two, begin, part, far, asks, bands, sides, factors, basis, *refs):
    here = number - 2 - begin
    near, beside, (lam, pieces) = refs[:here], refs[here:-2], refs[-2:]
    sums = updated(number, two, begin, part, far, asks, bands, sides, near, beside)
    phases, _, cells = factors.shape
    grads = []
    for d in range(2):
        rounded = sums[d].astype(BF16)
        lam[d] = rounded
        back = rounded.astype(F32)
        grad = back[:, :cells] * factors[0, d : d + 1, :]
        for p in range(1, phases):
            grad = grad + back[:, p * cells : (p + 1) * cells] * factors[p, d : d + 1, :]
        grads.append(grad)
    if two:
        half = grads[0].shape[0] // 2
        none = jnp.zeros((half, cells), F32)
        band = pieces.shape[1]
        for g in range(2):
            cuts = [grad[g * half : (g + 1) * half] for grad in grads]
            top = jnp.concatenate([x for cut in cuts for x in (cut, none)], axis=1)
            low = jnp.concatenate([x for cut in cuts for x in (none, cut)], axis=1)
            wing = jnp.concatenate([top, low], axis=0).astype(BF16)
            share = lax.dot_general(
                basis[...], wing, (((1,), (1,)), ((), ())), preferred_element_type=F32
            )
            for c in range(pieces.shape[0] // 2):
                pieces[2 * c + g] = share[c * band : (c + 1) * band].astype(BF16)
    else:
        terms = [dot(grad.astype(BF16), basis[d]) for d, grad in enumerate(grads)]
        pieces[...] = terms[0] + terms[1]


def sum_kernel(pieces, out):
    total = pieces[0].astype(F32)
    for i in range(1, pieces.shape[0]):
        total = total + pieces[i].astype(F32)
    half = total.shape[1] // 2
    out[...] = jnp.concatenate([total[:, :half], total[:, half:]], axis=0).astype(BF16)


def call(kernel, outs, ins, specs, scratch=(), flops=0, moved=0, out_specs=None):
    return pl.pallas_call(
        kernel,
        out_shape=outs,
        in_specs=specs,
        out_specs=out_specs or [VMEM] * len(outs),
        scratch_shapes=list(scratch),
        compiler_params=pltpu.CompilerParams(vmem_limit_bytes=LIMIT),
        cost_estimate=pl.CostEstimate(
            flops=flops, bytes_accessed=moved or flops // 200, transcendentals=0
        ),
    )(*ins)


def moved_by(x, pairs):
    return held(lax.ppermute(x, "areal", pairs))


def shift_pairs(columns, k):
    return [(i, (i - k) % columns) for i in range(columns)]


def beside_layers(tiles):
    groups = lax.axis_size("layer")
    if groups == 2:
        return [held(lax.ppermute(tiles[0], "layer", [(0, 1), (1, 0)]))]
    up = [(i, i + 1) for i in range(groups - 1)]
    down = [(i + 1, i) for i in range(groups - 1)]
    return [held(lax.ppermute(tiles[0], "layer", up)), held(lax.ppermute(tiles[-1], "layer", down))]


def outside(x):
    return pltpu.with_memory_space_constraint(x, pltpu.HBM)


def on_device(
    rhs,
    areal_blocks,
    vertical_blocks,
    conn_src,
    conn_count,
    tile_map,
    well_cells,
    well_gain,
    sens,
    basis,
):
    columns = lax.axis_size("areal")
    groups = lax.axis_size("layer")
    two = groups == 2
    rows, width = rhs.shape[2:]
    modes = basis.shape[-1]
    number = conn_src.shape[-1]
    swaps = near_swaps(number)
    routes = [swap_pairs(columns, k, color) for k, color in swaps]
    routes += [shift_pairs(columns, columns // 2 + 1), shift_pairs(columns, columns // 2)]
    rhs = rhs[0].reshape(2 * rows, width)
    me = lax.axis_index("areal").astype(jnp.int32).reshape(1)
    group = lax.axis_index("layer").astype(jnp.int32).reshape(1)

    tile = pltpu.VMEM((rows, width), BF16)
    pair = pltpu.VMEM((2 * rows, width), BF16)
    sums = pltpu.VMEM((2, rows, width), F32)
    one = 2 * rows * width * width
    partial = functools.partial

    masks_type = pltpu.VMEM((8, 128), F32)
    with jax.named_scope("plan"):
        table, asks, payload, both = call(
            partial(plan_kernel, columns, swaps),
            [
                jax.ShapeDtypeStruct((2 * number,), jnp.int32),
                masks_type,
                pltpu.VMEM((2 * rows + 16, width), BF16),
                pair,
            ],
            (outside(conn_src[0, 0]), conn_count[0], outside(tile_map), me, group, outside(rhs)),
            [SMEM] * 5 + [VMEM],
            out_specs=[SMEM] + [VMEM] * 3,
        )
        asks, payload, both = held(asks), held(payload), held(both)
        far_pair = moved_by(both, routes[-1])

    with jax.named_scope("load"):
        bands, sides = call(
            partial(load_kernel, number, two),
            [
                pltpu.VMEM((number, width, 2 * width), BF16),
                pltpu.VMEM((3 if two else 4, width, width), BF16),
            ],
            (table, group, outside(areal_blocks[0]), outside(vertical_blocks[0])),
            [SMEM] * 2 + [pl.BlockSpec(memory_space=pltpu.HBM)] * 2,
            [pltpu.SemaphoreType.DMA((2 * number + 4,))],
            moved=areal_blocks.size * 2 + vertical_blocks.size * 2,
        )
        bands, sides = held(bands), held(sides)
        (factors,) = call(
            weigh_kernel,
            [pltpu.VMEM((sens.shape[2], 2, sens.shape[3]), F32)],
            (well_cells[0], well_gain[0], sens[0].transpose(1, 0, 2)),
            [SMEM] * 2 + [VMEM],
        )
        weights = held(basis[0])
        if two:
            (weights,) = call(
                partial(turn_kernel, columns),
                [pltpu.VMEM((modes // 2, 4 * sens.shape[3]), BF16)],
                (basis[0],),
                [VMEM],
            )
        factors, weights = held(factors), held(weights)

    rhs_held = lam = both
    sends = [payload] * (number - 2)
    outer = [payload]
    half = len(swaps) // 2
    for step in range(ITERS):
        first = step == 0
        with jax.named_scope("apply"):
            arrived = [moved_by(x, pairs) for x, pairs in zip(sends, routes)]
            (part,) = call(own_kernel, [sums], (lam, rhs_held, sides), [VMEM] * 3, flops=one)
            part = held(part)
            if first:
                even, odd = (arrived[swaps.index((1, color))] for color in (1, 0))
                (relayed,) = call(
                    partial(relay_ask_kernel, number),
                    [masks_type],
                    (even, odd, asks),
                    [VMEM] * 3,
                    flops=4 * one,
                )
                relayed = held(relayed)
                (picked,) = call(
                    partial(far_pick_kernel, number),
                    [tile],
                    (far_pair, relayed, part),
                    [VMEM] * 3,
                )
                arrived = [*arrived, moved_by(picked, shift_pairs(columns, 1)), far_pair]
                told = [*arrived[:-2], moved_by(relayed, routes[-1])]
            beside = beside_layers(outer)
            (cross,) = call(
                cross_kernel,
                [sums],
                (asks, bands, factors, weights, *arrived[:half]),
                [VMEM] * (4 + half),
                flops=4 * one,
            )
            if first:
                (far,) = call(
                    far_kernel,
                    [sums],
                    (asks, bands, held(cross), *arrived[-2:]),
                    [VMEM] * 5,
                    flops=4 * one,
                )
            else:
                (nearer,) = call(
                    nearer_kernel,
                    [sums],
                    (asks, bands, arrived[-1]),
                    [VMEM] * 3,
                    flops=64 * one,
                )
                (far,) = call(
                    farther_kernel,
                    [sums],
                    (asks, bands, held(cross), held(nearer), arrived[-2]),
                    [VMEM] * 5,
                    flops=4 * one,
                )
            tiles = (part, held(far), asks, bands, sides)
            near = (*arrived[half:-2], *beside)
            if step < ITERS - 1:
                lam, *rest = call(
                    partial(update_kernel, number, two, half, first),
                    [pair] + [tile] * (number + len(beside)) + ([masks_type] if first else []),
                    (*tiles, *near, *told),
                    [VMEM] * (5 + len(near) + len(told)),
                    flops=one,
                )
                lam = held(lam)
                if first:
                    told = [held(rest.pop())]
                sends, outer = rest[:number], rest[number:]
            else:
                adjoint, pieces = call(
                    partial(last_kernel, number, two, half),
                    [
                        jax.ShapeDtypeStruct((2, rows, width), BF16),
                        pltpu.VMEM((2 * columns, modes // columns // 2, rows), BF16)
                        if two
                        else pltpu.VMEM((rows, modes), F32),
                    ],
                    (*tiles, factors, weights, *near),
                    [VMEM] * (7 + len(near)),
                    flops=one,
                )

    with jax.named_scope("project"):
        if two:
            landed = lax.all_to_all(pieces, ("areal", "layer"), 0, 0, tiled=True)
            (coefficients,) = call(
                sum_kernel,
                [jax.ShapeDtypeStruct((modes // columns, rows // 2), BF16)],
                (held(landed),),
                [VMEM],
            )
            coefficients = coefficients.T
        else:
            cut = pieces.reshape(groups, rows // groups, columns, modes // columns)
            cut = cut.transpose(2, 0, 1, 3).reshape(columns * groups, rows // groups, modes // columns)
            landed = lax.all_to_all(cut, ("areal", "layer"), 0, 0, tiled=True)
            coefficients = jnp.sum(landed, axis=0).astype(BF16)
    return (adjoint[None], coefficients)


def solution(mesh):
    in_specs = (
        P("areal", "layer", None, None),
        P("areal", "layer", None, None, None),
        P("areal", "layer", None, None, None),
        P("areal", "layer", None),
        P("areal", "layer"),
        P(),
        P("areal", "layer", None),
        P("areal", "layer", None),
        P("areal", "layer", None, None),
        P("areal", "layer", None, None),
    )
    out_specs = (P("areal", "layer", None, None), P("layer", "areal"))
    return jax.shard_map(
        on_device, mesh=mesh, in_specs=in_specs, out_specs=out_specs, check_vma=False
    )
```
